32 devices in a mesh: seq: 2 (over core), wide: 16 (over z, y, x).
Axes of the slice: x: 2, y: 2, z: 4, core: 2. Of those that a mesh axis runs over, the one named last changes fastest.
Arguments:
- streams: bfloat16 [16, 1024, 4, 768], P('wide', 'seq'), may hold values from -6 to 6
- cotangent: bfloat16 [16, 1024, 4, 768], P('wide', 'seq'), may hold values from -6 to 6
- doc_lengths: int32 [16, 8], P('wide'), may hold values from 1 to 768, as said below
- attn_in: bfloat16 [768, 2304], replicated, may hold values from -0.21875 to 0.21875
- attn_out: bfloat16 [768, 768], replicated, may hold values from -0.625 to 0.625
- ffn_in: bfloat16 [768, 6144], replicated, may hold values from -0.21875 to 0.21875
- ffn_out: bfloat16 [3072, 768], replicated, may hold values from -0.109375 to 0.109375
- norm_gains: bfloat16 [768, 2], replicated, may hold values from 0.5 to 1.5
- big_state: float32 [3, 12288, 768], P(None, ('seq', 'wide'))
- small_state: float32 [3, 1568], replicated
Outputs:
- new_streams: bfloat16 [16, 1024, 4, 768], P('wide', 'seq')
- streams_grad: bfloat16 [16, 1024, 4, 768], P('wide', 'seq')
- weights_next: float32 [12288, 768], P(('seq', 'wide'))
- first_next: float32 [12288, 768], P(('seq', 'wide'))
- second_next: float32 [12288, 768], P(('seq', 'wide'))
- weight_grads: float32 [12288, 768], P(('seq', 'wide'))
- small_weights_next: float32 [1568], replicated
- small_first_next: float32 [1568], replicated
- small_second_next: float32 [1568], replicated
- small_grads: float32 [1568], replicated
- weights_copy: bfloat16 [12288, 768], replicated
- gains_copy: bfloat16 [768, 2], replicated
The draws below stay inside these ranges and needn't reach their ends.
Inputs may be any that keep to these rules, and one draw needn't show every extreme that they name: `doc_lengths`: each row sums to 1024; in every sequence the fourth document covers the positions 128 to 895, the documents before it lie within the first 128 positions, those after it within the last 128, and the last document holds one token.
All inputs are finite; a program needn't handle non-finite values.
Results may differ from the reference program's by a relative error of at most 0.013.
Values may be sent and summed in bfloat16 or wider, within the bound.
A program may use at most 256 MiB of HBM per device.

```python
import math
import jax
import jax.numpy as jnp
from jax import lax

D = 768
HEADS = 12
HD = 64
FF = 3072
NS = 4
DOCS = 8
STEP = 10
LENGTH = 1024
SEQS = 16
TOKENS = 16384
ROWS = 12288
SMALL = 1568


def distinct_sorted(key, wanted, span):
    chosen = jnp.sort(jax.random.randint(key, (SEQS, wanted), 0, span - wanted + 1), axis=1)
    return (chosen + jnp.arange(wanted, dtype=jnp.int32)[None, :]).astype(jnp.int32)


def draw_doc_lengths(key, part):
    key = jax.random.fold_in(key, 11)
    lower_cuts_count = DOCS // 2 - 2
    upper_cuts_count = DOCS - DOCS // 2 - 2
    eighth = LENGTH // 8
    lower_cuts = 1 + distinct_sorted(jax.random.fold_in(key, 1), lower_cuts_count, eighth - 1)
    upper_cuts = 7 * eighth + 1 + distinct_sorted(jax.random.fold_in(key, 2), upper_cuts_count, eighth - 2)
    bounds = jnp.concatenate([jnp.zeros((SEQS, 1), jnp.int32), lower_cuts, jnp.full((SEQS, 1), eighth, jnp.int32), jnp.full((SEQS, 1), 7 * eighth, jnp.int32), upper_cuts, jnp.full((SEQS, 1), LENGTH - 1, jnp.int32), jnp.full((SEQS, 1), LENGTH, jnp.int32)], axis=1)
    return (bounds[:, 1:] - bounds[:, :-1]).astype(jnp.int32)


def moments(key, shape, grad_scale):
    first_moment = jax.random.normal(jax.random.fold_in(key, 2), shape, jnp.float32) * 0.5 * grad_scale
    spread = jnp.exp(jax.random.uniform(jax.random.fold_in(key, 3), shape, jnp.float32, math.log(0.01), 0.0))
    second_moment = spread * grad_scale * grad_scale
    return (first_moment, second_moment)


def draw_big_state(key, part):
    key = jax.random.fold_in(key, 21)
    rows = jnp.arange(ROWS, dtype=jnp.int32)[:, None]
    weight_scale = jnp.where(rows < 3 * D, D ** (-0.5), jnp.where(rows < 4 * D, (D // 8) ** (-0.5), jnp.where(rows < 4 * D + 2 * FF, D ** (-0.5), FF ** (-0.5)))).astype(jnp.float32)
    weight = jax.random.normal(jax.random.fold_in(key, 1), (ROWS, D), jnp.float32) * weight_scale
    first_moment, second_moment = moments(key, (ROWS, D), 100.0 / math.sqrt(TOKENS))
    return jnp.stack([weight, first_moment, second_moment])


def draw_small_state(key, part):
    key = jax.random.fold_in(key, 26)
    gains = 1.0 + jax.random.normal(jax.random.fold_in(key, 1), (2 * D,), jnp.float32) * 0.1
    mix_matrix = jax.random.normal(jax.random.fold_in(key, 4), (NS, NS), jnp.float32) * 0.25 + jnp.eye(NS, dtype=jnp.float32)
    read_columns = jax.random.uniform(jax.random.fold_in(key, 5), (NS, 4), jnp.float32, 0.3, 0.8)
    read_columns = read_columns * jnp.array([1.0, 2.0, 1.0, 2.0], jnp.float32)[None, :]
    weight = jnp.concatenate([gains, jnp.concatenate([mix_matrix, read_columns], axis=1).reshape(-1)])
    places = jnp.arange(SMALL, dtype=jnp.int32)
    grad_scale = jnp.where(places < 2 * D, 3.0, 1.5 * math.sqrt(D)).astype(jnp.float32) / math.sqrt(TOKENS)
    first_moment, second_moment = moments(key, (SMALL,), 1.0)
    first_moment = first_moment * grad_scale
    second_moment = second_moment * grad_scale * grad_scale
    return jnp.stack([weight, first_moment, second_moment])


def levels(key, dims, pieces, least, high):
    def one(axis_at, blocks):
        steps = jax.random.uniform(jax.random.fold_in(jax.random.fold_in(key, 6), axis_at), (blocks,), jnp.float32, least / len(pieces), high / len(pieces))
        return jnp.repeat(jnp.exp(steps), dims[axis_at] // blocks).reshape((-1,) + (1,) * (len(dims) - axis_at - 1))

    factor_of = one(*pieces[0])
    for cut in pieces[1:]:
        factor_of = factor_of * one(*cut)
    return factor_of


def scatter_about(own_key, extent, scale, bound, pieces=(), held_as=jnp.bfloat16):
    factor_of = levels(own_key, extent, pieces, -0.22, 0.18) if pieces else 1.0
    drawn = jax.random.normal(own_key, extent, jnp.float32) * scale * factor_of
    return jnp.minimum(jnp.maximum(drawn, -bound), bound).astype(held_as)


def setup_inputs(seed: int = 0) -> dict:
    splits = jax.random.split(jax.random.key(seed), 11)
    streams = scatter_about(splits[0], (SEQS, LENGTH, NS, D), 1.0, 6.0, ((0, 16), (1, 2)))
    cotangent = scatter_about(splits[1], (SEQS, LENGTH, NS, D), 1.0, 6.0, ((0, 16), (1, 2)))
    doc_lengths = draw_doc_lengths(jax.random.fold_in(splits[10], 71), 0)
    attn_in = scatter_about(splits[3], (D, 3 * D), D ** -0.5, 0.21875)
    attn_out = scatter_about(splits[4], (D, D), (D // 8) ** -0.5, 0.625)
    ffn_in = scatter_about(splits[5], (D, 2 * FF), D ** -0.5, 0.21875)
    ffn_out = scatter_about(splits[6], (FF, D), FF ** -0.5, 0.109375)
    norm_gains = jnp.clip(1.0 + 0.1 * jax.random.normal(splits[7], (D, 2), jnp.float32), 0.5, 1.5).astype(jnp.bfloat16)
    big_state = draw_big_state(jax.random.fold_in(splits[10], 71), 0)
    small_state = draw_small_state(jax.random.fold_in(splits[10], 71), 0)
    return {"streams": streams, "cotangent": cotangent, "doc_lengths": doc_lengths, "attn_in": attn_in, "attn_out": attn_out, "ffn_in": ffn_in, "ffn_out": ffn_out, "norm_gains": norm_gains, "big_state": big_state, "small_state": small_state}


norm_epsilon = 1e-05
rope_base = 10000.0
beta_first = 0.9
beta_second = 0.95
adam_epsilon = 1e-08
weight_decay = 0.1
learn_rate = 0.01
masked_score = -1e+30

@jax.custom_vjp
def low(v):
    return lax.optimization_barrier(v.astype(jnp.bfloat16)).astype(jnp.float32)

@jax.custom_vjp
def low_back(v):
    return v

def low_keep(v):
    return (low(v), None)

def low_pass(kept, grad):
    return (grad,)

def back_keep(v):
    return (v, None)

def back_low(kept, grad):
    return (low(grad),)
low.defvjp(low_keep, low_pass)
low_back.defvjp(back_keep, back_low)

def doc_layout(lengths, token_total):
    bounds = jnp.cumsum(lengths).astype(jnp.int32)
    starts = (bounds - lengths).astype(jnp.int32)
    places = jnp.arange(token_total, dtype=jnp.int32)
    segment = lax.optimization_barrier(jnp.sum((places[:, None] >= bounds[None, :]).astype(jnp.int32), axis=1)).astype(jnp.int32)
    picked = segment[:, None] == jnp.arange(lengths.shape[0], dtype=jnp.int32)[None, :]
    offset = lax.optimization_barrier(jnp.sum(jnp.where(picked, starts[None, :], 0), axis=1)).astype(jnp.int32)
    return (segment, (places - offset).astype(jnp.int32))

def rope_tables(position, head_size):
    exponent = jnp.arange(head_size // 2, dtype=jnp.float32) * (2.0 / head_size)
    frequency = jnp.power(jnp.float32(rope_base), -exponent)
    angles = position.astype(jnp.float32)[:, None] * frequency[None, :]
    return (jnp.cos(angles)[:, None, :], jnp.sin(angles)[:, None, :])

def rotate(values, cosine, sine_table):
    half_size = values.shape[-1] // 2
    leading = values[..., :half_size]
    trailing = values[..., half_size:]
    return jnp.concatenate([leading * cosine - trailing * sine_table, trailing * cosine + leading * sine_table], axis=-1)

def layer_norm(values, gain):
    centre = lax.optimization_barrier(jnp.mean(values, axis=-1, keepdims=True))
    centred = values - centre
    scaling = lax.rsqrt(lax.optimization_barrier(jnp.mean(centred * centred, axis=-1, keepdims=True)) + norm_epsilon)
    return centred * scaling * gain

def matmul(left, right):
    return jnp.dot(left, right, precision=lax.Precision.HIGHEST)

def layer_sequence(params, stream_values, lengths):
    attn_in, attn_out, ffn_in, ffn_out, gains, mixing = params
    token_total = stream_values.shape[0]
    stream_count = mixing.shape[0]
    model_width = attn_out.shape[0]
    hidden_units = ffn_out.shape[0]
    segment, position = doc_layout(lengths, token_total)
    cosine, sine_table = rope_tables(position, HD)
    branch_in = lax.optimization_barrier(jnp.sum(stream_values * mixing[None, :, stream_count, None], axis=1))
    mixed_streams = lax.optimization_barrier(jnp.sum(stream_values[:, :, None, :] * mixing[None, :, :stream_count, None], axis=1))
    normed = low(layer_norm(branch_in, gains[:, 0]))
    project = low_back(matmul(normed, attn_in))
    queries = low(rotate(project[:, :model_width].reshape(token_total, HEADS, HD), cosine, sine_table))
    keys_rot = low(rotate(project[:, model_width:2 * model_width].reshape(token_total, HEADS, HD), cosine, sine_table))
    values_in = low(project[:, 2 * model_width:].reshape(token_total, HEADS, HD))
    scores = jnp.einsum('qhd,khd->hqk', queries, keys_rot, precision=lax.Precision.HIGHEST) * HD ** (-0.5)
    scores = low_back(scores)
    places = jnp.arange(token_total, dtype=jnp.int32)
    allowed = (segment[:, None] == segment[None, :]) & (places[None, :] <= places[:, None])
    scores = jnp.where(allowed[None], scores, masked_score)
    row_top = lax.optimization_barrier(jnp.max(scores, axis=-1, keepdims=True))
    lifted = jnp.exp(scores - row_top)
    attend = low(lifted / lax.optimization_barrier(jnp.sum(lifted, axis=-1, keepdims=True)))
    context = jnp.einsum('hqk,khd->qhd', attend, values_in, precision=lax.Precision.HIGHEST).reshape(token_total, model_width)
    context = low_back(low(context))
    first_out = low_back(matmul(context, attn_out))
    streams_mid = mixed_streams + mixing[None, :, stream_count + 1, None] * first_out[:, None, :]
    ffn_read = lax.optimization_barrier(jnp.sum(streams_mid * mixing[None, :, stream_count + 2, None], axis=1))
    normed_two = low(layer_norm(ffn_read, gains[:, 1]))
    gate_up = low_back(matmul(normed_two, ffn_in))
    hidden = low(jax.nn.silu(gate_up[:, :hidden_units]) * gate_up[:, hidden_units:])
    second_out = low_back(matmul(hidden, ffn_out))
    return streams_mid + mixing[None, :, stream_count + 3, None] * second_out[:, None, :]

def adam_step(shard_state, shard_grad):
    weight = shard_state[0]
    first_new = beta_first * shard_state[1] + (1.0 - beta_first) * shard_grad
    second_new = beta_second * shard_state[2] + (1.0 - beta_second) * shard_grad * shard_grad
    first_hat = first_new / (1.0 - beta_first ** STEP)
    second_hat = second_new / (1.0 - beta_second ** STEP)
    update = first_hat / (jnp.sqrt(second_hat) + adam_epsilon) + weight_decay * weight
    weight_new = weight - learn_rate * update
    return (weight_new, first_new, second_new)

def reference(streams, cotangent, doc_lengths, attn_in, attn_out, ffn_in, ffn_out, norm_gains, big_state, small_state):
    mixing = small_state[0, 2 * D:].reshape(NS, NS + 4)
    params = (attn_in.astype(jnp.float32), attn_out.astype(jnp.float32), ffn_in.astype(jnp.float32), ffn_out.astype(jnp.float32), norm_gains.astype(jnp.float32), mixing)
    checked = jax.checkpoint(layer_sequence)

    def whole_layer(weights, inputs):

        def one_sequence(sequence_items):
            return checked(weights, sequence_items[0], sequence_items[1])
        return lax.map(one_sequence, (inputs, doc_lengths))
    outputs, pullback = jax.vjp(whole_layer, params, streams.astype(jnp.float32))
    param_grads, stream_grad = pullback(cotangent.astype(jnp.float32))
    token_count = SEQS * LENGTH
    flat_grads = jnp.concatenate([grad.reshape(-1, D) for grad in param_grads[:4]], axis=0) / token_count
    small_grads = jnp.concatenate([param_grads[4].T.reshape(-1), param_grads[5].reshape(-1)]) / token_count
    weight_new, first_new, second_new = adam_step(big_state, flat_grads)
    small_weight, small_first, small_second = adam_step(small_state, small_grads)
    gains_copy = small_weight[:2 * D].reshape(2, D).T.astype(jnp.bfloat16)
    return (outputs.astype(jnp.bfloat16), stream_grad.astype(jnp.bfloat16), weight_new, first_new, second_new, flat_grads, small_weight, small_first, small_second, small_grads, weight_new.astype(jnp.bfloat16), gains_copy)
```

```python
import functools

import jax
import jax.numpy as jnp
from jax import lax
from jax.experimental import pallas as pl
from jax.experimental.pallas import tpu as pltpu
from jax.sharding import PartitionSpec as P

HEADS = 12
HD = 64
NS = 4
STEP = 10


norm_epsilon = 1e-05
rope_base = 10000.0
beta_first = 0.9
beta_second = 0.95
adam_epsilon = 1e-08
weight_decay = 0.1
learn_rate = 0.01
MESH = pl.DeviceIdType.MESH
masked_score = -1e30


def shifted(value, axis, by):
    count = lax.axis_size(axis)
    pairs = [(i, i + by) for i in range(count) if 0 <= i + by < count]
    return lax.ppermute(value, axis, pairs)


def doc_layout(lengths, token_total):
    bounds = jnp.cumsum(lengths)
    starts = bounds - lengths
    places = jnp.arange(token_total, dtype=jnp.int32)
    segment = jnp.sum((places[:, None] >= bounds[None, :]).astype(jnp.int32), axis=1)
    picked = segment[:, None] == jnp.arange(lengths.shape[0], dtype=jnp.int32)[None, :]
    offset = jnp.sum(jnp.where(picked, starts[None, :], 0), axis=1)
    return (segment, places - offset)


def rope_tables(position, head_size):
    exponent = jnp.arange(head_size // 2, dtype=jnp.float32) * (2.0 / head_size)
    frequency = jnp.power(jnp.float32(rope_base), -exponent)
    angles = position.astype(jnp.float32)[:, None] * frequency[None, :]
    return (jnp.cos(angles)[:, None, :], jnp.sin(angles)[:, None, :])


def rotate(values, cosine, sine_table):
    half_size = values.shape[-1] // 2
    leading = values[..., :half_size]
    trailing = values[..., half_size:]
    return jnp.concatenate(
        [leading * cosine - trailing * sine_table, trailing * cosine + leading * sine_table],
        axis=-1,
    )


def rotate_back(grads, cosine, sine_table):
    half_size = grads.shape[-1] // 2
    leading = grads[..., :half_size]
    trailing = grads[..., half_size:]
    return jnp.concatenate(
        [leading * cosine + trailing * sine_table, trailing * cosine - leading * sine_table],
        axis=-1,
    )


def norm_parts(values):
    centre = jnp.mean(values, axis=-1, keepdims=True)
    centred = values - centre
    scaling = lax.rsqrt(jnp.mean(centred * centred, axis=-1, keepdims=True) + norm_epsilon)
    return (centred * scaling, scaling)


def norm_back(grads, normal, scaling, gain):
    gain_grad = jnp.sum(grads * normal, axis=0)
    scaled = grads * gain
    centre = jnp.mean(scaled, axis=-1, keepdims=True)
    along_normal = jnp.mean(scaled * normal, axis=-1, keepdims=True)
    return (gain_grad, scaling * (scaled - centre - normal * along_normal))


def right_product(left, right):
    return lax.dot_general(
        left, right, (((1,), (1,)), ((), ())), preferred_element_type=jnp.float32
    )


def left_product(left, right):
    return lax.dot_general(
        left, right, (((0,), (0,)), ((), ())), preferred_element_type=jnp.float32
    )


def forward_layer(stream_values, weights, gain_values, mixing, allowed, cosine, sine_table):
    attn_in, attn_out, ffn_in, ffn_out = weights
    row_count = stream_values.shape[0]
    model_width = attn_out.shape[0]
    stream_count = mixing.shape[0]
    hidden_units = ffn_out.shape[0]
    branch_in = jnp.sum(stream_values * mixing[None, :, stream_count, None], axis=1)
    mixed_streams = jnp.sum(
        stream_values[:, :, None, :] * mixing[None, :, :stream_count, None], axis=1
    )
    normal_one, scale_one = norm_parts(branch_in)
    normed = (normal_one * gain_values[:, 0]).astype(jnp.bfloat16)
    project = jnp.dot(normed, attn_in, preferred_element_type=jnp.float32)
    queries = rotate(
        project[:, :model_width].reshape(row_count, HEADS, HD), cosine, sine_table
    ).astype(jnp.bfloat16)
    keys_rot = rotate(
        project[:, model_width : 2 * model_width].reshape(row_count, HEADS, HD), cosine, sine_table
    ).astype(jnp.bfloat16)
    values_in = project[:, 2 * model_width :].astype(jnp.bfloat16)
    outgoing = jnp.concatenate([keys_rot.reshape(row_count, model_width), values_in], axis=1)
    earlier = shifted(outgoing, "seq", 1)
    key_rows = jnp.concatenate([earlier, outgoing], axis=0)
    keys_all = key_rows[:, :model_width].reshape(2 * row_count, HEADS, HD)
    values_all = key_rows[:, model_width:].reshape(2 * row_count, HEADS, HD)
    scores = jnp.einsum(
        "qhd,khd->hqk", queries, keys_all, preferred_element_type=jnp.float32
    ) * HD ** (-0.5)
    scores = jnp.where(allowed[None], scores, masked_score)
    row_top = jnp.max(scores, axis=-1, keepdims=True)
    lifted = jnp.exp(scores - row_top)
    attend = lifted / jnp.sum(lifted, axis=-1, keepdims=True)
    attend_low = attend.astype(jnp.bfloat16)
    context = jnp.einsum("hqk,khd->qhd", attend_low, values_all, preferred_element_type=jnp.float32)
    context = context.reshape(row_count, model_width).astype(jnp.bfloat16)
    first_out = jnp.dot(context, attn_out, preferred_element_type=jnp.float32)
    streams_mid = mixed_streams + mixing[None, :, stream_count + 1, None] * first_out[:, None, :]
    ffn_read = jnp.sum(streams_mid * mixing[None, :, stream_count + 2, None], axis=1)
    normal_two, scale_two = norm_parts(ffn_read)
    normed_two = (normal_two * gain_values[:, 1]).astype(jnp.bfloat16)
    gate_up = jnp.dot(normed_two, ffn_in, preferred_element_type=jnp.float32)
    gate_part = gate_up[:, :hidden_units]
    up_part = gate_up[:, hidden_units:]
    hidden = (jax.nn.silu(gate_part) * up_part).astype(jnp.bfloat16)
    second_out = jnp.dot(hidden, ffn_out, preferred_element_type=jnp.float32)
    result = streams_mid + mixing[None, :, stream_count + 3, None] * second_out[:, None, :]
    saved = (
        normal_one,
        scale_one,
        normed,
        queries,
        keys_all,
        values_all,
        attend,
        attend_low,
        context,
        first_out,
        streams_mid,
        normal_two,
        scale_two,
        normed_two,
        gate_part,
        up_part,
        hidden,
        second_out,
    )
    return (result, saved)


def backward_layer(
    stream_values, grad_out, weights, gain_values, mixing, cosine, sine_table, saved
):
    attn_in, attn_out, ffn_in, ffn_out = weights
    (
        normal_one,
        scale_one,
        normed,
        queries,
        keys_all,
        values_all,
        attend,
        attend_low,
        context,
        first_out,
        streams_mid,
        normal_two,
        scale_two,
        normed_two,
        gate_part,
        up_part,
        hidden,
        second_out,
    ) = saved
    row_count = stream_values.shape[0]
    model_width = attn_out.shape[0]
    stream_count = mixing.shape[0]
    second_low = jnp.sum(grad_out * mixing[None, :, stream_count + 3, None], axis=1).astype(
        jnp.bfloat16
    )
    grad_depth_two = jnp.sum(grad_out * second_out[:, None, :], axis=(0, 2))
    ffn_out_grad = left_product(hidden, second_low)
    hidden_grad = right_product(second_low, ffn_out)
    sigmoid_gate = jax.nn.sigmoid(gate_part)
    gate_grad = hidden_grad * up_part * sigmoid_gate * (1.0 + gate_part * (1.0 - sigmoid_gate))
    up_grad = hidden_grad * gate_part * sigmoid_gate
    gate_up_low = jnp.concatenate([gate_grad, up_grad], axis=1).astype(jnp.bfloat16)
    ffn_in_grad = left_product(normed_two, gate_up_low)
    normed_two_grad = right_product(gate_up_low, ffn_in)
    gain_two_grad, read_grad = norm_back(normed_two_grad, normal_two, scale_two, gain_values[:, 1])
    mid_grad = grad_out + mixing[None, :, stream_count + 2, None] * read_grad[:, None, :]
    grad_read_two = jnp.sum(streams_mid * read_grad[:, None, :], axis=(0, 2))
    first_low = jnp.sum(mid_grad * mixing[None, :, stream_count + 1, None], axis=1).astype(
        jnp.bfloat16
    )
    grad_depth_one = jnp.sum(mid_grad * first_out[:, None, :], axis=(0, 2))
    attn_out_grad = left_product(context, first_low)
    context_grad = (
        right_product(first_low, attn_out).astype(jnp.bfloat16).reshape(row_count, HEADS, HD)
    )
    attend_grad = jnp.einsum(
        "qhd,khd->hqk", context_grad, values_all, preferred_element_type=jnp.float32
    )
    values_grad = jnp.einsum(
        "hqk,qhd->khd", attend_low, context_grad, preferred_element_type=jnp.float32
    )
    inner_sum = jnp.sum(attend * attend_grad, axis=-1, keepdims=True)
    score_low = (attend * (attend_grad - inner_sum)).astype(jnp.bfloat16)
    query_grad = jnp.einsum(
        "hqk,khd->qhd", score_low, keys_all, preferred_element_type=jnp.float32
    ) * HD ** (-0.5)
    keys_grad = jnp.einsum(
        "hqk,qhd->khd", score_low, queries, preferred_element_type=jnp.float32
    ) * HD ** (-0.5)
    returned = jnp.concatenate(
        [
            keys_grad[:row_count].reshape(row_count, model_width),
            values_grad[:row_count].reshape(row_count, model_width),
        ],
        axis=1,
    )
    from_later = shifted(returned.astype(jnp.bfloat16), "seq", -1).astype(returned.dtype)
    own_keys = keys_grad[row_count:].reshape(row_count, model_width) + from_later[:, :model_width]
    own_values = (
        values_grad[row_count:].reshape(row_count, model_width) + from_later[:, model_width:]
    )
    query_back = rotate_back(query_grad, cosine, sine_table).reshape(row_count, model_width)
    key_back = rotate_back(own_keys.reshape(row_count, HEADS, HD), cosine, sine_table).reshape(
        row_count, model_width
    )
    project_low = jnp.concatenate([query_back, key_back, own_values], axis=1).astype(jnp.bfloat16)
    attn_in_grad = left_product(normed, project_low)
    normed_grad = right_product(project_low, attn_in)
    gain_one_grad, branch_grad = norm_back(normed_grad, normal_one, scale_one, gain_values[:, 0])
    stream_grad = jnp.sum(mid_grad[:, None, :, :] * mixing[None, :, :stream_count, None], axis=2)
    stream_grad = stream_grad + mixing[None, :, stream_count, None] * branch_grad[:, None, :]
    grad_mix = jnp.sum(stream_values[:, :, None, :] * mid_grad[:, None, :, :], axis=(0, 3))
    grad_read_one = jnp.sum(stream_values * branch_grad[:, None, :], axis=(0, 2))
    mixing_grad = jnp.concatenate(
        [
            grad_mix,
            grad_read_one[:, None],
            grad_depth_one[:, None],
            grad_read_two[:, None],
            grad_depth_two[:, None],
        ],
        axis=1,
    )
    gains_grad = jnp.stack([gain_one_grad, gain_two_grad], axis=1)
    return (
        stream_grad,
        (attn_in_grad, attn_out_grad, ffn_in_grad, ffn_out_grad),
        gains_grad,
        mixing_grad,
    )


def adam_step(shard_state, shard_grad):
    weight = shard_state[0]
    first_new = beta_first * shard_state[1] + (1.0 - beta_first) * shard_grad
    second_new = beta_second * shard_state[2] + (1.0 - beta_second) * shard_grad * shard_grad
    first_hat = first_new / (1.0 - beta_first**STEP)
    second_hat = second_new / (1.0 - beta_second**STEP)
    update = first_hat / (jnp.sqrt(second_hat) + adam_epsilon) + weight_decay * weight
    weight_new = weight - learn_rate * update
    return (weight_new, first_new, second_new)


def torus(mesh):
    wide = mesh.shape["wide"]
    where = [getattr(d, "coords", None) for d in mesh.devices.flat]
    if all(c is not None for c in where):
        x, y, z = (len({c[i] for c in where}) for i in range(3))
        if x * y * z == wide:
            return z, y, x
    known = {16: (4, 2, 2), 64: (4, 4, 4)}
    return known.get(wide, (wide, 1, 1))


def sync_kernel(
    dims, rows, half, lr_consts,
    grads, small_in, state_in,
    copy_out, weight_out, first_out, second_out, grad_out, small_out,
    acc, from_core, from_a0, from_a1, from_b0, from_b1, from_c,
    state, new_w, new_m, new_v, new_g, low, small_box,
    load_sem, store_sem, send_sem, recv_sem, small_send, small_recv,
):
    nz, ny, nx = dims
    chunk = 2 * half
    chunks = rows // chunk
    s = lax.axis_index("seq")
    w = lax.axis_index("wide")
    z, y, x = w // (ny * nx), (w // nx) % ny, w % nx

    def chip(cz, cy, cx):
        return (s, (cz * ny + cy) * nx + cx)

    core = (1 - s, w)
    z_peers = [chip((z + d) % nz, y, x) for d in range(1, nz)]
    y_peers = [chip(z, (y + d) % ny, x) for d in range(1, ny)]
    x_peers = [chip(z, y, (x + d) % nx) for d in range(1, nx)]
    peers = [core] + z_peers + y_peers + x_peers

    barrier = pltpu.get_barrier_semaphore()
    for peer in peers:
        pl.semaphore_signal(barrier, inc=1, device_id=peer, device_id_type=MESH)

    loads = [
        pltpu.make_async_copy(
            grads.at[s, :, :, :, pl.ds(c * chunk, chunk)],
            acc.at[:, :, :, pl.ds(c * chunk, chunk)],
            load_sem.at[c],
        )
        for c in range(chunks)
    ]
    for copy in loads:
        copy.start()
    state_load = pltpu.make_async_copy(state_in, state, load_sem.at[chunks])
    state_load.start()
    pl.semaphore_wait(barrier, len(peers))

    sends = []
    counter = [0]

    def remote(src, dst, peer):
        i = counter[0]
        counter[0] += 1
        copy = pltpu.make_async_remote_copy(
            src, dst, send_sem.at[i], recv_sem.at[i], device_id=peer, device_id_type=MESH
        )
        copy.start()
        sends.append(copy)
        return copy

    def lo(c):
        return pl.ds(c * chunk, half)

    def hi(c):
        return pl.ds(c * chunk + half, half)

    def both(c):
        return pl.ds(c * chunk, chunk)

    def packed(c):
        return pl.ds(c * half, half)

    f32 = jnp.float32

    def add_into(count, where, terms):
        def body(i, carry):
            ref, index = where(i)
            total = ref[index].astype(f32)
            for term_ref, term_index in terms(i):
                total = total + term_ref[term_index].astype(f32)
            ref[index] = total.astype(ref.dtype)
            return carry

        lax.fori_loop(0, count, body, 0)

    def small_step(k, mine, others, count):
        copies = []
        for j, peer in enumerate(others):
            i = small_index[0]
            small_index[0] += 1
            copy = pltpu.make_async_remote_copy(
                small_box.at[k, mine], small_box.at[k, mine], small_send.at[i], small_recv.at[i],
                device_id=peer, device_id_type=MESH,
            )
            copy.start()
            copies.append(copy)
        return copies

    def small_sum(k, copies, count):
        for copy in copies:
            copy.wait()
        total = small_box[k, 0]
        for j in range(1, count):
            total = total + small_box[k, j]
        return total

    small_index = [0]
    axes = [(s, [core], 2), (x, x_peers, nx), (y, y_peers, ny), (z, z_peers, nz)]
    small_box[0, s] = small_in[...]
    small_copies = [small_step(0, s, [core], 2)]

    def small_stage(k):
        total = small_sum(k, small_copies[k], axes[k][2])
        if k + 1 < len(axes):
            place, others, count = axes[k + 1]
            small_box[k + 1, place] = total
            small_copies.append(small_step(k + 1, place, others, count))
        else:
            small_out[...] = total

    state_done = [False]
    flying = {}

    def stage(k, c):
        if k == 0:
            loads[c].wait()
            for copy in flying[0, c]:
                copy.wait_recv()

            def where(i):
                return acc, (i // (ny * nx), (i // nx) % ny, i % nx, both(c))

            def terms(i):
                return [(from_core, (i // (ny * nx), (i // nx) % ny, i % nx, both(c)))]

            add_into(nz * ny * nx, where, terms)
            out = []
            for d in range(1, nx):
                out.append(remote(
                    acc.at[:, :, (x + d) % nx, lo(c)], from_a0.at[d - 1, :, :, packed(c)], x_peers[d - 1]))
            for d in range(1, ny):
                out.append(remote(
                    acc.at[:, (y + d) % ny, :, hi(c)], from_a1.at[d - 1, :, :, packed(c)], y_peers[d - 1]))
            flying[1, c] = out
        elif k == 1:
            for copy in flying[1, c]:
                copy.wait_recv()
            add_into(
                nz * ny,
                lambda i: (acc, (i // ny, i % ny, x, lo(c))),
                lambda i: [(from_a0, (d, i // ny, i % ny, packed(c))) for d in range(nx - 1)],
            )
            add_into(
                nz * nx,
                lambda i: (acc, (i // nx, y, i % nx, hi(c))),
                lambda i: [(from_a1, (d, i // nx, i % nx, packed(c))) for d in range(ny - 1)],
            )
            out = []
            for d in range(1, ny):
                out.append(remote(
                    acc.at[:, (y + d) % ny, x, lo(c)], from_b0.at[d - 1, :, packed(c)], y_peers[d - 1]))
            for d in range(1, nx):
                out.append(remote(
                    acc.at[:, y, (x + d) % nx, hi(c)], from_b1.at[d - 1, :, packed(c)], x_peers[d - 1]))
            flying[2, c] = out
        elif k == 2:
            for copy in flying[2, c]:
                copy.wait_recv()
            add_into(
                nz,
                lambda i: (acc, (i, y, x, lo(c))),
                lambda i: [(from_b0, (d, i, packed(c))) for d in range(ny - 1)],
            )
            add_into(
                nz,
                lambda i: (acc, (i, y, x, hi(c))),
                lambda i: [(from_b1, (d, i, packed(c))) for d in range(nx - 1)],
            )
            out = []
            for d in range(1, nz):
                out.append(remote(
                    acc.at[(z + d) % nz, y, x, both(c)], from_c.at[d - 1, both(c)], z_peers[d - 1]))
            flying[3, c] = out
        elif k == 3:
            for copy in flying[3, c]:
                copy.wait_recv()
            if not state_done[0]:
                state_load.wait()
                state_done[0] = True
            step = 16

            def body(i, carry):
                r = pl.ds(c * chunk + i * step, step)
                total = acc[z, y, x, r].astype(f32)
                for d in range(nz - 1):
                    total = total + from_c[d, r].astype(f32)
                grad = total * lr_consts
                w_new, m_new, v_new = adam_step((state[0, r], state[1, r], state[2, r]), grad)
                new_g[r] = grad
                new_w[r] = w_new
                new_m[r] = m_new
                new_v[r] = v_new
                low[r] = w_new.astype(low.dtype)
                return carry

            lax.fori_loop(0, chunk // step, body, 0)
            out = []
            for peer in z_peers:
                out.append(remote(low.at[both(c)], copy_out.at[s, z, y, x, both(c)], peer))
            own = pltpu.make_async_copy(low.at[both(c)], copy_out.at[s, z, y, x, both(c)], store_sem.at[0, c])
            own.start()
            for j, (a, b) in enumerate(((new_w, weight_out), (new_m, first_out), (new_v, second_out), (new_g, grad_out))):
                st = pltpu.make_async_copy(a.at[both(c)], b.at[both(c)], store_sem.at[j + 1, c])
                st.start()
                stores.append(st)
            flying[4, c] = (out, own)
        elif k == 4:
            out, own = flying[4, c]
            own.wait()
            for copy in out:
                copy.wait_recv()
            nxt = []
            for peer in y_peers:
                nxt.append(remote(copy_out.at[s, :, y, x, lo(c)], copy_out.at[s, :, y, x, lo(c)], peer))
            for peer in x_peers:
                nxt.append(remote(copy_out.at[s, :, y, x, hi(c)], copy_out.at[s, :, y, x, hi(c)], peer))
            flying[5, c] = nxt
        elif k == 5:
            for copy in flying[5, c]:
                copy.wait_recv()
            nxt = []
            for peer in x_peers:
                nxt.append(remote(copy_out.at[s, :, :, x, lo(c)], copy_out.at[s, :, :, x, lo(c)], peer))
            for peer in y_peers:
                nxt.append(remote(copy_out.at[s, :, y, :, hi(c)], copy_out.at[s, :, y, :, hi(c)], peer))
            flying[6, c] = nxt
        elif k == 6:
            for copy in flying[6, c]:
                copy.wait_recv()
            flying[7, c] = [
                remote(copy_out.at[s, :, :, :, both(c)], copy_out.at[s, :, :, :, both(c)], core)]
        elif k == 7:
            for copy in flying[7, c]:
                copy.wait_recv()

    stores = []
    for c in range(chunks):
        flying[0, c] = [remote(
            grads.at[1 - s, :, :, :, both(c)], from_core.at[:, :, :, both(c)], core)]
    stages = 8
    for t in range(chunks + stages - 1):
        for k in reversed(range(stages)):
            c = t - k
            if 0 <= c < chunks:
                stage(k, c)
        if 1 <= t <= 4:
            small_stage(t - 1)
    for copy in sends:
        copy.wait_send()
    for copy in stores:
        copy.wait()


def sync_grads(dims, flat_low, small_local, big_state, token_count):
    nz, ny, nx = dims
    wide = nz * ny * nx
    model_width = flat_low.shape[1]
    rows = big_state.shape[1]
    half = next(h for h in (48, 32, 16) if rows % (2 * h) == 0)
    chunks = rows // (2 * half)
    bf16, f32 = jnp.bfloat16, jnp.float32
    copies = chunks * (2 + 4 * (nx - 1) + 4 * (ny - 1) + 2 * (nz - 1))
    small_copies = 1 + (nx - 1) + (ny - 1) + (nz - 1)
    hbm = pl.BlockSpec(memory_space=pl.ANY)
    vmem = pl.BlockSpec(memory_space=pltpu.VMEM)
    state_shape = jax.ShapeDtypeStruct((rows, model_width), f32)
    small_shape = small_local.shape
    outs = pl.pallas_call(
        functools.partial(sync_kernel, dims, rows, half, 1.0 / token_count),
        out_shape=[
            jax.ShapeDtypeStruct((2, nz, ny, nx, rows, model_width), bf16),
            state_shape, state_shape, state_shape, state_shape,
            jax.ShapeDtypeStruct(small_shape, f32),
        ],
        in_specs=[hbm, vmem, hbm],
        out_specs=[hbm] * 5 + [vmem],
        scratch_shapes=[
            pltpu.VMEM((nz, ny, nx, rows, model_width), bf16),
            pltpu.VMEM((nz, ny, nx, rows, model_width), bf16),
            pltpu.VMEM((max(nx - 1, 1), nz, ny, rows // 2, model_width), bf16),
            pltpu.VMEM((max(ny - 1, 1), nz, nx, rows // 2, model_width), bf16),
            pltpu.VMEM((max(ny - 1, 1), nz, rows // 2, model_width), bf16),
            pltpu.VMEM((max(nx - 1, 1), nz, rows // 2, model_width), bf16),
            pltpu.VMEM((max(nz - 1, 1), rows, model_width), bf16),
            pltpu.VMEM((3, rows, model_width), f32),
            pltpu.VMEM((rows, model_width), f32),
            pltpu.VMEM((rows, model_width), f32),
            pltpu.VMEM((rows, model_width), f32),
            pltpu.VMEM((rows, model_width), f32),
            pltpu.VMEM((rows, model_width), bf16),
            pltpu.VMEM((4, max(2, nx, ny, nz)) + small_shape, f32),
            pltpu.SemaphoreType.DMA((chunks + 1,)),
            pltpu.SemaphoreType.DMA((5, chunks)),
            pltpu.SemaphoreType.DMA((copies,)),
            pltpu.SemaphoreType.DMA((copies,)),
            pltpu.SemaphoreType.DMA((small_copies,)),
            pltpu.SemaphoreType.DMA((small_copies,)),
        ],
        compiler_params=pltpu.CompilerParams(
            collective_id=1, has_side_effects=True, vmem_limit_bytes=56 * 2**20
        ),
        name="sync_grads",
    )(
        flat_low.reshape(2, nz, ny, nx, rows, model_width), small_local, big_state
    )
    return (outs[0].reshape(2 * wide * rows, model_width),) + tuple(outs[1:])


def on_device(
    dims,
    streams,
    cotangent,
    doc_lengths,
    attn_in,
    attn_out,
    ffn_in,
    ffn_out,
    norm_gains,
    big_state,
    small_state,
):
    row_count = streams.shape[1]
    model_width = attn_out.shape[0]
    member = lax.axis_index("seq")
    token_total = row_count * lax.axis_size("seq")
    token_count = token_total * lax.axis_size("wide")
    segment, position = doc_layout(doc_lengths[0], token_total)
    own_start = member * row_count
    own_index = own_start + jnp.arange(row_count, dtype=jnp.int32)
    seg_query = lax.dynamic_slice_in_dim(segment, own_start, row_count)
    pos_query = lax.dynamic_slice_in_dim(position, own_start, row_count)
    padded_seg = jnp.concatenate([jnp.full((row_count,), -1, jnp.int32), segment])
    key_seg = lax.dynamic_slice_in_dim(padded_seg, own_start, 2 * row_count)
    key_index = own_start - row_count + jnp.arange(2 * row_count, dtype=jnp.int32)
    allowed = (key_seg[None, :] == seg_query[:, None]) & (key_index[None, :] <= own_index[:, None])
    cosine, sine_table = rope_tables(pos_query, HD)
    weights = (attn_in, attn_out, ffn_in, ffn_out)
    gain_values = norm_gains.astype(jnp.float32)
    mixing = small_state[0, 2 * model_width :].reshape(NS, NS + 4)
    stream_values = streams[0].astype(jnp.float32)
    result, saved = forward_layer(
        stream_values, weights, gain_values, mixing, allowed, cosine, sine_table
    )
    grad_out = cotangent[0].astype(jnp.float32)
    stream_grad, matrix_grads, gains_local, mixing_local = backward_layer(
        stream_values, grad_out, weights, gain_values, mixing, cosine, sine_table, saved
    )
    flat_low = jnp.concatenate(
        [grad.astype(jnp.bfloat16).reshape(-1, model_width) for grad in matrix_grads], axis=0
    )
    small_local = jnp.concatenate([gains_local.T.reshape(-1), mixing_local.reshape(-1)])
    small_count = small_local.shape[0]
    padded = jnp.pad(small_local, (0, -small_count % 1024)).reshape(-1, 128)
    gathered, weight_new, first_new, second_new, owned_grads, small_total = sync_grads(
        dims, flat_low, padded, big_state, token_count
    )
    small_grads = small_total.reshape(-1)[:small_count] / token_count
    small_weight, small_first, small_second = adam_step(small_state, small_grads)
    gains_copy = small_weight[: 2 * model_width].reshape(2, model_width).T.astype(jnp.bfloat16)
    return (
        result.astype(jnp.bfloat16)[None],
        stream_grad.astype(jnp.bfloat16)[None],
        weight_new,
        first_new,
        second_new,
        owned_grads,
        small_weight,
        small_first,
        small_second,
        small_grads,
        gathered,
        gains_copy,
    )


def solution(mesh):
    in_specs = (
        P("wide", "seq", None, None),
        P("wide", "seq", None, None),
        P("wide", None),
        P(),
        P(),
        P(),
        P(),
        P(),
        P(None, ("seq", "wide"), None),
        P(),
    )
    out_specs = (
        P("wide", "seq", None, None),
        P("wide", "seq", None, None),
        P(("seq", "wide"), None),
        P(("seq", "wide"), None),
        P(("seq", "wide"), None),
        P(("seq", "wide"), None),
        P(),
        P(),
        P(),
        P(),
        P(),
        P(),
    )
    return jax.shard_map(
        functools.partial(on_device, torus(mesh)), mesh=mesh, in_specs=in_specs, out_specs=out_specs, check_vma=False
    )
```

```python
import functools

import jax
import jax.numpy as jnp
import numpy as np
from jax import lax
from jax.experimental import pallas as pl
from jax.experimental.pallas import tpu as pltpu
from jax.sharding import PartitionSpec as P

HEADS = 12
HD = 64
NS = 4
STEP = 10


norm_epsilon = 1e-05
rope_base = 10000.0
beta_first = 0.9
beta_second = 0.95
adam_epsilon = 1e-08
weight_decay = 0.1
learn_rate = 0.01
MESH = pl.DeviceIdType.MESH
masked_score = -1e30


def shifted(value, axis, by):
    count = lax.axis_size(axis)
    pairs = [(i, i + by) for i in range(count) if 0 <= i + by < count]
    return lax.ppermute(value, axis, pairs)


def doc_layout(lengths, token_total):
    bounds = jnp.cumsum(lengths)
    starts = bounds - lengths
    places = jnp.arange(token_total, dtype=jnp.int32)
    segment = jnp.sum((places[:, None] >= bounds[None, :]).astype(jnp.int32), axis=1)
    picked = segment[:, None] == jnp.arange(lengths.shape[0], dtype=jnp.int32)[None, :]
    offset = jnp.sum(jnp.where(picked, starts[None, :], 0), axis=1)
    return (segment, places - offset)


def rope_tables(position, head_size):
    exponent = jnp.arange(head_size // 2, dtype=jnp.float32) * (2.0 / head_size)
    frequency = jnp.power(jnp.float32(rope_base), -exponent)
    angles = position.astype(jnp.float32)[:, None] * frequency[None, :]
    return (jnp.cos(angles)[:, None, :], jnp.sin(angles)[:, None, :])


def rotate(values, cosine, sine_table):
    half_size = values.shape[-1] // 2
    leading = values[..., :half_size]
    trailing = values[..., half_size:]
    return jnp.concatenate(
        [leading * cosine - trailing * sine_table, trailing * cosine + leading * sine_table],
        axis=-1,
    )


def rotate_back(grads, cosine, sine_table):
    half_size = grads.shape[-1] // 2
    leading = grads[..., :half_size]
    trailing = grads[..., half_size:]
    return jnp.concatenate(
        [leading * cosine + trailing * sine_table, trailing * cosine - leading * sine_table],
        axis=-1,
    )


def norm_parts(values):
    centre = jnp.mean(values, axis=-1, keepdims=True)
    centred = values - centre
    scaling = lax.rsqrt(jnp.mean(centred * centred, axis=-1, keepdims=True) + norm_epsilon)
    return (centred * scaling, scaling)


def norm_back(grads, normal, scaling, gain):
    gain_grad = jnp.sum(grads * normal, axis=0)
    scaled = grads * gain
    centre = jnp.mean(scaled, axis=-1, keepdims=True)
    along_normal = jnp.mean(scaled * normal, axis=-1, keepdims=True)
    return (gain_grad, scaling * (scaled - centre - normal * along_normal))


def right_product(left, right):
    return lax.dot_general(
        left, right, (((1,), (1,)), ((), ())), preferred_element_type=jnp.float32
    )


def left_product(left, right):
    return lax.dot_general(
        left, right, (((0,), (0,)), ((), ())), preferred_element_type=jnp.float32
    )


def forward_layer(stream_values, weights, gain_values, mixing, allowed, cosine, sine_table):
    attn_in, attn_out, ffn_in, ffn_out = weights
    row_count = stream_values.shape[0]
    model_width = attn_out.shape[0]
    stream_count = mixing.shape[0]
    hidden_units = ffn_out.shape[0]
    branch_in = jnp.sum(stream_values * mixing[None, :, stream_count, None], axis=1)
    mixed_streams = jnp.sum(
        stream_values[:, :, None, :] * mixing[None, :, :stream_count, None], axis=1
    )
    normal_one, scale_one = norm_parts(branch_in)
    normed = (normal_one * gain_values[:, 0]).astype(jnp.bfloat16)
    project = jnp.dot(normed, attn_in, preferred_element_type=jnp.float32)
    queries = rotate(
        project[:, :model_width].reshape(row_count, HEADS, HD), cosine, sine_table
    ).astype(jnp.bfloat16)
    keys_rot = rotate(
        project[:, model_width : 2 * model_width].reshape(row_count, HEADS, HD), cosine, sine_table
    ).astype(jnp.bfloat16)
    values_in = project[:, 2 * model_width :].astype(jnp.bfloat16)
    outgoing = jnp.concatenate([keys_rot.reshape(row_count, model_width), values_in], axis=1)
    earlier = shifted(outgoing, "seq", 1)
    key_rows = jnp.concatenate([earlier, outgoing], axis=0)
    keys_all = key_rows[:, :model_width].reshape(2 * row_count, HEADS, HD)
    values_all = key_rows[:, model_width:].reshape(2 * row_count, HEADS, HD)
    scores = jnp.einsum(
        "qhd,khd->hqk", queries, keys_all, preferred_element_type=jnp.float32
    ) * HD ** (-0.5)
    scores = jnp.where(allowed[None], scores, masked_score)
    row_top = jnp.max(scores, axis=-1, keepdims=True)
    lifted = jnp.exp(scores - row_top)
    attend = lifted / jnp.sum(lifted, axis=-1, keepdims=True)
    attend_low = attend.astype(jnp.bfloat16)
    context = jnp.einsum("hqk,khd->qhd", attend_low, values_all, preferred_element_type=jnp.float32)
    context = context.reshape(row_count, model_width).astype(jnp.bfloat16)
    first_out = jnp.dot(context, attn_out, preferred_element_type=jnp.float32)
    streams_mid = mixed_streams + mixing[None, :, stream_count + 1, None] * first_out[:, None, :]
    ffn_read = jnp.sum(streams_mid * mixing[None, :, stream_count + 2, None], axis=1)
    normal_two, scale_two = norm_parts(ffn_read)
    normed_two = (normal_two * gain_values[:, 1]).astype(jnp.bfloat16)
    gate_up = jnp.dot(normed_two, ffn_in, preferred_element_type=jnp.float32)
    gate_part = gate_up[:, :hidden_units]
    up_part = gate_up[:, hidden_units:]
    hidden = (jax.nn.silu(gate_part) * up_part).astype(jnp.bfloat16)
    second_out = jnp.dot(hidden, ffn_out, preferred_element_type=jnp.float32)
    result = streams_mid + mixing[None, :, stream_count + 3, None] * second_out[:, None, :]
    saved = (
        normal_one,
        scale_one,
        normed,
        queries,
        keys_all,
        values_all,
        attend,
        attend_low,
        context,
        first_out,
        streams_mid,
        normal_two,
        scale_two,
        normed_two,
        gate_part,
        up_part,
        hidden,
        second_out,
    )
    return (result, saved)


def backward_layer(
    stream_values, grad_out, weights, gain_values, mixing, cosine, sine_table, saved
):
    attn_in, attn_out, ffn_in, ffn_out = weights
    (
        normal_one,
        scale_one,
        normed,
        queries,
        keys_all,
        values_all,
        attend,
        attend_low,
        context,
        first_out,
        streams_mid,
        normal_two,
        scale_two,
        normed_two,
        gate_part,
        up_part,
        hidden,
        second_out,
    ) = saved
    row_count = stream_values.shape[0]
    model_width = attn_out.shape[0]
    stream_count = mixing.shape[0]
    second_low = jnp.sum(grad_out * mixing[None, :, stream_count + 3, None], axis=1).astype(
        jnp.bfloat16
    )
    grad_depth_two = jnp.sum(grad_out * second_out[:, None, :], axis=(0, 2))
    ffn_out_grad = left_product(hidden, second_low)
    hidden_grad = right_product(second_low, ffn_out)
    sigmoid_gate = jax.nn.sigmoid(gate_part)
    gate_grad = hidden_grad * up_part * sigmoid_gate * (1.0 + gate_part * (1.0 - sigmoid_gate))
    up_grad = hidden_grad * gate_part * sigmoid_gate
    gate_up_low = jnp.concatenate([gate_grad, up_grad], axis=1).astype(jnp.bfloat16)
    ffn_in_grad = left_product(normed_two, gate_up_low)
    normed_two_grad = right_product(gate_up_low, ffn_in)
    gain_two_grad, read_grad = norm_back(normed_two_grad, normal_two, scale_two, gain_values[:, 1])
    mid_grad = grad_out + mixing[None, :, stream_count + 2, None] * read_grad[:, None, :]
    grad_read_two = jnp.sum(streams_mid * read_grad[:, None, :], axis=(0, 2))
    first_low = jnp.sum(mid_grad * mixing[None, :, stream_count + 1, None], axis=1).astype(
        jnp.bfloat16
    )
    grad_depth_one = jnp.sum(mid_grad * first_out[:, None, :], axis=(0, 2))
    attn_out_grad = left_product(context, first_low)
    context_grad = (
        right_product(first_low, attn_out).astype(jnp.bfloat16).reshape(row_count, HEADS, HD)
    )
    attend_grad = jnp.einsum(
        "qhd,khd->hqk", context_grad, values_all, preferred_element_type=jnp.float32
    )
    values_grad = jnp.einsum(
        "hqk,qhd->khd", attend_low, context_grad, preferred_element_type=jnp.float32
    )
    inner_sum = jnp.sum(attend * attend_grad, axis=-1, keepdims=True)
    score_low = (attend * (attend_grad - inner_sum)).astype(jnp.bfloat16)
    query_grad = jnp.einsum(
        "hqk,khd->qhd", score_low, keys_all, preferred_element_type=jnp.float32
    ) * HD ** (-0.5)
    keys_grad = jnp.einsum(
        "hqk,qhd->khd", score_low, queries, preferred_element_type=jnp.float32
    ) * HD ** (-0.5)
    returned = jnp.concatenate(
        [
            keys_grad[:row_count].reshape(row_count, model_width),
            values_grad[:row_count].reshape(row_count, model_width),
        ],
        axis=1,
    )
    from_later = shifted(returned.astype(jnp.bfloat16), "seq", -1).astype(returned.dtype)
    own_keys = keys_grad[row_count:].reshape(row_count, model_width) + from_later[:, :model_width]
    own_values = (
        values_grad[row_count:].reshape(row_count, model_width) + from_later[:, model_width:]
    )
    query_back = rotate_back(query_grad, cosine, sine_table).reshape(row_count, model_width)
    key_back = rotate_back(own_keys.reshape(row_count, HEADS, HD), cosine, sine_table).reshape(
        row_count, model_width
    )
    project_low = jnp.concatenate([query_back, key_back, own_values], axis=1).astype(jnp.bfloat16)
    attn_in_grad = left_product(normed, project_low)
    normed_grad = right_product(project_low, attn_in)
    gain_one_grad, branch_grad = norm_back(normed_grad, normal_one, scale_one, gain_values[:, 0])
    stream_grad = jnp.sum(mid_grad[:, None, :, :] * mixing[None, :, :stream_count, None], axis=2)
    stream_grad = stream_grad + mixing[None, :, stream_count, None] * branch_grad[:, None, :]
    grad_mix = jnp.sum(stream_values[:, :, None, :] * mid_grad[:, None, :, :], axis=(0, 3))
    grad_read_one = jnp.sum(stream_values * branch_grad[:, None, :], axis=(0, 2))
    mixing_grad = jnp.concatenate(
        [
            grad_mix,
            grad_read_one[:, None],
            grad_depth_one[:, None],
            grad_read_two[:, None],
            grad_depth_two[:, None],
        ],
        axis=1,
    )
    gains_grad = jnp.stack([gain_one_grad, gain_two_grad], axis=1)
    return (
        stream_grad,
        (attn_in_grad, attn_out_grad, ffn_in_grad, ffn_out_grad),
        gains_grad,
        mixing_grad,
    )


def adam_step(shard_state, shard_grad):
    weight = shard_state[0]
    first_new = beta_first * shard_state[1] + (1.0 - beta_first) * shard_grad
    second_new = beta_second * shard_state[2] + (1.0 - beta_second) * shard_grad * shard_grad
    first_hat = first_new / (1.0 - beta_first**STEP)
    second_hat = second_new / (1.0 - beta_second**STEP)
    update = first_hat / (jnp.sqrt(second_hat) + adam_epsilon) + weight_decay * weight
    weight_new = weight - learn_rate * update
    return (weight_new, first_new, second_new)


def rope_constants(length, head_size):
    half_size = head_size // 2
    exponent = np.arange(half_size, dtype=np.float32) * np.float32(2.0 / head_size)
    frequency = np.power(np.float64(rope_base), -exponent.astype(np.float64)).astype(np.float32)
    angles = np.arange(length, dtype=np.float32)[:, None] * frequency[None, :]
    cosine = np.cos(angles.astype(np.float64)).astype(np.float32)
    sine = np.sin(angles.astype(np.float64)).astype(np.float32)
    return np.tile(cosine, (1, 4)), np.tile(np.concatenate([-sine, sine], axis=1), (1, 2))


def swapped(values):
    lane = lax.broadcasted_iota(jnp.int32, values.shape, 1)
    return jnp.where(lane % HD < HD // 2, pltpu.roll(values, 128 - HD // 2, 1), pltpu.roll(values, HD // 2, 1))


def unpacked(block):
    count = block.shape[0]
    flat = block.reshape(count * NS, block.shape[2])
    row = lax.broadcasted_iota(jnp.int32, (count * NS, count * NS), 0)
    col = lax.broadcasted_iota(jnp.int32, (count * NS, count * NS), 1)
    pick = ((row % count) * NS + row // count == col).astype(jnp.bfloat16)
    out = jnp.dot(pick, flat, preferred_element_type=jnp.float32)
    return [out[i * count : (i + 1) * count] for i in range(NS)]


def packed_streams(parts):
    count = parts[0].shape[0]
    flat = jnp.concatenate(parts, axis=0)
    row = lax.broadcasted_iota(jnp.int32, (count * NS, count * NS), 0)
    col = lax.broadcasted_iota(jnp.int32, (count * NS, count * NS), 1)
    place = ((col % count) * NS + col // count == row).astype(jnp.bfloat16)
    out = jnp.dot(place, flat, preferred_element_type=jnp.float32).astype(jnp.bfloat16)
    return out.reshape(count, NS, parts[0].shape[1])


def normal_of(values):
    centre = jnp.mean(values, axis=-1, keepdims=True)
    centred = values - centre
    scaling = lax.rsqrt(jnp.mean(centred * centred, axis=-1, keepdims=True) + norm_epsilon)
    return centred * scaling, scaling


def nt(left, right):
    return lax.dot_general(left, right, (((1,), (1,)), ((), ())), preferred_element_type=jnp.float32)


def tn(left, right):
    return lax.dot_general(left, right, (((0,), (0,)), ((), ())), preferred_element_type=jnp.float32)


def nn(left, right):
    return jnp.dot(left, right, preferred_element_type=jnp.float32)


def doc_starts(docs, place):
    start = jnp.zeros(place.shape, jnp.int32)
    bound = 0
    for j in range(docs.shape[1] - 1):
        bound = bound + docs[0, j]
        start = jnp.where(place >= bound, bound, start)
    return start


EIGHTH = 128


def q_blocks(s):
    if s == 0:
        return [(0, 0, 1, False)] + [(i, 1, i, True) for i in (1, 2, 3)]
    return [(i - 4, 1, i, True) for i in (4, 5, 6)] + [(3, 7, 1, False)]


def block_mask(docs, s, block):
    row, key, count, single = block
    shape = (EIGHTH, 2 * EIGHTH)
    place = lax.broadcasted_iota(jnp.int32, shape, 1) % EIGHTH
    at = lax.broadcasted_iota(jnp.int32, shape, 0)
    if single:
        return at <= place
    first = (4 * s + row) * EIGHTH
    start = doc_starts(docs, place + first)
    return (at + first >= start) & (at <= place)


def two_heads(pair):
    lane = lax.broadcasted_iota(jnp.int32, pair.shape, 1)
    none = jnp.zeros_like(pair)
    return jnp.concatenate([jnp.where(lane < HD, pair, none), jnp.where(lane < HD, none, pair)], axis=0)


def one_pair(stacked):
    rows = stacked.shape[1] // 2
    return jnp.concatenate([stacked[:HD, :rows], stacked[HD:, rows:]], axis=0).T


def masked_scores(k2, qs, allow):
    scores = nt(k2, qs)
    keys = scores.shape[0]
    last = jnp.where(allow, scores[keys - EIGHTH :], masked_score)
    if keys == EIGHTH:
        return last
    return jnp.concatenate([scores[: keys - EIGHTH], last], axis=0)


def forward_kernel(
    docs, small, streams, attn_in, attn_out, gains, cos_table, sin_table,
    normed, queries, keys, values, context, lse, first_out, ffn_read, cos_own, sin_own,
    stream_out, send_sem, recv_sem,
):
    f32, bf16 = jnp.float32, jnp.bfloat16
    rows, width = normed.shape
    s = lax.axis_index("seq")
    w = lax.axis_index("wide")
    partner = (1 - s, w)
    barrier = pltpu.get_barrier_semaphore()
    pl.semaphore_signal(barrier, inc=1, device_id=partner, device_id_type=MESH)

    base = 2 * width
    mix = [[small[0, base + i * 2 * NS + j] for j in range(2 * NS)] for i in range(NS)]

    def norm_block(i, carry):
        r = pl.ds(i * 64, 64)
        parts = unpacked(streams[r])
        branch = parts[0] * mix[0][NS]
        for k in range(1, NS):
            branch = branch + parts[k] * mix[k][NS]
        for k in range(NS):
            stream_out[k, r] = parts[k].astype(bf16)
        normal, _ = normal_of(branch)
        normed[r] = (normal * gains[0:1].astype(f32)).astype(bf16)
        return carry

    lax.fori_loop(0, rows // 64, norm_block, 0)

    def tables(first_special, special, plain_rows, plain_from):
        place = lax.broadcasted_iota(jnp.int32, (EIGHTH, EIGHTH), 0) + first_special
        start = doc_starts(docs, place)
        lane = lax.broadcasted_iota(jnp.int32, (EIGHTH, EIGHTH), 1)
        pick = (place - start == lane).astype(f32)
        for table, own in ((cos_table, cos_own), (sin_table, sin_own)):
            own[special] = jnp.dot(pick, table[:EIGHTH], precision=lax.Precision.HIGHEST, preferred_element_type=f32)
            own[plain_rows] = table[plain_from]

    @pl.when(s == 0)
    def _():
        tables(0, pl.ds(0, EIGHTH), pl.ds(EIGHTH, 3 * EIGHTH), pl.ds(0, 3 * EIGHTH))

    @pl.when(s == 1)
    def _():
        tables(7 * EIGHTH, pl.ds(3 * EIGHTH, EIGHTH), pl.ds(0, 3 * EIGHTH), pl.ds(3 * EIGHTH, 3 * EIGHTH))

    own_rows = pl.ds(s * rows, rows)

    def rotated(dest, dest_rows, offset):
        def body(j, carry):
            cols = pl.ds(pl.multiple_of(j * 256, 256), 256)
            source = pl.ds(pl.multiple_of(offset + j * 256, 256), 256)
            part = nn(normed[...], attn_in[:, source])
            cosine, sine = cos_own[...], sin_own[...]
            halves = []
            for k in range(2):
                piece = part[:, k * 128 : (k + 1) * 128]
                halves.append(piece * cosine + swapped(piece) * sine)
            dest[dest_rows, cols] = jnp.concatenate(halves, axis=1).astype(bf16)
            return carry

        lax.fori_loop(0, width // 256, body, 0)

    def plain(j, carry):
        cols = pl.ds(pl.multiple_of(j * 256, 256), 256)
        source = pl.ds(pl.multiple_of(2 * width + j * 256, 256), 256)
        values[own_rows, cols] = nn(normed[...], attn_in[:, source]).astype(bf16)
        return carry

    lax.fori_loop(0, width // 256, plain, 0)
    rotated(keys, own_rows, width)
    pl.semaphore_wait(barrier, 1)

    shared = pl.ds(EIGHTH, 3 * EIGHTH)
    copies = [
        pltpu.make_async_remote_copy(
            ref.at[shared], ref.at[shared], send_sem.at[i], recv_sem.at[i],
            device_id=partner, device_id_type=MESH,
        )
        for i, ref in enumerate((keys, values))
    ]

    @pl.when(s == 0)
    def _():
        for copy in copies:
            copy.start()

    rotated(queries, pl.ds(0, rows), 0)

    def attend(side):
        for bi, block in enumerate(q_blocks(side)):
            row, key, count, single = block
            r = pl.ds(row * EIGHTH, EIGHTH)
            kr = pl.ds(key * EIGHTH, count * EIGHTH)
            allow = block_mask(docs, side, block)

            def pair(hp, carry):
                cols = pl.ds(pl.multiple_of(hp * 128, 128), 128)
                qs = two_heads(queries[r, cols]) * HD ** (-0.5)
                scores = masked_scores(keys[kr, cols], qs, allow)
                top = jnp.max(scores, axis=0, keepdims=True)
                lifted = jnp.exp(scores - top)
                total = jnp.sum(lifted, axis=0, keepdims=True)
                low = (lifted * (1.0 / total)).astype(bf16)
                context[r, cols] = one_pair(tn(values[kr, cols], low)).astype(bf16)
                lse[pl.ds(bi * 8 + hp, 1), :] = top + jnp.log(total)
                return carry

            lax.fori_loop(0, width // 128, pair, 0)

    @pl.when(s == 0)
    def _():
        attend(0)
        for copy in copies:
            copy.wait_send()

    @pl.when(s == 1)
    def _():
        for copy in copies:
            copy.wait_recv()
        attend(1)

    carry_first = sum(mix[j][NS + 1] * mix[j][NS + 2] for j in range(NS))
    carry_stream = [sum(mix[i][j] * mix[j][NS + 2] for j in range(NS)) for i in range(NS)]

    def out_block(j, carry):
        cols = pl.ds(pl.multiple_of(j * 256, 256), 256)
        first = nn(context[...], attn_out[:, cols])
        first_out[:, cols] = first
        total = first * carry_first
        for i in range(NS):
            total = total + stream_out[i, :, cols].astype(f32) * carry_stream[i]
        ffn_read[:, cols] = total
        return carry

    lax.fori_loop(0, width // 256, out_block, 0)


def forward_part(streams, docs, small_state, weights, gains):
    attn_in, attn_out = weights
    rows, width = streams.shape[0], attn_out.shape[0]
    bf16, f32 = jnp.bfloat16, jnp.float32
    cos_table, sin_table = rope_constants(6 * EIGHTH, HD)
    smem = pl.BlockSpec(memory_space=pltpu.SMEM)
    vmem = pl.BlockSpec(memory_space=pltpu.VMEM)
    shape = jax.ShapeDtypeStruct
    return pl.pallas_call(
        forward_kernel,
        out_shape=[
            shape((rows, width), bf16), shape((rows, width), bf16),
            shape((2 * rows, width), bf16), shape((2 * rows, width), bf16),
            shape((rows, width), bf16), shape((32, 2 * EIGHTH), f32),
            shape((rows, width), f32), shape((rows, width), f32),
            shape((rows, 128), f32), shape((rows, 128), f32),
        ],
        in_specs=[smem, smem] + [vmem] * 6,
        out_specs=[vmem] * 10,
        scratch_shapes=[pltpu.VMEM((NS, rows, width), bf16), pltpu.SemaphoreType.DMA((2,)), pltpu.SemaphoreType.DMA((2,))],
        compiler_params=pltpu.CompilerParams(
            collective_id=2, has_side_effects=True, vmem_limit_bytes=56 * 2**20
        ),
        name="forward_attention",
    )(docs, small_state, streams, attn_in, attn_out, gains, jnp.asarray(cos_table), jnp.asarray(sin_table))


def when(test, f):
    def go():
        f()

    pl.when(test)(go)


def rest_kernel(
    dims, token_count,
    docs, small, gains, small_rows, streams, cotangent, attn_in, attn_out, ffn_in, ffn_out, state_in,
    normed_in, queries_in, keys_in, values_in, context_in, lse_in, first_in, read_in, cos_in, sin_in,
    new_out, stream_grad_out, copy_out, weight_out, first_moment_out, second_moment_out, grad_out,
    small_out, from_core,
    grads, from_a0, from_a1, from_b0, from_b1, from_c, stage_box, kv_box, kv_send, gfirst, second, dread, read,
    low, small_box,
    send_sem, recv_sem, load_sem, local_sem, stage_sem, store_sem, out_sem, small_send, small_recv,
):
    f32, bf16 = jnp.float32, jnp.bfloat16
    nz, ny, nx = dims
    rows, width = second.shape
    hidden = ffn_out.shape[0]
    shard = low.shape[0]
    piece = shard // 3
    unit = 6 * piece
    half = unit // 2
    planes = nz // 2
    s = lax.axis_index("seq")
    w = lax.axis_index("wide")
    z, y, x = w // (ny * nx), (w // nx) % ny, w % nx

    def chip(cz, cy, cx):
        return (s, (cz * ny + cy) * nx + cx)

    core = (1 - s, w)
    z_peers = [chip((z + d) % nz, y, x) for d in range(1, nz)]
    y_peers = [chip(z, (y + d) % ny, x) for d in range(1, ny)]
    x_peers = [chip(z, y, (x + d) % nx) for d in range(1, nx)]
    peers = [core] + z_peers + y_peers + x_peers
    barrier = pltpu.get_barrier_semaphore()
    for peer in peers:
        pl.semaphore_signal(barrier, inc=1, device_id=peer, device_id_type=MESH)

    base = 2 * width
    mix = [[small[0, base + i * 2 * NS + j] for j in range(2 * NS)] for i in range(NS)]
    read_one = [mix[i][NS] for i in range(NS)]
    depth_one = [mix[i][NS + 1] for i in range(NS)]
    read_two = [mix[i][NS + 2] for i in range(NS)]
    depth_two = [mix[i][NS + 3] for i in range(NS)]

    ids = {}
    unsent = []

    def number(kind, key, count=1):
        if (kind, key) not in ids:
            ids[kind, key] = ids.get(kind, 0)
            ids[kind] = ids.get(kind, 0) + count
        return ids[kind, key]

    def remote(key, ends, guard=None, recv=None):
        sent = number("send", key)
        got = (lambda: number("recv", key)) if recv is None else recv

        def copy():
            src, dst, peer = ends()
            return pltpu.make_async_remote_copy(
                src, dst, send_sem.at[sent], recv_sem.at[got()], device_id=peer, device_id_type=MESH)

        copy().start()
        unsent.append((copy, guard))
        return copy

    def wait_sends():
        for copy, guard in unsent:
            if guard is None:
                copy().wait_send()
            else:
                pl.when(guard())(lambda copy=copy: copy().wait_send())
        unsent.clear()

    one, zero = s == 1, s == 0
    group_of = {"h": 1, "e": 0, "l": 0}
    guard_of = {"h": None, "e": lambda: one, "l": lambda: zero}
    flying = {}

    def zs_of(v):
        return pl.ds(planes * group_of[v], planes)

    def zlist(v):
        return list(range(planes * group_of[v], planes * (group_of[v] + 1)))

    def guarded(v, f):
        if guard_of[v] is None:
            f()
        else:
            pl.when(guard_of[v]())(f)

    def more(v, test):
        if guard_of[v] is None:
            return test
        return lambda: guard_of[v]() & test()

    lo, hi = pl.ds(0, half), pl.ds(half, half)

    def core_send(v, c):
        sender = {"h": None, "e": lambda: zero, "l": lambda: one}[v]

        def go():
            flying[0, v, c] = [remote(
                ("core", group_of[v], c),
                lambda: (grads.at[1 - s, zs_of(v), :, :, c], from_core.at[zs_of(v), :, :, c], core),
                guard=sender)]

        if sender is None:
            go()
        else:
            pl.when(sender())(go)

    def wait_recvs(k, v, c):
        for copy in flying[k, v, c]:
            copy().wait_recv()

    def add_core(v, c):
        def go():
            wait_recvs(0, v, c)
            g = group_of[v]
            load = pltpu.make_async_copy(from_core.at[zs_of(v), :, :, c], stage_box.at[g], stage_sem.at[g])
            load.start()
            load.wait()

            def body(i, carry):
                zi, yi, xi = i // (ny * nx), (i // nx) % ny, i % nx
                at = (s, planes * g + zi, yi, xi, c)
                grads[at] = (grads[at].astype(f32) + stage_box[g, zi, yi, xi].astype(f32)).astype(bf16)
                return carry

            lax.fori_loop(0, planes * ny * nx, body, 0)
            out = []
            for d in range(1, nx):
                out.append(remote(
                    ("a0", g, c, d),
                    lambda d=d: (grads.at[s, zs_of(v), :, (x + d) % nx, c, lo],
                                 from_a0.at[d - 1, zs_of(v), :, c], x_peers[d - 1]),
                    guard=guard_of[v]))
            for d in range(1, ny):
                out.append(remote(
                    ("a1", g, c, d),
                    lambda d=d: (grads.at[s, zs_of(v), (y + d) % ny, :, c, hi],
                                 from_a1.at[d - 1, zs_of(v), :, c], y_peers[d - 1]),
                    guard=guard_of[v]))
            flying[1, v, c] = out

        guarded(v, go)

    def add_a(v, c):
        def go():
            wait_recvs(1, v, c)
            g = group_of[v]

            def body_lo(i, carry):
                zi, yi = planes * g + i // ny, i % ny
                at = (s, zi, yi, x, c, lo)
                total = grads[at].astype(f32)
                for d in range(nx - 1):
                    total = total + from_a0[d, zi, yi, c].astype(f32)
                grads[at] = total.astype(bf16)
                return carry

            def body_hi(i, carry):
                zi, xi = planes * g + i // nx, i % nx
                at = (s, zi, y, xi, c, hi)
                total = grads[at].astype(f32)
                for d in range(ny - 1):
                    total = total + from_a1[d, zi, xi, c].astype(f32)
                grads[at] = total.astype(bf16)
                return carry

            lax.fori_loop(0, planes * ny, body_lo, 0)
            lax.fori_loop(0, planes * nx, body_hi, 0)
            out = []
            for d in range(1, ny):
                out.append(remote(
                    ("b0", g, c, d),
                    lambda d=d: (grads.at[s, zs_of(v), (y + d) % ny, x, c, lo],
                                 from_b0.at[d - 1, zs_of(v), c], y_peers[d - 1]),
                    guard=guard_of[v]))
            for d in range(1, nx):
                out.append(remote(
                    ("b1", g, c, d),
                    lambda d=d: (grads.at[s, zs_of(v), y, (x + d) % nx, c, hi],
                                 from_b1.at[d - 1, zs_of(v), c], x_peers[d - 1]),
                    guard=guard_of[v]))
            flying[2, v, c] = out

        guarded(v, go)

    def add_b(v, c):
        def go():
            wait_recvs(2, v, c)
            g = group_of[v]

            def body(i, carry):
                zi = planes * g + i
                for at_rows, box, count in ((lo, from_b0, ny - 1), (hi, from_b1, nx - 1)):
                    at = (s, zi, y, x, c, at_rows)
                    total = grads[at].astype(f32)
                    for d in range(count):
                        total = total + box[d, zi, c].astype(f32)
                    grads[at] = total.astype(bf16)
                return carry

            lax.fori_loop(0, planes, body, 0)
            for zd in zlist(v):
                first = number("recv", ("z", c), nz - 1)
                when(z != zd, lambda zd=zd, first=first: remote(
                    ("z", g, c, zd),
                    lambda: (grads.at[s, zd, y, x, c], from_c.at[(z - zd + nz) % nz - 1, c], chip(zd, y, x)),
                    guard=more(v, lambda: z != zd),
                    recv=lambda: first + (z - zd + nz) % nz - 1))

        guarded(v, go)

    def in_group(g):
        return (z // planes) == g

    def owner_update(state, flat, outs):
        for c in range(3):
            for slot in range(nz - 1):
                pltpu.make_async_remote_copy(
                    grads.at[s, z, y, x, c], from_c.at[slot, c], send_sem.at[0],
                    recv_sem.at[number("recv", ("z", c), nz - 1) + slot],
                    device_id=core, device_id_type=MESH,
                ).wait_recv()
        pltpu.make_async_copy(state_in, state, load_sem.at[0]).wait()
        index = s * (nz * ny * nx) + w
        in_rows = attn_in.shape[0] * attn_in.shape[1] // width // shard
        out_rows = in_rows + attn_out.shape[0] // shard
        ffn_rows = out_rows + ffn_in.shape[0] * ffn_in.shape[1] // width // shard
        blocks = ffn_in.shape[1] // width
        thirds = attn_in.shape[1] // width

        def total_of(c, at_rows):
            total = grads[s, z, y, x, c, at_rows].astype(f32)
            for slot in range(nz - 1):
                total = total + from_c[slot, c, at_rows].astype(f32)
            return total * (1.0 / token_count)

        @pl.when(index < in_rows)
        def _():
            for c in range(3):
                for lane in range(6):
                    flat[lane, pl.ds(c, piece, stride=thirds), :] = total_of(c, pl.ds(lane * piece, piece))

        @pl.when(((index >= in_rows) & (index < out_rows)) | (index >= ffn_rows))
        def _():
            for c in range(3):
                for lane in range(6):
                    flat[lane, pl.ds(c * piece, piece), :] = total_of(c, pl.ds(lane * piece, piece))

        @pl.when((index >= out_rows) & (index < ffn_rows))
        def _():
            part = shard // blocks
            for c in range(3):
                for side in range(2):
                    for j in range(blocks):
                        flat[side * 3 + c, pl.ds(j, part, stride=blocks), :] = total_of(
                            c, pl.ds(side * half + j * part, part))

        def body(i, carry):
            r = pl.ds(i * 16, 16)
            grad = jnp.concatenate([flat[lane, r] for lane in range(6)], axis=1)
            new = adam_step((state[0, r], state[1, r], state[2, r]), grad)
            for box, value in zip(outs, new + (grad,)):
                box[r] = value
            low[r] = new[0].astype(bf16)
            return carry

        lax.fori_loop(0, shard // 16, body, 0)
        for k, (box, dest) in enumerate(zip(outs, (weight_out, first_moment_out, second_moment_out, grad_out))):
            pltpu.make_async_copy(box, dest, store_sem.at[k]).start()
        keep = pltpu.make_async_copy(low, copy_out.at[s, z, y, x], store_sem.at[4])
        keep.start()
        keep.wait()

    gather_parts = 4
    part_rows = shard // gather_parts

    def part(k):
        return pl.ds(k * part_rows, part_rows)

    def part_lo(k):
        return pl.ds(k * part_rows, part_rows // 2)

    def part_hi(k):
        return pl.ds(k * part_rows + part_rows // 2, part_rows // 2)

    def gather_z(v, k):
        def go():
            for zd in zlist(v):
                got = number("recv", ("gz", zd, k))

                def send(zd=zd, got=got):
                    for d in range(1, nz):
                        remote(
                            ("gz", zd, k, d),
                            lambda d=d: (low.at[part(k)], copy_out.at[s, zd, y, x, part(k)],
                                         chip((zd + d) % nz, y, x)),
                            guard=more(v, lambda: z == zd), recv=lambda: got)

                pl.when(z == zd)(send)

        guarded(v, go)

    def gather_b(v, k):
        def go():
            g = group_of[v]
            for zd in zlist(v):
                when(z != zd, lambda zd=zd: pltpu.make_async_remote_copy(
                    low.at[part(k)], copy_out.at[s, zd, y, x, part(k)], send_sem.at[0],
                    recv_sem.at[number("recv", ("gz", zd, k))], device_id=core, device_id_type=MESH).wait_recv())
            out = []
            for d, peer in enumerate(y_peers):
                out.append(remote(
                    ("gb0", g, k, d), lambda peer=peer: (copy_out.at[s, zs_of(v), y, x, part_lo(k)],
                                                         copy_out.at[s, zs_of(v), y, x, part_lo(k)], peer),
                    guard=guard_of[v]))
            for d, peer in enumerate(x_peers):
                out.append(remote(
                    ("gb1", g, k, d), lambda peer=peer: (copy_out.at[s, zs_of(v), y, x, part_hi(k)],
                                                         copy_out.at[s, zs_of(v), y, x, part_hi(k)], peer),
                    guard=guard_of[v]))
            flying[5, v, k] = out

        guarded(v, go)

    def gather_a(v, k):
        def go():
            wait_recvs(5, v, k)
            g = group_of[v]
            out = []
            for d, peer in enumerate(x_peers):
                out.append(remote(
                    ("ga0", g, k, d), lambda peer=peer: (copy_out.at[s, zs_of(v), :, x, part_lo(k)],
                                                         copy_out.at[s, zs_of(v), :, x, part_lo(k)], peer),
                    guard=guard_of[v]))
            for d, peer in enumerate(y_peers):
                out.append(remote(
                    ("ga1", g, k, d), lambda peer=peer: (copy_out.at[s, zs_of(v), y, :, part_hi(k)],
                                                         copy_out.at[s, zs_of(v), y, :, part_hi(k)], peer),
                    guard=guard_of[v]))
            flying[6, v, k] = out

        guarded(v, go)

    def gather_core(v, k):
        def go():
            wait_recvs(6, v, k)
            flying[7, v, k] = [remote(
                ("gc", group_of[v], k), lambda: (copy_out.at[s, zs_of(v), :, :, part(k)],
                                                 copy_out.at[s, zs_of(v), :, :, part(k)], core),
                guard=guard_of[v])]

        guarded(v, go)

    def gather_end(v, k):
        taker = {"h": None, "e": lambda: zero, "l": lambda: one}[v]

        def go():
            other = copy_out.at[1 - s, zs_of(v), :, :, part(k)]
            pltpu.make_async_remote_copy(
                other, other, send_sem.at[0], recv_sem.at[number("recv", ("gc", group_of[v], k))],
                device_id=core, device_id_type=MESH).wait_recv()

        if taker is None:
            go()
        else:
            pl.when(taker())(go)

    wide_piece = piece
    tile = hidden // 3
    tile_pieces = tile // wide_piece

    def load(src, dst, sem):
        copy = pltpu.make_async_copy(src, dst, sem)
        copy.start()
        return copy

    read_load = load(read_in, read, load_sem.at[1])

    def ffn_scope(raw, gate_w, up_w, out_w, normed_two, normed_two_t, dsecond, gate_s, up_s, dhid_s, hid, dgate, dup):
        raw_load = load(cotangent, raw, load_sem.at[2])

        def tile_loads(c):
            slot = c % 2
            copies = []
            for p in range(tile_pieces):
                at = p * 3 * wide_piece + c * wide_piece
                to = pl.ds(p * wide_piece, wide_piece)
                for k, (src, dst) in enumerate((
                    (ffn_in.at[:, pl.ds(at, wide_piece)], gate_w.at[slot, :, to]),
                    (ffn_in.at[:, pl.ds(hidden + at, wide_piece)], up_w.at[slot, :, to]),
                    (ffn_out.at[pl.ds(at, wide_piece)], out_w.at[slot, to]),
                )):
                    copies.append(load(src, dst, local_sem.at[slot, k, p]))
            return copies

        loads = {0: tile_loads(0), 1: tile_loads(1)}
        raw_load.wait()
        read_load.wait()

        def first_block(i, carry):
            r = pl.ds(i * 64, 64)
            parts = unpacked(raw[r])
            dsecond[r] = sum(parts[j] * depth_two[j] for j in range(NS)).astype(bf16)
            gfirst[r] = sum(parts[j] * depth_one[j] for j in range(NS))
            normal, _ = normal_of(read[r])
            normed_two[r] = (normal * gains[1:2].astype(f32)).astype(bf16)
            second[r] = jnp.zeros((64, width), f32)
            dread[r] = jnp.zeros((64, width), f32)
            return carry

        lax.fori_loop(0, rows // 64, first_block, 0)
        normed_two_t[...] = normed_two[...].T

        for c in range(3):
            slot = c % 2
            for copy in loads[c]:
                copy.wait()

            def sub(u, carry, c=c, slot=slot):
                cols = pl.ds(pl.multiple_of(u * 2 * wide_piece, 2 * wide_piece), 2 * wide_piece)
                wg, wu, wo = gate_w[slot, :, cols], up_w[slot, :, cols], out_w[slot, cols]
                gate_s[...] = nn(normed_two[...], wg)
                up_s[...] = nn(normed_two[...], wu)
                dhid_s[...] = nt(dsecond[...], wo)
                for i in range(rows // 64):
                    r = pl.ds(i * 64, 64)
                    gate, up, dhid = gate_s[r], up_s[r], dhid_s[r]
                    sig = 1.0 / (1.0 + jnp.exp(-gate))
                    silu = gate * sig
                    hid[r] = (silu * up).astype(bf16)
                    dgate[r] = (dhid * up * sig * (1.0 + gate - silu)).astype(bf16)
                    dup[r] = (dhid * silu).astype(bf16)
                second[...] += nn(hid[...], wo)
                dread[...] += nt(dgate[...], wg) + nt(dup[...], wu)
                dwo = tn(hid[...], dsecond[...]).astype(bf16)
                for q in range(2):
                    p = 2 * u + q
                    zi, yi, xi = planes + p // (ny * nx), (p // nx) % ny, p % nx
                    for lane in range(6):
                        grads[1, zi, yi, xi, c, pl.ds(lane * piece, piece)] = dwo[
                            q * piece : (q + 1) * piece, lane * 128 : (lane + 1) * 128]
                blocks = 2 * (hidden // width)
                part = shard // blocks
                for k, dact in enumerate((dgate, dup)):
                    dwi = nn(normed_two_t[...], dact[...]).astype(bf16)
                    j = u + k * (blocks // 2)
                    for b in range(width // part):
                        at_half, at = b // (width // part // 2), b % (width // part // 2)
                        at = at + (nz * ny * nx // 2 if at_half == 0 else 0)
                        zi, yi, xi = at // (ny * nx), (at // nx) % ny, at % nx
                        for q in range(2):
                            grads[at_half, zi, yi, xi, c, pl.ds(pl.multiple_of(q * half + j * part, 16), part)] = dwi[
                                b * part : (b + 1) * part, q * 128 : (q + 1) * 128]
                return carry

            lax.fori_loop(0, tile_pieces // 2, sub, 0)
            if c == 0:
                loads[2] = tile_loads(2)
                pl.semaphore_wait(barrier, len(peers))
            core_send("h", c)
            core_send("e", c)
            if c >= 1:
                add_core("h", c - 1)
                add_core("e", c - 1)

    pl.run_scoped(
        ffn_scope,
        pltpu.VMEM((rows, NS, width), bf16),
        pltpu.VMEM((2, width, tile), bf16), pltpu.VMEM((2, width, tile), bf16), pltpu.VMEM((2, tile, width), bf16),
        pltpu.VMEM((rows, width), bf16), pltpu.VMEM((width, rows), bf16), pltpu.VMEM((rows, width), bf16),
        pltpu.VMEM((rows, 2 * piece), f32), pltpu.VMEM((rows, 2 * piece), f32), pltpu.VMEM((rows, 2 * piece), f32),
        pltpu.VMEM((rows, 2 * piece), bf16), pltpu.VMEM((rows, 2 * piece), bf16), pltpu.VMEM((rows, 2 * piece), bf16),
    )

    gain_sums = {}

    def attention_scope(normed, queries, keys, values, context, lse, cosine, sine, w_in, w_out, dfirst, dcontext,
                        dkeys, dvalues, dproject, turned):
        loads = [
            load(src, dst, load_sem.at[3 + k])
            for k, (src, dst) in enumerate((
                (attn_out, w_out), (context_in, context), (queries_in, queries), (keys_in, keys), (values_in, values),
                (lse_in, lse), (cos_in, cosine), (sin_in, sine), (normed_in, normed), (attn_in, w_in),
            ))
        ]
        carry_first = sum(depth_one[j] * read_two[j] for j in range(NS))

        def norm_block(i, total):
            r = pl.ds(i * 64, 64)
            normal, scaling = normal_of(read[r])
            grad = dread[r]
            total = total + jnp.sum((grad * normal).reshape(8, 8, width), axis=0)
            scaled = grad * gains[1:2].astype(f32)
            centre = jnp.mean(scaled, axis=-1, keepdims=True)
            along = jnp.mean(scaled * normal, axis=-1, keepdims=True)
            value = scaling * (scaled - centre - normal * along)
            dread[r] = value
            dfirst[r] = (gfirst[r] + carry_first * value).astype(bf16)
            return total

        gain_two = lax.fori_loop(0, rows // 64, norm_block, jnp.zeros((8, width), f32))
        row = jnp.sum(gain_two, axis=0, keepdims=True)
        for k in range(width // 128):
            small_box[0, s, width // 128 + k : width // 128 + k + 1, :] = row[:, k * 128 : (k + 1) * 128]

        for copy in loads[:2]:
            copy.wait()

        def context_block(j, carry):
            cols = pl.ds(pl.multiple_of(j * 256, 256), 256)
            dcontext[:, cols] = nt(dfirst[...], w_out[cols]).astype(bf16)
            return carry

        lax.fori_loop(0, width // 256, context_block, 0)
        turned[...] = context[...].T
        shards_in = w_in.shape[1] // width * (width // piece) // 3

        def out_block(j, carry):
            cols = pl.ds(pl.multiple_of(j * 256, 256), 256)
            part = nn(turned[...], dfirst[:, cols]).astype(bf16)
            for b in range(width // piece):
                at, c = shards_in + b // 3, b % 3
                zi, yi, xi = at // (ny * nx), (at // nx) % ny, at % nx
                for q in range(2):
                    grads[0, zi, yi, xi, c, pl.ds(pl.multiple_of((2 * j + q) * piece, piece), piece)] = part[
                        b * piece : (b + 1) * piece, q * 128 : (q + 1) * 128]
            return carry

        lax.fori_loop(0, width // 256, out_block, 0)
        for copy in loads[2:]:
            copy.wait()

        def clear(i, carry):
            r = pl.ds(i * 64, 64)
            dkeys[r] = jnp.zeros((64, width), f32)
            dvalues[r] = jnp.zeros((64, width), f32)
            return carry

        lax.fori_loop(0, 2 * rows // 64, clear, 0)

        def block_back(side, bi):
            block = q_blocks(side)[bi]
            row, key, count, single = block
            r = pl.ds(row * EIGHTH, EIGHTH)
            kr = pl.ds(key * EIGHTH, count * EIGHTH)
            allow = block_mask(docs, side, block)

            def pair(hp, carry):
                cols = pl.ds(pl.multiple_of(hp * 128, 128), 128)
                qs = two_heads(queries[r, cols]) * HD ** (-0.5)
                dstack = two_heads(dcontext[r, cols])
                k2 = keys[kr, cols]
                probs = jnp.exp(masked_scores(k2, qs, allow) - lse[pl.ds(bi * 8 + hp, 1), :])
                dprobs = nt(values[kr, cols], dstack)
                inner = jnp.sum(probs * dprobs, axis=0, keepdims=True)
                dscores = (probs * (dprobs - inner)).astype(bf16)
                dkeys[kr, cols] += nn(dscores, qs)
                dvalues[kr, cols] += nn(probs.astype(bf16), dstack)
                dq = one_pair(tn(k2, dscores)) * HD ** (-0.5)
                dproject[r, cols] = (dq * cosine[r] - swapped(dq) * sine[r]).astype(bf16)
                return carry

            lax.fori_loop(0, width // 128, pair, 0)

        between = {
            0: [lambda: add_core("h", 2), lambda: add_core("e", 2)],
            1: [lambda: add_a("h", 0), lambda: add_a("e", 0)],
            2: [lambda: add_a("h", 1), lambda: add_a("e", 1)],
            3: [lambda: add_b("h", 0), lambda: add_b("e", 0)],
        }
        for bi in range(4):
            for side in range(2):
                pl.when(s == side)(lambda side=side: block_back(side, bi))
            for action in between[bi]:
                action()

        shared = pl.ds(EIGHTH, 3 * EIGHTH)

        @pl.when(one)
        def _():
            def body(i, carry):
                r = pl.ds(i * 64, 64)
                kr = pl.ds(EIGHTH + i * 64, 64)
                kv_send[0, r] = dkeys[kr].astype(bf16)
                kv_send[1, r] = dvalues[kr].astype(bf16)
                return carry

            lax.fori_loop(0, 3 * EIGHTH // 64, body, 0)
            flying["kv"] = remote(("kv",), lambda: (kv_send, kv_box, core), guard=lambda: one)

        @pl.when(zero)
        def _():
            flying["kv"]().wait_recv()

            def body(i, carry):
                r = pl.ds(i * 64, 64)
                kr = pl.ds(EIGHTH + i * 64, 64)
                dkeys[kr] += kv_box[0, r].astype(f32)
                dvalues[kr] += kv_box[1, r].astype(f32)
                return carry

            lax.fori_loop(0, 3 * EIGHTH // 64, body, 0)

        def turn_block(i, carry):
            r = pl.ds(i * 64, 64)
            kr = pl.ds(s * rows + i * 64, 64)
            ct, st = cosine[r], sine[r]
            for k in range(width // 128):
                cols = pl.ds(k * 128, 128)
                dk = dkeys[kr, cols]
                dproject[r, pl.ds(width + k * 128, 128)] = (dk * ct - swapped(dk) * st).astype(bf16)
            dproject[r, pl.ds(2 * width, width)] = dvalues[kr].astype(bf16)
            return carry

        lax.fori_loop(0, rows // 64, turn_block, 0)
        turned[...] = normed[...].T

        for j in range(w_in.shape[1] // width):
            def in_block(cb, carry, j=j):
                cols = pl.ds(pl.multiple_of(j * width + cb * 256, 256), 256)
                part = nn(turned[...], dproject[:, cols]).astype(bf16)
                for b in range(width // piece):
                    zi, yi, xi = b // (ny * nx), (b // nx) % ny, b % nx
                    for q in range(2):
                        grads[0, zi, yi, xi, j, pl.ds(pl.multiple_of((2 * cb + q) * piece, piece), piece)] = part[
                            b * piece : (b + 1) * piece, q * 128 : (q + 1) * 128]
                return carry

            lax.fori_loop(0, width // 256, in_block, 0)
            core_send("l", j)

        def dnormed_block(j, carry):
            cols = pl.ds(pl.multiple_of(j * 256, 256), 256)
            gfirst[:, cols] = nt(dproject[...], w_in[cols])
            return carry

        lax.fori_loop(0, width // 256, dnormed_block, 0)

    pl.run_scoped(
        attention_scope,
        pltpu.VMEM((rows, width), bf16), pltpu.VMEM((rows, width), bf16),
        pltpu.VMEM((2 * rows, width), bf16), pltpu.VMEM((2 * rows, width), bf16),
        pltpu.VMEM((rows, width), bf16), pltpu.VMEM((32, 2 * EIGHTH), f32),
        pltpu.VMEM((rows, 128), f32), pltpu.VMEM((rows, 128), f32),
        pltpu.VMEM(attn_in.shape, bf16), pltpu.VMEM(attn_out.shape, bf16),
        pltpu.VMEM((rows, width), bf16), pltpu.VMEM((rows, width), bf16),
        pltpu.VMEM((2 * rows, width), f32), pltpu.VMEM((2 * rows, width), f32),
        pltpu.VMEM((rows, 3 * width), bf16), pltpu.VMEM((width, rows), bf16),
    )

    def tail_scope(raw_h, raw_g, first, new_box, back_box, state, flat, out_w, out_m, out_v, out_g):
        loads = [load(streams, raw_h, load_sem.at[13]), load(cotangent, raw_g, load_sem.at[14]),
                 load(first_in, first, load_sem.at[15]), load(state_in, state, load_sem.at[0])]
        for copy in loads[:3]:
            copy.wait()
        mixed_read = [sum(mix[i][j] * read_two[j] for j in range(NS)) for i in range(NS)]
        pairs = 33
        block = 32

        def out_copies(i, slot):
            r = pl.ds(i * block, block)
            return [pltpu.make_async_copy(new_box.at[slot], new_out.at[r], out_sem.at[0, slot]),
                    pltpu.make_async_copy(back_box.at[slot], stream_grad_out.at[r], out_sem.at[1, slot])]

        def body(i, carry):
            gain_one, sums = carry
            r = pl.ds(i * block, block)
            slot = i % 2

            @pl.when(i >= 2)
            def _():
                for copy in out_copies(i, slot):
                    copy.wait()

            hs, gs = unpacked(raw_h[r]), unpacked(raw_g[r])
            first_r, second_r, dread_r = first[r], second[r], dread[r]
            branch = sum(hs[k] * read_one[k] for k in range(NS))
            normal, scaling = normal_of(branch)
            grad = gfirst[r]
            gain_one = gain_one + jnp.sum((grad * normal).reshape(block // 8, 8, width), axis=0)
            scaled = grad * gains[0:1].astype(f32)
            centre = jnp.mean(scaled, axis=-1, keepdims=True)
            along = jnp.mean(scaled * normal, axis=-1, keepdims=True)
            dbranch = scaling * (scaled - centre - normal * along)
            back = [
                (sum(gs[j] * mix[k][j] for j in range(NS)) + dread_r * mixed_read[k] + dbranch * read_one[k]).astype(bf16)
                for k in range(NS)
            ]
            back_box[slot] = packed_streams(back)
            new = [
                (sum(hs[k] * mix[k][j] for k in range(NS)) + first_r * depth_one[j] + second_r * depth_two[j]).astype(bf16)
                for j in range(NS)
            ]
            new_box[slot] = packed_streams(new)
            for copy in out_copies(i, slot):
                copy.start()
            products = [(hs[a], gs[b]) for a in range(NS) for b in range(NS)]
            products += [(hs[a], dread_r) for a in range(NS)]
            products += [(hs[a], dbranch) for a in range(NS)]
            products += [(first_r, gs[b]) for b in range(NS)] + [(first_r, dread_r)]
            products += [(second_r, gs[b]) for b in range(NS)]
            new_sums = []
            for total, (a, b) in zip(sums, products):
                p = jnp.sum((a * b).reshape(block // 8, 8, width), axis=0)
                new_sums.append(total + sum(p[:, q * 128 : (q + 1) * 128] for q in range(width // 128)))
            return gain_one, tuple(new_sums)

        zero_tile = jnp.zeros((8, 128), f32)
        gain_one, sums = lax.fori_loop(
            0, rows // block, body, (jnp.zeros((8, width), f32), tuple(zero_tile for _ in range(pairs))))
        for i in (rows // block - 2, rows // block - 1):
            for copy in out_copies(i, i % 2):
                copy.wait()
        row = jnp.sum(gain_one, axis=0, keepdims=True)
        for k in range(width // 128):
            small_box[0, s, k : k + 1, :] = row[:, k * 128 : (k + 1) * 128]
        sums = [jnp.sum(jnp.sum(t, axis=0, keepdims=True), axis=1, keepdims=True) for t in sums]
        hg = [[sums[a * NS + b] for b in range(NS)] for a in range(NS)]
        h_read = sums[16:20]
        h_branch = sums[20:24]
        first_g, first_read, second_g = sums[24:28], sums[28], sums[29:33]
        lane = lax.broadcasted_iota(jnp.int32, (1, 128), 1)
        line = jnp.zeros((1, 128), f32)
        for i in range(NS):
            entries = [hg[i][j] + read_two[j] * h_read[i] for j in range(NS)]
            entries.append(h_branch[i])
            entries.append(first_g[i] + read_two[i] * first_read)
            entries.append(sum(mix[k][i] * h_read[k] for k in range(NS)) + depth_one[i] * first_read)
            entries.append(second_g[i])
            for j, value in enumerate(entries):
                line = jnp.where(lane == i * 2 * NS + j, value, line)
        last = 2 * width // 128
        small_box[0, s, last : last + 1, :] = line
        small_box[0, s, last + 1 :, :] = jnp.zeros((small_box.shape[2] - last - 1, 128), f32)

        small_index = [0]
        axes = [(s, [core], 2), (x, x_peers, nx), (y, y_peers, ny), (z, z_peers, nz)]
        small_copies = []

        def small_send_all(k, place, others):
            copies = []
            for peer in others:
                i = small_index[0]
                small_index[0] += 1
                copy = pltpu.make_async_remote_copy(
                    small_box.at[k, place], small_box.at[k, place], small_send.at[i], small_recv.at[i],
                    device_id=peer, device_id_type=MESH)
                copy.start()
                copies.append(copy)
            small_copies.append(copies)

        def small_stage(k):
            for copy in small_copies[k]:
                copy.wait()
            total = small_box[k, 0]
            for j in range(1, axes[k][2]):
                total = total + small_box[k, j]
            if k + 1 < len(axes):
                small_box[k + 1, axes[k + 1][0]] = total
                small_send_all(k + 1, axes[k + 1][0], axes[k + 1][1])
            else:
                grad = total * (1.0 / token_count)
                new = adam_step((small_rows[0], small_rows[1], small_rows[2]), grad)
                for k2, value in enumerate(new + (grad,)):
                    small_out[k2] = value

        small_send_all(0, axes[0][0], axes[0][1])

        boxes = (out_w, out_m, out_v, out_g)
        parts = range(gather_parts)
        for c in range(3):
            add_core("l", c)
        add_a("h", 2)
        add_a("e", 2)
        add_b("h", 1)
        add_b("e", 1)
        small_stage(0)
        add_a("l", 0)
        add_b("h", 2)
        add_b("e", 2)
        small_stage(1)
        add_a("l", 1)
        add_a("l", 2)
        small_stage(2)

        @pl.when(in_group(1) | one)
        def _():
            owner_update(state, flat, boxes)

        for k in parts:
            gather_z("h", k)
            gather_z("e", k)
        for c in range(3):
            add_b("l", c)
        small_stage(3)
        for k in parts:
            gather_b("h", k)
            gather_b("e", k)

        @pl.when(in_group(0) & zero)
        def _():
            owner_update(state, flat, boxes)

        for k in parts:
            gather_z("l", k)
        for k in parts:
            gather_a("h", k)
            gather_a("e", k)
            gather_b("l", k)
        for k in parts:
            gather_core("h", k)
            gather_core("e", k)
            gather_a("l", k)
        for k in parts:
            gather_core("l", k)
        for k in parts:
            for v in ("h", "e", "l"):
                gather_end(v, k)

        wait_sends()
        for k2, (box, dest) in enumerate(zip(boxes, (weight_out, first_moment_out, second_moment_out, grad_out))):
            pltpu.make_async_copy(box, dest, store_sem.at[k2]).wait()

    pl.run_scoped(
        tail_scope,
        pltpu.VMEM((rows, NS, width), bf16), pltpu.VMEM((rows, NS, width), bf16), pltpu.VMEM((rows, width), f32),
        pltpu.VMEM((2, 32, NS, width), bf16), pltpu.VMEM((2, 32, NS, width), bf16),
        pltpu.VMEM((3, shard, width), f32), pltpu.VMEM((6, shard, 128), f32),
        pltpu.VMEM((shard, width), f32), pltpu.VMEM((shard, width), f32),
        pltpu.VMEM((shard, width), f32), pltpu.VMEM((shard, width), f32),
    )
    assert ids["send"] <= send_sem.shape[0] and ids["recv"] <= recv_sem.shape[0], ids


def rest_part(dims, token_count, docs, small_state, gains, streams, cotangent, weights, big_state, kept):
    attn_in, attn_out, ffn_in, ffn_out = weights
    nz, ny, nx = dims
    rows, width = streams.shape[0], attn_out.shape[0]
    shard = big_state.shape[1]
    unit, half, hidden = 2 * shard, shard, ffn_out.shape[0]
    bf16, f32 = jnp.bfloat16, jnp.float32
    shape = jax.ShapeDtypeStruct
    small_count = small_state.shape[1]
    small_rows = jnp.pad(small_state, ((0, 0), (0, -small_count % 1024))).reshape(3, -1, 128)
    small_shape = small_rows.shape[1:]
    smem = pl.BlockSpec(memory_space=pltpu.SMEM)
    vmem = pl.BlockSpec(memory_space=pltpu.VMEM)
    hbm = pl.BlockSpec(memory_space=pl.ANY)
    state_shape = shape((shard, width), f32)
    stream_shape = shape((rows, NS, width), bf16)
    outs = pl.pallas_call(
        functools.partial(rest_kernel, dims, token_count),
        out_shape=[
            stream_shape, stream_shape, shape((2, nz, ny, nx, shard, width), bf16),
            state_shape, state_shape, state_shape, state_shape, shape((4,) + small_shape, f32),
            shape((nz, ny, nx, 3, unit, 128), bf16),
        ],
        in_specs=[smem, smem, vmem, vmem] + [hbm] * 17,
        out_specs=[hbm] * 7 + [vmem, hbm],
        scratch_shapes=[
            pltpu.VMEM((2, nz, ny, nx, 3, unit, 128), bf16),
            pltpu.VMEM((max(nx - 1, 1), nz, ny, 3, half, 128), bf16),
            pltpu.VMEM((max(ny - 1, 1), nz, nx, 3, half, 128), bf16),
            pltpu.VMEM((max(ny - 1, 1), nz, 3, half, 128), bf16),
            pltpu.VMEM((max(nx - 1, 1), nz, 3, half, 128), bf16),
            pltpu.VMEM((max(nz - 1, 1), 3, unit, 128), bf16),
            pltpu.VMEM((2, nz // 2, ny, nx, unit, 128), bf16),
            pltpu.VMEM((2, 3 * EIGHTH, width), bf16),
            pltpu.VMEM((2, 3 * EIGHTH, width), bf16),
            pltpu.VMEM((rows, width), f32), pltpu.VMEM((rows, width), f32),
            pltpu.VMEM((rows, width), f32), pltpu.VMEM((rows, width), f32),
            pltpu.VMEM((shard, width), bf16),
            pltpu.VMEM((4, max(2, nx, ny, nz)) + small_shape, f32),
            pltpu.SemaphoreType.DMA((180,)), pltpu.SemaphoreType.DMA((120,)),
            pltpu.SemaphoreType.DMA((16,)), pltpu.SemaphoreType.DMA((2, 3, 8)),
            pltpu.SemaphoreType.DMA((2,)), pltpu.SemaphoreType.DMA((5,)), pltpu.SemaphoreType.DMA((2, 2)),
            pltpu.SemaphoreType.DMA((8,)), pltpu.SemaphoreType.DMA((8,)),
        ],
        compiler_params=pltpu.CompilerParams(
            collective_id=1, has_side_effects=True, vmem_limit_bytes=63 * 2**20
        ),
        name="backward_sync",
    )(docs, small_state, gains, small_rows, streams, cotangent, attn_in, attn_out, ffn_in, ffn_out, big_state, *kept)
    small_out = outs[7].reshape(4, -1)[:, :small_count]
    copy = outs[2].reshape(-1, width)
    return outs[0], outs[1], copy, outs[3], outs[4], outs[5], outs[6], small_out


def torus(mesh):
    wide = mesh.shape["wide"]
    where = [getattr(d, "coords", None) for d in mesh.devices.flat]
    if all(c is not None for c in where):
        x, y, z = (len({c[i] for c in where}) for i in range(3))
        if x * y * z == wide:
            return z, y, x
    known = {16: (4, 2, 2), 64: (4, 4, 4)}
    return known.get(wide, (wide, 1, 1))


def sync_kernel(
    dims, rows, half, lr_consts,
    grads, small_in, state_in,
    copy_out, weight_out, first_out, second_out, grad_out, small_out,
    acc, from_core, from_a0, from_a1, from_b0, from_b1, from_c,
    state, new_w, new_m, new_v, new_g, low, small_box,
    load_sem, store_sem, send_sem, recv_sem, small_send, small_recv,
):
    nz, ny, nx = dims
    chunk = 2 * half
    chunks = rows // chunk
    s = lax.axis_index("seq")
    w = lax.axis_index("wide")
    z, y, x = w // (ny * nx), (w // nx) % ny, w % nx

    def chip(cz, cy, cx):
        return (s, (cz * ny + cy) * nx + cx)

    core = (1 - s, w)
    z_peers = [chip((z + d) % nz, y, x) for d in range(1, nz)]
    y_peers = [chip(z, (y + d) % ny, x) for d in range(1, ny)]
    x_peers = [chip(z, y, (x + d) % nx) for d in range(1, nx)]
    peers = [core] + z_peers + y_peers + x_peers

    barrier = pltpu.get_barrier_semaphore()
    for peer in peers:
        pl.semaphore_signal(barrier, inc=1, device_id=peer, device_id_type=MESH)

    loads = [
        pltpu.make_async_copy(
            grads.at[s, :, :, :, pl.ds(c * chunk, chunk)],
            acc.at[:, :, :, pl.ds(c * chunk, chunk)],
            load_sem.at[c],
        )
        for c in range(chunks)
    ]
    for copy in loads:
        copy.start()
    state_load = pltpu.make_async_copy(state_in, state, load_sem.at[chunks])
    state_load.start()
    pl.semaphore_wait(barrier, len(peers))

    sends = []
    counter = [0]

    def remote(src, dst, peer):
        i = counter[0]
        counter[0] += 1
        copy = pltpu.make_async_remote_copy(
            src, dst, send_sem.at[i], recv_sem.at[i], device_id=peer, device_id_type=MESH
        )
        copy.start()
        sends.append(copy)
        return copy

    def lo(c):
        return pl.ds(c * chunk, half)

    def hi(c):
        return pl.ds(c * chunk + half, half)

    def both(c):
        return pl.ds(c * chunk, chunk)

    def packed(c):
        return pl.ds(c * half, half)

    f32 = jnp.float32

    def add_into(count, where, terms):
        def body(i, carry):
            ref, index = where(i)
            total = ref[index].astype(f32)
            for term_ref, term_index in terms(i):
                total = total + term_ref[term_index].astype(f32)
            ref[index] = total.astype(ref.dtype)
            return carry

        lax.fori_loop(0, count, body, 0)

    def small_step(k, mine, others, count):
        copies = []
        for j, peer in enumerate(others):
            i = small_index[0]
            small_index[0] += 1
            copy = pltpu.make_async_remote_copy(
                small_box.at[k, mine], small_box.at[k, mine], small_send.at[i], small_recv.at[i],
                device_id=peer, device_id_type=MESH,
            )
            copy.start()
            copies.append(copy)
        return copies

    def small_sum(k, copies, count):
        for copy in copies:
            copy.wait()
        total = small_box[k, 0]
        for j in range(1, count):
            total = total + small_box[k, j]
        return total

    small_index = [0]
    axes = [(s, [core], 2), (x, x_peers, nx), (y, y_peers, ny), (z, z_peers, nz)]
    small_box[0, s] = small_in[...]
    small_copies = [small_step(0, s, [core], 2)]

    def small_stage(k):
        total = small_sum(k, small_copies[k], axes[k][2])
        if k + 1 < len(axes):
            place, others, count = axes[k + 1]
            small_box[k + 1, place] = total
            small_copies.append(small_step(k + 1, place, others, count))
        else:
            small_out[...] = total

    state_done = [False]
    flying = {}

    def stage(k, c):
        if k == 0:
            loads[c].wait()
            for copy in flying[0, c]:
                copy.wait_recv()

            def where(i):
                return acc, (i // (ny * nx), (i // nx) % ny, i % nx, both(c))

            def terms(i):
                return [(from_core, (i // (ny * nx), (i // nx) % ny, i % nx, both(c)))]

            add_into(nz * ny * nx, where, terms)
            out = []
            for d in range(1, nx):
                out.append(remote(
                    acc.at[:, :, (x + d) % nx, lo(c)], from_a0.at[d - 1, :, :, packed(c)], x_peers[d - 1]))
            for d in range(1, ny):
                out.append(remote(
                    acc.at[:, (y + d) % ny, :, hi(c)], from_a1.at[d - 1, :, :, packed(c)], y_peers[d - 1]))
            flying[1, c] = out
        elif k == 1:
            for copy in flying[1, c]:
                copy.wait_recv()
            add_into(
                nz * ny,
                lambda i: (acc, (i // ny, i % ny, x, lo(c))),
                lambda i: [(from_a0, (d, i // ny, i % ny, packed(c))) for d in range(nx - 1)],
            )
            add_into(
                nz * nx,
                lambda i: (acc, (i // nx, y, i % nx, hi(c))),
                lambda i: [(from_a1, (d, i // nx, i % nx, packed(c))) for d in range(ny - 1)],
            )
            out = []
            for d in range(1, ny):
                out.append(remote(
                    acc.at[:, (y + d) % ny, x, lo(c)], from_b0.at[d - 1, :, packed(c)], y_peers[d - 1]))
            for d in range(1, nx):
                out.append(remote(
                    acc.at[:, y, (x + d) % nx, hi(c)], from_b1.at[d - 1, :, packed(c)], x_peers[d - 1]))
            flying[2, c] = out
        elif k == 2:
            for copy in flying[2, c]:
                copy.wait_recv()
            add_into(
                nz,
                lambda i: (acc, (i, y, x, lo(c))),
                lambda i: [(from_b0, (d, i, packed(c))) for d in range(ny - 1)],
            )
            add_into(
                nz,
                lambda i: (acc, (i, y, x, hi(c))),
                lambda i: [(from_b1, (d, i, packed(c))) for d in range(nx - 1)],
            )
            out = []
            for d in range(1, nz):
                out.append(remote(
                    acc.at[(z + d) % nz, y, x, both(c)], from_c.at[d - 1, both(c)], z_peers[d - 1]))
            flying[3, c] = out
        elif k == 3:
            for copy in flying[3, c]:
                copy.wait_recv()
            if not state_done[0]:
                state_load.wait()
                state_done[0] = True
            step = 16

            def body(i, carry):
                r = pl.ds(c * chunk + i * step, step)
                total = acc[z, y, x, r].astype(f32)
                for d in range(nz - 1):
                    total = total + from_c[d, r].astype(f32)
                grad = total * lr_consts
                w_new, m_new, v_new = adam_step((state[0, r], state[1, r], state[2, r]), grad)
                new_g[r] = grad
                new_w[r] = w_new
                new_m[r] = m_new
                new_v[r] = v_new
                low[r] = w_new.astype(low.dtype)
                return carry

            lax.fori_loop(0, chunk // step, body, 0)
            out = []
            for peer in z_peers:
                out.append(remote(low.at[both(c)], copy_out.at[s, z, y, x, both(c)], peer))
            own = pltpu.make_async_copy(low.at[both(c)], copy_out.at[s, z, y, x, both(c)], store_sem.at[0, c])
            own.start()
            for j, (a, b) in enumerate(((new_w, weight_out), (new_m, first_out), (new_v, second_out), (new_g, grad_out))):
                st = pltpu.make_async_copy(a.at[both(c)], b.at[both(c)], store_sem.at[j + 1, c])
                st.start()
                stores.append(st)
            flying[4, c] = (out, own)
        elif k == 4:
            out, own = flying[4, c]
            own.wait()
            for copy in out:
                copy.wait_recv()
            nxt = []
            for peer in y_peers:
                nxt.append(remote(copy_out.at[s, :, y, x, lo(c)], copy_out.at[s, :, y, x, lo(c)], peer))
            for peer in x_peers:
                nxt.append(remote(copy_out.at[s, :, y, x, hi(c)], copy_out.at[s, :, y, x, hi(c)], peer))
            flying[5, c] = nxt
        elif k == 5:
            for copy in flying[5, c]:
                copy.wait_recv()
            nxt = []
            for peer in x_peers:
                nxt.append(remote(copy_out.at[s, :, :, x, lo(c)], copy_out.at[s, :, :, x, lo(c)], peer))
            for peer in y_peers:
                nxt.append(remote(copy_out.at[s, :, y, :, hi(c)], copy_out.at[s, :, y, :, hi(c)], peer))
            flying[6, c] = nxt
        elif k == 6:
            for copy in flying[6, c]:
                copy.wait_recv()
            flying[7, c] = [
                remote(copy_out.at[s, :, :, :, both(c)], copy_out.at[s, :, :, :, both(c)], core)]
        elif k == 7:
            for copy in flying[7, c]:
                copy.wait_recv()

    stores = []
    for c in range(chunks):
        flying[0, c] = [remote(
            grads.at[1 - s, :, :, :, both(c)], from_core.at[:, :, :, both(c)], core)]
    stages = 8
    for t in range(chunks + stages - 1):
        for k in reversed(range(stages)):
            c = t - k
            if 0 <= c < chunks:
                stage(k, c)
        if 1 <= t <= 4:
            small_stage(t - 1)
    for copy in sends:
        copy.wait_send()
    for copy in stores:
        copy.wait()


def sync_grads(dims, flat_low, small_local, big_state, token_count):
    nz, ny, nx = dims
    wide = nz * ny * nx
    model_width = flat_low.shape[1]
    rows = big_state.shape[1]
    half = next(h for h in (48, 32, 16) if rows % (2 * h) == 0)
    chunks = rows // (2 * half)
    bf16, f32 = jnp.bfloat16, jnp.float32
    copies = chunks * (2 + 4 * (nx - 1) + 4 * (ny - 1) + 2 * (nz - 1))
    small_copies = 1 + (nx - 1) + (ny - 1) + (nz - 1)
    hbm = pl.BlockSpec(memory_space=pl.ANY)
    vmem = pl.BlockSpec(memory_space=pltpu.VMEM)
    state_shape = jax.ShapeDtypeStruct((rows, model_width), f32)
    small_shape = small_local.shape
    outs = pl.pallas_call(
        functools.partial(sync_kernel, dims, rows, half, 1.0 / token_count),
        out_shape=[
            jax.ShapeDtypeStruct((2, nz, ny, nx, rows, model_width), bf16),
            state_shape, state_shape, state_shape, state_shape,
            jax.ShapeDtypeStruct(small_shape, f32),
        ],
        in_specs=[hbm, vmem, hbm],
        out_specs=[hbm] * 5 + [vmem],
        scratch_shapes=[
            pltpu.VMEM((nz, ny, nx, rows, model_width), bf16),
            pltpu.VMEM((nz, ny, nx, rows, model_width), bf16),
            pltpu.VMEM((max(nx - 1, 1), nz, ny, rows // 2, model_width), bf16),
            pltpu.VMEM((max(ny - 1, 1), nz, nx, rows // 2, model_width), bf16),
            pltpu.VMEM((max(ny - 1, 1), nz, rows // 2, model_width), bf16),
            pltpu.VMEM((max(nx - 1, 1), nz, rows // 2, model_width), bf16),
            pltpu.VMEM((max(nz - 1, 1), rows, model_width), bf16),
            pltpu.VMEM((3, rows, model_width), f32),
            pltpu.VMEM((rows, model_width), f32),
            pltpu.VMEM((rows, model_width), f32),
            pltpu.VMEM((rows, model_width), f32),
            pltpu.VMEM((rows, model_width), f32),
            pltpu.VMEM((rows, model_width), bf16),
            pltpu.VMEM((4, max(2, nx, ny, nz)) + small_shape, f32),
            pltpu.SemaphoreType.DMA((chunks + 1,)),
            pltpu.SemaphoreType.DMA((5, chunks)),
            pltpu.SemaphoreType.DMA((copies,)),
            pltpu.SemaphoreType.DMA((copies,)),
            pltpu.SemaphoreType.DMA((small_copies,)),
            pltpu.SemaphoreType.DMA((small_copies,)),
        ],
        compiler_params=pltpu.CompilerParams(
            collective_id=1, has_side_effects=True, vmem_limit_bytes=56 * 2**20
        ),
        name="sync_grads",
    )(
        flat_low.reshape(2, nz, ny, nx, rows, model_width), small_local, big_state
    )
    return (outs[0].reshape(2 * wide * rows, model_width),) + tuple(outs[1:])


def on_device(
    dims,
    streams,
    cotangent,
    doc_lengths,
    attn_in,
    attn_out,
    ffn_in,
    ffn_out,
    norm_gains,
    big_state,
    small_state,
):
    row_count = streams.shape[1]
    model_width = attn_out.shape[0]
    fits = (
        big_state.shape[1] == 384 and model_width == 768 and row_count == 512 and dims[0] % 2 == 0
        and ffn_out.shape[0] == 3072 and dims[0] * dims[1] * dims[2] == 16
    )
    if fits:
        kept = forward_part(streams[0], doc_lengths, small_state, (attn_in, attn_out), norm_gains.T)
        token_count = 2 * row_count * lax.axis_size("wide")
        result, stream_grad, gathered, weight_new, first_new, second_new, owned_grads, small_out = rest_part(
            dims, token_count, doc_lengths, small_state, norm_gains.T, streams[0], cotangent[0],
            (attn_in, attn_out, ffn_in, ffn_out), big_state, kept,
        )
        gains_copy = small_out[0, : 2 * model_width].reshape(2, model_width).T.astype(jnp.bfloat16)
        return (
            result[None], stream_grad[None], weight_new, first_new, second_new, owned_grads,
            small_out[0], small_out[1], small_out[2], small_out[3], gathered, gains_copy,
        )
    member = lax.axis_index("seq")
    token_total = row_count * lax.axis_size("seq")
    token_count = token_total * lax.axis_size("wide")
    segment, position = doc_layout(doc_lengths[0], token_total)
    own_start = member * row_count
    own_index = own_start + jnp.arange(row_count, dtype=jnp.int32)
    seg_query = lax.dynamic_slice_in_dim(segment, own_start, row_count)
    pos_query = lax.dynamic_slice_in_dim(position, own_start, row_count)
    padded_seg = jnp.concatenate([jnp.full((row_count,), -1, jnp.int32), segment])
    key_seg = lax.dynamic_slice_in_dim(padded_seg, own_start, 2 * row_count)
    key_index = own_start - row_count + jnp.arange(2 * row_count, dtype=jnp.int32)
    allowed = (key_seg[None, :] == seg_query[:, None]) & (key_index[None, :] <= own_index[:, None])
    cosine, sine_table = rope_tables(pos_query, HD)
    weights = (attn_in, attn_out, ffn_in, ffn_out)
    gain_values = norm_gains.astype(jnp.float32)
    mixing = small_state[0, 2 * model_width :].reshape(NS, NS + 4)
    stream_values = streams[0].astype(jnp.float32)
    result, saved = forward_layer(
        stream_values, weights, gain_values, mixing, allowed, cosine, sine_table
    )
    grad_out = cotangent[0].astype(jnp.float32)
    stream_grad, matrix_grads, gains_local, mixing_local = backward_layer(
        stream_values, grad_out, weights, gain_values, mixing, cosine, sine_table, saved
    )
    flat_low = jnp.concatenate(
        [grad.astype(jnp.bfloat16).reshape(-1, model_width) for grad in matrix_grads], axis=0
    )
    small_local = jnp.concatenate([gains_local.T.reshape(-1), mixing_local.reshape(-1)])
    small_count = small_local.shape[0]
    padded = jnp.pad(small_local, (0, -small_count % 1024)).reshape(-1, 128)
    gathered, weight_new, first_new, second_new, owned_grads, small_total = sync_grads(
        dims, flat_low, padded, big_state, token_count
    )
    small_grads = small_total.reshape(-1)[:small_count] / token_count
    small_weight, small_first, small_second = adam_step(small_state, small_grads)
    gains_copy = small_weight[: 2 * model_width].reshape(2, model_width).T.astype(jnp.bfloat16)
    return (
        result.astype(jnp.bfloat16)[None],
        stream_grad.astype(jnp.bfloat16)[None],
        weight_new,
        first_new,
        second_new,
        owned_grads,
        small_weight,
        small_first,
        small_second,
        small_grads,
        gathered,
        gains_copy,
    )


def solution(mesh):
    in_specs = (
        P("wide", "seq", None, None),
        P("wide", "seq", None, None),
        P("wide", None),
        P(),
        P(),
        P(),
        P(),
        P(),
        P(None, ("seq", "wide"), None),
        P(),
    )
    out_specs = (
        P("wide", "seq", None, None),
        P("wide", "seq", None, None),
        P(("seq", "wide"), None),
        P(("seq", "wide"), None),
        P(("seq", "wide"), None),
        P(("seq", "wide"), None),
        P(),
        P(),
        P(),
        P(),
        P(),
        P(),
    )
    return jax.shard_map(
        functools.partial(on_device, torus(mesh)), mesh=mesh, in_specs=in_specs, out_specs=out_specs, check_vma=False
    )
```

```python
import functools

import jax
import jax.numpy as jnp
import numpy as np
from jax import lax
from jax.experimental import pallas as pl
from jax.experimental.pallas import tpu as pltpu
from jax.sharding import PartitionSpec as P

HEADS = 12
HD = 64
NS = 4
STEP = 10


norm_epsilon = 1e-05
rope_base = 10000.0
beta_first = 0.9
beta_second = 0.95
adam_epsilon = 1e-08
weight_decay = 0.1
learn_rate = 0.01
MESH = pl.DeviceIdType.MESH
masked_score = -1e30


def shifted(value, axis, by):
    count = lax.axis_size(axis)
    pairs = [(i, i + by) for i in range(count) if 0 <= i + by < count]
    return lax.ppermute(value, axis, pairs)


def doc_layout(lengths, token_total):
    bounds = jnp.cumsum(lengths)
    starts = bounds - lengths
    places = jnp.arange(token_total, dtype=jnp.int32)
    segment = jnp.sum((places[:, None] >= bounds[None, :]).astype(jnp.int32), axis=1)
    picked = segment[:, None] == jnp.arange(lengths.shape[0], dtype=jnp.int32)[None, :]
    offset = jnp.sum(jnp.where(picked, starts[None, :], 0), axis=1)
    return (segment, places - offset)


def rope_tables(position, head_size):
    exponent = jnp.arange(head_size // 2, dtype=jnp.float32) * (2.0 / head_size)
    frequency = jnp.power(jnp.float32(rope_base), -exponent)
    angles = position.astype(jnp.float32)[:, None] * frequency[None, :]
    return (jnp.cos(angles)[:, None, :], jnp.sin(angles)[:, None, :])


def rotate(values, cosine, sine_table):
    half_size = values.shape[-1] // 2
    leading = values[..., :half_size]
    trailing = values[..., half_size:]
    return jnp.concatenate(
        [leading * cosine - trailing * sine_table, trailing * cosine + leading * sine_table],
        axis=-1,
    )


def rotate_back(grads, cosine, sine_table):
    half_size = grads.shape[-1] // 2
    leading = grads[..., :half_size]
    trailing = grads[..., half_size:]
    return jnp.concatenate(
        [leading * cosine + trailing * sine_table, trailing * cosine - leading * sine_table],
        axis=-1,
    )


def norm_parts(values):
    centre = jnp.mean(values, axis=-1, keepdims=True)
    centred = values - centre
    scaling = lax.rsqrt(jnp.mean(centred * centred, axis=-1, keepdims=True) + norm_epsilon)
    return (centred * scaling, scaling)


def norm_back(grads, normal, scaling, gain):
    gain_grad = jnp.sum(grads * normal, axis=0)
    scaled = grads * gain
    centre = jnp.mean(scaled, axis=-1, keepdims=True)
    along_normal = jnp.mean(scaled * normal, axis=-1, keepdims=True)
    return (gain_grad, scaling * (scaled - centre - normal * along_normal))


def right_product(left, right):
    return lax.dot_general(
        left, right, (((1,), (1,)), ((), ())), preferred_element_type=jnp.float32
    )


def left_product(left, right):
    return lax.dot_general(
        left, right, (((0,), (0,)), ((), ())), preferred_element_type=jnp.float32
    )


def forward_layer(stream_values, weights, gain_values, mixing, allowed, cosine, sine_table):
    attn_in, attn_out, ffn_in, ffn_out = weights
    row_count = stream_values.shape[0]
    model_width = attn_out.shape[0]
    stream_count = mixing.shape[0]
    hidden_units = ffn_out.shape[0]
    branch_in = jnp.sum(stream_values * mixing[None, :, stream_count, None], axis=1)
    mixed_streams = jnp.sum(
        stream_values[:, :, None, :] * mixing[None, :, :stream_count, None], axis=1
    )
    normal_one, scale_one = norm_parts(branch_in)
    normed = (normal_one * gain_values[:, 0]).astype(jnp.bfloat16)
    project = jnp.dot(normed, attn_in, preferred_element_type=jnp.float32)
    queries = rotate(
        project[:, :model_width].reshape(row_count, HEADS, HD), cosine, sine_table
    ).astype(jnp.bfloat16)
    keys_rot = rotate(
        project[:, model_width : 2 * model_width].reshape(row_count, HEADS, HD), cosine, sine_table
    ).astype(jnp.bfloat16)
    values_in = project[:, 2 * model_width :].astype(jnp.bfloat16)
    outgoing = jnp.concatenate([keys_rot.reshape(row_count, model_width), values_in], axis=1)
    earlier = shifted(outgoing, "seq", 1)
    key_rows = jnp.concatenate([earlier, outgoing], axis=0)
    keys_all = key_rows[:, :model_width].reshape(2 * row_count, HEADS, HD)
    values_all = key_rows[:, model_width:].reshape(2 * row_count, HEADS, HD)
    scores = jnp.einsum(
        "qhd,khd->hqk", queries, keys_all, preferred_element_type=jnp.float32
    ) * HD ** (-0.5)
    scores = jnp.where(allowed[None], scores, masked_score)
    row_top = jnp.max(scores, axis=-1, keepdims=True)
    lifted = jnp.exp(scores - row_top)
    attend = lifted / jnp.sum(lifted, axis=-1, keepdims=True)
    attend_low = attend.astype(jnp.bfloat16)
    context = jnp.einsum("hqk,khd->qhd", attend_low, values_all, preferred_element_type=jnp.float32)
    context = context.reshape(row_count, model_width).astype(jnp.bfloat16)
    first_out = jnp.dot(context, attn_out, preferred_element_type=jnp.float32)
    streams_mid = mixed_streams + mixing[None, :, stream_count + 1, None] * first_out[:, None, :]
    ffn_read = jnp.sum(streams_mid * mixing[None, :, stream_count + 2, None], axis=1)
    normal_two, scale_two = norm_parts(ffn_read)
    normed_two = (normal_two * gain_values[:, 1]).astype(jnp.bfloat16)
    gate_up = jnp.dot(normed_two, ffn_in, preferred_element_type=jnp.float32)
    gate_part = gate_up[:, :hidden_units]
    up_part = gate_up[:, hidden_units:]
    hidden = (jax.nn.silu(gate_part) * up_part).astype(jnp.bfloat16)
    second_out = jnp.dot(hidden, ffn_out, preferred_element_type=jnp.float32)
    result = streams_mid + mixing[None, :, stream_count + 3, None] * second_out[:, None, :]
    saved = (
        normal_one,
        scale_one,
        normed,
        queries,
        keys_all,
        values_all,
        attend,
        attend_low,
        context,
        first_out,
        streams_mid,
        normal_two,
        scale_two,
        normed_two,
        gate_part,
        up_part,
        hidden,
        second_out,
    )
    return (result, saved)


def backward_layer(
    stream_values, grad_out, weights, gain_values, mixing, cosine, sine_table, saved
):
    attn_in, attn_out, ffn_in, ffn_out = weights
    (
        normal_one,
        scale_one,
        normed,
        queries,
        keys_all,
        values_all,
        attend,
        attend_low,
        context,
        first_out,
        streams_mid,
        normal_two,
        scale_two,
        normed_two,
        gate_part,
        up_part,
        hidden,
        second_out,
    ) = saved
    row_count = stream_values.shape[0]
    model_width = attn_out.shape[0]
    stream_count = mixing.shape[0]
    second_low = jnp.sum(grad_out * mixing[None, :, stream_count + 3, None], axis=1).astype(
        jnp.bfloat16
    )
    grad_depth_two = jnp.sum(grad_out * second_out[:, None, :], axis=(0, 2))
    ffn_out_grad = left_product(hidden, second_low)
    hidden_grad = right_product(second_low, ffn_out)
    sigmoid_gate = jax.nn.sigmoid(gate_part)
    gate_grad = hidden_grad * up_part * sigmoid_gate * (1.0 + gate_part * (1.0 - sigmoid_gate))
    up_grad = hidden_grad * gate_part * sigmoid_gate
    gate_up_low = jnp.concatenate([gate_grad, up_grad], axis=1).astype(jnp.bfloat16)
    ffn_in_grad = left_product(normed_two, gate_up_low)
    normed_two_grad = right_product(gate_up_low, ffn_in)
    gain_two_grad, read_grad = norm_back(normed_two_grad, normal_two, scale_two, gain_values[:, 1])
    mid_grad = grad_out + mixing[None, :, stream_count + 2, None] * read_grad[:, None, :]
    grad_read_two = jnp.sum(streams_mid * read_grad[:, None, :], axis=(0, 2))
    first_low = jnp.sum(mid_grad * mixing[None, :, stream_count + 1, None], axis=1).astype(
        jnp.bfloat16
    )
    grad_depth_one = jnp.sum(mid_grad * first_out[:, None, :], axis=(0, 2))
    attn_out_grad = left_product(context, first_low)
    context_grad = (
        right_product(first_low, attn_out).astype(jnp.bfloat16).reshape(row_count, HEADS, HD)
    )
    attend_grad = jnp.einsum(
        "qhd,khd->hqk", context_grad, values_all, preferred_element_type=jnp.float32
    )
    values_grad = jnp.einsum(
        "hqk,qhd->khd", attend_low, context_grad, preferred_element_type=jnp.float32
    )
    inner_sum = jnp.sum(attend * attend_grad, axis=-1, keepdims=True)
    score_low = (attend * (attend_grad - inner_sum)).astype(jnp.bfloat16)
    query_grad = jnp.einsum(
        "hqk,khd->qhd", score_low, keys_all, preferred_element_type=jnp.float32
    ) * HD ** (-0.5)
    keys_grad = jnp.einsum(
        "hqk,qhd->khd", score_low, queries, preferred_element_type=jnp.float32
    ) * HD ** (-0.5)
    returned = jnp.concatenate(
        [
            keys_grad[:row_count].reshape(row_count, model_width),
            values_grad[:row_count].reshape(row_count, model_width),
        ],
        axis=1,
    )
    from_later = shifted(returned.astype(jnp.bfloat16), "seq", -1).astype(returned.dtype)
    own_keys = keys_grad[row_count:].reshape(row_count, model_width) + from_later[:, :model_width]
    own_values = (
        values_grad[row_count:].reshape(row_count, model_width) + from_later[:, model_width:]
    )
    query_back = rotate_back(query_grad, cosine, sine_table).reshape(row_count, model_width)
    key_back = rotate_back(own_keys.reshape(row_count, HEADS, HD), cosine, sine_table).reshape(
        row_count, model_width
    )
    project_low = jnp.concatenate([query_back, key_back, own_values], axis=1).astype(jnp.bfloat16)
    attn_in_grad = left_product(normed, project_low)
    normed_grad = right_product(project_low, attn_in)
    gain_one_grad, branch_grad = norm_back(normed_grad, normal_one, scale_one, gain_values[:, 0])
    stream_grad = jnp.sum(mid_grad[:, None, :, :] * mixing[None, :, :stream_count, None], axis=2)
    stream_grad = stream_grad + mixing[None, :, stream_count, None] * branch_grad[:, None, :]
    grad_mix = jnp.sum(stream_values[:, :, None, :] * mid_grad[:, None, :, :], axis=(0, 3))
    grad_read_one = jnp.sum(stream_values * branch_grad[:, None, :], axis=(0, 2))
    mixing_grad = jnp.concatenate(
        [
            grad_mix,
            grad_read_one[:, None],
            grad_depth_one[:, None],
            grad_read_two[:, None],
            grad_depth_two[:, None],
        ],
        axis=1,
    )
    gains_grad = jnp.stack([gain_one_grad, gain_two_grad], axis=1)
    return (
        stream_grad,
        (attn_in_grad, attn_out_grad, ffn_in_grad, ffn_out_grad),
        gains_grad,
        mixing_grad,
    )


def adam_step(shard_state, shard_grad):
    weight = shard_state[0]
    first_new = beta_first * shard_state[1] + (1.0 - beta_first) * shard_grad
    second_new = beta_second * shard_state[2] + (1.0 - beta_second) * shard_grad * shard_grad
    first_hat = first_new / (1.0 - beta_first**STEP)
    second_hat = second_new / (1.0 - beta_second**STEP)
    update = first_hat / (jnp.sqrt(second_hat) + adam_epsilon) + weight_decay * weight
    weight_new = weight - learn_rate * update
    return (weight_new, first_new, second_new)


def rope_constants(length, head_size):
    half_size = head_size // 2
    exponent = np.arange(half_size, dtype=np.float32) * np.float32(2.0 / head_size)
    frequency = np.power(np.float64(rope_base), -exponent.astype(np.float64)).astype(np.float32)
    angles = np.arange(length, dtype=np.float32)[:, None] * frequency[None, :]
    cosine = np.cos(angles.astype(np.float64)).astype(np.float32)
    sine = np.sin(angles.astype(np.float64)).astype(np.float32)
    return np.tile(cosine, (1, 4)), np.tile(np.concatenate([-sine, sine], axis=1), (1, 2))


def swapped(values):
    lane = lax.broadcasted_iota(jnp.int32, values.shape, 1)
    return jnp.where(lane % HD < HD // 2, pltpu.roll(values, 128 - HD // 2, 1), pltpu.roll(values, HD // 2, 1))


def unpacked(block):
    count = block.shape[0]
    flat = block.reshape(count * NS, block.shape[2])
    row = lax.broadcasted_iota(jnp.int32, (count * NS, count * NS), 0)
    col = lax.broadcasted_iota(jnp.int32, (count * NS, count * NS), 1)
    pick = ((row % count) * NS + row // count == col).astype(jnp.bfloat16)
    out = jnp.dot(pick, flat, preferred_element_type=jnp.float32)
    return [out[i * count : (i + 1) * count] for i in range(NS)]


def packed_streams(parts):
    count = parts[0].shape[0]
    flat = jnp.concatenate(parts, axis=0)
    row = lax.broadcasted_iota(jnp.int32, (count * NS, count * NS), 0)
    col = lax.broadcasted_iota(jnp.int32, (count * NS, count * NS), 1)
    place = ((col % count) * NS + col // count == row).astype(jnp.bfloat16)
    out = jnp.dot(place, flat, preferred_element_type=jnp.float32).astype(jnp.bfloat16)
    return out.reshape(count, NS, parts[0].shape[1])


def normal_of(values):
    centre = jnp.mean(values, axis=-1, keepdims=True)
    centred = values - centre
    scaling = lax.rsqrt(jnp.mean(centred * centred, axis=-1, keepdims=True) + norm_epsilon)
    return centred * scaling, scaling


def nt(left, right):
    return lax.dot_general(left, right, (((1,), (1,)), ((), ())), preferred_element_type=jnp.float32)


def tn(left, right):
    return lax.dot_general(left, right, (((0,), (0,)), ((), ())), preferred_element_type=jnp.float32)


def nn(left, right):
    return jnp.dot(left, right, preferred_element_type=jnp.float32)


def doc_starts(docs, place):
    start = jnp.zeros(place.shape, jnp.int32)
    bound = 0
    for j in range(docs.shape[1] - 1):
        bound = bound + docs[0, j]
        start = jnp.where(place >= bound, bound, start)
    return start


EIGHTH = 128


def q_blocks(s):
    if s == 0:
        return [(0, 0, 1, False)] + [(i, 1, i, True) for i in (1, 2, 3)]
    return [(i - 4, 1, i, True) for i in (4, 5, 6)] + [(3, 7, 1, False)]


def block_mask(docs, s, block):
    row, key, count, single = block
    shape = (EIGHTH, 2 * EIGHTH)
    place = lax.broadcasted_iota(jnp.int32, shape, 1) % EIGHTH
    at = lax.broadcasted_iota(jnp.int32, shape, 0)
    if single:
        return at <= place
    first = (4 * s + row) * EIGHTH
    start = doc_starts(docs, place + first)
    return (at + first >= start) & (at <= place)


def two_heads(pair):
    lane = lax.broadcasted_iota(jnp.int32, pair.shape, 1)
    none = jnp.zeros_like(pair)
    return jnp.concatenate([jnp.where(lane < HD, pair, none), jnp.where(lane < HD, none, pair)], axis=0)


def one_pair(stacked):
    rows = stacked.shape[1] // 2
    return jnp.concatenate([stacked[:HD, :rows], stacked[HD:, rows:]], axis=0).T


def masked_scores(k2, qs, allow):
    scores = nt(k2, qs)
    keys = scores.shape[0]
    last = jnp.where(allow, scores[keys - EIGHTH :], masked_score)
    if keys == EIGHTH:
        return last
    return jnp.concatenate([scores[: keys - EIGHTH], last], axis=0)


def when(test, f):
    def go():
        f()

    pl.when(test)(go)


UP, EARLY, LATE = range(3)
(
    CORE_SEND,
    ADD_CORE,
    ADD_A,
    ADD_B,
    Z_MID,
    Z_LAST,
    GATHER_Z,
    RELAY_ONE,
    RELAY_TWO,
    GATHER_B,
    GATHER_A,
    GATHER_CORE,
    GATHER_END,
    H_B,
    H_A,
    H_Z,
    H_R1,
    H_R2,
    SMALL,
    OWNER,
) = range(20)
PARTS = 4
Z_LAST = ((UP, 0), (EARLY, 0), )
PLAN = {
    4: (
        ((CORE_SEND, UP, 0),),
        ((CORE_SEND, UP, 0),),
    ),
    5: (
        (),
        ((ADD_CORE, UP, 0),),
    ),
    8: (
        ((CORE_SEND, UP, 1), (CORE_SEND, EARLY, 0),),
        ((ADD_CORE, UP, 1), (CORE_SEND, UP, 1),),
    ),
    9: (
        ((ADD_CORE, UP, 0),),
        ((ADD_A, UP, 0), (ADD_CORE, EARLY, 1),),
    ),
    10: (
        ((CORE_SEND, EARLY, 1),),
        (),
    ),
    12: (
        ((CORE_SEND, UP, 2), (CORE_SEND, EARLY, 2), (ADD_A, UP, 0),),
        ((ADD_A, UP, 1), (ADD_B, UP, 0), (ADD_CORE, EARLY, 0), (CORE_SEND, UP, 2), (ADD_A, EARLY, 1),
         (ADD_CORE, UP, 2), (ADD_CORE, EARLY, 2),),
    ),
    14: (
        ((ADD_B, UP, 0),),
        ((Z_MID, UP, 0), (ADD_B, UP, 1),),
    ),
    16: (
        ((ADD_CORE, UP, 2), (Z_MID, UP, 0),),
        (),
    ),
    17: (
        (),
        ((ADD_B, EARLY, 1), (ADD_A, UP, 2), (Z_MID, UP, 1), (ADD_A, EARLY, 2),),
    ),
    18: (
        ((ADD_A, UP, 2),),
        (),
    ),
    19: (
        ((ADD_CORE, UP, 1), (ADD_B, UP, 2),),
        ((ADD_B, UP, 2),),
    ),
    22: (
        ((ADD_A, UP, 1), (ADD_CORE, LATE, 0),),
        ((CORE_SEND, LATE, 0), (Z_MID, UP, 2), (ADD_B, EARLY, 2), (Z_LAST, UP, 1), (ADD_A, EARLY, 0), (Z_LAST,
         UP, 0), (Z_MID, EARLY, 1),),
    ),
    23: (
        ((ADD_CORE, LATE, 1), (Z_MID, UP, 2), (Z_LAST, UP, 0),),
        ((CORE_SEND, LATE, 1), (Z_MID, EARLY, 2), (ADD_B, EARLY, 0),),
    ),
    24: (
        ((ADD_A, LATE, 0), (ADD_B, UP, 1), (ADD_CORE, LATE, 2), (ADD_A, LATE, 1), (ADD_B, LATE, 0), (Z_MID,
         UP, 1),),
        ((CORE_SEND, LATE, 2), (Z_LAST, UP, 2),),
    ),
    25: (
        ((Z_LAST, UP, 2),),
        ((Z_LAST, EARLY, 1), (Z_MID, EARLY, 0),),
    ),
    26: (
        ((ADD_A, LATE, 2), (ADD_B, LATE, 1),),
        ((OWNER, UP, 0), (GATHER_Z, UP, 3),),
    ),
    27: (
        (),
        ((Z_LAST, EARLY, 2), (Z_LAST, EARLY, 0), (OWNER, EARLY, 0), (GATHER_Z, EARLY, 1), (RELAY_TWO, UP, 3),
         (H_B, EARLY, 0), (RELAY_ONE, UP, 3), (GATHER_Z, UP, 1),),
    ),
    28: (
        ((Z_LAST, UP, 1),),
        ((GATHER_Z, UP, 2),),
    ),
    29: (
        ((Z_MID, LATE, 0), (Z_LAST, LATE, 0), (ADD_B, LATE, 2), (Z_MID, LATE, 1), (OWNER, UP, 0), (Z_LAST,
         LATE, 1), (Z_MID, LATE, 2), (GATHER_Z, UP, 2),),
        (),
    ),
    30: (
        ((Z_LAST, LATE, 2), (H_B, UP, 0),),
        ((RELAY_ONE, UP, 2), (GATHER_B, UP, 3), (RELAY_TWO, UP, 2), (H_B, UP, 0),),
    ),
    31: (
        ((RELAY_ONE, UP, 2), (RELAY_TWO, UP, 2), (GATHER_Z, UP, 1),),
        ((GATHER_Z, EARLY, 3), (RELAY_TWO, UP, 1), (H_A, EARLY, 0),),
    ),
    32: (
        ((GATHER_Z, UP, 3), (OWNER, LATE, 0), (GATHER_Z, LATE, 2), (RELAY_ONE, UP, 1), (GATHER_B, UP, 2),),
        ((RELAY_ONE, UP, 1), (GATHER_Z, EARLY, 2), (GATHER_B, UP, 2), (RELAY_ONE, EARLY, 1), (GATHER_A, UP,
         3),),
    ),
    33: (
        ((RELAY_TWO, UP, 1), (RELAY_TWO, UP, 3), (RELAY_ONE, UP, 3), (GATHER_Z, LATE, 0),),
        ((H_A, UP, 0), (GATHER_A, UP, 2), (GATHER_B, UP, 1), (RELAY_ONE, EARLY, 3),),
    ),
    34: (
        ((GATHER_B, UP, 1), (GATHER_Z, LATE, 1),),
        (),
    ),
    35: (
        ((H_A, UP, 0), (GATHER_Z, LATE, 3), (H_Z, UP, 0),),
        ((RELAY_ONE, EARLY, 2), (RELAY_TWO, EARLY, 1), (H_Z, EARLY, 0), (GATHER_CORE, UP, 3),),
    ),
    36: (
        ((RELAY_ONE, LATE, 0), (GATHER_A, UP, 2),),
        ((RELAY_TWO, EARLY, 3), (GATHER_B, EARLY, 1), (GATHER_B, EARLY, 3),),
    ),
    37: (
        ((RELAY_ONE, LATE, 2), (GATHER_B, UP, 3),),
        (),
    ),
    38: (
        ((RELAY_TWO, LATE, 2), (RELAY_TWO, LATE, 0),),
        ((RELAY_TWO, EARLY, 2), (GATHER_A, UP, 1), (GATHER_A, EARLY, 3), (H_Z, UP, 0), (GATHER_CORE, UP, 2),
         (H_R1, EARLY, 0),),
    ),
    39: (
        ((GATHER_A, UP, 1), (H_R1, UP, 0),),
        (),
    ),
    40: (
        (),
        ((GATHER_A, EARLY, 1),),
    ),
    41: (
        ((GATHER_A, UP, 3), (GATHER_CORE, UP, 2), (GATHER_B, LATE, 0), (RELAY_ONE, LATE, 1), (GATHER_B, LATE,
         2), (RELAY_TWO, LATE, 1),),
        (),
    ),
    42: (
        ((RELAY_ONE, LATE, 3), (GATHER_B, LATE, 1), (GATHER_A, LATE, 0), (GATHER_A, LATE, 2), (GATHER_CORE,
         UP, 3), (RELAY_TWO, LATE, 3), (H_R2, UP, 0), (GATHER_END, EARLY, 1), (SMALL, UP, 0), (GATHER_END, UP,
         1), (GATHER_END, EARLY, 3), (SMALL, UP, 1), (GATHER_CORE, LATE, 0), (GATHER_B, LATE, 3), (GATHER_A,
         LATE, 1), (GATHER_CORE, UP, 1), (GATHER_END, EARLY, 2), (GATHER_CORE, UP, 0), (GATHER_A, LATE, 3),
         (GATHER_CORE, LATE, 2), (GATHER_CORE, LATE, 1), (SMALL, UP, 2), (GATHER_CORE, LATE, 3), (SMALL, UP,
         3), (GATHER_END, UP, 2), (SMALL, UP, 4), (GATHER_END, UP, 0), (GATHER_END, UP, 3), (GATHER_END,
         EARLY, 0),),
        ((GATHER_B, EARLY, 2), (GATHER_CORE, EARLY, 3), (GATHER_CORE, EARLY, 1), (SMALL, UP, 0), (GATHER_CORE,
         UP, 1), (GATHER_A, EARLY, 2), (H_R1, UP, 0), (SMALL, UP, 1), (H_R2, UP, 0), (GATHER_CORE, EARLY, 2),
         (GATHER_END, UP, 2), (H_R2, EARLY, 0), (GATHER_END, LATE, 0), (GATHER_CORE, EARLY, 0), (GATHER_END,
         UP, 1), (SMALL, UP, 2), (GATHER_CORE, UP, 0), (GATHER_END, UP, 3), (GATHER_END, LATE, 1), (SMALL, UP,
         3), (SMALL, UP, 4), (GATHER_END, UP, 0), (GATHER_END, LATE, 2), (GATHER_END, LATE, 3),),
    ),
}


def layer_kernel(
    dims, token_count,
    docs, small, gains, small_rows, streams, cotangent, attn_in, attn_out, ffn_in, ffn_out, state_in,
    cos_table, sin_table,
    new_out, stream_grad_out, copy_out, grad_out, small_out, from_core,
    grads, from_a0, from_a1, from_b0, from_b1, from_c, stage_box, kv_box, gfirst, second, dread, read, first,
    normed, queries, keys, values, context, lse, cosine, sine, starts, low, small_box,
    kv_send_sem, kv_recv_sem, send_sem, recv_sem, load_sem, local_sem, stage_sem, store_sem, out_sem, small_send, small_recv,
):
    f32, bf16 = jnp.float32, jnp.bfloat16
    nz, ny, nx = dims
    rows, width = second.shape
    hidden = ffn_out.shape[0]
    shard = low.shape[0]
    piece = shard // 3
    unit = 6 * piece
    half = unit // 2
    planes = nz // 2
    s = lax.axis_index("seq")
    w = lax.axis_index("wide")
    z, y, x = w // (ny * nx), (w // nx) % ny, w % nx

    def chip(cz, cy, cx):
        return (s, (cz * ny + cy) * nx + cx)

    core = (1 - s, w)
    z_peers = [chip((z + d) % nz, y, x) for d in range(1, nz)]
    y_peers = [chip(z, (y + d) % ny, x) for d in range(1, ny)]
    x_peers = [chip(z, y, (x + d) % nx) for d in range(1, nx)]
    peers = [core] + z_peers + y_peers + x_peers
    barrier = pltpu.get_barrier_semaphore()
    for peer in peers:
        pl.semaphore_signal(barrier, inc=1, device_id=peer, device_id_type=MESH)

    base = 2 * width
    mix = [[small[0, base + i * 2 * NS + j] for j in range(2 * NS)] for i in range(NS)]
    read_one = [mix[i][NS] for i in range(NS)]
    depth_one = [mix[i][NS + 1] for i in range(NS)]
    read_two = [mix[i][NS + 2] for i in range(NS)]
    depth_two = [mix[i][NS + 3] for i in range(NS)]

    def load(src, dst, sem):
        copy = pltpu.make_async_copy(src, dst, sem)
        copy.start()
        return copy

    ids = {}
    unsent = {}
    unit_now = [None]

    def number(kind, key, count=1):
        if (kind, key) not in ids:
            ids[kind, key] = ids.get(kind, 0)
            ids[kind] = ids.get(kind, 0) + count
        return ids[kind, key]

    def copy_of(key, ends, recv=None):
        src, dst, peer = ends()
        got = number("recv", key) if recv is None else recv()
        return pltpu.make_async_remote_copy(
            src, dst, send_sem.at[number("send", key)], recv_sem.at[got], device_id=peer, device_id_type=MESH)

    def remote(key, ends, guard=None, recv=None):
        copy_of(key, ends, recv).start()
        unsent.setdefault((key, unit_now[-1]), (lambda: copy_of(key, ends, recv), guard))

    def wait_sends():
        for copy, guard in unsent.values():
            if guard is None:
                copy().wait_send()
            else:
                pl.when(guard())(lambda copy=copy: copy().wait_send())
        unsent.clear()

    one, zero = s == 1, s == 0
    group_of = {UP: 1, EARLY: 0, LATE: 0}
    guard_of = {UP: None, EARLY: lambda: one, LATE: lambda: zero}

    def zs_of(v):
        return pl.ds(planes * group_of[v], planes)

    def zlist(v):
        return list(range(planes * group_of[v], planes * (group_of[v] + 1)))

    def guarded(v, f):
        f()

    def more(v, test):
        if guard_of[v] is None:
            return test
        return lambda: guard_of[v]() & test()

    lo, hi = pl.ds(0, half), pl.ds(half, half)

    def core_moves(v, c):
        return [(
            ("core", group_of[v], c),
            lambda: (grads.at[1 - s, zs_of(v), :, :, c], from_core.at[zs_of(v), :, :, c], core))]

    def a_moves(v, c):
        g = group_of[v]
        return [
            (("a0", g, c, d), lambda d=d: (
                grads.at[s, zs_of(v), :, (x + d) % nx, c, lo], from_a0.at[d - 1, zs_of(v), :, c], x_peers[d - 1]))
            for d in range(1, nx)
        ] + [
            (("a1", g, c, d), lambda d=d: (
                grads.at[s, zs_of(v), (y + d) % ny, :, c, hi], from_a1.at[d - 1, zs_of(v), :, c], y_peers[d - 1]))
            for d in range(1, ny)
        ]

    def b_moves(v, c):
        g = group_of[v]
        return [
            (("b0", g, c, d), lambda d=d: (
                grads.at[s, zs_of(v), (y + d) % ny, x, c, lo], from_b0.at[d - 1, zs_of(v), c], y_peers[d - 1]))
            for d in range(1, ny)
        ] + [
            (("b1", g, c, d), lambda d=d: (
                grads.at[s, zs_of(v), y, (x + d) % nx, c, hi], from_b1.at[d - 1, zs_of(v), c], x_peers[d - 1]))
            for d in range(1, nx)
        ]

    def same(ref, peer):
        return ref, ref, peer

    def gb_moves(v, k):
        g = group_of[v]
        return [
            (("gb0", g, k, d), lambda peer=peer: same(copy_out.at[s, zs_of(v), y, x, part_lo(k)], peer))
            for d, peer in enumerate(y_peers)
        ] + [
            (("gb1", g, k, d), lambda peer=peer: same(copy_out.at[s, zs_of(v), y, x, part_hi(k)], peer))
            for d, peer in enumerate(x_peers)
        ]

    def ga_moves(v, k):
        g = group_of[v]
        return [
            (("ga0", g, k, d), lambda peer=peer: same(copy_out.at[s, zs_of(v), :, x, part_lo(k)], peer))
            for d, peer in enumerate(x_peers)
        ] + [
            (("ga1", g, k, d), lambda peer=peer: same(copy_out.at[s, zs_of(v), y, :, part_hi(k)], peer))
            for d, peer in enumerate(y_peers)
        ]

    def gc_moves(v, k):
        return [(("gc", group_of[v], k), lambda: same(copy_out.at[s, zs_of(v), :, :, part(k)], core))]

    def start(moves, v, c, guard="unit"):
        for key, ends in moves(v, c):
            remote(key, ends, guard=guard_of[v] if guard == "unit" else guard)

    def wait_recvs(moves, v, c):
        for key, ends in moves(v, c):
            copy_of(key, ends).wait_recv()

    def core_send(v, c):
        start(core_moves, v, c, {UP: None, EARLY: lambda: zero, LATE: lambda: one}[v])

    def add_core(v, c):
        def go():
            wait_recvs(core_moves, v, c)
            g = group_of[v]
            loads = [
                load(from_core.at[planes * g + i, :, :, c], stage_box.at[i], stage_sem.at[i]) for i in range(planes)
            ]
            for plane, copy in enumerate(loads):
                copy.wait()

                def body(i, carry, plane=plane):
                    yi, xi = i // nx, i % nx
                    at = (s, planes * g + plane, yi, xi, c)
                    grads[at] = (grads[at].astype(f32) + stage_box[plane, yi, xi].astype(f32)).astype(bf16)
                    return carry

                lax.fori_loop(0, ny * nx, body, 0)
            start(a_moves, v, c)

        guarded(v, go)

    def add_a(v, c):
        def go():
            wait_recvs(a_moves, v, c)
            g = group_of[v]

            def body_lo(i, carry):
                zi, yi = planes * g + i // ny, i % ny
                at = (s, zi, yi, x, c, lo)
                total = grads[at].astype(f32)
                for d in range(nx - 1):
                    total = total + from_a0[d, zi, yi, c].astype(f32)
                grads[at] = total.astype(bf16)
                return carry

            def body_hi(i, carry):
                zi, xi = planes * g + i // nx, i % nx
                at = (s, zi, y, xi, c, hi)
                total = grads[at].astype(f32)
                for d in range(ny - 1):
                    total = total + from_a1[d, zi, xi, c].astype(f32)
                grads[at] = total.astype(bf16)
                return carry

            lax.fori_loop(0, planes * ny, body_lo, 0)
            lax.fori_loop(0, planes * nx, body_hi, 0)
            start(b_moves, v, c)

        guarded(v, go)

    def add_b(v, c):
        def go():
            wait_recvs(b_moves, v, c)
            g = group_of[v]

            def body(i, carry):
                zi = planes * g + i
                for at_rows, box, count in ((lo, from_b0, ny - 1), (hi, from_b1, nx - 1)):
                    at = (s, zi, y, x, c, at_rows)
                    total = grads[at].astype(f32)
                    for d in range(count):
                        total = total + box[d, zi, c].astype(f32)
                    grads[at] = total.astype(bf16)
                return carry

            lax.fori_loop(0, planes, body, 0)
            hop(v, c, 0)

        guarded(v, go)

    def place_of(v):
        return z if group_of[v] == 1 else nz - 1 - z

    def z_at(v, place):
        return place if group_of[v] == 1 else nz - 1 - place

    def hop(v, c, place):
        g = group_of[v]
        if place == 0:
            moves = [(0, 1, 2, 0), (0, 1, 3, 1), (3, 2, 2, 2)]
        elif place == 1:
            moves = [(1, 2, 2, 0), (1, 2, 3, 1)]
        else:
            moves = [(2, 3, 3, 1)]
        for start, end, owner, slot in moves:
            when(place_of(v) == start, lambda start=start, end=end, owner=owner, slot=slot: remote(
                ("z", g, c, start, owner),
                lambda: (grads.at[s, z_at(v, owner), y, x, c], from_c.at[g, slot, c], chip(z_at(v, end), y, x)),
                guard=more(v, lambda: place_of(v) == start),
                recv=lambda: number("recv", ("z", g, c, slot))))

    def hop_wait(v, c, slot):
        g = group_of[v]
        pltpu.make_async_remote_copy(
            grads.at[s, z, y, x, c], from_c.at[g, slot, c], send_sem.at[0],
            recv_sem.at[number("recv", ("z", g, c, slot))], device_id=core, device_id_type=MESH).wait_recv()

    def hop_add(v, c, place):
        def go():
            for owner, slot in ((2, 0), (3, 1)) if place == 1 else ((3, 1),):
                hop_wait(v, c, slot)
                g = group_of[v]

                def body(i, carry, owner=owner, slot=slot):
                    r = pl.ds(i * 128, 128)
                    at = (s, z_at(v, owner), y, x, c, r)
                    grads[at] = (grads[at].astype(f32) + from_c[g, slot, c, r].astype(f32)).astype(bf16)
                    return carry

                lax.fori_loop(0, unit // 128, body, 0)
            hop(v, c, place)

        guarded(v, lambda: when(place_of(v) == place, go))

    def z_mid(v, c):
        hop_add(v, c, 1)

    def z_last(v, c):
        hop_add(v, c, 2)

    def in_group(g):
        return (z // planes) == g

    def owner_update(units, state, flat, sums):
        for v in units:
            g = group_of[v]

            def total_at(slots, v=v, g=g):
                for c in range(3):
                    for slot in slots:
                        hop_wait(v, c, slot)

                def body(i, carry):
                    r = pl.ds(i * 128, 128)
                    for c in range(3):
                        total = grads[s, z, y, x, c, r].astype(f32)
                        for slot in slots:
                            total = total + from_c[g, slot, c, r].astype(f32)
                        sums[c, r] = total * (1.0 / token_count)
                    return carry

                lax.fori_loop(0, unit // 128, body, 0)

            guarded(v, lambda v=v, f=total_at: when(place_of(v) == 2, lambda: f((0, 2))))
            guarded(v, lambda v=v, f=total_at: when(place_of(v) == 3, lambda: f((1,))))
        mine = {UP: in_group(1), EARLY: in_group(0) & one, LATE: in_group(0) & zero}[units[0]]
        pl.when(mine)(lambda: owner_step(state, flat, sums))

    def owner_step(state, flat, sums):
        pltpu.make_async_copy(state_in, state, load_sem.at[0]).wait()
        index = s * (nz * ny * nx) + w
        in_rows = attn_in.shape[0] * attn_in.shape[1] // width // shard
        out_rows = in_rows + attn_out.shape[0] // shard
        ffn_rows = out_rows + ffn_in.shape[0] * ffn_in.shape[1] // width // shard
        blocks = ffn_in.shape[1] // width
        thirds = attn_in.shape[1] // width

        def total_of(c, at_rows):
            return sums[c, at_rows]

        @pl.when(index < in_rows)
        def _():
            for c in range(3):
                for lane in range(6):
                    flat[lane, pl.ds(c, piece, stride=thirds), :] = total_of(c, pl.ds(lane * piece, piece))

        @pl.when(((index >= in_rows) & (index < out_rows)) | (index >= ffn_rows))
        def _():
            for c in range(3):
                for lane in range(6):
                    flat[lane, pl.ds(c * piece, piece), :] = total_of(c, pl.ds(lane * piece, piece))

        @pl.when((index >= out_rows) & (index < ffn_rows))
        def _():
            part = shard // blocks
            for c in range(3):
                for side in range(2):
                    for j in range(blocks):
                        flat[side * 3 + c, pl.ds(j, part, stride=blocks), :] = total_of(
                            c, pl.ds(side * half + j * part, part))

        def body(i, carry):
            r = pl.ds(i * 16, 16)
            grad = jnp.concatenate([flat[lane, r] for lane in range(6)], axis=1)
            read[r] = grad
            low[r] = adam_step((state[0, r], state[1, r], state[2, r]), grad)[0].astype(bf16)
            return carry

        lax.fori_loop(0, shard // 16, body, 0)
        pltpu.make_async_copy(read.at[pl.ds(0, shard)], grad_out, store_sem.at[0]).start()
        keep = pltpu.make_async_copy(low, copy_out.at[s, z, y, x], store_sem.at[4])
        keep.start()
        keep.wait()

    gather_parts = PARTS
    part_rows = shard // gather_parts

    def part(k):
        return pl.ds(k * part_rows, part_rows)

    def part_lo(k):
        return pl.ds(k * part_rows, part_rows // 2)

    def part_hi(k):
        return pl.ds(k * part_rows + part_rows // 2, part_rows // 2)

    def relay(v, k, moves):
        for start, end, owner, mine in moves:
            def send(start=start, end=end, owner=owner, mine=mine):
                zd = z_at(v, owner)

                def ends():
                    dst = copy_out.at[s, zd, y, x, part(k)]
                    return (low.at[part(k)] if mine else dst), dst, chip(z_at(v, end), y, x)

                remote(("gz", zd, k, start, end), ends, guard=more(v, lambda: place_of(v) == start),
                       recv=lambda: number("recv", ("gz", zd, k)))

            when(place_of(v) == start, send)

    def relay_wait(v, k, place, owner):
        zd = z_at(v, owner)
        when(place_of(v) == place, lambda: pltpu.make_async_remote_copy(
            low.at[part(k)], copy_out.at[s, zd, y, x, part(k)], send_sem.at[0],
            recv_sem.at[number("recv", ("gz", zd, k))], device_id=core, device_id_type=MESH).wait_recv())

    def gather_z(v, k):
        guarded(v, lambda: relay(v, k, [(2, 1, 2, True), (2, 3, 2, True), (3, 2, 3, True)]))

    def relay_one(v, k):
        def go():
            relay_wait(v, k, 2, 3)
            relay_wait(v, k, 1, 2)
            relay(v, k, [(2, 1, 3, False), (1, 0, 2, False)])

        guarded(v, go)

    def relay_two(v, k):
        def go():
            relay_wait(v, k, 1, 3)
            relay(v, k, [(1, 0, 3, False)])

        guarded(v, go)

    def gather_b(v, k):
        def go():
            g = group_of[v]
            relay_wait(v, k, 0, 2)
            relay_wait(v, k, 0, 3)
            relay_wait(v, k, 3, 2)
            start(gb_moves, v, k)

        guarded(v, go)

    def gather_a(v, k):
        def go():
            wait_recvs(gb_moves, v, k)
            g = group_of[v]
            start(ga_moves, v, k)

        guarded(v, go)

    def hb_moves(v, k):
        g = group_of[v]
        return [
            (("hb0", g, k, d), lambda peer=peer: same(copy_out.at[s, z, y, x, part_lo(k)], peer))
            for d, peer in enumerate(y_peers)
        ] + [
            (("hb1", g, k, d), lambda peer=peer: same(copy_out.at[s, z, y, x, part_hi(k)], peer))
            for d, peer in enumerate(x_peers)
        ]

    def ha_moves(v, k):
        g = group_of[v]
        return [
            (("ha0", g, k, d), lambda peer=peer: same(copy_out.at[s, z, :, x, part_lo(k)], peer))
            for d, peer in enumerate(x_peers)
        ] + [
            (("ha1", g, k, d), lambda peer=peer: same(copy_out.at[s, z, y, :, part_hi(k)], peer))
            for d, peer in enumerate(y_peers)
        ]

    def owner_place(v):
        return lambda: place_of(v) >= 2

    def h_b(v, k):
        when(place_of(v) >= 2, lambda: start(hb_moves, v, k, more(v, owner_place(v))))

    def h_a(v, k):
        def go():
            wait_recvs(hb_moves, v, k)
            start(ha_moves, v, k, more(v, owner_place(v)))

        when(place_of(v) >= 2, go)

    def plane_ends(v, k, owner, end):
        return lambda: same(copy_out.at[s, z_at(v, owner), :, :, part(k)], chip(z_at(v, end), y, x))

    def plane_send(v, k, at, end, owner):
        when(place_of(v) == at, lambda: remote(
            ("hz", z_at(v, owner), k, at, end), plane_ends(v, k, owner, end), guard=more(v, lambda: place_of(v) == at),
            recv=lambda: number("recv", ("hz", z_at(v, owner), k))))

    def plane_wait(v, k, at, owner):
        when(place_of(v) == at, lambda: copy_of(
            ("hz", z_at(v, owner), k, 2, 1), plane_ends(v, k, owner, 2),
            lambda: number("recv", ("hz", z_at(v, owner), k))).wait_recv())

    def h_z(v, k):
        when(place_of(v) >= 2, lambda: wait_recvs(ha_moves, v, k))
        plane_send(v, k, 2, 1, 2)
        plane_send(v, k, 2, 3, 2)
        plane_send(v, k, 3, 2, 3)

    def h_r1(v, k):
        plane_wait(v, k, 2, 3)
        plane_wait(v, k, 1, 2)
        plane_send(v, k, 2, 1, 3)
        plane_send(v, k, 1, 0, 2)

    def h_r2(v, k):
        plane_wait(v, k, 1, 3)
        plane_send(v, k, 1, 0, 3)

    def gather_core(v, k):
        def go():
            if (v, k) in Z_LAST:
                plane_wait(v, k, 0, 2)
                plane_wait(v, k, 0, 3)
                plane_wait(v, k, 3, 2)
            else:
                wait_recvs(ga_moves, v, k)
            start(gc_moves, v, k)

        guarded(v, go)

    def gather_end(v, k):
        wait_recvs(gc_moves, v, k)

    wide_piece = piece
    tile = hidden // 3
    tile_pieces = tile // wide_piece
    steps = tile_pieces // 2

    tiles = []

    def kv_copy(hp):
        cols = pl.ds(pl.multiple_of(hp * 128, 128), 128)
        return pltpu.make_async_remote_copy(
            kv_box.at[:, cols], kv_box.at[:, cols], kv_send_sem.at[hp], kv_recv_sem.at[hp],
            device_id=core, device_id_type=MESH)

    def tile_loads(c):
        slot = c % 2
        copies = []
        for p in range(tile_pieces):
            at = p * 3 * wide_piece + c * wide_piece
            to = pl.ds(p * wide_piece, wide_piece)
            for k, (src, dst) in enumerate((
                (ffn_in.at[:, pl.ds(at, wide_piece)], tiles[0].at[slot, :, to]),
                (ffn_in.at[:, pl.ds(hidden + at, wide_piece)], tiles[1].at[slot, :, to]),
                (ffn_out.at[pl.ds(at, wide_piece)], tiles[2].at[slot, to]),
            )):
                copies.append(pltpu.make_async_copy(src, dst, local_sem.at[slot, k, p]))
        return copies

    def forward_scope(raw, w_in):
        w_out = kv_box
        loads = [load(src, dst, load_sem.at[1 + k]) for k, (src, dst) in enumerate((
            (streams, raw), (attn_in, w_in), (cos_table.at[pl.ds(0, EIGHTH)], starts.at[0]),
            (sin_table.at[pl.ds(0, EIGHTH)], starts.at[1]), (attn_out, w_out)))]
        plain_rows = [pl.ds(EIGHTH, 3 * EIGHTH), pl.ds(0, 3 * EIGHTH)]
        plain_loads = [
            [pltpu.make_async_copy(table.at[pl.ds(side * 3 * EIGHTH, 3 * EIGHTH)], own.at[plain_rows[side]],
                                   load_sem.at[11 + k])
             for k, (table, own) in enumerate(((cos_table, cosine), (sin_table, sine)))]
            for side in range(2)
        ]
        for side in range(2):
            @pl.when(s == side)
            def _(side=side):
                for copy in plain_loads[side]:
                    copy.start()

        carry_first = sum(depth_one[j] * read_two[j] for j in range(NS))
        carry_stream = [sum(mix[i][j] * read_two[j] for j in range(NS)) for i in range(NS)]
        loads[0].wait()

        def norm_block(i, carry):
            r = pl.ds(i * 64, 64)
            parts = unpacked(raw[r])
            branch = sum(parts[k] * read_one[k] for k in range(NS))
            read[r] = sum(parts[k] * carry_stream[k] for k in range(NS))
            normal, _ = normal_of(branch)
            normed[r] = (normal * gains[0:1].astype(f32)).astype(bf16)
            return carry

        lax.fori_loop(0, rows // 64, norm_block, 0)
        for copy in loads[1:]:
            copy.wait()
        load(cotangent, raw, load_sem.at[6])
        for c in range(2):
            for copy in tile_loads(c):
                copy.start()

        def tables(side):
            first_special = 7 * EIGHTH * side
            special = pl.ds(3 * EIGHTH * side, EIGHTH)
            place = lax.broadcasted_iota(jnp.int32, (EIGHTH, EIGHTH), 0) + first_special
            start = doc_starts(docs, place)
            lane = lax.broadcasted_iota(jnp.int32, (EIGHTH, EIGHTH), 1)
            pick = (place - start == lane).astype(f32)
            for k, own in enumerate((cosine, sine)):
                own[special] = jnp.dot(
                    pick, starts[k], precision=lax.Precision.HIGHEST, preferred_element_type=f32)
            for copy in plain_loads[side]:
                copy.wait()

        for side in range(2):
            pl.when(s == side)(lambda side=side: tables(side))

        own_rows = pl.ds(s * rows, rows)

        def rotated(dest, dest_rows, offset):
            def body(j, carry):
                cols = pl.ds(pl.multiple_of(j * 256, 256), 256)
                source = pl.ds(pl.multiple_of(offset + j * 256, 256), 256)
                part = nn(normed[...], w_in[:, source])
                halves = []
                for k in range(2):
                    turn = part[:, k * 128 : (k + 1) * 128]
                    halves.append(turn * cosine[...] + swapped(turn) * sine[...])
                dest[dest_rows, cols] = jnp.concatenate(halves, axis=1).astype(bf16)
                return carry

            lax.fori_loop(0, width // 256, body, 0)

        def plain(j, carry):
            cols = pl.ds(pl.multiple_of(j * 256, 256), 256)
            source = pl.ds(pl.multiple_of(2 * width + j * 256, 256), 256)
            values[own_rows, cols] = nn(normed[...], w_in[:, source]).astype(bf16)
            return carry

        lax.fori_loop(0, width // 256, plain, 0)
        rotated(keys, own_rows, width)
        pl.semaphore_wait(barrier, len(peers))
        shared = pl.ds(EIGHTH, 3 * EIGHTH)
        copies = [
            pltpu.make_async_remote_copy(
                ref.at[shared], ref.at[shared], kv_send_sem.at[6 + i], kv_recv_sem.at[6 + i],
                device_id=core, device_id_type=MESH)
            for i, ref in enumerate((keys, values))
        ]

        @pl.when(zero)
        def _():
            for copy in copies:
                copy.start()

        rotated(queries, pl.ds(0, rows), 0)

        def attend(side):
            blocks = q_blocks(side)
            masks = [block_mask(docs, side, block) for block in blocks]

            def pair(hp, carry):
                jobs = [
                    (2 * hp + q, pl.ds(pl.multiple_of((2 * hp + q) * 128, 128), 128), bi,
                     pl.ds(row * EIGHTH, EIGHTH), pl.ds(key * EIGHTH, count * EIGHTH))
                    for q in range(2) for bi, (row, key, count, _) in enumerate(blocks)
                ]
                scores = [
                    masked_scores(keys[kr, cols], two_heads(queries[r, cols]) * HD ** (-0.5), masks[bi])
                    for _, cols, bi, r, kr in jobs
                ]
                tops = [jnp.max(score, axis=0, keepdims=True) for score in scores]
                lifted = [jnp.exp(score - top) for score, top in zip(scores, tops)]
                totals = [jnp.sum(lift, axis=0, keepdims=True) for lift in lifted]
                probs = [(lift * (1.0 / total)).astype(bf16) for lift, total in zip(lifted, totals)]
                outs = [tn(values[job[4], job[1]], prob) for job, prob in zip(jobs, probs)]
                for (pair_at, cols, bi, r, kr), out, top, total in zip(jobs, outs, tops, totals):
                    context[r, cols] = one_pair(out).astype(bf16)
                    lse[pl.ds(bi * 8 + pair_at, 1), :] = top + jnp.log(total)
                return carry

            lax.fori_loop(0, width // 256, pair, 0)

        @pl.when(zero)
        def _():
            attend(0)
            for copy in copies:
                copy.wait_send()

        @pl.when(one)
        def _():
            for copy in copies:
                copy.wait_recv()
            attend(1)

        def out_block(j, carry):
            cols = pl.ds(pl.multiple_of(j * 256, 256), 256)
            part = nn(context[...], w_out[:, cols])
            first[:, cols] = part
            read[:, cols] += part * carry_first
            return carry

        lax.fori_loop(0, width // 256, out_block, 0)

    def ffn_scope(raw, normed_two, normed_two_t, dsecond, gate_s, up_s, dhid_s, hid, dgate, dup):
        pltpu.make_async_copy(cotangent, raw, load_sem.at[6]).wait()

        def first_block(i, carry):
            r = pl.ds(i * 64, 64)
            parts = unpacked(raw[r])
            dsecond[r] = sum(parts[j] * depth_two[j] for j in range(NS)).astype(bf16)
            gfirst[r] = sum(parts[j] * depth_one[j] for j in range(NS))
            normal, _ = normal_of(read[r])
            normed_two[r] = (normal * gains[1:2].astype(f32)).astype(bf16)
            second[r] = jnp.zeros((64, width), f32)
            dread[r] = jnp.zeros((64, width), f32)
            return carry

        lax.fori_loop(0, rows // 64, first_block, 0)
        normed_two_t[...] = normed_two[...].T

        if True:
            def sub(step, carry):
                c, u = step // steps, step % steps
                slot = c % 2
                for k in range(3):
                    def arrive(k=k):
                        for copy in tile_loads(k):
                            copy.wait()

                    pl.when(step == k * steps)(arrive)
                cols = pl.ds(pl.multiple_of(u * 2 * wide_piece, 2 * wide_piece), 2 * wide_piece)
                wg, wu, wo = tiles[0][slot, :, cols], tiles[1][slot, :, cols], tiles[2][slot, cols]
                gate_s[...] = nn(normed_two[...], wg)
                up_s[...] = nn(normed_two[...], wu)
                dhid_s[...] = nt(dsecond[...], wo)
                for i in range(rows // 64):
                    r = pl.ds(i * 64, 64)
                    gate, up, dhid = gate_s[r], up_s[r], dhid_s[r]
                    sig = 1.0 / (1.0 + jnp.exp(-gate))
                    silu = gate * sig
                    hid[r] = (silu * up).astype(bf16)
                    dgate[r] = (dhid * up * sig * (1.0 + gate - silu)).astype(bf16)
                    dup[r] = (dhid * silu).astype(bf16)
                second[...] += nn(hid[...], wo)
                dread[...] += nt(dgate[...], wg) + nt(dup[...], wu)
                dwo = tn(hid[...], dsecond[...]).astype(bf16)
                for q in range(2):
                    p = 2 * u + q
                    zi, yi, xi = planes + p // (ny * nx), (p // nx) % ny, p % nx
                    for lane in range(6):
                        grads[1, zi, yi, xi, c, pl.ds(lane * piece, piece)] = dwo[
                            q * piece : (q + 1) * piece, lane * 128 : (lane + 1) * 128]
                blocks = 2 * (hidden // width)
                part = shard // blocks
                for k, dact in enumerate((dgate, dup)):
                    dwi = nn(normed_two_t[...], dact[...]).astype(bf16)
                    j = u + k * (blocks // 2)
                    for b in range(width // part):
                        at_half, at = b // (width // part // 2), b % (width // part // 2)
                        at = at + (nz * ny * nx // 2 if at_half == 0 else 0)
                        zi, yi, xi = at // (ny * nx), (at // nx) % ny, at % nx
                        for q in range(2):
                            grads[at_half, zi, yi, xi, c, pl.ds(pl.multiple_of(q * half + j * part, 16), part)] = dwi[
                                b * part : (b + 1) * part, q * 128 : (q + 1) * 128]
                def more_weights():
                    for copy in tile_loads(2):
                        copy.start()

                pl.when(step == steps - 1)(more_weights)
                poll_loop(1, 3 * steps, step)
                return carry

            lax.fori_loop(0, 3 * steps, sub, 0)

    stages = {
        CORE_SEND: core_send,
        ADD_CORE: add_core,
        ADD_A: add_a,
        ADD_B: add_b,
        Z_MID: z_mid,
        Z_LAST: z_last,
        GATHER_Z: gather_z,
        RELAY_ONE: relay_one,
        RELAY_TWO: relay_two,
        GATHER_B: gather_b,
        GATHER_A: gather_a,
        GATHER_CORE: gather_core,
        GATHER_END: gather_end,
        H_B: h_b,
        H_A: h_a,
        H_Z: h_z,
        H_R1: h_r1,
        H_R2: h_r2,
    }

    def run(actions):
        for name, v, c in actions:
            unit_now.append(v)
            stages[name](v, c)
            unit_now.pop()

    def poll(at):
        for side in range(2):
            actions = PLAN.get(at, ((), ()))[side]
            if actions:
                pl.when(s == side)(lambda actions=actions: run(actions))

    def poll_loop(first, count, step):
        for i in range(count):
            for side in range(2):
                actions = PLAN.get(first + i, ((), ()))[side]
                if actions:
                    pl.when((step == i) & (s == side))(lambda actions=actions: run(actions))

    def both_scopes(raw, gate_w, up_w, out_w):
        tiles.extend((gate_w, up_w, out_w))
        pl.run_scoped(
            functools.partial(forward_scope, raw),
            pltpu.VMEM(attn_in.shape, bf16))
        pl.run_scoped(
            functools.partial(ffn_scope, raw),
            pltpu.VMEM((rows, width), bf16), pltpu.VMEM((width, rows), bf16), pltpu.VMEM((rows, width), bf16),
            pltpu.VMEM((rows, 2 * piece), f32), pltpu.VMEM((rows, 2 * piece), f32), pltpu.VMEM((rows, 2 * piece), f32),
            pltpu.VMEM((rows, 2 * piece), bf16), pltpu.VMEM((rows, 2 * piece), bf16), pltpu.VMEM((rows, 2 * piece), bf16))

    pl.run_scoped(
        both_scopes,
        pltpu.VMEM((rows, NS, width), bf16), pltpu.VMEM((2, width, tile), bf16),
        pltpu.VMEM((2, width, tile), bf16), pltpu.VMEM((2, tile, width), bf16))

    gain_sums = {}

    def attention_scope(w_in, w_out, dfirst, dcontext, dkeys, dvalues, own_keys, own_values, dproject, turned):
        loads = [load(attn_out, w_out, load_sem.at[7]), load(attn_in, w_in, load_sem.at[8])]
        carry_first = sum(depth_one[j] * read_two[j] for j in range(NS))

        def norm_block(i, total):
            r = pl.ds(i * 64, 64)
            normal, scaling = normal_of(read[r])
            grad = dread[r]
            total = total + jnp.sum((grad * normal).reshape(8, 8, width), axis=0)
            scaled = grad * gains[1:2].astype(f32)
            centre = jnp.mean(scaled, axis=-1, keepdims=True)
            along = jnp.mean(scaled * normal, axis=-1, keepdims=True)
            value = scaling * (scaled - centre - normal * along)
            dread[r] = value
            dfirst[r] = (gfirst[r] + carry_first * value).astype(bf16)
            return total

        gain_two = lax.fori_loop(0, rows // 64, norm_block, jnp.zeros((8, width), f32))
        row = jnp.sum(gain_two, axis=0, keepdims=True)
        for k in range(width // 128):
            small_box[0, s, width // 128 + k : width // 128 + k + 1, :] = row[:, k * 128 : (k + 1) * 128]

        loads[0].wait()
        poll(13)

        def context_block(j, carry):
            cols = pl.ds(pl.multiple_of(j * 256, 256), 256)
            dcontext[:, cols] = nt(dfirst[...], w_out[cols]).astype(bf16)
            return carry

        lax.fori_loop(0, width // 256, context_block, 0)
        turned[...] = context[...].T
        shards_in = w_in.shape[1] // width * (width // piece) // 3

        def out_block(j, carry):
            cols = pl.ds(pl.multiple_of(j * 256, 256), 256)
            part = nn(turned[...], dfirst[:, cols]).astype(bf16)
            for b in range(width // piece):
                at, c = shards_in + b // 3, b % 3
                zi, yi, xi = at // (ny * nx), (at // nx) % ny, at % nx
                for q in range(2):
                    grads[0, zi, yi, xi, c, pl.ds(pl.multiple_of((2 * j + q) * piece, piece), piece)] = part[
                        b * piece : (b + 1) * piece, q * 128 : (q + 1) * 128]
            return carry

        lax.fori_loop(0, width // 256, out_block, 0)
        poll(14)

        def blocks_back(side, hp):
            blocks = q_blocks(side)
            cols = pl.ds(pl.multiple_of(hp * 128, 128), 128)
            spans = [
                (pl.ds(row * EIGHTH, EIGHTH), pl.ds(key * EIGHTH, count * EIGHTH)) for row, key, count, _ in blocks
            ]
            qs = [two_heads(queries[r, cols]) * HD ** (-0.5) for r, kr in spans]
            dstack = [two_heads(dcontext[r, cols]) for r, kr in spans]
            scores = [
                masked_scores(keys[kr, cols], qs[bi], block_mask(docs, side, blocks[bi]))
                for bi, (r, kr) in enumerate(spans)
            ]
            dprobs = [nt(values[kr, cols], dstack[bi]) for bi, (r, kr) in enumerate(spans)]
            probs = [jnp.exp(score - lse[pl.ds(bi * 8 + hp, 1), :]) for bi, score in enumerate(scores)]
            inner = [jnp.sum(p * dp, axis=0, keepdims=True) for p, dp in zip(probs, dprobs)]
            dscores = [(p * (dp - i)).astype(bf16) for p, dp, i in zip(probs, dprobs, inner)]
            for bi, (r, kr) in enumerate(spans):
                dkeys[kr] += nn(dscores[bi], qs[bi])
                dvalues[kr] += nn(probs[bi].astype(bf16), dstack[bi])
            dqs = [tn(keys[kr, cols], dscores[bi]) for bi, (r, kr) in enumerate(spans)]
            for bi, (r, kr) in enumerate(spans):
                dq = one_pair(dqs[bi]) * HD ** (-0.5)
                dproject[r, cols] = (dq * cosine[r] - swapped(dq) * sine[r]).astype(bf16)

        shared = pl.ds(EIGHTH, 3 * EIGHTH)

        key_rows, value_rows = pl.ds(0, 3 * EIGHTH), pl.ds(3 * EIGHTH, 3 * EIGHTH)

        def turned_back(dk):
            return (dk * cosine[...] - swapped(dk) * sine[...]).astype(bf16)

        def pair_back(hp, carry):
            cols = pl.ds(pl.multiple_of(hp * 128, 128), 128)
            key_cols = pl.ds(pl.multiple_of(width + hp * 128, 128), 128)
            value_cols = pl.ds(pl.multiple_of(2 * width + hp * 128, 128), 128)
            dkeys[...] = jnp.zeros_like(dkeys)
            dvalues[...] = jnp.zeros_like(dvalues)

            @pl.when(zero)
            def _():
                blocks_back(0, hp)
                own_keys[:, cols] = dkeys[pl.ds(0, rows)]
                own_values[:, cols] = dvalues[pl.ds(0, rows)]

            @pl.when(one)
            def _():
                blocks_back(1, hp)
                kv_box[key_rows, cols] = dkeys[shared].astype(bf16)
                kv_box[value_rows, cols] = dvalues[shared].astype(bf16)
                kv_copy(hp).start()
                dproject[:, key_cols] = turned_back(dkeys[pl.ds(rows, rows)])
                dproject[:, value_cols] = dvalues[pl.ds(rows, rows)].astype(bf16)

            poll_loop(15, width // 128, hp)
            return carry

        lax.fori_loop(0, width // 128, pair_back, 0)

        @pl.when(zero)
        def _():
            def finish(hp, carry):
                cols = pl.ds(pl.multiple_of(hp * 128, 128), 128)
                key_cols = pl.ds(pl.multiple_of(width + hp * 128, 128), 128)
                value_cols = pl.ds(pl.multiple_of(2 * width + hp * 128, 128), 128)
                kv_copy(hp).wait_recv()
                own_keys[shared, cols] += kv_box[key_rows, cols].astype(f32)
                own_values[shared, cols] += kv_box[value_rows, cols].astype(f32)
                dproject[:, key_cols] = turned_back(own_keys[:, cols])
                dproject[:, value_cols] = own_values[:, cols].astype(bf16)
                return carry

            lax.fori_loop(0, width // 128, finish, 0)

        @pl.when(one)
        def _():
            def finish(hp, carry):
                kv_copy(hp).wait_send()
                return carry

            lax.fori_loop(0, width // 128, finish, 0)

        poll(21)
        loads[1].wait()
        turned[...] = normed[...].T

        for j in range(w_in.shape[1] // width):
            def in_block(cb, carry, j=j):
                cols = pl.ds(pl.multiple_of(j * width + cb * 256, 256), 256)
                part = nn(turned[...], dproject[:, cols]).astype(bf16)
                for b in range(width // piece):
                    zi, yi, xi = b // (ny * nx), (b // nx) % ny, b % nx
                    for q in range(2):
                        grads[0, zi, yi, xi, j, pl.ds(pl.multiple_of((2 * cb + q) * piece, piece), piece)] = part[
                            b * piece : (b + 1) * piece, q * 128 : (q + 1) * 128]
                return carry

            lax.fori_loop(0, width // 256, in_block, 0)
            poll(22 + j)

        def dnormed_block(j, carry):
            cols = pl.ds(pl.multiple_of(j * 256, 256), 256)
            gfirst[:, cols] = nt(dproject[...], w_in[cols])
            return carry

        lax.fori_loop(0, width // 256, dnormed_block, 0)
        poll(25)

    pl.run_scoped(
        attention_scope,
        pltpu.VMEM(attn_in.shape, bf16), pltpu.VMEM(attn_out.shape, bf16),
        pltpu.VMEM((rows, width), bf16), pltpu.VMEM((rows, width), bf16),
        pltpu.VMEM((2 * rows, 128), f32), pltpu.VMEM((2 * rows, 128), f32),
        pltpu.VMEM((rows, width), f32), pltpu.VMEM((rows, width), f32),
        pltpu.VMEM((rows, 3 * width), bf16), pltpu.VMEM((width, rows), bf16),
    )

    def tail_scope(raw_h, raw_g, new_box, back_box, state, flat, sums_box):
        axes = [(s, [core], 2), (x, x_peers, nx), (y, y_peers, ny), (z, z_peers, nz)]

        def small_copies(k):
            first = sum(len(axis[1]) for axis in axes[:k])
            place, others, count = axes[k]
            return [
                pltpu.make_async_remote_copy(
                    small_box.at[k, place], small_box.at[k, place], small_send.at[first + i], small_recv.at[first + i],
                    device_id=peer, device_id_type=MESH)
                for i, peer in enumerate(others)
            ]

        def small_stage(v, k):
            if k > 0:
                for copy in small_copies(k - 1):
                    copy.wait()
                total = small_box[k - 1, 0]
                for j in range(1, axes[k - 1][2]):
                    total = total + small_box[k - 1, j]
            if k == len(axes):
                grad = total * (1.0 / token_count)
                new = adam_step((small_rows[0], small_rows[1], small_rows[2]), grad)
                for k2, value in enumerate(new + (grad,)):
                    small_out[k2] = value
                return
            if k > 0:
                small_box[k, axes[k][0]] = total
            for copy in small_copies(k):
                copy.start()

        stages[SMALL] = small_stage
        stages[OWNER] = lambda v, c: owner_update((v,), state, flat, sums_box)
        loads = [load(streams, raw_h, load_sem.at[9]), load(cotangent, raw_g, load_sem.at[10]),
                 load(state_in, state, load_sem.at[0])]
        for copy in loads[:2]:
            copy.wait()
        poll(26)
        mixed_read = [sum(mix[i][j] * read_two[j] for j in range(NS)) for i in range(NS)]
        pairs = 33
        block = 32

        def out_copies(i, slot):
            r = pl.ds(i * block, block)
            return [pltpu.make_async_copy(new_box.at[slot], new_out.at[r], out_sem.at[0, slot]),
                    pltpu.make_async_copy(back_box.at[slot], stream_grad_out.at[r], out_sem.at[1, slot])]

        def body(i, carry):
            gain_one, sums = carry
            r = pl.ds(i * block, block)
            slot = i % 2

            @pl.when(i >= 2)
            def _():
                for copy in out_copies(i, slot):
                    copy.wait()

            hs, gs = unpacked(raw_h[r]), unpacked(raw_g[r])
            first_r, second_r, dread_r = first[r], second[r], dread[r]
            branch = sum(hs[k] * read_one[k] for k in range(NS))
            normal, scaling = normal_of(branch)
            grad = gfirst[r]
            gain_one = gain_one + jnp.sum((grad * normal).reshape(block // 8, 8, width), axis=0)
            scaled = grad * gains[0:1].astype(f32)
            centre = jnp.mean(scaled, axis=-1, keepdims=True)
            along = jnp.mean(scaled * normal, axis=-1, keepdims=True)
            dbranch = scaling * (scaled - centre - normal * along)
            back = [
                (sum(gs[j] * mix[k][j] for j in range(NS)) + dread_r * mixed_read[k] + dbranch * read_one[k]).astype(bf16)
                for k in range(NS)
            ]
            back_box[slot] = packed_streams(back)
            new = [
                (sum(hs[k] * mix[k][j] for k in range(NS)) + first_r * depth_one[j] + second_r * depth_two[j]).astype(bf16)
                for j in range(NS)
            ]
            new_box[slot] = packed_streams(new)
            for copy in out_copies(i, slot):
                copy.start()
            products = [(hs[a], gs[b]) for a in range(NS) for b in range(NS)]
            products += [(hs[a], dread_r) for a in range(NS)]
            products += [(hs[a], dbranch) for a in range(NS)]
            products += [(first_r, gs[b]) for b in range(NS)] + [(first_r, dread_r)]
            products += [(second_r, gs[b]) for b in range(NS)]
            new_sums = []
            for total, (a, b) in zip(sums, products):
                p = jnp.sum((a * b).reshape(block // 8, 8, width), axis=0)
                new_sums.append(total + sum(p[:, q * 128 : (q + 1) * 128] for q in range(width // 128)))
            poll_loop(27, rows // block - 1, i)
            return gain_one, tuple(new_sums)

        zero_tile = jnp.zeros((8, 128), f32)
        gain_one, sums = lax.fori_loop(
            0, rows // block, body, (jnp.zeros((8, width), f32), tuple(zero_tile for _ in range(pairs))))
        for i in (rows // block - 2, rows // block - 1):
            for copy in out_copies(i, i % 2):
                copy.wait()
        row = jnp.sum(gain_one, axis=0, keepdims=True)
        for k in range(width // 128):
            small_box[0, s, k : k + 1, :] = row[:, k * 128 : (k + 1) * 128]
        sums = [jnp.sum(jnp.sum(t, axis=0, keepdims=True), axis=1, keepdims=True) for t in sums]
        hg = [[sums[a * NS + b] for b in range(NS)] for a in range(NS)]
        h_read = sums[16:20]
        h_branch = sums[20:24]
        first_g, first_read, second_g = sums[24:28], sums[28], sums[29:33]
        lane = lax.broadcasted_iota(jnp.int32, (1, 128), 1)
        line = jnp.zeros((1, 128), f32)
        for i in range(NS):
            entries = [hg[i][j] + read_two[j] * h_read[i] for j in range(NS)]
            entries.append(h_branch[i])
            entries.append(first_g[i] + read_two[i] * first_read)
            entries.append(sum(mix[k][i] * h_read[k] for k in range(NS)) + depth_one[i] * first_read)
            entries.append(second_g[i])
            for j, value in enumerate(entries):
                line = jnp.where(lane == i * 2 * NS + j, value, line)
        last = 2 * width // 128
        small_box[0, s, last : last + 1, :] = line
        small_box[0, s, last + 1 :, :] = jnp.zeros((small_box.shape[2] - last - 1, 128), f32)

        poll(42)
        wait_sends()
        pltpu.make_async_copy(read.at[pl.ds(0, shard)], grad_out, store_sem.at[0]).wait()

    pl.run_scoped(
        tail_scope,
        pltpu.VMEM((rows, NS, width), bf16), pltpu.VMEM((rows, NS, width), bf16),
        pltpu.VMEM((2, 32, NS, width), bf16), pltpu.VMEM((2, 32, NS, width), bf16),
        pltpu.VMEM((3, shard, width), f32), pltpu.VMEM((6, shard, 128), f32),
        pltpu.VMEM((3, unit, 128), f32),
    )
    assert ids["send"] <= send_sem.shape[0] and ids["recv"] <= recv_sem.shape[0], ids


def finish_kernel(
    new_in, back_in, copy_in, grad_in, state_in,
    new_out, back_out, copy_out, weight_out, first_out, second_out, grad_out,
    new_box, back_box, copy_box, grad, state, weight, first, second, in_sem, out_sem, copy_sem,
):
    parts = 4
    rows = grad.shape[0] // parts
    tokens = new_box.shape[0] // parts

    def of_rows(k):
        return pl.ds(k * rows, rows)

    def of_tokens(k):
        return pl.ds(k * tokens, tokens)

    def loads(k):
        return [
            pltpu.make_async_copy(grad_in.at[of_rows(k)], grad.at[of_rows(k)], in_sem.at[0, k]),
            pltpu.make_async_copy(state_in.at[:, of_rows(k)], state.at[:, of_rows(k)], in_sem.at[1, k]),
            pltpu.make_async_copy(new_in.at[of_tokens(k)], new_box.at[of_tokens(k)], in_sem.at[2, k]),
            pltpu.make_async_copy(back_in.at[of_tokens(k)], back_box.at[of_tokens(k)], in_sem.at[3, k]),
        ]

    def stores(k):
        pairs = [(box.at[of_rows(k)], out.at[of_rows(k)]) for box, out in (
            (grad, grad_out), (weight, weight_out), (first, first_out), (second, second_out))]
        pairs += [(new_box.at[of_tokens(k)], new_out.at[of_tokens(k)]), (back_box.at[of_tokens(k)], back_out.at[of_tokens(k)])]
        return [pltpu.make_async_copy(a, b, out_sem.at[i, k]) for i, (a, b) in enumerate(pairs)]

    pieces = copy_sem.shape[1]
    copy_rows = copy_box.shape[0] // pieces

    def move(k, out):
        r = pl.ds(k * copy_rows, copy_rows)
        if out:
            return pltpu.make_async_copy(copy_box.at[r], copy_out.at[r], copy_sem.at[1, k])
        return pltpu.make_async_copy(copy_in.at[r], copy_box.at[r], copy_sem.at[0, k])

    for k in range(parts):
        for copy in loads(k):
            copy.start()
    for k in range(pieces):
        move(k, False).start()
    for k in range(parts):
        for copy in loads(k):
            copy.wait()

        def body(i, carry, k=k):
            r = pl.ds(k * rows + i * 16, 16)
            weight[r], first[r], second[r] = adam_step((state[0, r], state[1, r], state[2, r]), grad[r])
            return carry

        lax.fori_loop(0, rows // 16, body, 0)
        for copy in stores(k):
            copy.start()
    for k in range(pieces):
        move(k, False).wait()
        move(k, True).start()
    for k in range(parts):
        for copy in stores(k):
            copy.wait()
    for k in range(pieces):
        move(k, True).wait()


def finish(new, back, copy, grad, big_state):
    shape = jax.ShapeDtypeStruct
    hbm = pl.BlockSpec(memory_space=pl.ANY)
    like = shape(grad.shape, grad.dtype)
    box = pltpu.VMEM(grad.shape, grad.dtype)
    return pl.pallas_call(
        finish_kernel,
        out_shape=[shape(new.shape, new.dtype), shape(back.shape, back.dtype), shape(copy.shape, copy.dtype),
                   like, like, like, like],
        in_specs=[hbm] * 5,
        out_specs=[hbm] * 7,
        scratch_shapes=[
            pltpu.VMEM(new.shape, new.dtype), pltpu.VMEM(back.shape, back.dtype),
            pltpu.VMEM(copy.shape, copy.dtype), box, pltpu.VMEM(big_state.shape, big_state.dtype), box, box, box,
            pltpu.SemaphoreType.DMA((4, 4)), pltpu.SemaphoreType.DMA((6, 4)), pltpu.SemaphoreType.DMA((2, 12)),
        ],
        compiler_params=pltpu.CompilerParams(vmem_limit_bytes=60 * 2**20),
        name="finish",
    )(new, back, copy, grad, big_state)


def layer_part(dims, token_count, docs, small_state, gains, streams, cotangent, weights, big_state):
    attn_in, attn_out, ffn_in, ffn_out = weights
    nz, ny, nx = dims
    rows, width = streams.shape[0], attn_out.shape[0]
    shard = big_state.shape[1]
    unit, half, hidden = 2 * shard, shard, ffn_out.shape[0]
    bf16, f32 = jnp.bfloat16, jnp.float32
    shape = jax.ShapeDtypeStruct
    cos_table, sin_table = rope_constants(6 * EIGHTH, HD)
    small_count = small_state.shape[1]
    small_rows = jnp.pad(small_state, ((0, 0), (0, -small_count % 1024))).reshape(3, -1, 128)
    small_shape = small_rows.shape[1:]
    smem = pl.BlockSpec(memory_space=pltpu.SMEM)
    vmem = pl.BlockSpec(memory_space=pltpu.VMEM)
    hbm = pl.BlockSpec(memory_space=pl.ANY)
    state_shape = shape((shard, width), f32)
    stream_shape = shape((rows, NS, width), bf16)
    outs = pl.pallas_call(
        functools.partial(layer_kernel, dims, token_count),
        out_shape=[
            stream_shape, stream_shape, shape((2, nz, ny, nx, shard, width), bf16),
            state_shape, shape((4,) + small_shape, f32),
            shape((nz, ny, nx, 3, unit, 128), bf16),
        ],
        in_specs=[smem, smem, vmem, vmem] + [hbm] * 9,
        out_specs=[hbm] * 4 + [vmem, hbm],
        scratch_shapes=[
            pltpu.VMEM((2, nz, ny, nx, 3, unit, 128), bf16),
            pltpu.VMEM((max(nx - 1, 1), nz, ny, 3, half, 128), bf16),
            pltpu.VMEM((max(ny - 1, 1), nz, nx, 3, half, 128), bf16),
            pltpu.VMEM((max(ny - 1, 1), nz, 3, half, 128), bf16),
            pltpu.VMEM((max(nx - 1, 1), nz, 3, half, 128), bf16),
            pltpu.VMEM((2, 3, 3, unit, 128), bf16),
            pltpu.VMEM((nz // 2, ny, nx, unit, 128), bf16),
            pltpu.VMEM((6 * EIGHTH, width), bf16),
            pltpu.VMEM((rows, width), f32), pltpu.VMEM((rows, width), f32), pltpu.VMEM((rows, width), f32),
            pltpu.VMEM((rows, width), f32), pltpu.VMEM((rows, width), f32),
            pltpu.VMEM((rows, width), bf16), pltpu.VMEM((rows, width), bf16),
            pltpu.VMEM((2 * rows, width), bf16), pltpu.VMEM((2 * rows, width), bf16),
            pltpu.VMEM((rows, width), bf16), pltpu.VMEM((32, 2 * EIGHTH), f32),
            pltpu.VMEM((rows, 128), f32), pltpu.VMEM((rows, 128), f32), pltpu.VMEM((2, EIGHTH, EIGHTH), f32),
            pltpu.VMEM((shard, width), bf16),
            pltpu.VMEM((4, max(2, nx, ny, nz)) + small_shape, f32),
            pltpu.SemaphoreType.DMA((8,)), pltpu.SemaphoreType.DMA((8,)),
            pltpu.SemaphoreType.DMA((240,)), pltpu.SemaphoreType.DMA((180,)),
            pltpu.SemaphoreType.DMA((16,)), pltpu.SemaphoreType.DMA((2, 3, 8)),
            pltpu.SemaphoreType.DMA((2,)), pltpu.SemaphoreType.DMA((5,)), pltpu.SemaphoreType.DMA((2, 2)),
            pltpu.SemaphoreType.DMA((8,)), pltpu.SemaphoreType.DMA((8,)),
        ],
        compiler_params=pltpu.CompilerParams(
            collective_id=1, has_side_effects=True, vmem_limit_bytes=255 * 2**18
        ),
        name="layer_step",
    )(docs, small_state, gains, small_rows, streams, cotangent, attn_in, attn_out, ffn_in, ffn_out, big_state,
      jnp.asarray(cos_table), jnp.asarray(sin_table))
    small_out = outs[4].reshape(4, -1)[:, :small_count]
    copy = outs[2].reshape(-1, width)
    new, back, copy, weight_new, first_new, second_new, grad = finish(outs[0], outs[1], copy, outs[3], big_state)
    return new, back, copy, weight_new, first_new, second_new, grad, small_out


def torus(mesh):
    wide = mesh.shape["wide"]
    where = [getattr(d, "coords", None) for d in mesh.devices.flat]
    if all(c is not None for c in where):
        x, y, z = (len({c[i] for c in where}) for i in range(3))
        if x * y * z == wide:
            return z, y, x
    known = {16: (4, 2, 2), 64: (4, 4, 4)}
    return known.get(wide, (wide, 1, 1))


def sync_kernel(
    dims, rows, half, lr_consts,
    grads, small_in, state_in,
    copy_out, weight_out, first_out, second_out, grad_out, small_out,
    acc, from_core, from_a0, from_a1, from_b0, from_b1, from_c,
    state, new_w, new_m, new_v, new_g, low, small_box,
    load_sem, store_sem, send_sem, recv_sem, small_send, small_recv,
):
    nz, ny, nx = dims
    chunk = 2 * half
    chunks = rows // chunk
    s = lax.axis_index("seq")
    w = lax.axis_index("wide")
    z, y, x = w // (ny * nx), (w // nx) % ny, w % nx

    def chip(cz, cy, cx):
        return (s, (cz * ny + cy) * nx + cx)

    core = (1 - s, w)
    z_peers = [chip((z + d) % nz, y, x) for d in range(1, nz)]
    y_peers = [chip(z, (y + d) % ny, x) for d in range(1, ny)]
    x_peers = [chip(z, y, (x + d) % nx) for d in range(1, nx)]
    peers = [core] + z_peers + y_peers + x_peers

    barrier = pltpu.get_barrier_semaphore()
    for peer in peers:
        pl.semaphore_signal(barrier, inc=1, device_id=peer, device_id_type=MESH)

    loads = [
        pltpu.make_async_copy(
            grads.at[s, :, :, :, pl.ds(c * chunk, chunk)],
            acc.at[:, :, :, pl.ds(c * chunk, chunk)],
            load_sem.at[c],
        )
        for c in range(chunks)
    ]
    for copy in loads:
        copy.start()
    state_load = pltpu.make_async_copy(state_in, state, load_sem.at[chunks])
    state_load.start()
    pl.semaphore_wait(barrier, len(peers))

    sends = []
    counter = [0]

    def remote(src, dst, peer):
        i = counter[0]
        counter[0] += 1
        copy = pltpu.make_async_remote_copy(
            src, dst, send_sem.at[i], recv_sem.at[i], device_id=peer, device_id_type=MESH
        )
        copy.start()
        sends.append(copy)
        return copy

    def lo(c):
        return pl.ds(c * chunk, half)

    def hi(c):
        return pl.ds(c * chunk + half, half)

    def both(c):
        return pl.ds(c * chunk, chunk)

    def packed(c):
        return pl.ds(c * half, half)

    f32 = jnp.float32

    def add_into(count, where, terms):
        def body(i, carry):
            ref, index = where(i)
            total = ref[index].astype(f32)
            for term_ref, term_index in terms(i):
                total = total + term_ref[term_index].astype(f32)
            ref[index] = total.astype(ref.dtype)
            return carry

        lax.fori_loop(0, count, body, 0)

    def small_step(k, mine, others, count):
        copies = []
        for j, peer in enumerate(others):
            i = small_index[0]
            small_index[0] += 1
            copy = pltpu.make_async_remote_copy(
                small_box.at[k, mine], small_box.at[k, mine], small_send.at[i], small_recv.at[i],
                device_id=peer, device_id_type=MESH,
            )
            copy.start()
            copies.append(copy)
        return copies

    def small_sum(k, copies, count):
        for copy in copies:
            copy.wait()
        total = small_box[k, 0]
        for j in range(1, count):
            total = total + small_box[k, j]
        return total

    small_index = [0]
    axes = [(s, [core], 2), (x, x_peers, nx), (y, y_peers, ny), (z, z_peers, nz)]
    small_box[0, s] = small_in[...]
    small_copies = [small_step(0, s, [core], 2)]

    def small_stage(k):
        total = small_sum(k, small_copies[k], axes[k][2])
        if k + 1 < len(axes):
            place, others, count = axes[k + 1]
            small_box[k + 1, place] = total
            small_copies.append(small_step(k + 1, place, others, count))
        else:
            small_out[...] = total

    state_done = [False]
    flying = {}

    def stage(k, c):
        if k == 0:
            loads[c].wait()
            for copy in flying[0, c]:
                copy.wait_recv()

            def where(i):
                return acc, (i // (ny * nx), (i // nx) % ny, i % nx, both(c))

            def terms(i):
                return [(from_core, (i // (ny * nx), (i // nx) % ny, i % nx, both(c)))]

            add_into(nz * ny * nx, where, terms)
            out = []
            for d in range(1, nx):
                out.append(remote(
                    acc.at[:, :, (x + d) % nx, lo(c)], from_a0.at[d - 1, :, :, packed(c)], x_peers[d - 1]))
            for d in range(1, ny):
                out.append(remote(
                    acc.at[:, (y + d) % ny, :, hi(c)], from_a1.at[d - 1, :, :, packed(c)], y_peers[d - 1]))
            flying[1, c] = out
        elif k == 1:
            for copy in flying[1, c]:
                copy.wait_recv()
            add_into(
                nz * ny,
                lambda i: (acc, (i // ny, i % ny, x, lo(c))),
                lambda i: [(from_a0, (d, i // ny, i % ny, packed(c))) for d in range(nx - 1)],
            )
            add_into(
                nz * nx,
                lambda i: (acc, (i // nx, y, i % nx, hi(c))),
                lambda i: [(from_a1, (d, i // nx, i % nx, packed(c))) for d in range(ny - 1)],
            )
            out = []
            for d in range(1, ny):
                out.append(remote(
                    acc.at[:, (y + d) % ny, x, lo(c)], from_b0.at[d - 1, :, packed(c)], y_peers[d - 1]))
            for d in range(1, nx):
                out.append(remote(
                    acc.at[:, y, (x + d) % nx, hi(c)], from_b1.at[d - 1, :, packed(c)], x_peers[d - 1]))
            flying[2, c] = out
        elif k == 2:
            for copy in flying[2, c]:
                copy.wait_recv()
            add_into(
                nz,
                lambda i: (acc, (i, y, x, lo(c))),
                lambda i: [(from_b0, (d, i, packed(c))) for d in range(ny - 1)],
            )
            add_into(
                nz,
                lambda i: (acc, (i, y, x, hi(c))),
                lambda i: [(from_b1, (d, i, packed(c))) for d in range(nx - 1)],
            )
            out = []
            for d in range(1, nz):
                out.append(remote(
                    acc.at[(z + d) % nz, y, x, both(c)], from_c.at[d - 1, both(c)], z_peers[d - 1]))
            flying[3, c] = out
        elif k == 3:
            for copy in flying[3, c]:
                copy.wait_recv()
            if not state_done[0]:
                state_load.wait()
                state_done[0] = True
            step = 16

            def body(i, carry):
                r = pl.ds(c * chunk + i * step, step)
                total = acc[z, y, x, r].astype(f32)
                for d in range(nz - 1):
                    total = total + from_c[d, r].astype(f32)
                grad = total * lr_consts
                w_new, m_new, v_new = adam_step((state[0, r], state[1, r], state[2, r]), grad)
                new_g[r] = grad
                new_w[r] = w_new
                new_m[r] = m_new
                new_v[r] = v_new
                low[r] = w_new.astype(low.dtype)
                return carry

            lax.fori_loop(0, chunk // step, body, 0)
            out = []
            for peer in z_peers:
                out.append(remote(low.at[both(c)], copy_out.at[s, z, y, x, both(c)], peer))
            own = pltpu.make_async_copy(low.at[both(c)], copy_out.at[s, z, y, x, both(c)], store_sem.at[0, c])
            own.start()
            for j, (a, b) in enumerate(((new_w, weight_out), (new_m, first_out), (new_v, second_out), (new_g, grad_out))):
                st = pltpu.make_async_copy(a.at[both(c)], b.at[both(c)], store_sem.at[j + 1, c])
                st.start()
                stores.append(st)
            flying[4, c] = (out, own)
        elif k == 4:
            out, own = flying[4, c]
            own.wait()
            for copy in out:
                copy.wait_recv()
            nxt = []
            for peer in y_peers:
                nxt.append(remote(copy_out.at[s, :, y, x, lo(c)], copy_out.at[s, :, y, x, lo(c)], peer))
            for peer in x_peers:
                nxt.append(remote(copy_out.at[s, :, y, x, hi(c)], copy_out.at[s, :, y, x, hi(c)], peer))
            flying[5, c] = nxt
        elif k == 5:
            for copy in flying[5, c]:
                copy.wait_recv()
            nxt = []
            for peer in x_peers:
                nxt.append(remote(copy_out.at[s, :, :, x, lo(c)], copy_out.at[s, :, :, x, lo(c)], peer))
            for peer in y_peers:
                nxt.append(remote(copy_out.at[s, :, y, :, hi(c)], copy_out.at[s, :, y, :, hi(c)], peer))
            flying[6, c] = nxt
        elif k == 6:
            for copy in flying[6, c]:
                copy.wait_recv()
            flying[7, c] = [
                remote(copy_out.at[s, :, :, :, both(c)], copy_out.at[s, :, :, :, both(c)], core)]
        elif k == 7:
            for copy in flying[7, c]:
                copy.wait_recv()

    stores = []
    for c in range(chunks):
        flying[0, c] = [remote(
            grads.at[1 - s, :, :, :, both(c)], from_core.at[:, :, :, both(c)], core)]
    stages = 8
    for t in range(chunks + stages - 1):
        for k in reversed(range(stages)):
            c = t - k
            if 0 <= c < chunks:
                stage(k, c)
        if 1 <= t <= 4:
            small_stage(t - 1)
    for copy in sends:
        copy.wait_send()
    for copy in stores:
        copy.wait()


def sync_grads(dims, flat_low, small_local, big_state, token_count):
    nz, ny, nx = dims
    wide = nz * ny * nx
    model_width = flat_low.shape[1]
    rows = big_state.shape[1]
    half = next(h for h in (48, 32, 16) if rows % (2 * h) == 0)
    chunks = rows // (2 * half)
    bf16, f32 = jnp.bfloat16, jnp.float32
    copies = chunks * (2 + 4 * (nx - 1) + 4 * (ny - 1) + 2 * (nz - 1))
    small_copies = 1 + (nx - 1) + (ny - 1) + (nz - 1)
    hbm = pl.BlockSpec(memory_space=pl.ANY)
    vmem = pl.BlockSpec(memory_space=pltpu.VMEM)
    state_shape = jax.ShapeDtypeStruct((rows, model_width), f32)
    small_shape = small_local.shape
    outs = pl.pallas_call(
        functools.partial(sync_kernel, dims, rows, half, 1.0 / token_count),
        out_shape=[
            jax.ShapeDtypeStruct((2, nz, ny, nx, rows, model_width), bf16),
            state_shape, state_shape, state_shape, state_shape,
            jax.ShapeDtypeStruct(small_shape, f32),
        ],
        in_specs=[hbm, vmem, hbm],
        out_specs=[hbm] * 5 + [vmem],
        scratch_shapes=[
            pltpu.VMEM((nz, ny, nx, rows, model_width), bf16),
            pltpu.VMEM((nz, ny, nx, rows, model_width), bf16),
            pltpu.VMEM((max(nx - 1, 1), nz, ny, rows // 2, model_width), bf16),
            pltpu.VMEM((max(ny - 1, 1), nz, nx, rows // 2, model_width), bf16),
            pltpu.VMEM((max(ny - 1, 1), nz, rows // 2, model_width), bf16),
            pltpu.VMEM((max(nx - 1, 1), nz, rows // 2, model_width), bf16),
            pltpu.VMEM((max(nz - 1, 1), rows, model_width), bf16),
            pltpu.VMEM((3, rows, model_width), f32),
            pltpu.VMEM((rows, model_width), f32),
            pltpu.VMEM((rows, model_width), f32),
            pltpu.VMEM((rows, model_width), f32),
            pltpu.VMEM((rows, model_width), f32),
            pltpu.VMEM((rows, model_width), bf16),
            pltpu.VMEM((4, max(2, nx, ny, nz)) + small_shape, f32),
            pltpu.SemaphoreType.DMA((chunks + 1,)),
            pltpu.SemaphoreType.DMA((5, chunks)),
            pltpu.SemaphoreType.DMA((copies,)),
            pltpu.SemaphoreType.DMA((copies,)),
            pltpu.SemaphoreType.DMA((small_copies,)),
            pltpu.SemaphoreType.DMA((small_copies,)),
        ],
        compiler_params=pltpu.CompilerParams(
            collective_id=1, has_side_effects=True, vmem_limit_bytes=56 * 2**20
        ),
        name="sync_grads",
    )(
        flat_low.reshape(2, nz, ny, nx, rows, model_width), small_local, big_state
    )
    return (outs[0].reshape(2 * wide * rows, model_width),) + tuple(outs[1:])


def on_device(
    dims,
    streams,
    cotangent,
    doc_lengths,
    attn_in,
    attn_out,
    ffn_in,
    ffn_out,
    norm_gains,
    big_state,
    small_state,
):
    row_count = streams.shape[1]
    model_width = attn_out.shape[0]
    fits = (
        big_state.shape[1] == 384 and model_width == 768 and row_count == 512
        and ffn_out.shape[0] == 3072 and dims == (4, 2, 2)
    )
    if fits:
        token_count = 2 * row_count * lax.axis_size("wide")
        result, stream_grad, gathered, weight_new, first_new, second_new, owned_grads, small_out = layer_part(
            dims, token_count, doc_lengths, small_state, norm_gains.T, streams[0], cotangent[0],
            (attn_in, attn_out, ffn_in, ffn_out), big_state,
        )
        gains_copy = small_out[0, : 2 * model_width].reshape(2, model_width).T.astype(jnp.bfloat16)
        return (
            result[None], stream_grad[None], weight_new, first_new, second_new, owned_grads,
            small_out[0], small_out[1], small_out[2], small_out[3], gathered, gains_copy,
        )
    member = lax.axis_index("seq")
    token_total = row_count * lax.axis_size("seq")
    token_count = token_total * lax.axis_size("wide")
    segment, position = doc_layout(doc_lengths[0], token_total)
    own_start = member * row_count
    own_index = own_start + jnp.arange(row_count, dtype=jnp.int32)
    seg_query = lax.dynamic_slice_in_dim(segment, own_start, row_count)
    pos_query = lax.dynamic_slice_in_dim(position, own_start, row_count)
    padded_seg = jnp.concatenate([jnp.full((row_count,), -1, jnp.int32), segment])
    key_seg = lax.dynamic_slice_in_dim(padded_seg, own_start, 2 * row_count)
    key_index = own_start - row_count + jnp.arange(2 * row_count, dtype=jnp.int32)
    allowed = (key_seg[None, :] == seg_query[:, None]) & (key_index[None, :] <= own_index[:, None])
    cosine, sine_table = rope_tables(pos_query, HD)
    weights = (attn_in, attn_out, ffn_in, ffn_out)
    gain_values = norm_gains.astype(jnp.float32)
    mixing = small_state[0, 2 * model_width :].reshape(NS, NS + 4)
    stream_values = streams[0].astype(jnp.float32)
    result, saved = forward_layer(
        stream_values, weights, gain_values, mixing, allowed, cosine, sine_table
    )
    grad_out = cotangent[0].astype(jnp.float32)
    stream_grad, matrix_grads, gains_local, mixing_local = backward_layer(
        stream_values, grad_out, weights, gain_values, mixing, cosine, sine_table, saved
    )
    flat_low = jnp.concatenate(
        [grad.astype(jnp.bfloat16).reshape(-1, model_width) for grad in matrix_grads], axis=0
    )
    small_local = jnp.concatenate([gains_local.T.reshape(-1), mixing_local.reshape(-1)])
    small_count = small_local.shape[0]
    padded = jnp.pad(small_local, (0, -small_count % 1024)).reshape(-1, 128)
    gathered, weight_new, first_new, second_new, owned_grads, small_total = sync_grads(
        dims, flat_low, padded, big_state, token_count
    )
    small_grads = small_total.reshape(-1)[:small_count] / token_count
    small_weight, small_first, small_second = adam_step(small_state, small_grads)
    gains_copy = small_weight[: 2 * model_width].reshape(2, model_width).T.astype(jnp.bfloat16)
    return (
        result.astype(jnp.bfloat16)[None],
        stream_grad.astype(jnp.bfloat16)[None],
        weight_new,
        first_new,
        second_new,
        owned_grads,
        small_weight,
        small_first,
        small_second,
        small_grads,
        gathered,
        gains_copy,
    )


def solution(mesh):
    in_specs = (
        P("wide", "seq", None, None),
        P("wide", "seq", None, None),
        P("wide", None),
        P(),
        P(),
        P(),
        P(),
        P(),
        P(None, ("seq", "wide"), None),
        P(),
    )
    out_specs = (
        P("wide", "seq", None, None),
        P("wide", "seq", None, None),
        P(("seq", "wide"), None),
        P(("seq", "wide"), None),
        P(("seq", "wide"), None),
        P(("seq", "wide"), None),
        P(),
        P(),
        P(),
        P(),
        P(),
        P(),
    )
    return jax.shard_map(
        functools.partial(on_device, torus(mesh)), mesh=mesh, in_specs=in_specs, out_specs=out_specs, check_vma=False
    )
```

```python
import functools

import jax
import jax.numpy as jnp
import numpy as np
from jax import lax
from jax.experimental import pallas as pl
from jax.experimental.pallas import tpu as pltpu
from jax.sharding import PartitionSpec as P

HEADS = 12
HD = 64
NS = 4
STEP = 10


norm_epsilon = 1e-05
rope_base = 10000.0
beta_first = 0.9
beta_second = 0.95
adam_epsilon = 1e-08
weight_decay = 0.1
learn_rate = 0.01
MESH = pl.DeviceIdType.MESH
masked_score = -1e30


def shifted(value, axis, by):
    count = lax.axis_size(axis)
    pairs = [(i, i + by) for i in range(count) if 0 <= i + by < count]
    return lax.ppermute(value, axis, pairs)


def doc_layout(lengths, token_total):
    bounds = jnp.cumsum(lengths)
    starts = bounds - lengths
    places = jnp.arange(token_total, dtype=jnp.int32)
    segment = jnp.sum((places[:, None] >= bounds[None, :]).astype(jnp.int32), axis=1)
    picked = segment[:, None] == jnp.arange(lengths.shape[0], dtype=jnp.int32)[None, :]
    offset = jnp.sum(jnp.where(picked, starts[None, :], 0), axis=1)
    return (segment, places - offset)


def rope_tables(position, head_size):
    exponent = jnp.arange(head_size // 2, dtype=jnp.float32) * (2.0 / head_size)
    frequency = jnp.power(jnp.float32(rope_base), -exponent)
    angles = position.astype(jnp.float32)[:, None] * frequency[None, :]
    return (jnp.cos(angles)[:, None, :], jnp.sin(angles)[:, None, :])


def rotate(values, cosine, sine_table):
    half_size = values.shape[-1] // 2
    leading = values[..., :half_size]
    trailing = values[..., half_size:]
    return jnp.concatenate(
        [leading * cosine - trailing * sine_table, trailing * cosine + leading * sine_table],
        axis=-1,
    )


def rotate_back(grads, cosine, sine_table):
    half_size = grads.shape[-1] // 2
    leading = grads[..., :half_size]
    trailing = grads[..., half_size:]
    return jnp.concatenate(
        [leading * cosine + trailing * sine_table, trailing * cosine - leading * sine_table],
        axis=-1,
    )


def norm_parts(values):
    centre = jnp.mean(values, axis=-1, keepdims=True)
    centred = values - centre
    scaling = lax.rsqrt(jnp.mean(centred * centred, axis=-1, keepdims=True) + norm_epsilon)
    return (centred * scaling, scaling)


def norm_back(grads, normal, scaling, gain):
    gain_grad = jnp.sum(grads * normal, axis=0)
    scaled = grads * gain
    centre = jnp.mean(scaled, axis=-1, keepdims=True)
    along_normal = jnp.mean(scaled * normal, axis=-1, keepdims=True)
    return (gain_grad, scaling * (scaled - centre - normal * along_normal))


def right_product(left, right):
    return lax.dot_general(
        left, right, (((1,), (1,)), ((), ())), preferred_element_type=jnp.float32
    )


def left_product(left, right):
    return lax.dot_general(
        left, right, (((0,), (0,)), ((), ())), preferred_element_type=jnp.float32
    )


def forward_layer(stream_values, weights, gain_values, mixing, allowed, cosine, sine_table):
    attn_in, attn_out, ffn_in, ffn_out = weights
    row_count = stream_values.shape[0]
    model_width = attn_out.shape[0]
    stream_count = mixing.shape[0]
    hidden_units = ffn_out.shape[0]
    branch_in = jnp.sum(stream_values * mixing[None, :, stream_count, None], axis=1)
    mixed_streams = jnp.sum(
        stream_values[:, :, None, :] * mixing[None, :, :stream_count, None], axis=1
    )
    normal_one, scale_one = norm_parts(branch_in)
    normed = (normal_one * gain_values[:, 0]).astype(jnp.bfloat16)
    project = jnp.dot(normed, attn_in, preferred_element_type=jnp.float32)
    queries = rotate(
        project[:, :model_width].reshape(row_count, HEADS, HD), cosine, sine_table
    ).astype(jnp.bfloat16)
    keys_rot = rotate(
        project[:, model_width : 2 * model_width].reshape(row_count, HEADS, HD), cosine, sine_table
    ).astype(jnp.bfloat16)
    values_in = project[:, 2 * model_width :].astype(jnp.bfloat16)
    outgoing = jnp.concatenate([keys_rot.reshape(row_count, model_width), values_in], axis=1)
    earlier = shifted(outgoing, "seq", 1)
    key_rows = jnp.concatenate([earlier, outgoing], axis=0)
    keys_all = key_rows[:, :model_width].reshape(2 * row_count, HEADS, HD)
    values_all = key_rows[:, model_width:].reshape(2 * row_count, HEADS, HD)
    scores = jnp.einsum(
        "qhd,khd->hqk", queries, keys_all, preferred_element_type=jnp.float32
    ) * HD ** (-0.5)
    scores = jnp.where(allowed[None], scores, masked_score)
    row_top = jnp.max(scores, axis=-1, keepdims=True)
    lifted = jnp.exp(scores - row_top)
    attend = lifted / jnp.sum(lifted, axis=-1, keepdims=True)
    attend_low = attend.astype(jnp.bfloat16)
    context = jnp.einsum("hqk,khd->qhd", attend_low, values_all, preferred_element_type=jnp.float32)
    context = context.reshape(row_count, model_width).astype(jnp.bfloat16)
    first_out = jnp.dot(context, attn_out, preferred_element_type=jnp.float32)
    streams_mid = mixed_streams + mixing[None, :, stream_count + 1, None] * first_out[:, None, :]
    ffn_read = jnp.sum(streams_mid * mixing[None, :, stream_count + 2, None], axis=1)
    normal_two, scale_two = norm_parts(ffn_read)
    normed_two = (normal_two * gain_values[:, 1]).astype(jnp.bfloat16)
    gate_up = jnp.dot(normed_two, ffn_in, preferred_element_type=jnp.float32)
    gate_part = gate_up[:, :hidden_units]
    up_part = gate_up[:, hidden_units:]
    hidden = (jax.nn.silu(gate_part) * up_part).astype(jnp.bfloat16)
    second_out = jnp.dot(hidden, ffn_out, preferred_element_type=jnp.float32)
    result = streams_mid + mixing[None, :, stream_count + 3, None] * second_out[:, None, :]
    saved = (
        normal_one,
        scale_one,
        normed,
        queries,
        keys_all,
        values_all,
        attend,
        attend_low,
        context,
        first_out,
        streams_mid,
        normal_two,
        scale_two,
        normed_two,
        gate_part,
        up_part,
        hidden,
        second_out,
    )
    return (result, saved)


def backward_layer(
    stream_values, grad_out, weights, gain_values, mixing, cosine, sine_table, saved
):
    attn_in, attn_out, ffn_in, ffn_out = weights
    (
        normal_one,
        scale_one,
        normed,
        queries,
        keys_all,
        values_all,
        attend,
        attend_low,
        context,
        first_out,
        streams_mid,
        normal_two,
        scale_two,
        normed_two,
        gate_part,
        up_part,
        hidden,
        second_out,
    ) = saved
    row_count = stream_values.shape[0]
    model_width = attn_out.shape[0]
    stream_count = mixing.shape[0]
    second_low = jnp.sum(grad_out * mixing[None, :, stream_count + 3, None], axis=1).astype(
        jnp.bfloat16
    )
    grad_depth_two = jnp.sum(grad_out * second_out[:, None, :], axis=(0, 2))
    ffn_out_grad = left_product(hidden, second_low)
    hidden_grad = right_product(second_low, ffn_out)
    sigmoid_gate = jax.nn.sigmoid(gate_part)
    gate_grad = hidden_grad * up_part * sigmoid_gate * (1.0 + gate_part * (1.0 - sigmoid_gate))
    up_grad = hidden_grad * gate_part * sigmoid_gate
    gate_up_low = jnp.concatenate([gate_grad, up_grad], axis=1).astype(jnp.bfloat16)
    ffn_in_grad = left_product(normed_two, gate_up_low)
    normed_two_grad = right_product(gate_up_low, ffn_in)
    gain_two_grad, read_grad = norm_back(normed_two_grad, normal_two, scale_two, gain_values[:, 1])
    mid_grad = grad_out + mixing[None, :, stream_count + 2, None] * read_grad[:, None, :]
    grad_read_two = jnp.sum(streams_mid * read_grad[:, None, :], axis=(0, 2))
    first_low = jnp.sum(mid_grad * mixing[None, :, stream_count + 1, None], axis=1).astype(
        jnp.bfloat16
    )
    grad_depth_one = jnp.sum(mid_grad * first_out[:, None, :], axis=(0, 2))
    attn_out_grad = left_product(context, first_low)
    context_grad = (
        right_product(first_low, attn_out).astype(jnp.bfloat16).reshape(row_count, HEADS, HD)
    )
    attend_grad = jnp.einsum(
        "qhd,khd->hqk", context_grad, values_all, preferred_element_type=jnp.float32
    )
    values_grad = jnp.einsum(
        "hqk,qhd->khd", attend_low, context_grad, preferred_element_type=jnp.float32
    )
    inner_sum = jnp.sum(attend * attend_grad, axis=-1, keepdims=True)
    score_low = (attend * (attend_grad - inner_sum)).astype(jnp.bfloat16)
    query_grad = jnp.einsum(
        "hqk,khd->qhd", score_low, keys_all, preferred_element_type=jnp.float32
    ) * HD ** (-0.5)
    keys_grad = jnp.einsum(
        "hqk,qhd->khd", score_low, queries, preferred_element_type=jnp.float32
    ) * HD ** (-0.5)
    returned = jnp.concatenate(
        [
            keys_grad[:row_count].reshape(row_count, model_width),
            values_grad[:row_count].reshape(row_count, model_width),
        ],
        axis=1,
    )
    from_later = shifted(returned.astype(jnp.bfloat16), "seq", -1).astype(returned.dtype)
    own_keys = keys_grad[row_count:].reshape(row_count, model_width) + from_later[:, :model_width]
    own_values = (
        values_grad[row_count:].reshape(row_count, model_width) + from_later[:, model_width:]
    )
    query_back = rotate_back(query_grad, cosine, sine_table).reshape(row_count, model_width)
    key_back = rotate_back(own_keys.reshape(row_count, HEADS, HD), cosine, sine_table).reshape(
        row_count, model_width
    )
    project_low = jnp.concatenate([query_back, key_back, own_values], axis=1).astype(jnp.bfloat16)
    attn_in_grad = left_product(normed, project_low)
    normed_grad = right_product(project_low, attn_in)
    gain_one_grad, branch_grad = norm_back(normed_grad, normal_one, scale_one, gain_values[:, 0])
    stream_grad = jnp.sum(mid_grad[:, None, :, :] * mixing[None, :, :stream_count, None], axis=2)
    stream_grad = stream_grad + mixing[None, :, stream_count, None] * branch_grad[:, None, :]
    grad_mix = jnp.sum(stream_values[:, :, None, :] * mid_grad[:, None, :, :], axis=(0, 3))
    grad_read_one = jnp.sum(stream_values * branch_grad[:, None, :], axis=(0, 2))
    mixing_grad = jnp.concatenate(
        [
            grad_mix,
            grad_read_one[:, None],
            grad_depth_one[:, None],
            grad_read_two[:, None],
            grad_depth_two[:, None],
        ],
        axis=1,
    )
    gains_grad = jnp.stack([gain_one_grad, gain_two_grad], axis=1)
    return (
        stream_grad,
        (attn_in_grad, attn_out_grad, ffn_in_grad, ffn_out_grad),
        gains_grad,
        mixing_grad,
    )


def adam_step(shard_state, shard_grad):
    weight = shard_state[0]
    first_new = beta_first * shard_state[1] + (1.0 - beta_first) * shard_grad
    second_new = beta_second * shard_state[2] + (1.0 - beta_second) * shard_grad * shard_grad
    first_hat = first_new / (1.0 - beta_first**STEP)
    second_hat = second_new / (1.0 - beta_second**STEP)
    update = first_hat / (jnp.sqrt(second_hat) + adam_epsilon) + weight_decay * weight
    weight_new = weight - learn_rate * update
    return (weight_new, first_new, second_new)


def rope_constants(length, head_size):
    half_size = head_size // 2
    exponent = np.arange(half_size, dtype=np.float32) * np.float32(2.0 / head_size)
    frequency = np.power(np.float64(rope_base), -exponent.astype(np.float64)).astype(np.float32)
    angles = np.arange(length, dtype=np.float32)[:, None] * frequency[None, :]
    cosine = np.cos(angles.astype(np.float64)).astype(np.float32)
    sine = np.sin(angles.astype(np.float64)).astype(np.float32)
    return np.tile(cosine, (1, 4)), np.tile(np.concatenate([-sine, sine], axis=1), (1, 2))


def swapped(values):
    lane = lax.broadcasted_iota(jnp.int32, values.shape, 1)
    return jnp.where(lane % HD < HD // 2, pltpu.roll(values, 128 - HD // 2, 1), pltpu.roll(values, HD // 2, 1))


def unpacked(block):
    count = block.shape[0]
    flat = block.reshape(count * NS, block.shape[2])
    row = lax.broadcasted_iota(jnp.int32, (count * NS, count * NS), 0)
    col = lax.broadcasted_iota(jnp.int32, (count * NS, count * NS), 1)
    pick = ((row % count) * NS + row // count == col).astype(jnp.bfloat16)
    out = jnp.dot(pick, flat, preferred_element_type=jnp.float32)
    return [out[i * count : (i + 1) * count] for i in range(NS)]


def packed_streams(parts):
    count = parts[0].shape[0]
    flat = jnp.concatenate(parts, axis=0)
    row = lax.broadcasted_iota(jnp.int32, (count * NS, count * NS), 0)
    col = lax.broadcasted_iota(jnp.int32, (count * NS, count * NS), 1)
    place = ((col % count) * NS + col // count == row).astype(jnp.bfloat16)
    out = jnp.dot(place, flat, preferred_element_type=jnp.float32).astype(jnp.bfloat16)
    return out.reshape(count, NS, parts[0].shape[1])


def normal_of(values):
    centre = jnp.mean(values, axis=-1, keepdims=True)
    centred = values - centre
    scaling = lax.rsqrt(jnp.mean(centred * centred, axis=-1, keepdims=True) + norm_epsilon)
    return centred * scaling, scaling


def nt(left, right):
    return lax.dot_general(left, right, (((1,), (1,)), ((), ())), preferred_element_type=jnp.float32)


def tn(left, right):
    return lax.dot_general(left, right, (((0,), (0,)), ((), ())), preferred_element_type=jnp.float32)


def nn(left, right):
    return jnp.dot(left, right, preferred_element_type=jnp.float32)


def doc_starts(docs, place):
    start = jnp.zeros(place.shape, jnp.int32)
    bound = 0
    for j in range(docs.shape[1] - 1):
        bound = bound + docs[0, j]
        start = jnp.where(place >= bound, bound, start)
    return start


EIGHTH = 128


def q_blocks(s):
    if s == 0:
        return [(0, 0, 1, False)] + [(i, 1, i, True) for i in (1, 2, 3)]
    return [(i - 4, 1, i, True) for i in (4, 5, 6)] + [(3, 7, 1, False)]


def block_mask(docs, s, block):
    row, key, count, single = block
    shape = (EIGHTH, 2 * EIGHTH)
    place = lax.broadcasted_iota(jnp.int32, shape, 1) % EIGHTH
    at = lax.broadcasted_iota(jnp.int32, shape, 0)
    if single:
        return at <= place
    first = (4 * s + row) * EIGHTH
    start = doc_starts(docs, place + first)
    return (at + first >= start) & (at <= place)


def two_heads(pair):
    lane = lax.broadcasted_iota(jnp.int32, pair.shape, 1)
    none = jnp.zeros_like(pair)
    return jnp.concatenate([jnp.where(lane < HD, pair, none), jnp.where(lane < HD, none, pair)], axis=0)


def one_pair(stacked):
    rows = stacked.shape[1] // 2
    return jnp.concatenate([stacked[:HD, :rows], stacked[HD:, rows:]], axis=0).T


def masked_scores(k2, qs, allow):
    scores = nt(k2, qs)
    keys = scores.shape[0]
    last = jnp.where(allow, scores[keys - EIGHTH :], masked_score)
    if keys == EIGHTH:
        return last
    return jnp.concatenate([scores[: keys - EIGHTH], last], axis=0)


def when(test, f):
    def go():
        f()

    pl.when(test)(go)


UP, EARLY, LATE = range(3)
(
    CORE_SEND,
    ADD_CORE,
    ADD_A,
    ADD_B,
    Z_MID,
    Z_LAST,
    GATHER_Z,
    RELAY_ONE,
    RELAY_TWO,
    GATHER_B,
    GATHER_A,
    GATHER_CORE,
    GATHER_END,
    H_B,
    H_A,
    H_Z,
    H_R1,
    H_R2,
    SMALL,
    OWNER,
) = range(20)
PARTS = 4
Z_LAST = ((UP, 0), (EARLY, 0), )
PLAN = {
    4: (
        ((CORE_SEND, UP, 0),),
        ((CORE_SEND, UP, 0),),
    ),
    5: (
        (),
        ((ADD_CORE, UP, 0),),
    ),
    8: (
        ((CORE_SEND, EARLY, 1), (CORE_SEND, UP, 1), (ADD_CORE, UP, 0),),
        ((CORE_SEND, UP, 1), (ADD_A, UP, 0), (ADD_CORE, EARLY, 1),),
    ),
    9: (
        (),
        ((ADD_CORE, UP, 1), (ADD_B, UP, 0),),
    ),
    11: (
        ((ADD_A, UP, 0),),
        (),
    ),
    12: (
        ((CORE_SEND, EARLY, 2), (CORE_SEND, UP, 2), (ADD_CORE, UP, 1),),
        (),
    ),
    13: (
        (),
        ((ADD_A, EARLY, 1), (ADD_CORE, UP, 2), (CORE_SEND, UP, 2),),
    ),
    14: (
        ((ADD_A, UP, 1), (ADD_B, UP, 0),),
        (),
    ),
    15: (
        ((ADD_CORE, UP, 2),),
        ((ADD_A, UP, 1), (ADD_B, EARLY, 1),),
    ),
    16: (
        ((CORE_SEND, EARLY, 0), (ADD_B, UP, 1), (Z_MID, UP, 1),),
        ((ADD_A, UP, 2), (Z_MID, UP, 0),),
    ),
    17: (
        ((Z_MID, UP, 0),),
        ((ADD_CORE, EARLY, 2),),
    ),
    18: (
        (),
        ((ADD_B, UP, 1), (ADD_CORE, EARLY, 0), (ADD_B, UP, 2), (Z_MID, UP, 1),),
    ),
    19: (
        (),
        ((ADD_A, EARLY, 2),),
    ),
    20: (
        ((ADD_A, UP, 2), (ADD_B, UP, 2), (Z_LAST, UP, 1),),
        (),
    ),
    22: (
        ((Z_MID, UP, 2),),
        ((CORE_SEND, LATE, 0), (Z_MID, UP, 2),),
    ),
    23: (
        ((Z_LAST, UP, 0), (ADD_CORE, LATE, 0),),
        ((ADD_A, EARLY, 0), (CORE_SEND, LATE, 1), (Z_MID, EARLY, 1), (Z_LAST, UP, 0), (ADD_B, EARLY, 2),),
    ),
    24: (
        ((ADD_CORE, LATE, 1),),
        (),
    ),
    25: (
        ((Z_LAST, UP, 2), (ADD_A, LATE, 0), (ADD_CORE, LATE, 2),),
        ((Z_LAST, UP, 1), (ADD_B, EARLY, 0),),
    ),
    26: (
        ((OWNER, UP, 0), (GATHER_Z, UP, 1), (H_B, UP, 0), (GATHER_Z, UP, 3),),
        ((Z_MID, EARLY, 2), (Z_LAST, UP, 2), (CORE_SEND, LATE, 2),),
    ),
    27: (
        ((ADD_A, LATE, 1), (ADD_B, LATE, 0),),
        (),
    ),
    28: (
        ((RELAY_ONE, UP, 1), (ADD_A, LATE, 2),),
        ((Z_MID, EARLY, 0), (OWNER, UP, 0), (GATHER_Z, UP, 2), (Z_LAST, EARLY, 1),),
    ),
    29: (
        ((RELAY_TWO, UP, 1), (Z_LAST, LATE, 0), (RELAY_ONE, UP, 3), (Z_MID, LATE, 0), (GATHER_B, UP, 1),),
        ((Z_LAST, EARLY, 2), (GATHER_Z, UP, 3), (GATHER_Z, UP, 1),),
    ),
    30: (
        ((RELAY_TWO, UP, 3), (ADD_B, LATE, 1), (Z_LAST, LATE, 1),),
        (),
    ),
    31: (
        ((H_A, UP, 0), (ADD_B, LATE, 2), (Z_MID, LATE, 1),),
        ((Z_LAST, EARLY, 0), (RELAY_ONE, UP, 2), (OWNER, EARLY, 0), (H_B, UP, 0), (GATHER_Z, EARLY, 1),
         (RELAY_TWO, UP, 2), (H_B, EARLY, 0),),
    ),
    32: (
        (),
        ((GATHER_B, UP, 2), (RELAY_ONE, UP, 3), (RELAY_TWO, UP, 3), (GATHER_Z, EARLY, 3), (H_A, EARLY, 0),),
    ),
    33: (
        (),
        ((RELAY_ONE, UP, 1), (GATHER_Z, EARLY, 2), (GATHER_B, UP, 3), (GATHER_A, UP, 2), (RELAY_ONE, EARLY,
         1), (RELAY_ONE, EARLY, 2), (GATHER_A, UP, 3), (RELAY_TWO, EARLY, 1), (RELAY_ONE, EARLY, 3), (H_Z,
         EARLY, 0), (GATHER_CORE, UP, 2), (GATHER_B, EARLY, 1), (RELAY_TWO, EARLY, 2), (GATHER_B, EARLY, 2),
         (RELAY_TWO, EARLY, 3), (GATHER_B, EARLY, 3),),
    ),
    34: (
        ((GATHER_B, UP, 3), (Z_MID, LATE, 2), (GATHER_Z, UP, 2), (Z_LAST, LATE, 2),),
        (),
    ),
    35: (
        (),
        ((H_A, UP, 0),),
    ),
    36: (
        ((GATHER_A, UP, 1),),
        (),
    ),
    37: (
        ((RELAY_ONE, UP, 2), (RELAY_TWO, UP, 2), (OWNER, LATE, 0), (GATHER_Z, LATE, 1), (GATHER_Z, LATE, 2),
         (H_Z, UP, 0),),
        (),
    ),
    38: (
        ((GATHER_B, UP, 2),),
        ((GATHER_A, EARLY, 1), (GATHER_A, EARLY, 3),),
    ),
    39: (
        ((H_R1, UP, 0), (GATHER_Z, LATE, 3), (GATHER_A, UP, 3),),
        (),
    ),
    40: (
        ((RELAY_ONE, LATE, 1),),
        ((GATHER_A, EARLY, 2),),
    ),
    41: (
        ((GATHER_CORE, UP, 1),),
        ((H_R1, EARLY, 0),),
    ),
    42: (
        ((SMALL, UP, 0), (RELAY_ONE, LATE, 2), (SMALL, UP, 1), (GATHER_A, UP, 2), (RELAY_TWO, LATE, 1),
         (GATHER_B, LATE, 1), (RELAY_TWO, LATE, 2), (GATHER_Z, LATE, 0), (RELAY_ONE, LATE, 3), (GATHER_B,
         LATE, 2), (RELAY_TWO, LATE, 3), (H_R2, UP, 0), (RELAY_TWO, LATE, 0), (RELAY_ONE, LATE, 0), (GATHER_A,
         LATE, 1), (SMALL, UP, 2), (GATHER_CORE, UP, 2), (GATHER_B, LATE, 3), (GATHER_A, LATE, 2), (GATHER_B,
         LATE, 0), (GATHER_END, UP, 1), (GATHER_END, EARLY, 3), (GATHER_END, UP, 2), (GATHER_CORE, LATE, 1),
         (GATHER_A, LATE, 3), (GATHER_CORE, UP, 3), (GATHER_CORE, UP, 0), (GATHER_CORE, LATE, 2), (GATHER_A,
         LATE, 0), (GATHER_CORE, LATE, 3), (GATHER_CORE, LATE, 0), (SMALL, UP, 3), (GATHER_END, UP, 0),
         (GATHER_END, EARLY, 2), (SMALL, UP, 4), (GATHER_END, EARLY, 0), (GATHER_END, UP, 3), (GATHER_END,
         EARLY, 1),),
        ((SMALL, UP, 0), (GATHER_CORE, UP, 3), (RELAY_TWO, UP, 1), (H_Z, UP, 0), (GATHER_B, UP, 1),
         (GATHER_CORE, EARLY, 3), (GATHER_CORE, EARLY, 1), (SMALL, UP, 1), (H_R1, UP, 0), (GATHER_A, UP, 1),
         (GATHER_CORE, UP, 1), (H_R2, UP, 0), (H_R2, EARLY, 0), (GATHER_CORE, EARLY, 0), (SMALL, UP, 2),
         (GATHER_CORE, EARLY, 2), (SMALL, UP, 3), (GATHER_END, LATE, 1), (GATHER_CORE, UP, 0), (GATHER_END,
         UP, 2), (SMALL, UP, 4), (GATHER_END, UP, 0), (GATHER_END, UP, 3), (GATHER_END, UP, 1), (GATHER_END,
         LATE, 2), (GATHER_END, LATE, 3), (GATHER_END, LATE, 0),),
    ),
}


def layer_kernel(
    dims, token_count,
    docs, small, gains, small_rows, streams, cotangent, attn_in, attn_out, ffn_in, ffn_out, state_in,
    cos_table, sin_table,
    new_out, stream_grad_out, copy_out, grad_out, small_out, from_core,
    grads, from_a0, from_a1, from_b0, from_b1, from_c, stage_box, kv_box, gfirst, second, dread, read, first,
    normed, queries, keys, values, context, lse, cosine, sine, starts, low, small_box,
    kv_send_sem, kv_recv_sem, send_sem, recv_sem, load_sem, local_sem, stage_sem, store_sem, out_sem, small_send, small_recv,
):
    f32, bf16 = jnp.float32, jnp.bfloat16
    nz, ny, nx = dims
    rows, width = second.shape
    hidden = ffn_out.shape[0]
    shard = low.shape[0]
    piece = shard // 3
    unit = 6 * piece
    half = unit // 2
    planes = nz // 2
    s = lax.axis_index("seq")
    w = lax.axis_index("wide")
    z, y, x = w // (ny * nx), (w // nx) % ny, w % nx

    def chip(cz, cy, cx):
        return (s, (cz * ny + cy) * nx + cx)

    core = (1 - s, w)
    z_peers = [chip((z + d) % nz, y, x) for d in range(1, nz)]
    y_peers = [chip(z, (y + d) % ny, x) for d in range(1, ny)]
    x_peers = [chip(z, y, (x + d) % nx) for d in range(1, nx)]
    peers = [core] + z_peers + y_peers + x_peers
    barrier = pltpu.get_barrier_semaphore()
    for peer in peers:
        pl.semaphore_signal(barrier, inc=1, device_id=peer, device_id_type=MESH)

    base = 2 * width
    mix = [[small[0, base + i * 2 * NS + j] for j in range(2 * NS)] for i in range(NS)]
    read_one = [mix[i][NS] for i in range(NS)]
    depth_one = [mix[i][NS + 1] for i in range(NS)]
    read_two = [mix[i][NS + 2] for i in range(NS)]
    depth_two = [mix[i][NS + 3] for i in range(NS)]

    def load(src, dst, sem):
        copy = pltpu.make_async_copy(src, dst, sem)
        copy.start()
        return copy

    ids = {}
    unsent = {}
    unit_now = [None]

    def number(kind, key, count=1):
        if (kind, key) not in ids:
            ids[kind, key] = ids.get(kind, 0)
            ids[kind] = ids.get(kind, 0) + count
        return ids[kind, key]

    def copy_of(key, ends, recv=None):
        src, dst, peer = ends()
        got = number("recv", key) if recv is None else recv()
        return pltpu.make_async_remote_copy(
            src, dst, send_sem.at[number("send", key)], recv_sem.at[got], device_id=peer, device_id_type=MESH)

    def remote(key, ends, guard=None, recv=None):
        copy_of(key, ends, recv).start()
        unsent.setdefault((key, unit_now[-1]), (lambda: copy_of(key, ends, recv), guard))

    def wait_sends():
        for copy, guard in unsent.values():
            if guard is None:
                copy().wait_send()
            else:
                pl.when(guard())(lambda copy=copy: copy().wait_send())
        unsent.clear()

    one, zero = s == 1, s == 0
    group_of = {UP: 1, EARLY: 0, LATE: 0}
    guard_of = {UP: None, EARLY: lambda: one, LATE: lambda: zero}

    def zs_of(v):
        return pl.ds(planes * group_of[v], planes)

    def zlist(v):
        return list(range(planes * group_of[v], planes * (group_of[v] + 1)))

    def guarded(v, f):
        f()

    def more(v, test):
        if guard_of[v] is None:
            return test
        return lambda: guard_of[v]() & test()

    lo, hi = pl.ds(0, half), pl.ds(half, half)

    def core_moves(v, c):
        return [(
            ("core", group_of[v], c),
            lambda: (grads.at[1 - s, zs_of(v), :, :, c], from_core.at[zs_of(v), :, :, c], core))]

    def a_moves(v, c):
        g = group_of[v]
        return [
            (("a0", g, c, d), lambda d=d: (
                grads.at[s, zs_of(v), :, (x + d) % nx, c, lo], from_a0.at[d - 1, zs_of(v), :, c], x_peers[d - 1]))
            for d in range(1, nx)
        ] + [
            (("a1", g, c, d), lambda d=d: (
                grads.at[s, zs_of(v), (y + d) % ny, :, c, hi], from_a1.at[d - 1, zs_of(v), :, c], y_peers[d - 1]))
            for d in range(1, ny)
        ]

    def b_moves(v, c):
        g = group_of[v]
        return [
            (("b0", g, c, d), lambda d=d: (
                grads.at[s, zs_of(v), (y + d) % ny, x, c, lo], from_b0.at[d - 1, zs_of(v), c], y_peers[d - 1]))
            for d in range(1, ny)
        ] + [
            (("b1", g, c, d), lambda d=d: (
                grads.at[s, zs_of(v), y, (x + d) % nx, c, hi], from_b1.at[d - 1, zs_of(v), c], x_peers[d - 1]))
            for d in range(1, nx)
        ]

    def same(ref, peer):
        return ref, ref, peer

    def gb_moves(v, k):
        g = group_of[v]
        return [
            (("gb0", g, k, d), lambda peer=peer: same(copy_out.at[s, zs_of(v), y, x, part_lo(k)], peer))
            for d, peer in enumerate(y_peers)
        ] + [
            (("gb1", g, k, d), lambda peer=peer: same(copy_out.at[s, zs_of(v), y, x, part_hi(k)], peer))
            for d, peer in enumerate(x_peers)
        ]

    def ga_moves(v, k):
        g = group_of[v]
        return [
            (("ga0", g, k, d), lambda peer=peer: same(copy_out.at[s, zs_of(v), :, x, part_lo(k)], peer))
            for d, peer in enumerate(x_peers)
        ] + [
            (("ga1", g, k, d), lambda peer=peer: same(copy_out.at[s, zs_of(v), y, :, part_hi(k)], peer))
            for d, peer in enumerate(y_peers)
        ]

    def gc_moves(v, k):
        return [(("gc", group_of[v], k), lambda: same(copy_out.at[s, zs_of(v), :, :, part(k)], core))]

    def start(moves, v, c, guard="unit"):
        for key, ends in moves(v, c):
            remote(key, ends, guard=guard_of[v] if guard == "unit" else guard)

    def wait_recvs(moves, v, c):
        for key, ends in moves(v, c):
            copy_of(key, ends).wait_recv()

    def core_send(v, c):
        start(core_moves, v, c, {UP: None, EARLY: lambda: zero, LATE: lambda: one}[v])

    def add_core(v, c):
        def go():
            wait_recvs(core_moves, v, c)
            g = group_of[v]
            loads = [
                load(from_core.at[planes * g + i, :, :, c], stage_box.at[i], stage_sem.at[i]) for i in range(planes)
            ]
            for plane, copy in enumerate(loads):
                copy.wait()

                def body(i, carry, plane=plane):
                    yi, xi = i // nx, i % nx
                    at = (s, planes * g + plane, yi, xi, c)
                    grads[at] = (grads[at].astype(f32) + stage_box[plane, yi, xi].astype(f32)).astype(bf16)
                    return carry

                lax.fori_loop(0, ny * nx, body, 0)
            start(a_moves, v, c)

        guarded(v, go)

    def add_a(v, c):
        def go():
            wait_recvs(a_moves, v, c)
            g = group_of[v]

            def body_lo(i, carry):
                zi, yi = planes * g + i // ny, i % ny
                at = (s, zi, yi, x, c, lo)
                total = grads[at].astype(f32)
                for d in range(nx - 1):
                    total = total + from_a0[d, zi, yi, c].astype(f32)
                grads[at] = total.astype(bf16)
                return carry

            def body_hi(i, carry):
                zi, xi = planes * g + i // nx, i % nx
                at = (s, zi, y, xi, c, hi)
                total = grads[at].astype(f32)
                for d in range(ny - 1):
                    total = total + from_a1[d, zi, xi, c].astype(f32)
                grads[at] = total.astype(bf16)
                return carry

            lax.fori_loop(0, planes * ny, body_lo, 0)
            lax.fori_loop(0, planes * nx, body_hi, 0)
            start(b_moves, v, c)

        guarded(v, go)

    def add_b(v, c):
        def go():
            wait_recvs(b_moves, v, c)
            g = group_of[v]

            def body(i, carry):
                zi = planes * g + i
                for at_rows, box, count in ((lo, from_b0, ny - 1), (hi, from_b1, nx - 1)):
                    at = (s, zi, y, x, c, at_rows)
                    total = grads[at].astype(f32)
                    for d in range(count):
                        total = total + box[d, zi, c].astype(f32)
                    grads[at] = total.astype(bf16)
                return carry

            lax.fori_loop(0, planes, body, 0)
            hop(v, c, 0)

        guarded(v, go)

    def place_of(v):
        return z if group_of[v] == 1 else nz - 1 - z

    def z_at(v, place):
        return place if group_of[v] == 1 else nz - 1 - place

    def hop(v, c, place):
        g = group_of[v]
        if place == 0:
            moves = [(0, 1, 2, 0), (0, 1, 3, 1), (3, 2, 2, 2)]
        elif place == 1:
            moves = [(1, 2, 2, 0), (1, 2, 3, 1)]
        else:
            moves = [(2, 3, 3, 1)]
        for start, end, owner, slot in moves:
            when(place_of(v) == start, lambda start=start, end=end, owner=owner, slot=slot: remote(
                ("z", g, c, start, owner),
                lambda: (grads.at[s, z_at(v, owner), y, x, c], from_c.at[g, slot, c], chip(z_at(v, end), y, x)),
                guard=more(v, lambda: place_of(v) == start),
                recv=lambda: number("recv", ("z", g, c, slot))))

    def hop_wait(v, c, slot):
        g = group_of[v]
        pltpu.make_async_remote_copy(
            grads.at[s, z, y, x, c], from_c.at[g, slot, c], send_sem.at[0],
            recv_sem.at[number("recv", ("z", g, c, slot))], device_id=core, device_id_type=MESH).wait_recv()

    def hop_add(v, c, place):
        def go():
            for owner, slot in ((2, 0), (3, 1)) if place == 1 else ((3, 1),):
                hop_wait(v, c, slot)
                g = group_of[v]

                def body(i, carry, owner=owner, slot=slot):
                    r = pl.ds(i * 128, 128)
                    at = (s, z_at(v, owner), y, x, c, r)
                    grads[at] = (grads[at].astype(f32) + from_c[g, slot, c, r].astype(f32)).astype(bf16)
                    return carry

                lax.fori_loop(0, unit // 128, body, 0)
            hop(v, c, place)

        guarded(v, lambda: when(place_of(v) == place, go))

    def z_mid(v, c):
        hop_add(v, c, 1)

    def z_last(v, c):
        hop_add(v, c, 2)

    def in_group(g):
        return (z // planes) == g

    def owner_update(units, state, flat, sums):
        for v in units:
            g = group_of[v]

            def total_at(slots, v=v, g=g):
                for c in range(3):
                    for slot in slots:
                        hop_wait(v, c, slot)

                def body(i, carry):
                    r = pl.ds(i * 128, 128)
                    for c in range(3):
                        total = grads[s, z, y, x, c, r].astype(f32)
                        for slot in slots:
                            total = total + from_c[g, slot, c, r].astype(f32)
                        sums[c, r] = total * (1.0 / token_count)
                    return carry

                lax.fori_loop(0, unit // 128, body, 0)

            guarded(v, lambda v=v, f=total_at: when(place_of(v) == 2, lambda: f((0, 2))))
            guarded(v, lambda v=v, f=total_at: when(place_of(v) == 3, lambda: f((1,))))
        mine = {UP: in_group(1), EARLY: in_group(0) & one, LATE: in_group(0) & zero}[units[0]]
        pl.when(mine)(lambda: owner_step(state, flat, sums))

    def owner_step(state, flat, sums):
        pltpu.make_async_copy(state_in, state, load_sem.at[0]).wait()
        index = s * (nz * ny * nx) + w
        in_rows = attn_in.shape[0] * attn_in.shape[1] // width // shard
        out_rows = in_rows + attn_out.shape[0] // shard
        ffn_rows = out_rows + ffn_in.shape[0] * ffn_in.shape[1] // width // shard
        blocks = ffn_in.shape[1] // width
        thirds = attn_in.shape[1] // width

        def total_of(c, at_rows):
            return sums[c, at_rows]

        @pl.when(index < in_rows)
        def _():
            for c in range(3):
                for lane in range(6):
                    flat[lane, pl.ds(c, piece, stride=thirds), :] = total_of(c, pl.ds(lane * piece, piece))

        @pl.when(((index >= in_rows) & (index < out_rows)) | (index >= ffn_rows))
        def _():
            for c in range(3):
                for lane in range(6):
                    flat[lane, pl.ds(c * piece, piece), :] = total_of(c, pl.ds(lane * piece, piece))

        @pl.when((index >= out_rows) & (index < ffn_rows))
        def _():
            part = shard // blocks
            for c in range(3):
                for side in range(2):
                    for j in range(blocks):
                        flat[side * 3 + c, pl.ds(j, part, stride=blocks), :] = total_of(
                            c, pl.ds(side * half + j * part, part))

        def body(i, carry):
            r = pl.ds(i * 16, 16)
            grad = jnp.concatenate([flat[lane, r] for lane in range(6)], axis=1)
            read[r] = grad
            low[r] = adam_step((state[0, r], state[1, r], state[2, r]), grad)[0].astype(bf16)
            return carry

        lax.fori_loop(0, shard // 16, body, 0)
        pltpu.make_async_copy(read.at[pl.ds(0, shard)], grad_out, store_sem.at[0]).start()
        keep = pltpu.make_async_copy(low, copy_out.at[s, z, y, x], store_sem.at[4])
        keep.start()
        keep.wait()

    gather_parts = PARTS
    part_rows = shard // gather_parts

    def part(k):
        return pl.ds(k * part_rows, part_rows)

    def part_lo(k):
        return pl.ds(k * part_rows, part_rows // 2)

    def part_hi(k):
        return pl.ds(k * part_rows + part_rows // 2, part_rows // 2)

    def relay(v, k, moves):
        for start, end, owner, mine in moves:
            def send(start=start, end=end, owner=owner, mine=mine):
                zd = z_at(v, owner)

                def ends():
                    dst = copy_out.at[s, zd, y, x, part(k)]
                    return (low.at[part(k)] if mine else dst), dst, chip(z_at(v, end), y, x)

                remote(("gz", zd, k, start, end), ends, guard=more(v, lambda: place_of(v) == start),
                       recv=lambda: number("recv", ("gz", zd, k)))

            when(place_of(v) == start, send)

    def relay_wait(v, k, place, owner):
        zd = z_at(v, owner)
        when(place_of(v) == place, lambda: pltpu.make_async_remote_copy(
            low.at[part(k)], copy_out.at[s, zd, y, x, part(k)], send_sem.at[0],
            recv_sem.at[number("recv", ("gz", zd, k))], device_id=core, device_id_type=MESH).wait_recv())

    def gather_z(v, k):
        guarded(v, lambda: relay(v, k, [(2, 1, 2, True), (2, 3, 2, True), (3, 2, 3, True)]))

    def relay_one(v, k):
        def go():
            relay_wait(v, k, 2, 3)
            relay_wait(v, k, 1, 2)
            relay(v, k, [(2, 1, 3, False), (1, 0, 2, False)])

        guarded(v, go)

    def relay_two(v, k):
        def go():
            relay_wait(v, k, 1, 3)
            relay(v, k, [(1, 0, 3, False)])

        guarded(v, go)

    def gather_b(v, k):
        def go():
            g = group_of[v]
            relay_wait(v, k, 0, 2)
            relay_wait(v, k, 0, 3)
            relay_wait(v, k, 3, 2)
            start(gb_moves, v, k)

        guarded(v, go)

    def gather_a(v, k):
        def go():
            wait_recvs(gb_moves, v, k)
            g = group_of[v]
            start(ga_moves, v, k)

        guarded(v, go)

    def hb_moves(v, k):
        g = group_of[v]
        return [
            (("hb0", g, k, d), lambda peer=peer: same(copy_out.at[s, z, y, x, part_lo(k)], peer))
            for d, peer in enumerate(y_peers)
        ] + [
            (("hb1", g, k, d), lambda peer=peer: same(copy_out.at[s, z, y, x, part_hi(k)], peer))
            for d, peer in enumerate(x_peers)
        ]

    def ha_moves(v, k):
        g = group_of[v]
        return [
            (("ha0", g, k, d), lambda peer=peer: same(copy_out.at[s, z, :, x, part_lo(k)], peer))
            for d, peer in enumerate(x_peers)
        ] + [
            (("ha1", g, k, d), lambda peer=peer: same(copy_out.at[s, z, y, :, part_hi(k)], peer))
            for d, peer in enumerate(y_peers)
        ]

    def owner_place(v):
        return lambda: place_of(v) >= 2

    def h_b(v, k):
        when(place_of(v) >= 2, lambda: start(hb_moves, v, k, more(v, owner_place(v))))

    def h_a(v, k):
        def go():
            wait_recvs(hb_moves, v, k)
            start(ha_moves, v, k, more(v, owner_place(v)))

        when(place_of(v) >= 2, go)

    def plane_ends(v, k, owner, end):
        return lambda: same(copy_out.at[s, z_at(v, owner), :, :, part(k)], chip(z_at(v, end), y, x))

    def plane_send(v, k, at, end, owner):
        when(place_of(v) == at, lambda: remote(
            ("hz", z_at(v, owner), k, at, end), plane_ends(v, k, owner, end), guard=more(v, lambda: place_of(v) == at),
            recv=lambda: number("recv", ("hz", z_at(v, owner), k))))

    def plane_wait(v, k, at, owner):
        when(place_of(v) == at, lambda: copy_of(
            ("hz", z_at(v, owner), k, 2, 1), plane_ends(v, k, owner, 2),
            lambda: number("recv", ("hz", z_at(v, owner), k))).wait_recv())

    def h_z(v, k):
        when(place_of(v) >= 2, lambda: wait_recvs(ha_moves, v, k))
        plane_send(v, k, 2, 1, 2)
        plane_send(v, k, 2, 3, 2)
        plane_send(v, k, 3, 2, 3)

    def h_r1(v, k):
        plane_wait(v, k, 2, 3)
        plane_wait(v, k, 1, 2)
        plane_send(v, k, 2, 1, 3)
        plane_send(v, k, 1, 0, 2)

    def h_r2(v, k):
        plane_wait(v, k, 1, 3)
        plane_send(v, k, 1, 0, 3)

    def gather_core(v, k):
        def go():
            if (v, k) in Z_LAST:
                plane_wait(v, k, 0, 2)
                plane_wait(v, k, 0, 3)
                plane_wait(v, k, 3, 2)
            else:
                wait_recvs(ga_moves, v, k)
            start(gc_moves, v, k)

        guarded(v, go)

    def gather_end(v, k):
        wait_recvs(gc_moves, v, k)

    wide_piece = piece
    tile = hidden // 3
    tile_pieces = tile // wide_piece
    steps = tile_pieces // 2

    tiles = []

    def kv_copy(hp):
        cols = pl.ds(pl.multiple_of(hp * 128, 128), 128)
        return pltpu.make_async_remote_copy(
            kv_box.at[:, cols], kv_box.at[:, cols], kv_send_sem.at[hp], kv_recv_sem.at[hp],
            device_id=core, device_id_type=MESH)

    def tile_loads(c):
        slot = c % 2
        copies = []
        for p in range(tile_pieces):
            at = p * 3 * wide_piece + c * wide_piece
            to = pl.ds(p * wide_piece, wide_piece)
            for k, (src, dst) in enumerate((
                (ffn_in.at[:, pl.ds(at, wide_piece)], tiles[0].at[slot, :, to]),
                (ffn_in.at[:, pl.ds(hidden + at, wide_piece)], tiles[1].at[slot, :, to]),
                (ffn_out.at[pl.ds(at, wide_piece)], tiles[2].at[slot, to]),
            )):
                copies.append(pltpu.make_async_copy(src, dst, local_sem.at[slot, k, p]))
        return copies

    def forward_scope(raw, w_in):
        w_out = kv_box
        loads = [load(src, dst, load_sem.at[1 + k]) for k, (src, dst) in enumerate((
            (streams, raw), (attn_in, w_in), (cos_table.at[pl.ds(0, EIGHTH)], starts.at[0]),
            (sin_table.at[pl.ds(0, EIGHTH)], starts.at[1]), (attn_out, w_out)))]
        plain_rows = [pl.ds(EIGHTH, 3 * EIGHTH), pl.ds(0, 3 * EIGHTH)]
        plain_loads = [
            [pltpu.make_async_copy(table.at[pl.ds(side * 3 * EIGHTH, 3 * EIGHTH)], own.at[plain_rows[side]],
                                   load_sem.at[11 + k])
             for k, (table, own) in enumerate(((cos_table, cosine), (sin_table, sine)))]
            for side in range(2)
        ]
        for side in range(2):
            @pl.when(s == side)
            def _(side=side):
                for copy in plain_loads[side]:
                    copy.start()

        carry_first = sum(depth_one[j] * read_two[j] for j in range(NS))
        carry_stream = [sum(mix[i][j] * read_two[j] for j in range(NS)) for i in range(NS)]
        loads[0].wait()

        def norm_block(i, carry):
            r = pl.ds(i * 64, 64)
            parts = unpacked(raw[r])
            branch = sum(parts[k] * read_one[k] for k in range(NS))
            read[r] = sum(parts[k] * carry_stream[k] for k in range(NS))
            normal, _ = normal_of(branch)
            normed[r] = (normal * gains[0:1].astype(f32)).astype(bf16)
            return carry

        lax.fori_loop(0, rows // 64, norm_block, 0)
        for copy in loads[1:]:
            copy.wait()
        load(cotangent, raw, load_sem.at[6])
        for c in range(2):
            for copy in tile_loads(c):
                copy.start()

        def tables(side):
            first_special = 7 * EIGHTH * side
            special = pl.ds(3 * EIGHTH * side, EIGHTH)
            place = lax.broadcasted_iota(jnp.int32, (EIGHTH, EIGHTH), 0) + first_special
            start = doc_starts(docs, place)
            lane = lax.broadcasted_iota(jnp.int32, (EIGHTH, EIGHTH), 1)
            pick = (place - start == lane).astype(f32)
            for k, own in enumerate((cosine, sine)):
                own[special] = jnp.dot(
                    pick, starts[k], precision=lax.Precision.HIGHEST, preferred_element_type=f32)
            for copy in plain_loads[side]:
                copy.wait()

        for side in range(2):
            pl.when(s == side)(lambda side=side: tables(side))

        own_rows = pl.ds(s * rows, rows)

        def rotated(dest, dest_rows, offset):
            def body(j, carry):
                cols = pl.ds(pl.multiple_of(j * 256, 256), 256)
                source = pl.ds(pl.multiple_of(offset + j * 256, 256), 256)
                part = nn(normed[...], w_in[:, source])
                halves = []
                for k in range(2):
                    turn = part[:, k * 128 : (k + 1) * 128]
                    halves.append(turn * cosine[...] + swapped(turn) * sine[...])
                dest[dest_rows, cols] = jnp.concatenate(halves, axis=1).astype(bf16)
                return carry

            lax.fori_loop(0, width // 256, body, 0)

        def plain(j, carry):
            cols = pl.ds(pl.multiple_of(j * 256, 256), 256)
            source = pl.ds(pl.multiple_of(2 * width + j * 256, 256), 256)
            values[own_rows, cols] = nn(normed[...], w_in[:, source]).astype(bf16)
            return carry

        lax.fori_loop(0, width // 256, plain, 0)
        rotated(keys, own_rows, width)
        pl.semaphore_wait(barrier, len(peers))
        shared = pl.ds(EIGHTH, 3 * EIGHTH)
        copies = [
            pltpu.make_async_remote_copy(
                ref.at[shared], ref.at[shared], kv_send_sem.at[6 + i], kv_recv_sem.at[6 + i],
                device_id=core, device_id_type=MESH)
            for i, ref in enumerate((keys, values))
        ]

        @pl.when(zero)
        def _():
            for copy in copies:
                copy.start()

        rotated(queries, pl.ds(0, rows), 0)

        def attend(side):
            blocks = q_blocks(side)
            masks = [block_mask(docs, side, block) for block in blocks]

            def pair(hp, carry):
                jobs = [
                    (2 * hp + q, pl.ds(pl.multiple_of((2 * hp + q) * 128, 128), 128), bi,
                     pl.ds(row * EIGHTH, EIGHTH), pl.ds(key * EIGHTH, count * EIGHTH))
                    for q in range(2) for bi, (row, key, count, _) in enumerate(blocks)
                ]
                scores = [
                    masked_scores(keys[kr, cols], two_heads(queries[r, cols]) * HD ** (-0.5), masks[bi])
                    for _, cols, bi, r, kr in jobs
                ]
                tops = [jnp.max(score, axis=0, keepdims=True) for score in scores]
                lifted = [jnp.exp(score - top) for score, top in zip(scores, tops)]
                totals = [jnp.sum(lift, axis=0, keepdims=True) for lift in lifted]
                probs = [(lift * (1.0 / total)).astype(bf16) for lift, total in zip(lifted, totals)]
                outs = [tn(values[job[4], job[1]], prob) for job, prob in zip(jobs, probs)]
                for (pair_at, cols, bi, r, kr), out, top, total in zip(jobs, outs, tops, totals):
                    context[r, cols] = one_pair(out).astype(bf16)
                    lse[pl.ds(bi * 8 + pair_at, 1), :] = top + jnp.log(total)
                return carry

            lax.fori_loop(0, width // 256, pair, 0)

        @pl.when(zero)
        def _():
            attend(0)
            for copy in copies:
                copy.wait_send()

        @pl.when(one)
        def _():
            for copy in copies:
                copy.wait_recv()
            attend(1)

        def out_block(j, carry):
            cols = pl.ds(pl.multiple_of(j * 256, 256), 256)
            part = nn(context[...], w_out[:, cols])
            first[:, cols] = part
            read[:, cols] += part * carry_first
            return carry

        lax.fori_loop(0, width // 256, out_block, 0)

    def ffn_scope(raw, normed_two, normed_two_t, dsecond, gate_s, up_s, dhid_s, hid, dgate, dup):
        pltpu.make_async_copy(cotangent, raw, load_sem.at[6]).wait()

        def first_block(i, carry):
            r = pl.ds(i * 64, 64)
            parts = unpacked(raw[r])
            dsecond[r] = sum(parts[j] * depth_two[j] for j in range(NS)).astype(bf16)
            gfirst[r] = sum(parts[j] * depth_one[j] for j in range(NS))
            normal, _ = normal_of(read[r])
            normed_two[r] = (normal * gains[1:2].astype(f32)).astype(bf16)
            second[r] = jnp.zeros((64, width), f32)
            dread[r] = jnp.zeros((64, width), f32)
            return carry

        lax.fori_loop(0, rows // 64, first_block, 0)
        normed_two_t[...] = normed_two[...].T

        if True:
            def sub(step, carry):
                c, u = step // steps, step % steps
                slot = c % 2
                for k in range(3):
                    def arrive(k=k):
                        for copy in tile_loads(k):
                            copy.wait()

                    pl.when(step == k * steps)(arrive)
                cols = pl.ds(pl.multiple_of(u * 2 * wide_piece, 2 * wide_piece), 2 * wide_piece)
                wg, wu, wo = tiles[0][slot, :, cols], tiles[1][slot, :, cols], tiles[2][slot, cols]
                gate_s[...] = nn(normed_two[...], wg)
                up_s[...] = nn(normed_two[...], wu)
                dhid_s[...] = nt(dsecond[...], wo)
                for i in range(rows // 64):
                    r = pl.ds(i * 64, 64)
                    gate, up, dhid = gate_s[r], up_s[r], dhid_s[r]
                    sig = 1.0 / (1.0 + jnp.exp(-gate))
                    silu = gate * sig
                    hid[r] = (silu * up).astype(bf16)
                    dgate[r] = (dhid * up * sig * (1.0 + gate - silu)).astype(bf16)
                    dup[r] = (dhid * silu).astype(bf16)
                second[...] += nn(hid[...], wo)
                dread[...] += nt(dgate[...], wg) + nt(dup[...], wu)
                dwo = tn(hid[...], dsecond[...]).astype(bf16)
                for q in range(2):
                    p = 2 * u + q
                    zi, yi, xi = planes + p // (ny * nx), (p // nx) % ny, p % nx
                    for lane in range(6):
                        grads[1, zi, yi, xi, c, pl.ds(lane * piece, piece)] = dwo[
                            q * piece : (q + 1) * piece, lane * 128 : (lane + 1) * 128]
                blocks = 2 * (hidden // width)
                part = shard // blocks
                for k, dact in enumerate((dgate, dup)):
                    dwi = nn(normed_two_t[...], dact[...]).astype(bf16)
                    j = u + k * (blocks // 2)
                    for b in range(width // part):
                        at_half, at = b // (width // part // 2), b % (width // part // 2)
                        at = at + (nz * ny * nx // 2 if at_half == 0 else 0)
                        zi, yi, xi = at // (ny * nx), (at // nx) % ny, at % nx
                        for q in range(2):
                            grads[at_half, zi, yi, xi, c, pl.ds(pl.multiple_of(q * half + j * part, 16), part)] = dwi[
                                b * part : (b + 1) * part, q * 128 : (q + 1) * 128]
                def more_weights():
                    for copy in tile_loads(2):
                        copy.start()

                pl.when(step == steps - 1)(more_weights)
                poll_loop(1, 3 * steps, step)
                return carry

            lax.fori_loop(0, 3 * steps, sub, 0)

    stages = {
        CORE_SEND: core_send,
        ADD_CORE: add_core,
        ADD_A: add_a,
        ADD_B: add_b,
        Z_MID: z_mid,
        Z_LAST: z_last,
        GATHER_Z: gather_z,
        RELAY_ONE: relay_one,
        RELAY_TWO: relay_two,
        GATHER_B: gather_b,
        GATHER_A: gather_a,
        GATHER_CORE: gather_core,
        GATHER_END: gather_end,
        H_B: h_b,
        H_A: h_a,
        H_Z: h_z,
        H_R1: h_r1,
        H_R2: h_r2,
    }

    def run(actions):
        for name, v, c in actions:
            unit_now.append(v)
            stages[name](v, c)
            unit_now.pop()

    def poll(at):
        for side in range(2):
            actions = PLAN.get(at, ((), ()))[side]
            if actions:
                pl.when(s == side)(lambda actions=actions: run(actions))

    def poll_loop(first, count, step):
        for i in range(count):
            for side in range(2):
                actions = PLAN.get(first + i, ((), ()))[side]
                if actions:
                    pl.when((step == i) & (s == side))(lambda actions=actions: run(actions))

    def both_scopes(raw, gate_w, up_w, out_w):
        tiles.extend((gate_w, up_w, out_w))
        pl.run_scoped(
            functools.partial(forward_scope, raw),
            pltpu.VMEM(attn_in.shape, bf16))
        pl.run_scoped(
            functools.partial(ffn_scope, raw),
            pltpu.VMEM((rows, width), bf16), pltpu.VMEM((width, rows), bf16), pltpu.VMEM((rows, width), bf16),
            pltpu.VMEM((rows, 2 * piece), f32), pltpu.VMEM((rows, 2 * piece), f32), pltpu.VMEM((rows, 2 * piece), f32),
            pltpu.VMEM((rows, 2 * piece), bf16), pltpu.VMEM((rows, 2 * piece), bf16), pltpu.VMEM((rows, 2 * piece), bf16))

    pl.run_scoped(
        both_scopes,
        pltpu.VMEM((rows, NS, width), bf16), pltpu.VMEM((2, width, tile), bf16),
        pltpu.VMEM((2, width, tile), bf16), pltpu.VMEM((2, tile, width), bf16))

    gain_sums = {}

    def attention_scope(w_in, w_out, dfirst, dcontext, dkeys, dvalues, own_keys, own_values, dproject, turned):
        loads = [load(attn_out, w_out, load_sem.at[7]), load(attn_in, w_in, load_sem.at[8])]
        carry_first = sum(depth_one[j] * read_two[j] for j in range(NS))

        def norm_block(i, total):
            r = pl.ds(i * 64, 64)
            normal, scaling = normal_of(read[r])
            grad = dread[r]
            total = total + jnp.sum((grad * normal).reshape(8, 8, width), axis=0)
            scaled = grad * gains[1:2].astype(f32)
            centre = jnp.mean(scaled, axis=-1, keepdims=True)
            along = jnp.mean(scaled * normal, axis=-1, keepdims=True)
            value = scaling * (scaled - centre - normal * along)
            dread[r] = value
            dfirst[r] = (gfirst[r] + carry_first * value).astype(bf16)
            return total

        gain_two = lax.fori_loop(0, rows // 64, norm_block, jnp.zeros((8, width), f32))
        row = jnp.sum(gain_two, axis=0, keepdims=True)
        for k in range(width // 128):
            small_box[0, s, width // 128 + k : width // 128 + k + 1, :] = row[:, k * 128 : (k + 1) * 128]

        loads[0].wait()
        poll(13)

        def context_block(j, carry):
            cols = pl.ds(pl.multiple_of(j * 256, 256), 256)
            dcontext[:, cols] = nt(dfirst[...], w_out[cols]).astype(bf16)
            return carry

        lax.fori_loop(0, width // 256, context_block, 0)
        turned[...] = context[...].T
        shards_in = w_in.shape[1] // width * (width // piece) // 3

        def out_block(j, carry):
            cols = pl.ds(pl.multiple_of(j * 256, 256), 256)
            part = nn(turned[...], dfirst[:, cols]).astype(bf16)
            for b in range(width // piece):
                at, c = shards_in + b // 3, b % 3
                zi, yi, xi = at // (ny * nx), (at // nx) % ny, at % nx
                for q in range(2):
                    grads[0, zi, yi, xi, c, pl.ds(pl.multiple_of((2 * j + q) * piece, piece), piece)] = part[
                        b * piece : (b + 1) * piece, q * 128 : (q + 1) * 128]
            return carry

        lax.fori_loop(0, width // 256, out_block, 0)
        poll(14)

        def blocks_back(side, hp):
            blocks = q_blocks(side)
            cols = pl.ds(pl.multiple_of(hp * 128, 128), 128)
            spans = [
                (pl.ds(row * EIGHTH, EIGHTH), pl.ds(key * EIGHTH, count * EIGHTH)) for row, key, count, _ in blocks
            ]
            qs = [two_heads(queries[r, cols]) * HD ** (-0.5) for r, kr in spans]
            dstack = [two_heads(dcontext[r, cols]) for r, kr in spans]
            scores = [
                masked_scores(keys[kr, cols], qs[bi], block_mask(docs, side, blocks[bi]))
                for bi, (r, kr) in enumerate(spans)
            ]
            dprobs = [nt(values[kr, cols], dstack[bi]) for bi, (r, kr) in enumerate(spans)]
            probs = [jnp.exp(score - lse[pl.ds(bi * 8 + hp, 1), :]) for bi, score in enumerate(scores)]
            inner = [jnp.sum(p * dp, axis=0, keepdims=True) for p, dp in zip(probs, dprobs)]
            dscores = [(p * (dp - i)).astype(bf16) for p, dp, i in zip(probs, dprobs, inner)]
            for bi, (r, kr) in enumerate(spans):
                dkeys[kr] += nn(dscores[bi], qs[bi])
                dvalues[kr] += nn(probs[bi].astype(bf16), dstack[bi])
            dqs = [tn(keys[kr, cols], dscores[bi]) for bi, (r, kr) in enumerate(spans)]
            for bi, (r, kr) in enumerate(spans):
                dq = one_pair(dqs[bi]) * HD ** (-0.5)
                dproject[r, cols] = (dq * cosine[r] - swapped(dq) * sine[r]).astype(bf16)

        shared = pl.ds(EIGHTH, 3 * EIGHTH)

        key_rows, value_rows = pl.ds(0, 3 * EIGHTH), pl.ds(3 * EIGHTH, 3 * EIGHTH)

        def turned_back(dk):
            return (dk * cosine[...] - swapped(dk) * sine[...]).astype(bf16)

        def pair_back(hp, carry):
            cols = pl.ds(pl.multiple_of(hp * 128, 128), 128)
            key_cols = pl.ds(pl.multiple_of(width + hp * 128, 128), 128)
            value_cols = pl.ds(pl.multiple_of(2 * width + hp * 128, 128), 128)
            dkeys[...] = jnp.zeros_like(dkeys)
            dvalues[...] = jnp.zeros_like(dvalues)

            @pl.when(zero)
            def _():
                blocks_back(0, hp)
                own_keys[:, cols] = dkeys[pl.ds(0, rows)]
                own_values[:, cols] = dvalues[pl.ds(0, rows)]

            @pl.when(one)
            def _():
                blocks_back(1, hp)
                kv_box[key_rows, cols] = dkeys[shared].astype(bf16)
                kv_box[value_rows, cols] = dvalues[shared].astype(bf16)
                kv_copy(hp).start()
                dproject[:, key_cols] = turned_back(dkeys[pl.ds(rows, rows)])
                dproject[:, value_cols] = dvalues[pl.ds(rows, rows)].astype(bf16)

            poll_loop(15, width // 128, hp)
            return carry

        lax.fori_loop(0, width // 128, pair_back, 0)

        @pl.when(zero)
        def _():
            def finish(hp, carry):
                cols = pl.ds(pl.multiple_of(hp * 128, 128), 128)
                key_cols = pl.ds(pl.multiple_of(width + hp * 128, 128), 128)
                value_cols = pl.ds(pl.multiple_of(2 * width + hp * 128, 128), 128)
                kv_copy(hp).wait_recv()
                own_keys[shared, cols] += kv_box[key_rows, cols].astype(f32)
                own_values[shared, cols] += kv_box[value_rows, cols].astype(f32)
                dproject[:, key_cols] = turned_back(own_keys[:, cols])
                dproject[:, value_cols] = own_values[:, cols].astype(bf16)
                return carry

            lax.fori_loop(0, width // 128, finish, 0)

        @pl.when(one)
        def _():
            def finish(hp, carry):
                kv_copy(hp).wait_send()
                return carry

            lax.fori_loop(0, width // 128, finish, 0)

        poll(21)
        loads[1].wait()
        turned[...] = normed[...].T

        for j in range(w_in.shape[1] // width):
            def in_block(cb, carry, j=j):
                cols = pl.ds(pl.multiple_of(j * width + cb * 256, 256), 256)
                part = nn(turned[...], dproject[:, cols]).astype(bf16)
                for b in range(width // piece):
                    zi, yi, xi = b // (ny * nx), (b // nx) % ny, b % nx
                    for q in range(2):
                        grads[0, zi, yi, xi, j, pl.ds(pl.multiple_of((2 * cb + q) * piece, piece), piece)] = part[
                            b * piece : (b + 1) * piece, q * 128 : (q + 1) * 128]
                return carry

            lax.fori_loop(0, width // 256, in_block, 0)
            poll(22 + j)

        def dnormed_block(j, carry):
            cols = pl.ds(pl.multiple_of(j * 256, 256), 256)
            gfirst[:, cols] = nt(dproject[...], w_in[cols])
            return carry

        lax.fori_loop(0, width // 256, dnormed_block, 0)
        poll(25)

    pl.run_scoped(
        attention_scope,
        pltpu.VMEM(attn_in.shape, bf16), pltpu.VMEM(attn_out.shape, bf16),
        pltpu.VMEM((rows, width), bf16), pltpu.VMEM((rows, width), bf16),
        pltpu.VMEM((2 * rows, 128), f32), pltpu.VMEM((2 * rows, 128), f32),
        pltpu.VMEM((rows, width), f32), pltpu.VMEM((rows, width), f32),
        pltpu.VMEM((rows, 3 * width), bf16), pltpu.VMEM((width, rows), bf16),
    )

    def tail_scope(raw_h, raw_g, new_box, back_box, state, flat, sums_box):
        axes = [(s, [core], 2), (x, x_peers, nx), (y, y_peers, ny), (z, z_peers, nz)]

        def small_copies(k):
            first = sum(len(axis[1]) for axis in axes[:k])
            place, others, count = axes[k]
            return [
                pltpu.make_async_remote_copy(
                    small_box.at[k, place], small_box.at[k, place], small_send.at[first + i], small_recv.at[first + i],
                    device_id=peer, device_id_type=MESH)
                for i, peer in enumerate(others)
            ]

        def small_stage(v, k):
            if k > 0:
                for copy in small_copies(k - 1):
                    copy.wait()
                total = small_box[k - 1, 0]
                for j in range(1, axes[k - 1][2]):
                    total = total + small_box[k - 1, j]
            if k == len(axes):
                grad = total * (1.0 / token_count)
                new = adam_step((small_rows[0], small_rows[1], small_rows[2]), grad)
                for k2, value in enumerate(new + (grad,)):
                    small_out[k2] = value
                return
            if k > 0:
                small_box[k, axes[k][0]] = total
            for copy in small_copies(k):
                copy.start()

        stages[SMALL] = small_stage
        stages[OWNER] = lambda v, c: owner_update((v,), state, flat, sums_box)
        loads = [load(streams, raw_h, load_sem.at[9]), load(cotangent, raw_g, load_sem.at[10]),
                 load(state_in, state, load_sem.at[0])]
        for copy in loads[:2]:
            copy.wait()
        poll(26)
        mixed_read = [sum(mix[i][j] * read_two[j] for j in range(NS)) for i in range(NS)]
        pairs = 33
        block = 32

        def out_copies(i, slot):
            r = pl.ds(i * block, block)
            return [pltpu.make_async_copy(new_box.at[slot], new_out.at[r], out_sem.at[0, slot]),
                    pltpu.make_async_copy(back_box.at[slot], stream_grad_out.at[r], out_sem.at[1, slot])]

        def body(i, carry):
            gain_one, sums = carry
            r = pl.ds(i * block, block)
            slot = i % 2

            @pl.when(i >= 2)
            def _():
                for copy in out_copies(i, slot):
                    copy.wait()

            hs, gs = unpacked(raw_h[r]), unpacked(raw_g[r])
            first_r, second_r, dread_r = first[r], second[r], dread[r]
            branch = sum(hs[k] * read_one[k] for k in range(NS))
            normal, scaling = normal_of(branch)
            grad = gfirst[r]
            gain_one = gain_one + jnp.sum((grad * normal).reshape(block // 8, 8, width), axis=0)
            scaled = grad * gains[0:1].astype(f32)
            centre = jnp.mean(scaled, axis=-1, keepdims=True)
            along = jnp.mean(scaled * normal, axis=-1, keepdims=True)
            dbranch = scaling * (scaled - centre - normal * along)
            back = [
                (sum(gs[j] * mix[k][j] for j in range(NS)) + dread_r * mixed_read[k] + dbranch * read_one[k]).astype(bf16)
                for k in range(NS)
            ]
            back_box[slot] = packed_streams(back)
            new = [
                (sum(hs[k] * mix[k][j] for k in range(NS)) + first_r * depth_one[j] + second_r * depth_two[j]).astype(bf16)
                for j in range(NS)
            ]
            new_box[slot] = packed_streams(new)
            for copy in out_copies(i, slot):
                copy.start()
            products = [(hs[a], gs[b]) for a in range(NS) for b in range(NS)]
            products += [(hs[a], dread_r) for a in range(NS)]
            products += [(hs[a], dbranch) for a in range(NS)]
            products += [(first_r, gs[b]) for b in range(NS)] + [(first_r, dread_r)]
            products += [(second_r, gs[b]) for b in range(NS)]
            new_sums = []
            for total, (a, b) in zip(sums, products):
                p = jnp.sum((a * b).reshape(block // 8, 8, width), axis=0)
                new_sums.append(total + sum(p[:, q * 128 : (q + 1) * 128] for q in range(width // 128)))
            poll_loop(27, rows // block - 1, i)
            return gain_one, tuple(new_sums)

        zero_tile = jnp.zeros((8, 128), f32)
        gain_one, sums = lax.fori_loop(
            0, rows // block, body, (jnp.zeros((8, width), f32), tuple(zero_tile for _ in range(pairs))))
        for i in (rows // block - 2, rows // block - 1):
            for copy in out_copies(i, i % 2):
                copy.wait()
        row = jnp.sum(gain_one, axis=0, keepdims=True)
        for k in range(width // 128):
            small_box[0, s, k : k + 1, :] = row[:, k * 128 : (k + 1) * 128]
        sums = [jnp.sum(jnp.sum(t, axis=0, keepdims=True), axis=1, keepdims=True) for t in sums]
        hg = [[sums[a * NS + b] for b in range(NS)] for a in range(NS)]
        h_read = sums[16:20]
        h_branch = sums[20:24]
        first_g, first_read, second_g = sums[24:28], sums[28], sums[29:33]
        lane = lax.broadcasted_iota(jnp.int32, (1, 128), 1)
        line = jnp.zeros((1, 128), f32)
        for i in range(NS):
            entries = [hg[i][j] + read_two[j] * h_read[i] for j in range(NS)]
            entries.append(h_branch[i])
            entries.append(first_g[i] + read_two[i] * first_read)
            entries.append(sum(mix[k][i] * h_read[k] for k in range(NS)) + depth_one[i] * first_read)
            entries.append(second_g[i])
            for j, value in enumerate(entries):
                line = jnp.where(lane == i * 2 * NS + j, value, line)
        last = 2 * width // 128
        small_box[0, s, last : last + 1, :] = line
        small_box[0, s, last + 1 :, :] = jnp.zeros((small_box.shape[2] - last - 1, 128), f32)

        poll(42)
        wait_sends()
        pltpu.make_async_copy(read.at[pl.ds(0, shard)], grad_out, store_sem.at[0]).wait()

    pl.run_scoped(
        tail_scope,
        pltpu.VMEM((rows, NS, width), bf16), pltpu.VMEM((rows, NS, width), bf16),
        pltpu.VMEM((2, 32, NS, width), bf16), pltpu.VMEM((2, 32, NS, width), bf16),
        pltpu.VMEM((3, shard, width), f32), pltpu.VMEM((6, shard, 128), f32),
        pltpu.VMEM((3, unit, 128), f32),
    )
    assert ids["send"] <= send_sem.shape[0] and ids["recv"] <= recv_sem.shape[0], ids


def finish_kernel(
    new_in, back_in, copy_in, grad_in, state_in,
    new_out, back_out, copy_out, weight_out, first_out, second_out, grad_out,
    new_box, back_box, copy_box, grad, state, weight, first, second, in_sem, out_sem, copy_sem,
):
    parts = 4
    rows = grad.shape[0] // parts
    tokens = new_box.shape[0] // parts

    def of_rows(k):
        return pl.ds(k * rows, rows)

    def of_tokens(k):
        return pl.ds(k * tokens, tokens)

    def loads(k):
        return [
            pltpu.make_async_copy(grad_in.at[of_rows(k)], grad.at[of_rows(k)], in_sem.at[0, k]),
            pltpu.make_async_copy(state_in.at[:, of_rows(k)], state.at[:, of_rows(k)], in_sem.at[1, k]),
            pltpu.make_async_copy(new_in.at[of_tokens(k)], new_box.at[of_tokens(k)], in_sem.at[2, k]),
            pltpu.make_async_copy(back_in.at[of_tokens(k)], back_box.at[of_tokens(k)], in_sem.at[3, k]),
        ]

    def stores(k):
        pairs = [(box.at[of_rows(k)], out.at[of_rows(k)]) for box, out in (
            (grad, grad_out), (weight, weight_out), (first, first_out), (second, second_out))]
        pairs += [(new_box.at[of_tokens(k)], new_out.at[of_tokens(k)]), (back_box.at[of_tokens(k)], back_out.at[of_tokens(k)])]
        return [pltpu.make_async_copy(a, b, out_sem.at[i, k]) for i, (a, b) in enumerate(pairs)]

    pieces = copy_sem.shape[1]
    copy_rows = copy_box.shape[0] // pieces

    def move(k, out):
        r = pl.ds(k * copy_rows, copy_rows)
        if out:
            return pltpu.make_async_copy(copy_box.at[r], copy_out.at[r], copy_sem.at[1, k])
        return pltpu.make_async_copy(copy_in.at[r], copy_box.at[r], copy_sem.at[0, k])

    for k in range(parts):
        for copy in loads(k):
            copy.start()
    for k in range(pieces):
        move(k, False).start()
    for k in range(parts):
        for copy in loads(k):
            copy.wait()

        def body(i, carry, k=k):
            r = pl.ds(k * rows + i * 16, 16)
            weight[r], first[r], second[r] = adam_step((state[0, r], state[1, r], state[2, r]), grad[r])
            return carry

        lax.fori_loop(0, rows // 16, body, 0)
        for copy in stores(k):
            copy.start()
    for k in range(pieces):
        move(k, False).wait()
        move(k, True).start()
    for k in range(parts):
        for copy in stores(k):
            copy.wait()
    for k in range(pieces):
        move(k, True).wait()


def finish(new, back, copy, grad, big_state):
    shape = jax.ShapeDtypeStruct
    hbm = pl.BlockSpec(memory_space=pl.ANY)
    like = shape(grad.shape, grad.dtype)
    box = pltpu.VMEM(grad.shape, grad.dtype)
    return pl.pallas_call(
        finish_kernel,
        out_shape=[shape(new.shape, new.dtype), shape(back.shape, back.dtype), shape(copy.shape, copy.dtype),
                   like, like, like, like],
        in_specs=[hbm] * 5,
        out_specs=[hbm] * 7,
        scratch_shapes=[
            pltpu.VMEM(new.shape, new.dtype), pltpu.VMEM(back.shape, back.dtype),
            pltpu.VMEM(copy.shape, copy.dtype), box, pltpu.VMEM(big_state.shape, big_state.dtype), box, box, box,
            pltpu.SemaphoreType.DMA((4, 4)), pltpu.SemaphoreType.DMA((6, 4)), pltpu.SemaphoreType.DMA((2, 12)),
        ],
        compiler_params=pltpu.CompilerParams(vmem_limit_bytes=60 * 2**20),
        name="finish",
    )(new, back, copy, grad, big_state)


def layer_part(dims, token_count, docs, small_state, gains, streams, cotangent, weights, big_state):
    attn_in, attn_out, ffn_in, ffn_out = weights
    nz, ny, nx = dims
    rows, width = streams.shape[0], attn_out.shape[0]
    shard = big_state.shape[1]
    unit, half, hidden = 2 * shard, shard, ffn_out.shape[0]
    bf16, f32 = jnp.bfloat16, jnp.float32
    shape = jax.ShapeDtypeStruct
    cos_table, sin_table = rope_constants(6 * EIGHTH, HD)
    small_count = small_state.shape[1]
    small_rows = jnp.pad(small_state, ((0, 0), (0, -small_count % 1024))).reshape(3, -1, 128)
    small_shape = small_rows.shape[1:]
    smem = pl.BlockSpec(memory_space=pltpu.SMEM)
    vmem = pl.BlockSpec(memory_space=pltpu.VMEM)
    hbm = pl.BlockSpec(memory_space=pl.ANY)
    state_shape = shape((shard, width), f32)
    stream_shape = shape((rows, NS, width), bf16)
    outs = pl.pallas_call(
        functools.partial(layer_kernel, dims, token_count),
        out_shape=[
            stream_shape, stream_shape, shape((2, nz, ny, nx, shard, width), bf16),
            state_shape, shape((4,) + small_shape, f32),
            shape((nz, ny, nx, 3, unit, 128), bf16),
        ],
        in_specs=[smem, smem, vmem, vmem] + [hbm] * 9,
        out_specs=[hbm] * 4 + [vmem, hbm],
        scratch_shapes=[
            pltpu.VMEM((2, nz, ny, nx, 3, unit, 128), bf16),
            pltpu.VMEM((max(nx - 1, 1), nz, ny, 3, half, 128), bf16),
            pltpu.VMEM((max(ny - 1, 1), nz, nx, 3, half, 128), bf16),
            pltpu.VMEM((max(ny - 1, 1), nz, 3, half, 128), bf16),
            pltpu.VMEM((max(nx - 1, 1), nz, 3, half, 128), bf16),
            pltpu.VMEM((2, 3, 3, unit, 128), bf16),
            pltpu.VMEM((nz // 2, ny, nx, unit, 128), bf16),
            pltpu.VMEM((6 * EIGHTH, width), bf16),
            pltpu.VMEM((rows, width), f32), pltpu.VMEM((rows, width), f32), pltpu.VMEM((rows, width), f32),
            pltpu.VMEM((rows, width), f32), pltpu.VMEM((rows, width), f32),
            pltpu.VMEM((rows, width), bf16), pltpu.VMEM((rows, width), bf16),
            pltpu.VMEM((2 * rows, width), bf16), pltpu.VMEM((2 * rows, width), bf16),
            pltpu.VMEM((rows, width), bf16), pltpu.VMEM((32, 2 * EIGHTH), f32),
            pltpu.VMEM((rows, 128), f32), pltpu.VMEM((rows, 128), f32), pltpu.VMEM((2, EIGHTH, EIGHTH), f32),
            pltpu.VMEM((shard, width), bf16),
            pltpu.VMEM((4, max(2, nx, ny, nz)) + small_shape, f32),
            pltpu.SemaphoreType.DMA((8,)), pltpu.SemaphoreType.DMA((8,)),
            pltpu.SemaphoreType.DMA((240,)), pltpu.SemaphoreType.DMA((180,)),
            pltpu.SemaphoreType.DMA((16,)), pltpu.SemaphoreType.DMA((2, 3, 8)),
            pltpu.SemaphoreType.DMA((2,)), pltpu.SemaphoreType.DMA((5,)), pltpu.SemaphoreType.DMA((2, 2)),
            pltpu.SemaphoreType.DMA((8,)), pltpu.SemaphoreType.DMA((8,)),
        ],
        compiler_params=pltpu.CompilerParams(
            collective_id=1, has_side_effects=True, vmem_limit_bytes=255 * 2**18
        ),
        name="layer_step",
    )(docs, small_state, gains, small_rows, streams, cotangent, attn_in, attn_out, ffn_in, ffn_out, big_state,
      jnp.asarray(cos_table), jnp.asarray(sin_table))
    small_out = outs[4].reshape(4, -1)[:, :small_count]
    copy = outs[2].reshape(-1, width)
    new, back, copy, weight_new, first_new, second_new, grad = finish(outs[0], outs[1], copy, outs[3], big_state)
    return new, back, copy, weight_new, first_new, second_new, grad, small_out


def torus(mesh):
    wide = mesh.shape["wide"]
    where = [getattr(d, "coords", None) for d in mesh.devices.flat]
    if all(c is not None for c in where):
        x, y, z = (len({c[i] for c in where}) for i in range(3))
        if x * y * z == wide:
            return z, y, x
    known = {16: (4, 2, 2), 64: (4, 4, 4)}
    return known.get(wide, (wide, 1, 1))


def sync_kernel(
    dims, rows, half, lr_consts,
    grads, small_in, state_in,
    copy_out, weight_out, first_out, second_out, grad_out, small_out,
    acc, from_core, from_a0, from_a1, from_b0, from_b1, from_c,
    state, new_w, new_m, new_v, new_g, low, small_box,
    load_sem, store_sem, send_sem, recv_sem, small_send, small_recv,
):
    nz, ny, nx = dims
    chunk = 2 * half
    chunks = rows // chunk
    s = lax.axis_index("seq")
    w = lax.axis_index("wide")
    z, y, x = w // (ny * nx), (w // nx) % ny, w % nx

    def chip(cz, cy, cx):
        return (s, (cz * ny + cy) * nx + cx)

    core = (1 - s, w)
    z_peers = [chip((z + d) % nz, y, x) for d in range(1, nz)]
    y_peers = [chip(z, (y + d) % ny, x) for d in range(1, ny)]
    x_peers = [chip(z, y, (x + d) % nx) for d in range(1, nx)]
    peers = [core] + z_peers + y_peers + x_peers

    barrier = pltpu.get_barrier_semaphore()
    for peer in peers:
        pl.semaphore_signal(barrier, inc=1, device_id=peer, device_id_type=MESH)

    loads = [
        pltpu.make_async_copy(
            grads.at[s, :, :, :, pl.ds(c * chunk, chunk)],
            acc.at[:, :, :, pl.ds(c * chunk, chunk)],
            load_sem.at[c],
        )
        for c in range(chunks)
    ]
    for copy in loads:
        copy.start()
    state_load = pltpu.make_async_copy(state_in, state, load_sem.at[chunks])
    state_load.start()
    pl.semaphore_wait(barrier, len(peers))

    sends = []
    counter = [0]

    def remote(src, dst, peer):
        i = counter[0]
        counter[0] += 1
        copy = pltpu.make_async_remote_copy(
            src, dst, send_sem.at[i], recv_sem.at[i], device_id=peer, device_id_type=MESH
        )
        copy.start()
        sends.append(copy)
        return copy

    def lo(c):
        return pl.ds(c * chunk, half)

    def hi(c):
        return pl.ds(c * chunk + half, half)

    def both(c):
        return pl.ds(c * chunk, chunk)

    def packed(c):
        return pl.ds(c * half, half)

    f32 = jnp.float32

    def add_into(count, where, terms):
        def body(i, carry):
            ref, index = where(i)
            total = ref[index].astype(f32)
            for term_ref, term_index in terms(i):
                total = total + term_ref[term_index].astype(f32)
            ref[index] = total.astype(ref.dtype)
            return carry

        lax.fori_loop(0, count, body, 0)

    def small_step(k, mine, others, count):
        copies = []
        for j, peer in enumerate(others):
            i = small_index[0]
            small_index[0] += 1
            copy = pltpu.make_async_remote_copy(
                small_box.at[k, mine], small_box.at[k, mine], small_send.at[i], small_recv.at[i],
                device_id=peer, device_id_type=MESH,
            )
            copy.start()
            copies.append(copy)
        return copies

    def small_sum(k, copies, count):
        for copy in copies:
            copy.wait()
        total = small_box[k, 0]
        for j in range(1, count):
            total = total + small_box[k, j]
        return total

    small_index = [0]
    axes = [(s, [core], 2), (x, x_peers, nx), (y, y_peers, ny), (z, z_peers, nz)]
    small_box[0, s] = small_in[...]
    small_copies = [small_step(0, s, [core], 2)]

    def small_stage(k):
        total = small_sum(k, small_copies[k], axes[k][2])
        if k + 1 < len(axes):
            place, others, count = axes[k + 1]
            small_box[k + 1, place] = total
            small_copies.append(small_step(k + 1, place, others, count))
        else:
            small_out[...] = total

    state_done = [False]
    flying = {}

    def stage(k, c):
        if k == 0:
            loads[c].wait()
            for copy in flying[0, c]:
                copy.wait_recv()

            def where(i):
                return acc, (i // (ny * nx), (i // nx) % ny, i % nx, both(c))

            def terms(i):
                return [(from_core, (i // (ny * nx), (i // nx) % ny, i % nx, both(c)))]

            add_into(nz * ny * nx, where, terms)
            out = []
            for d in range(1, nx):
                out.append(remote(
                    acc.at[:, :, (x + d) % nx, lo(c)], from_a0.at[d - 1, :, :, packed(c)], x_peers[d - 1]))
            for d in range(1, ny):
                out.append(remote(
                    acc.at[:, (y + d) % ny, :, hi(c)], from_a1.at[d - 1, :, :, packed(c)], y_peers[d - 1]))
            flying[1, c] = out
        elif k == 1:
            for copy in flying[1, c]:
                copy.wait_recv()
            add_into(
                nz * ny,
                lambda i: (acc, (i // ny, i % ny, x, lo(c))),
                lambda i: [(from_a0, (d, i // ny, i % ny, packed(c))) for d in range(nx - 1)],
            )
            add_into(
                nz * nx,
                lambda i: (acc, (i // nx, y, i % nx, hi(c))),
                lambda i: [(from_a1, (d, i // nx, i % nx, packed(c))) for d in range(ny - 1)],
            )
            out = []
            for d in range(1, ny):
                out.append(remote(
                    acc.at[:, (y + d) % ny, x, lo(c)], from_b0.at[d - 1, :, packed(c)], y_peers[d - 1]))
            for d in range(1, nx):
                out.append(remote(
                    acc.at[:, y, (x + d) % nx, hi(c)], from_b1.at[d - 1, :, packed(c)], x_peers[d - 1]))
            flying[2, c] = out
        elif k == 2:
            for copy in flying[2, c]:
                copy.wait_recv()
            add_into(
                nz,
                lambda i: (acc, (i, y, x, lo(c))),
                lambda i: [(from_b0, (d, i, packed(c))) for d in range(ny - 1)],
            )
            add_into(
                nz,
                lambda i: (acc, (i, y, x, hi(c))),
                lambda i: [(from_b1, (d, i, packed(c))) for d in range(nx - 1)],
            )
            out = []
            for d in range(1, nz):
                out.append(remote(
                    acc.at[(z + d) % nz, y, x, both(c)], from_c.at[d - 1, both(c)], z_peers[d - 1]))
            flying[3, c] = out
        elif k == 3:
            for copy in flying[3, c]:
                copy.wait_recv()
            if not state_done[0]:
                state_load.wait()
                state_done[0] = True
            step = 16

            def body(i, carry):
                r = pl.ds(c * chunk + i * step, step)
                total = acc[z, y, x, r].astype(f32)
                for d in range(nz - 1):
                    total = total + from_c[d, r].astype(f32)
                grad = total * lr_consts
                w_new, m_new, v_new = adam_step((state[0, r], state[1, r], state[2, r]), grad)
                new_g[r] = grad
                new_w[r] = w_new
                new_m[r] = m_new
                new_v[r] = v_new
                low[r] = w_new.astype(low.dtype)
                return carry

            lax.fori_loop(0, chunk // step, body, 0)
            out = []
            for peer in z_peers:
                out.append(remote(low.at[both(c)], copy_out.at[s, z, y, x, both(c)], peer))
            own = pltpu.make_async_copy(low.at[both(c)], copy_out.at[s, z, y, x, both(c)], store_sem.at[0, c])
            own.start()
            for j, (a, b) in enumerate(((new_w, weight_out), (new_m, first_out), (new_v, second_out), (new_g, grad_out))):
                st = pltpu.make_async_copy(a.at[both(c)], b.at[both(c)], store_sem.at[j + 1, c])
                st.start()
                stores.append(st)
            flying[4, c] = (out, own)
        elif k == 4:
            out, own = flying[4, c]
            own.wait()
            for copy in out:
                copy.wait_recv()
            nxt = []
            for peer in y_peers:
                nxt.append(remote(copy_out.at[s, :, y, x, lo(c)], copy_out.at[s, :, y, x, lo(c)], peer))
            for peer in x_peers:
                nxt.append(remote(copy_out.at[s, :, y, x, hi(c)], copy_out.at[s, :, y, x, hi(c)], peer))
            flying[5, c] = nxt
        elif k == 5:
            for copy in flying[5, c]:
                copy.wait_recv()
            nxt = []
            for peer in x_peers:
                nxt.append(remote(copy_out.at[s, :, :, x, lo(c)], copy_out.at[s, :, :, x, lo(c)], peer))
            for peer in y_peers:
                nxt.append(remote(copy_out.at[s, :, y, :, hi(c)], copy_out.at[s, :, y, :, hi(c)], peer))
            flying[6, c] = nxt
        elif k == 6:
            for copy in flying[6, c]:
                copy.wait_recv()
            flying[7, c] = [
                remote(copy_out.at[s, :, :, :, both(c)], copy_out.at[s, :, :, :, both(c)], core)]
        elif k == 7:
            for copy in flying[7, c]:
                copy.wait_recv()

    stores = []
    for c in range(chunks):
        flying[0, c] = [remote(
            grads.at[1 - s, :, :, :, both(c)], from_core.at[:, :, :, both(c)], core)]
    stages = 8
    for t in range(chunks + stages - 1):
        for k in reversed(range(stages)):
            c = t - k
            if 0 <= c < chunks:
                stage(k, c)
        if 1 <= t <= 4:
            small_stage(t - 1)
    for copy in sends:
        copy.wait_send()
    for copy in stores:
        copy.wait()


def sync_grads(dims, flat_low, small_local, big_state, token_count):
    nz, ny, nx = dims
    wide = nz * ny * nx
    model_width = flat_low.shape[1]
    rows = big_state.shape[1]
    half = next(h for h in (48, 32, 16) if rows % (2 * h) == 0)
    chunks = rows // (2 * half)
    bf16, f32 = jnp.bfloat16, jnp.float32
    copies = chunks * (2 + 4 * (nx - 1) + 4 * (ny - 1) + 2 * (nz - 1))
    small_copies = 1 + (nx - 1) + (ny - 1) + (nz - 1)
    hbm = pl.BlockSpec(memory_space=pl.ANY)
    vmem = pl.BlockSpec(memory_space=pltpu.VMEM)
    state_shape = jax.ShapeDtypeStruct((rows, model_width), f32)
    small_shape = small_local.shape
    outs = pl.pallas_call(
        functools.partial(sync_kernel, dims, rows, half, 1.0 / token_count),
        out_shape=[
            jax.ShapeDtypeStruct((2, nz, ny, nx, rows, model_width), bf16),
            state_shape, state_shape, state_shape, state_shape,
            jax.ShapeDtypeStruct(small_shape, f32),
        ],
        in_specs=[hbm, vmem, hbm],
        out_specs=[hbm] * 5 + [vmem],
        scratch_shapes=[
            pltpu.VMEM((nz, ny, nx, rows, model_width), bf16),
            pltpu.VMEM((nz, ny, nx, rows, model_width), bf16),
            pltpu.VMEM((max(nx - 1, 1), nz, ny, rows // 2, model_width), bf16),
            pltpu.VMEM((max(ny - 1, 1), nz, nx, rows // 2, model_width), bf16),
            pltpu.VMEM((max(ny - 1, 1), nz, rows // 2, model_width), bf16),
            pltpu.VMEM((max(nx - 1, 1), nz, rows // 2, model_width), bf16),
            pltpu.VMEM((max(nz - 1, 1), rows, model_width), bf16),
            pltpu.VMEM((3, rows, model_width), f32),
            pltpu.VMEM((rows, model_width), f32),
            pltpu.VMEM((rows, model_width), f32),
            pltpu.VMEM((rows, model_width), f32),
            pltpu.VMEM((rows, model_width), f32),
            pltpu.VMEM((rows, model_width), bf16),
            pltpu.VMEM((4, max(2, nx, ny, nz)) + small_shape, f32),
            pltpu.SemaphoreType.DMA((chunks + 1,)),
            pltpu.SemaphoreType.DMA((5, chunks)),
            pltpu.SemaphoreType.DMA((copies,)),
            pltpu.SemaphoreType.DMA((copies,)),
            pltpu.SemaphoreType.DMA((small_copies,)),
            pltpu.SemaphoreType.DMA((small_copies,)),
        ],
        compiler_params=pltpu.CompilerParams(
            collective_id=1, has_side_effects=True, vmem_limit_bytes=56 * 2**20
        ),
        name="sync_grads",
    )(
        flat_low.reshape(2, nz, ny, nx, rows, model_width), small_local, big_state
    )
    return (outs[0].reshape(2 * wide * rows, model_width),) + tuple(outs[1:])


def on_device(
    dims,
    streams,
    cotangent,
    doc_lengths,
    attn_in,
    attn_out,
    ffn_in,
    ffn_out,
    norm_gains,
    big_state,
    small_state,
):
    row_count = streams.shape[1]
    model_width = attn_out.shape[0]
    fits = (
        big_state.shape[1] == 384 and model_width == 768 and row_count == 512
        and ffn_out.shape[0] == 3072 and dims == (4, 2, 2)
    )
    if fits:
        token_count = 2 * row_count * lax.axis_size("wide")
        result, stream_grad, gathered, weight_new, first_new, second_new, owned_grads, small_out = layer_part(
            dims, token_count, doc_lengths, small_state, norm_gains.T, streams[0], cotangent[0],
            (attn_in, attn_out, ffn_in, ffn_out), big_state,
        )
        gains_copy = small_out[0, : 2 * model_width].reshape(2, model_width).T.astype(jnp.bfloat16)
        return (
            result[None], stream_grad[None], weight_new, first_new, second_new, owned_grads,
            small_out[0], small_out[1], small_out[2], small_out[3], gathered, gains_copy,
        )
    member = lax.axis_index("seq")
    token_total = row_count * lax.axis_size("seq")
    token_count = token_total * lax.axis_size("wide")
    segment, position = doc_layout(doc_lengths[0], token_total)
    own_start = member * row_count
    own_index = own_start + jnp.arange(row_count, dtype=jnp.int32)
    seg_query = lax.dynamic_slice_in_dim(segment, own_start, row_count)
    pos_query = lax.dynamic_slice_in_dim(position, own_start, row_count)
    padded_seg = jnp.concatenate([jnp.full((row_count,), -1, jnp.int32), segment])
    key_seg = lax.dynamic_slice_in_dim(padded_seg, own_start, 2 * row_count)
    key_index = own_start - row_count + jnp.arange(2 * row_count, dtype=jnp.int32)
    allowed = (key_seg[None, :] == seg_query[:, None]) & (key_index[None, :] <= own_index[:, None])
    cosine, sine_table = rope_tables(pos_query, HD)
    weights = (attn_in, attn_out, ffn_in, ffn_out)
    gain_values = norm_gains.astype(jnp.float32)
    mixing = small_state[0, 2 * model_width :].reshape(NS, NS + 4)
    stream_values = streams[0].astype(jnp.float32)
    result, saved = forward_layer(
        stream_values, weights, gain_values, mixing, allowed, cosine, sine_table
    )
    grad_out = cotangent[0].astype(jnp.float32)
    stream_grad, matrix_grads, gains_local, mixing_local = backward_layer(
        stream_values, grad_out, weights, gain_values, mixing, cosine, sine_table, saved
    )
    flat_low = jnp.concatenate(
        [grad.astype(jnp.bfloat16).reshape(-1, model_width) for grad in matrix_grads], axis=0
    )
    small_local = jnp.concatenate([gains_local.T.reshape(-1), mixing_local.reshape(-1)])
    small_count = small_local.shape[0]
    padded = jnp.pad(small_local, (0, -small_count % 1024)).reshape(-1, 128)
    gathered, weight_new, first_new, second_new, owned_grads, small_total = sync_grads(
        dims, flat_low, padded, big_state, token_count
    )
    small_grads = small_total.reshape(-1)[:small_count] / token_count
    small_weight, small_first, small_second = adam_step(small_state, small_grads)
    gains_copy = small_weight[: 2 * model_width].reshape(2, model_width).T.astype(jnp.bfloat16)
    return (
        result.astype(jnp.bfloat16)[None],
        stream_grad.astype(jnp.bfloat16)[None],
        weight_new,
        first_new,
        second_new,
        owned_grads,
        small_weight,
        small_first,
        small_second,
        small_grads,
        gathered,
        gains_copy,
    )


def solution(mesh):
    in_specs = (
        P("wide", "seq", None, None),
        P("wide", "seq", None, None),
        P("wide", None),
        P(),
        P(),
        P(),
        P(),
        P(),
        P(None, ("seq", "wide"), None),
        P(),
    )
    out_specs = (
        P("wide", "seq", None, None),
        P("wide", "seq", None, None),
        P(("seq", "wide"), None),
        P(("seq", "wide"), None),
        P(("seq", "wide"), None),
        P(("seq", "wide"), None),
        P(),
        P(),
        P(),
        P(),
        P(),
        P(),
    )
    return jax.shard_map(
        functools.partial(on_device, torus(mesh)), mesh=mesh, in_specs=in_specs, out_specs=out_specs, check_vma=False
    )
```

```python
import functools

import jax
import jax.numpy as jnp
import numpy as np
from jax import lax
from jax.experimental import pallas as pl
from jax.experimental.pallas import tpu as pltpu
from jax.sharding import PartitionSpec as P

HEADS = 12
HD = 64
NS = 4
STEP = 10


norm_epsilon = 1e-05
rope_base = 10000.0
beta_first = 0.9
beta_second = 0.95
adam_epsilon = 1e-08
weight_decay = 0.1
learn_rate = 0.01
MESH = pl.DeviceIdType.MESH
masked_score = -1e30


def shifted(value, axis, by):
    count = lax.axis_size(axis)
    pairs = [(i, i + by) for i in range(count) if 0 <= i + by < count]
    return lax.ppermute(value, axis, pairs)


def doc_layout(lengths, token_total):
    bounds = jnp.cumsum(lengths)
    starts = bounds - lengths
    places = jnp.arange(token_total, dtype=jnp.int32)
    segment = jnp.sum((places[:, None] >= bounds[None, :]).astype(jnp.int32), axis=1)
    picked = segment[:, None] == jnp.arange(lengths.shape[0], dtype=jnp.int32)[None, :]
    offset = jnp.sum(jnp.where(picked, starts[None, :], 0), axis=1)
    return (segment, places - offset)


def rope_tables(position, head_size):
    exponent = jnp.arange(head_size // 2, dtype=jnp.float32) * (2.0 / head_size)
    frequency = jnp.power(jnp.float32(rope_base), -exponent)
    angles = position.astype(jnp.float32)[:, None] * frequency[None, :]
    return (jnp.cos(angles)[:, None, :], jnp.sin(angles)[:, None, :])


def rotate(values, cosine, sine_table):
    half_size = values.shape[-1] // 2
    leading = values[..., :half_size]
    trailing = values[..., half_size:]
    return jnp.concatenate(
        [leading * cosine - trailing * sine_table, trailing * cosine + leading * sine_table],
        axis=-1,
    )


def rotate_back(grads, cosine, sine_table):
    half_size = grads.shape[-1] // 2
    leading = grads[..., :half_size]
    trailing = grads[..., half_size:]
    return jnp.concatenate(
        [leading * cosine + trailing * sine_table, trailing * cosine - leading * sine_table],
        axis=-1,
    )


def norm_parts(values):
    centre = jnp.mean(values, axis=-1, keepdims=True)
    centred = values - centre
    scaling = lax.rsqrt(jnp.mean(centred * centred, axis=-1, keepdims=True) + norm_epsilon)
    return (centred * scaling, scaling)


def norm_back(grads, normal, scaling, gain):
    gain_grad = jnp.sum(grads * normal, axis=0)
    scaled = grads * gain
    centre = jnp.mean(scaled, axis=-1, keepdims=True)
    along_normal = jnp.mean(scaled * normal, axis=-1, keepdims=True)
    return (gain_grad, scaling * (scaled - centre - normal * along_normal))


def right_product(left, right):
    return lax.dot_general(
        left, right, (((1,), (1,)), ((), ())), preferred_element_type=jnp.float32
    )


def left_product(left, right):
    return lax.dot_general(
        left, right, (((0,), (0,)), ((), ())), preferred_element_type=jnp.float32
    )


def forward_layer(stream_values, weights, gain_values, mixing, allowed, cosine, sine_table):
    attn_in, attn_out, ffn_in, ffn_out = weights
    row_count = stream_values.shape[0]
    model_width = attn_out.shape[0]
    stream_count = mixing.shape[0]
    hidden_units = ffn_out.shape[0]
    branch_in = jnp.sum(stream_values * mixing[None, :, stream_count, None], axis=1)
    mixed_streams = jnp.sum(
        stream_values[:, :, None, :] * mixing[None, :, :stream_count, None], axis=1
    )
    normal_one, scale_one = norm_parts(branch_in)
    normed = (normal_one * gain_values[:, 0]).astype(jnp.bfloat16)
    project = jnp.dot(normed, attn_in, preferred_element_type=jnp.float32)
    queries = rotate(
        project[:, :model_width].reshape(row_count, HEADS, HD), cosine, sine_table
    ).astype(jnp.bfloat16)
    keys_rot = rotate(
        project[:, model_width : 2 * model_width].reshape(row_count, HEADS, HD), cosine, sine_table
    ).astype(jnp.bfloat16)
    values_in = project[:, 2 * model_width :].astype(jnp.bfloat16)
    outgoing = jnp.concatenate([keys_rot.reshape(row_count, model_width), values_in], axis=1)
    earlier = shifted(outgoing, "seq", 1)
    key_rows = jnp.concatenate([earlier, outgoing], axis=0)
    keys_all = key_rows[:, :model_width].reshape(2 * row_count, HEADS, HD)
    values_all = key_rows[:, model_width:].reshape(2 * row_count, HEADS, HD)
    scores = jnp.einsum(
        "qhd,khd->hqk", queries, keys_all, preferred_element_type=jnp.float32
    ) * HD ** (-0.5)
    scores = jnp.where(allowed[None], scores, masked_score)
    row_top = jnp.max(scores, axis=-1, keepdims=True)
    lifted = jnp.exp(scores - row_top)
    attend = lifted / jnp.sum(lifted, axis=-1, keepdims=True)
    attend_low = attend.astype(jnp.bfloat16)
    context = jnp.einsum("hqk,khd->qhd", attend_low, values_all, preferred_element_type=jnp.float32)
    context = context.reshape(row_count, model_width).astype(jnp.bfloat16)
    first_out = jnp.dot(context, attn_out, preferred_element_type=jnp.float32)
    streams_mid = mixed_streams + mixing[None, :, stream_count + 1, None] * first_out[:, None, :]
    ffn_read = jnp.sum(streams_mid * mixing[None, :, stream_count + 2, None], axis=1)
    normal_two, scale_two = norm_parts(ffn_read)
    normed_two = (normal_two * gain_values[:, 1]).astype(jnp.bfloat16)
    gate_up = jnp.dot(normed_two, ffn_in, preferred_element_type=jnp.float32)
    gate_part = gate_up[:, :hidden_units]
    up_part = gate_up[:, hidden_units:]
    hidden = (jax.nn.silu(gate_part) * up_part).astype(jnp.bfloat16)
    second_out = jnp.dot(hidden, ffn_out, preferred_element_type=jnp.float32)
    result = streams_mid + mixing[None, :, stream_count + 3, None] * second_out[:, None, :]
    saved = (
        normal_one,
        scale_one,
        normed,
        queries,
        keys_all,
        values_all,
        attend,
        attend_low,
        context,
        first_out,
        streams_mid,
        normal_two,
        scale_two,
        normed_two,
        gate_part,
        up_part,
        hidden,
        second_out,
    )
    return (result, saved)


def backward_layer(
    stream_values, grad_out, weights, gain_values, mixing, cosine, sine_table, saved
):
    attn_in, attn_out, ffn_in, ffn_out = weights
    (
        normal_one,
        scale_one,
        normed,
        queries,
        keys_all,
        values_all,
        attend,
        attend_low,
        context,
        first_out,
        streams_mid,
        normal_two,
        scale_two,
        normed_two,
        gate_part,
        up_part,
        hidden,
        second_out,
    ) = saved
    row_count = stream_values.shape[0]
    model_width = attn_out.shape[0]
    stream_count = mixing.shape[0]
    second_low = jnp.sum(grad_out * mixing[None, :, stream_count + 3, None], axis=1).astype(
        jnp.bfloat16
    )
    grad_depth_two = jnp.sum(grad_out * second_out[:, None, :], axis=(0, 2))
    ffn_out_grad = left_product(hidden, second_low)
    hidden_grad = right_product(second_low, ffn_out)
    sigmoid_gate = jax.nn.sigmoid(gate_part)
    gate_grad = hidden_grad * up_part * sigmoid_gate * (1.0 + gate_part * (1.0 - sigmoid_gate))
    up_grad = hidden_grad * gate_part * sigmoid_gate
    gate_up_low = jnp.concatenate([gate_grad, up_grad], axis=1).astype(jnp.bfloat16)
    ffn_in_grad = left_product(normed_two, gate_up_low)
    normed_two_grad = right_product(gate_up_low, ffn_in)
    gain_two_grad, read_grad = norm_back(normed_two_grad, normal_two, scale_two, gain_values[:, 1])
    mid_grad = grad_out + mixing[None, :, stream_count + 2, None] * read_grad[:, None, :]
    grad_read_two = jnp.sum(streams_mid * read_grad[:, None, :], axis=(0, 2))
    first_low = jnp.sum(mid_grad * mixing[None, :, stream_count + 1, None], axis=1).astype(
        jnp.bfloat16
    )
    grad_depth_one = jnp.sum(mid_grad * first_out[:, None, :], axis=(0, 2))
    attn_out_grad = left_product(context, first_low)
    context_grad = (
        right_product(first_low, attn_out).astype(jnp.bfloat16).reshape(row_count, HEADS, HD)
    )
    attend_grad = jnp.einsum(
        "qhd,khd->hqk", context_grad, values_all, preferred_element_type=jnp.float32
    )
    values_grad = jnp.einsum(
        "hqk,qhd->khd", attend_low, context_grad, preferred_element_type=jnp.float32
    )
    inner_sum = jnp.sum(attend * attend_grad, axis=-1, keepdims=True)
    score_low = (attend * (attend_grad - inner_sum)).astype(jnp.bfloat16)
    query_grad = jnp.einsum(
        "hqk,khd->qhd", score_low, keys_all, preferred_element_type=jnp.float32
    ) * HD ** (-0.5)
    keys_grad = jnp.einsum(
        "hqk,qhd->khd", score_low, queries, preferred_element_type=jnp.float32
    ) * HD ** (-0.5)
    returned = jnp.concatenate(
        [
            keys_grad[:row_count].reshape(row_count, model_width),
            values_grad[:row_count].reshape(row_count, model_width),
        ],
        axis=1,
    )
    from_later = shifted(returned.astype(jnp.bfloat16), "seq", -1).astype(returned.dtype)
    own_keys = keys_grad[row_count:].reshape(row_count, model_width) + from_later[:, :model_width]
    own_values = (
        values_grad[row_count:].reshape(row_count, model_width) + from_later[:, model_width:]
    )
    query_back = rotate_back(query_grad, cosine, sine_table).reshape(row_count, model_width)
    key_back = rotate_back(own_keys.reshape(row_count, HEADS, HD), cosine, sine_table).reshape(
        row_count, model_width
    )
    project_low = jnp.concatenate([query_back, key_back, own_values], axis=1).astype(jnp.bfloat16)
    attn_in_grad = left_product(normed, project_low)
    normed_grad = right_product(project_low, attn_in)
    gain_one_grad, branch_grad = norm_back(normed_grad, normal_one, scale_one, gain_values[:, 0])
    stream_grad = jnp.sum(mid_grad[:, None, :, :] * mixing[None, :, :stream_count, None], axis=2)
    stream_grad = stream_grad + mixing[None, :, stream_count, None] * branch_grad[:, None, :]
    grad_mix = jnp.sum(stream_values[:, :, None, :] * mid_grad[:, None, :, :], axis=(0, 3))
    grad_read_one = jnp.sum(stream_values * branch_grad[:, None, :], axis=(0, 2))
    mixing_grad = jnp.concatenate(
        [
            grad_mix,
            grad_read_one[:, None],
            grad_depth_one[:, None],
            grad_read_two[:, None],
            grad_depth_two[:, None],
        ],
        axis=1,
    )
    gains_grad = jnp.stack([gain_one_grad, gain_two_grad], axis=1)
    return (
        stream_grad,
        (attn_in_grad, attn_out_grad, ffn_in_grad, ffn_out_grad),
        gains_grad,
        mixing_grad,
    )


def adam_step(shard_state, shard_grad):
    weight = shard_state[0]
    first_new = beta_first * shard_state[1] + (1.0 - beta_first) * shard_grad
    second_new = beta_second * shard_state[2] + (1.0 - beta_second) * shard_grad * shard_grad
    first_hat = first_new / (1.0 - beta_first**STEP)
    second_hat = second_new / (1.0 - beta_second**STEP)
    update = first_hat / (jnp.sqrt(second_hat) + adam_epsilon) + weight_decay * weight
    weight_new = weight - learn_rate * update
    return (weight_new, first_new, second_new)


def rope_constants(length, head_size):
    half_size = head_size // 2
    exponent = np.arange(half_size, dtype=np.float32) * np.float32(2.0 / head_size)
    frequency = np.power(np.float64(rope_base), -exponent.astype(np.float64)).astype(np.float32)
    angles = np.arange(length, dtype=np.float32)[:, None] * frequency[None, :]
    cosine = np.cos(angles.astype(np.float64)).astype(np.float32)
    sine = np.sin(angles.astype(np.float64)).astype(np.float32)
    return np.tile(cosine, (1, 4)), np.tile(np.concatenate([-sine, sine], axis=1), (1, 2))


def swapped(values):
    lane = lax.broadcasted_iota(jnp.int32, values.shape, 1)
    return jnp.where(lane % HD < HD // 2, pltpu.roll(values, 128 - HD // 2, 1), pltpu.roll(values, HD // 2, 1))


def unpacked(block):
    count = block.shape[0]
    flat = block.reshape(count * NS, block.shape[2])
    row = lax.broadcasted_iota(jnp.int32, (count * NS, count * NS), 0)
    col = lax.broadcasted_iota(jnp.int32, (count * NS, count * NS), 1)
    pick = ((row % count) * NS + row // count == col).astype(jnp.bfloat16)
    out = jnp.dot(pick, flat, preferred_element_type=jnp.float32)
    return [out[i * count : (i + 1) * count] for i in range(NS)]


def packed_streams(parts):
    count = parts[0].shape[0]
    flat = jnp.concatenate(parts, axis=0)
    row = lax.broadcasted_iota(jnp.int32, (count * NS, count * NS), 0)
    col = lax.broadcasted_iota(jnp.int32, (count * NS, count * NS), 1)
    place = ((col % count) * NS + col // count == row).astype(jnp.bfloat16)
    out = jnp.dot(place, flat, preferred_element_type=jnp.float32).astype(jnp.bfloat16)
    return out.reshape(count, NS, parts[0].shape[1])


def normal_of(values):
    centre = jnp.mean(values, axis=-1, keepdims=True)
    centred = values - centre
    scaling = lax.rsqrt(jnp.mean(centred * centred, axis=-1, keepdims=True) + norm_epsilon)
    return centred * scaling, scaling


def nt(left, right):
    return lax.dot_general(left, right, (((1,), (1,)), ((), ())), preferred_element_type=jnp.float32)


def tn(left, right):
    return lax.dot_general(left, right, (((0,), (0,)), ((), ())), preferred_element_type=jnp.float32)


def nn(left, right):
    return jnp.dot(left, right, preferred_element_type=jnp.float32)


def doc_starts(docs, place):
    start = jnp.zeros(place.shape, jnp.int32)
    bound = 0
    for j in range(docs.shape[1] - 1):
        bound = bound + docs[0, j]
        start = jnp.where(place >= bound, bound, start)
    return start


EIGHTH = 128


def q_blocks(s):
    if s == 0:
        return [(0, 0, 1, False)] + [(i, 1, i, True) for i in (1, 2, 3)]
    return [(i - 4, 1, i, True) for i in (4, 5, 6)] + [(3, 7, 1, False)]


def block_mask(docs, s, block):
    row, key, count, single = block
    shape = (EIGHTH, 2 * EIGHTH)
    place = lax.broadcasted_iota(jnp.int32, shape, 1) % EIGHTH
    at = lax.broadcasted_iota(jnp.int32, shape, 0)
    if single:
        return at <= place
    first = (4 * s + row) * EIGHTH
    start = doc_starts(docs, place + first)
    return (at + first >= start) & (at <= place)


def two_heads(pair):
    lane = lax.broadcasted_iota(jnp.int32, pair.shape, 1)
    none = jnp.zeros_like(pair)
    return jnp.concatenate([jnp.where(lane < HD, pair, none), jnp.where(lane < HD, none, pair)], axis=0)


def one_pair(stacked):
    rows = stacked.shape[1] // 2
    return jnp.concatenate([stacked[:HD, :rows], stacked[HD:, rows:]], axis=0).T


def masked_scores(k2, qs, allow):
    scores = nt(k2, qs)
    keys = scores.shape[0]
    last = jnp.where(allow, scores[keys - EIGHTH :], masked_score)
    if keys == EIGHTH:
        return last
    return jnp.concatenate([scores[: keys - EIGHTH], last], axis=0)


def when(test, f):
    def go():
        f()

    pl.when(test)(go)


UP, EARLY, LATE = range(3)
(
    CORE_SEND,
    ADD_CORE,
    ADD_A,
    ADD_B,
    Z_MID,
    Z_LAST,
    GATHER_Z,
    RELAY_ONE,
    RELAY_TWO,
    GATHER_B,
    GATHER_A,
    GATHER_CORE,
    GATHER_END,
    H_B,
    H_A,
    H_Z,
    H_R1,
    H_R2,
    SMALL,
    OWNER,
) = range(20)
PARTS = 4
Z_LAST = ((UP, 0), (EARLY, 0), )
PLAN = {
    4: (
        ((CORE_SEND, UP, 0),),
        ((CORE_SEND, UP, 0),),
    ),
    5: (
        (),
        ((ADD_CORE, UP, 0),),
    ),
    8: (
        ((CORE_SEND, EARLY, 1), (CORE_SEND, UP, 1), (ADD_CORE, UP, 0),),
        ((CORE_SEND, UP, 1), (ADD_A, UP, 0), (ADD_CORE, EARLY, 1),),
    ),
    9: (
        (),
        ((ADD_CORE, UP, 1), (ADD_B, UP, 0),),
    ),
    11: (
        ((ADD_A, UP, 0),),
        (),
    ),
    12: (
        ((CORE_SEND, EARLY, 2), (CORE_SEND, UP, 2), (ADD_CORE, UP, 1),),
        (),
    ),
    13: (
        (),
        ((ADD_A, EARLY, 1), (ADD_CORE, UP, 2), (CORE_SEND, UP, 2),),
    ),
    14: (
        ((ADD_A, UP, 1), (ADD_B, UP, 0),),
        (),
    ),
    15: (
        ((ADD_CORE, UP, 2),),
        ((ADD_A, UP, 1), (ADD_B, EARLY, 1),),
    ),
    16: (
        ((CORE_SEND, EARLY, 0), (ADD_B, UP, 1), (Z_MID, UP, 1),),
        ((ADD_A, UP, 2), (Z_MID, UP, 0),),
    ),
    17: (
        ((Z_MID, UP, 0),),
        ((ADD_CORE, EARLY, 2),),
    ),
    18: (
        (),
        ((ADD_B, UP, 1), (ADD_CORE, EARLY, 0), (ADD_B, UP, 2), (Z_MID, UP, 1),),
    ),
    19: (
        (),
        ((ADD_A, EARLY, 2),),
    ),
    20: (
        ((ADD_A, UP, 2), (ADD_B, UP, 2), (Z_LAST, UP, 1),),
        (),
    ),
    22: (
        ((Z_MID, UP, 2),),
        ((CORE_SEND, LATE, 0), (Z_MID, UP, 2),),
    ),
    23: (
        ((Z_LAST, UP, 0), (ADD_CORE, LATE, 0),),
        ((ADD_A, EARLY, 0), (CORE_SEND, LATE, 1), (Z_MID, EARLY, 1), (Z_LAST, UP, 0), (ADD_B, EARLY, 2),),
    ),
    24: (
        ((ADD_CORE, LATE, 1),),
        (),
    ),
    25: (
        ((Z_LAST, UP, 2), (ADD_A, LATE, 0), (ADD_CORE, LATE, 2),),
        ((Z_LAST, UP, 1), (ADD_B, EARLY, 0),),
    ),
    26: (
        ((OWNER, UP, 0), (GATHER_Z, UP, 1), (H_B, UP, 0), (GATHER_Z, UP, 3),),
        ((Z_MID, EARLY, 2), (Z_LAST, UP, 2), (CORE_SEND, LATE, 2),),
    ),
    27: (
        ((ADD_A, LATE, 1), (ADD_B, LATE, 0),),
        (),
    ),
    28: (
        ((RELAY_ONE, UP, 1), (ADD_A, LATE, 2),),
        ((Z_MID, EARLY, 0), (OWNER, UP, 0), (GATHER_Z, UP, 2), (Z_LAST, EARLY, 1),),
    ),
    29: (
        ((RELAY_TWO, UP, 1), (Z_LAST, LATE, 0), (RELAY_ONE, UP, 3), (Z_MID, LATE, 0), (GATHER_B, UP, 1),),
        ((Z_LAST, EARLY, 2), (GATHER_Z, UP, 3), (GATHER_Z, UP, 1),),
    ),
    30: (
        ((RELAY_TWO, UP, 3), (ADD_B, LATE, 1), (Z_LAST, LATE, 1),),
        (),
    ),
    31: (
        ((H_A, UP, 0), (ADD_B, LATE, 2), (Z_MID, LATE, 1),),
        ((Z_LAST, EARLY, 0), (RELAY_ONE, UP, 2), (OWNER, EARLY, 0), (H_B, UP, 0), (GATHER_Z, EARLY, 1),
         (RELAY_TWO, UP, 2), (H_B, EARLY, 0),),
    ),
    32: (
        (),
        ((GATHER_B, UP, 2), (RELAY_ONE, UP, 3), (RELAY_TWO, UP, 3), (GATHER_Z, EARLY, 3), (H_A, EARLY, 0),),
    ),
    33: (
        (),
        ((RELAY_ONE, UP, 1), (GATHER_Z, EARLY, 2), (GATHER_B, UP, 3), (GATHER_A, UP, 2), (RELAY_ONE, EARLY,
         1), (RELAY_ONE, EARLY, 2), (GATHER_A, UP, 3), (RELAY_TWO, EARLY, 1), (RELAY_ONE, EARLY, 3), (H_Z,
         EARLY, 0), (GATHER_CORE, UP, 2), (GATHER_B, EARLY, 1), (RELAY_TWO, EARLY, 2), (GATHER_B, EARLY, 2),
         (RELAY_TWO, EARLY, 3), (GATHER_B, EARLY, 3),),
    ),
    34: (
        ((GATHER_B, UP, 3), (Z_MID, LATE, 2), (GATHER_Z, UP, 2), (Z_LAST, LATE, 2),),
        (),
    ),
    35: (
        (),
        ((H_A, UP, 0),),
    ),
    36: (
        ((GATHER_A, UP, 1),),
        (),
    ),
    37: (
        ((RELAY_ONE, UP, 2), (RELAY_TWO, UP, 2), (OWNER, LATE, 0), (GATHER_Z, LATE, 1), (GATHER_Z, LATE, 2),
         (H_Z, UP, 0),),
        (),
    ),
    38: (
        ((GATHER_B, UP, 2),),
        ((GATHER_A, EARLY, 1), (GATHER_A, EARLY, 3),),
    ),
    39: (
        ((H_R1, UP, 0), (GATHER_Z, LATE, 3), (GATHER_A, UP, 3),),
        (),
    ),
    40: (
        ((RELAY_ONE, LATE, 1),),
        ((GATHER_A, EARLY, 2),),
    ),
    41: (
        ((GATHER_CORE, UP, 1),),
        ((H_R1, EARLY, 0),),
    ),
    42: (
        ((SMALL, UP, 0), (RELAY_ONE, LATE, 2), (SMALL, UP, 1), (GATHER_A, UP, 2), (RELAY_TWO, LATE, 1),
         (GATHER_B, LATE, 1), (RELAY_TWO, LATE, 2), (GATHER_Z, LATE, 0), (RELAY_ONE, LATE, 3), (GATHER_B,
         LATE, 2), (RELAY_TWO, LATE, 3), (H_R2, UP, 0), (RELAY_TWO, LATE, 0), (RELAY_ONE, LATE, 0), (GATHER_A,
         LATE, 1), (SMALL, UP, 2), (GATHER_CORE, UP, 2), (GATHER_B, LATE, 3), (GATHER_A, LATE, 2), (GATHER_B,
         LATE, 0), (GATHER_END, UP, 1), (GATHER_END, EARLY, 3), (GATHER_END, UP, 2), (GATHER_CORE, LATE, 1),
         (GATHER_A, LATE, 3), (GATHER_CORE, UP, 3), (GATHER_CORE, UP, 0), (GATHER_CORE, LATE, 2), (GATHER_A,
         LATE, 0), (GATHER_CORE, LATE, 3), (GATHER_CORE, LATE, 0), (SMALL, UP, 3), (GATHER_END, UP, 0),
         (GATHER_END, EARLY, 2), (SMALL, UP, 4), (GATHER_END, EARLY, 0), (GATHER_END, UP, 3), (GATHER_END,
         EARLY, 1),),
        ((SMALL, UP, 0), (GATHER_CORE, UP, 3), (RELAY_TWO, UP, 1), (H_Z, UP, 0), (GATHER_B, UP, 1),
         (GATHER_CORE, EARLY, 3), (GATHER_CORE, EARLY, 1), (SMALL, UP, 1), (H_R1, UP, 0), (GATHER_A, UP, 1),
         (GATHER_CORE, UP, 1), (H_R2, UP, 0), (H_R2, EARLY, 0), (GATHER_CORE, EARLY, 0), (SMALL, UP, 2),
         (GATHER_CORE, EARLY, 2), (SMALL, UP, 3), (GATHER_END, LATE, 1), (GATHER_CORE, UP, 0), (GATHER_END,
         UP, 2), (SMALL, UP, 4), (GATHER_END, UP, 0), (GATHER_END, UP, 3), (GATHER_END, UP, 1), (GATHER_END,
         LATE, 2), (GATHER_END, LATE, 3), (GATHER_END, LATE, 0),),
    ),
}


def layer_kernel(
    dims, token_count,
    docs, small, gains, small_rows, streams, cotangent, attn_in, attn_out, ffn_in, ffn_out, state_in,
    cos_table, sin_table,
    new_out, stream_grad_out, copy_out, grad_out, small_out, from_core,
    grads, from_a0, from_a1, from_b0, from_b1, from_c, stage_box, kv_box, gfirst, second, dread, read, first,
    normed, queries, keys, values, context, lse, cosine, sine, starts, low, small_box,
    kv_send_sem, kv_recv_sem, send_sem, recv_sem, load_sem, local_sem, stage_sem, store_sem, out_sem, small_send, small_recv,
):
    f32, bf16 = jnp.float32, jnp.bfloat16
    nz, ny, nx = dims
    rows, width = second.shape
    hidden = ffn_out.shape[0]
    shard = low.shape[0]
    piece = shard // 3
    unit = 6 * piece
    half = unit // 2
    planes = nz // 2
    s = lax.axis_index("seq")
    w = lax.axis_index("wide")
    z, y, x = w // (ny * nx), (w // nx) % ny, w % nx

    def chip(cz, cy, cx):
        return (s, (cz * ny + cy) * nx + cx)

    core = (1 - s, w)
    z_peers = [chip((z + d) % nz, y, x) for d in range(1, nz)]
    y_peers = [chip(z, (y + d) % ny, x) for d in range(1, ny)]
    x_peers = [chip(z, y, (x + d) % nx) for d in range(1, nx)]
    peers = [core] + z_peers + y_peers + x_peers
    barrier = pltpu.get_barrier_semaphore()
    for peer in peers:
        pl.semaphore_signal(barrier, inc=1, device_id=peer, device_id_type=MESH)

    base = 2 * width
    mix = [[small[0, base + i * 2 * NS + j] for j in range(2 * NS)] for i in range(NS)]
    read_one = [mix[i][NS] for i in range(NS)]
    depth_one = [mix[i][NS + 1] for i in range(NS)]
    read_two = [mix[i][NS + 2] for i in range(NS)]
    depth_two = [mix[i][NS + 3] for i in range(NS)]

    def load(src, dst, sem):
        copy = pltpu.make_async_copy(src, dst, sem)
        copy.start()
        return copy

    ids = {}
    unsent = {}
    unit_now = [None]

    def number(kind, key, count=1):
        if (kind, key) not in ids:
            ids[kind, key] = ids.get(kind, 0)
            ids[kind] = ids.get(kind, 0) + count
        return ids[kind, key]

    def copy_of(key, ends, recv=None):
        src, dst, peer = ends()
        got = number("recv", key) if recv is None else recv()
        return pltpu.make_async_remote_copy(
            src, dst, send_sem.at[number("send", key)], recv_sem.at[got], device_id=peer, device_id_type=MESH)

    def remote(key, ends, guard=None, recv=None):
        copy_of(key, ends, recv).start()
        unsent.setdefault((key, unit_now[-1]), (lambda: copy_of(key, ends, recv), guard))

    def wait_sends():
        for copy, guard in unsent.values():
            if guard is None:
                copy().wait_send()
            else:
                pl.when(guard())(lambda copy=copy: copy().wait_send())
        unsent.clear()

    one, zero = s == 1, s == 0
    group_of = {UP: 1, EARLY: 0, LATE: 0}
    guard_of = {UP: None, EARLY: lambda: one, LATE: lambda: zero}

    def zs_of(v):
        return pl.ds(planes * group_of[v], planes)

    def zlist(v):
        return list(range(planes * group_of[v], planes * (group_of[v] + 1)))

    def guarded(v, f):
        f()

    def more(v, test):
        if guard_of[v] is None:
            return test
        return lambda: guard_of[v]() & test()

    lo, hi = pl.ds(0, half), pl.ds(half, half)

    def core_moves(v, c):
        return [(
            ("core", group_of[v], c),
            lambda: (grads.at[1 - s, zs_of(v), :, :, c], from_core.at[zs_of(v), :, :, c], core))]

    def a_moves(v, c, only=None):
        planes_of = [zd for zd in zlist(v) if only is None or zd == only]
        return [
            (("a0", zd, c, d), lambda d=d, zd=zd: (
                grads.at[s, zd, :, (x + d) % nx, c, lo], from_a0.at[d - 1, zd, :, c], x_peers[d - 1]))
            for zd in planes_of for d in range(1, nx)
        ] + [
            (("a1", zd, c, d), lambda d=d, zd=zd: (
                grads.at[s, zd, (y + d) % ny, :, c, hi], from_a1.at[d - 1, zd, :, c], y_peers[d - 1]))
            for zd in planes_of for d in range(1, ny)
        ]

    def b_moves(v, c):
        g = group_of[v]
        return [
            (("b0", g, c, d), lambda d=d: (
                grads.at[s, zs_of(v), (y + d) % ny, x, c, lo], from_b0.at[d - 1, zs_of(v), c], y_peers[d - 1]))
            for d in range(1, ny)
        ] + [
            (("b1", g, c, d), lambda d=d: (
                grads.at[s, zs_of(v), y, (x + d) % nx, c, hi], from_b1.at[d - 1, zs_of(v), c], x_peers[d - 1]))
            for d in range(1, nx)
        ]

    def same(ref, peer):
        return ref, ref, peer

    def gb_moves(v, k):
        g = group_of[v]
        return [
            (("gb0", g, k, d), lambda peer=peer: same(copy_out.at[s, zs_of(v), y, x, part_lo(k)], peer))
            for d, peer in enumerate(y_peers)
        ] + [
            (("gb1", g, k, d), lambda peer=peer: same(copy_out.at[s, zs_of(v), y, x, part_hi(k)], peer))
            for d, peer in enumerate(x_peers)
        ]

    def ga_moves(v, k):
        g = group_of[v]
        return [
            (("ga0", g, k, d), lambda peer=peer: same(copy_out.at[s, zs_of(v), :, x, part_lo(k)], peer))
            for d, peer in enumerate(x_peers)
        ] + [
            (("ga1", g, k, d), lambda peer=peer: same(copy_out.at[s, zs_of(v), y, :, part_hi(k)], peer))
            for d, peer in enumerate(y_peers)
        ]

    def gc_moves(v, k):
        return [(("gc", group_of[v], k), lambda: same(copy_out.at[s, zs_of(v), :, :, part(k)], core))]

    def gc_first(v, k):
        g = group_of[v]
        return [
            (("gc0", g, k), lambda: same(copy_out.at[s, zs_of(v), :, x, part_lo(k)], core)),
            (("gc1", g, k), lambda: same(copy_out.at[s, zs_of(v), y, :, part_hi(k)], core)),
        ]

    def gc_second(v, k):
        g = group_of[v]
        return [
            (("gc2", g, k, d), lambda d=d: same(copy_out.at[s, zs_of(v), :, (x + d) % nx, part_lo(k)], core))
            for d in range(1, nx)
        ] + [
            (("gc3", g, k, d), lambda d=d: same(copy_out.at[s, zs_of(v), (y + d) % ny, :, part_hi(k)], core))
            for d in range(1, ny)
        ]

    def start(moves, v, c, guard="unit"):
        for key, ends in moves(v, c):
            remote(key, ends, guard=guard_of[v] if guard == "unit" else guard)

    def wait_recvs(moves, v, c):
        for key, ends in moves(v, c):
            copy_of(key, ends).wait_recv()

    def core_send(v, c):
        start(core_moves, v, c, {UP: None, EARLY: lambda: zero, LATE: lambda: one}[v])

    def add_core(v, c):
        def go():
            wait_recvs(core_moves, v, c)
            g = group_of[v]
            loads = [
                load(from_core.at[planes * g + i, :, :, c], stage_box.at[i], stage_sem.at[i]) for i in range(planes)
            ]
            for plane, copy in enumerate(loads):
                copy.wait()

                def body(i, carry, plane=plane):
                    yi, xi = i // nx, i % nx
                    at = (s, planes * g + plane, yi, xi, c)
                    grads[at] = (grads[at].astype(f32) + stage_box[plane, yi, xi].astype(f32)).astype(bf16)
                    return carry

                lax.fori_loop(0, ny * nx, body, 0)
                start(functools.partial(a_moves, only=planes * g + plane), v, c)

        guarded(v, go)

    def add_a(v, c):
        def go():
            wait_recvs(a_moves, v, c)
            g = group_of[v]

            def body_lo(i, carry):
                zi, yi = planes * g + i // ny, i % ny
                at = (s, zi, yi, x, c, lo)
                total = grads[at].astype(f32)
                for d in range(nx - 1):
                    total = total + from_a0[d, zi, yi, c].astype(f32)
                grads[at] = total.astype(bf16)
                return carry

            def body_hi(i, carry):
                zi, xi = planes * g + i // nx, i % nx
                at = (s, zi, y, xi, c, hi)
                total = grads[at].astype(f32)
                for d in range(ny - 1):
                    total = total + from_a1[d, zi, xi, c].astype(f32)
                grads[at] = total.astype(bf16)
                return carry

            lax.fori_loop(0, planes * ny, body_lo, 0)
            lax.fori_loop(0, planes * nx, body_hi, 0)
            start(b_moves, v, c)

        guarded(v, go)

    def add_b(v, c):
        def go():
            wait_recvs(b_moves, v, c)
            g = group_of[v]

            def body(i, carry):
                zi = planes * g + i
                for at_rows, box, count in ((lo, from_b0, ny - 1), (hi, from_b1, nx - 1)):
                    at = (s, zi, y, x, c, at_rows)
                    total = grads[at].astype(f32)
                    for d in range(count):
                        total = total + box[d, zi, c].astype(f32)
                    grads[at] = total.astype(bf16)
                return carry

            lax.fori_loop(0, planes, body, 0)
            hop(v, c, 0)

        guarded(v, go)

    def place_of(v):
        return z if group_of[v] == 1 else nz - 1 - z

    def z_at(v, place):
        return place if group_of[v] == 1 else nz - 1 - place

    def hop(v, c, place):
        g = group_of[v]
        if place == 0:
            moves = [(0, 1, 2, 0), (0, 1, 3, 1), (3, 2, 2, 2)]
        elif place == 1:
            moves = [(1, 2, 2, 0), (1, 2, 3, 1)]
        else:
            moves = [(2, 3, 3, 1)]
        for start, end, owner, slot in moves:
            when(place_of(v) == start, lambda start=start, end=end, owner=owner, slot=slot: remote(
                ("z", g, c, start, owner),
                lambda: (grads.at[s, z_at(v, owner), y, x, c], from_c.at[g, slot, c], chip(z_at(v, end), y, x)),
                guard=more(v, lambda: place_of(v) == start),
                recv=lambda: number("recv", ("z", g, c, slot))))

    def hop_wait(v, c, slot):
        g = group_of[v]
        pltpu.make_async_remote_copy(
            grads.at[s, z, y, x, c], from_c.at[g, slot, c], send_sem.at[0],
            recv_sem.at[number("recv", ("z", g, c, slot))], device_id=core, device_id_type=MESH).wait_recv()

    def hop_add(v, c, place):
        def go():
            for owner, slot in ((2, 0), (3, 1)) if place == 1 else ((3, 1),):
                hop_wait(v, c, slot)
                g = group_of[v]

                def body(i, carry, owner=owner, slot=slot):
                    r = pl.ds(i * 128, 128)
                    at = (s, z_at(v, owner), y, x, c, r)
                    grads[at] = (grads[at].astype(f32) + from_c[g, slot, c, r].astype(f32)).astype(bf16)
                    return carry

                lax.fori_loop(0, unit // 128, body, 0)
            hop(v, c, place)

        guarded(v, lambda: when(place_of(v) == place, go))

    def z_mid(v, c):
        hop_add(v, c, 1)

    def z_last(v, c):
        hop_add(v, c, 2)

    def in_group(g):
        return (z // planes) == g

    def owner_update(units, state, flat, sums):
        for v in units:
            g = group_of[v]

            def total_at(slots, v=v, g=g):
                for c in range(3):
                    for slot in slots:
                        hop_wait(v, c, slot)

                def body(i, carry):
                    r = pl.ds(i * 128, 128)
                    for c in range(3):
                        total = grads[s, z, y, x, c, r].astype(f32)
                        for slot in slots:
                            total = total + from_c[g, slot, c, r].astype(f32)
                        sums[c, r] = total * (1.0 / token_count)
                    return carry

                lax.fori_loop(0, unit // 128, body, 0)

            guarded(v, lambda v=v, f=total_at: when(place_of(v) == 2, lambda: f((0, 2))))
            guarded(v, lambda v=v, f=total_at: when(place_of(v) == 3, lambda: f((1,))))
        mine = {UP: in_group(1), EARLY: in_group(0) & one, LATE: in_group(0) & zero}[units[0]]
        pl.when(mine)(lambda: owner_step(state, flat, sums))

    def owner_step(state, flat, sums):
        pltpu.make_async_copy(state_in, state, load_sem.at[0]).wait()
        index = s * (nz * ny * nx) + w
        in_rows = attn_in.shape[0] * attn_in.shape[1] // width // shard
        out_rows = in_rows + attn_out.shape[0] // shard
        ffn_rows = out_rows + ffn_in.shape[0] * ffn_in.shape[1] // width // shard
        blocks = ffn_in.shape[1] // width
        thirds = attn_in.shape[1] // width

        def total_of(c, at_rows):
            return sums[c, at_rows]

        @pl.when(index < in_rows)
        def _():
            for c in range(3):
                for lane in range(6):
                    flat[lane, pl.ds(c, piece, stride=thirds), :] = total_of(c, pl.ds(lane * piece, piece))

        @pl.when(((index >= in_rows) & (index < out_rows)) | (index >= ffn_rows))
        def _():
            for c in range(3):
                for lane in range(6):
                    flat[lane, pl.ds(c * piece, piece), :] = total_of(c, pl.ds(lane * piece, piece))

        @pl.when((index >= out_rows) & (index < ffn_rows))
        def _():
            part = shard // blocks
            for c in range(3):
                for side in range(2):
                    for j in range(blocks):
                        flat[side * 3 + c, pl.ds(j, part, stride=blocks), :] = total_of(
                            c, pl.ds(side * half + j * part, part))

        def body(i, carry):
            r = pl.ds(i * 16, 16)
            grad = jnp.concatenate([flat[lane, r] for lane in range(6)], axis=1)
            read[r] = grad
            low[r] = adam_step((state[0, r], state[1, r], state[2, r]), grad)[0].astype(bf16)
            return carry

        lax.fori_loop(0, shard // 16, body, 0)
        pltpu.make_async_copy(read.at[pl.ds(0, shard)], grad_out, store_sem.at[0]).start()
        keep = pltpu.make_async_copy(low, copy_out.at[s, z, y, x], store_sem.at[4])
        keep.start()
        keep.wait()

    gather_parts = PARTS
    part_rows = shard // gather_parts

    def part(k):
        return pl.ds(k * part_rows, part_rows)

    def part_lo(k):
        return pl.ds(k * part_rows, part_rows // 2)

    def part_hi(k):
        return pl.ds(k * part_rows + part_rows // 2, part_rows // 2)

    def relay(v, k, moves):
        for start, end, owner, mine in moves:
            def send(start=start, end=end, owner=owner, mine=mine):
                zd = z_at(v, owner)

                def ends():
                    dst = copy_out.at[s, zd, y, x, part(k)]
                    return (low.at[part(k)] if mine else dst), dst, chip(z_at(v, end), y, x)

                remote(("gz", zd, k, start, end), ends, guard=more(v, lambda: place_of(v) == start),
                       recv=lambda: number("recv", ("gz", zd, k)))

            when(place_of(v) == start, send)

    def relay_wait(v, k, place, owner):
        zd = z_at(v, owner)
        when(place_of(v) == place, lambda: pltpu.make_async_remote_copy(
            low.at[part(k)], copy_out.at[s, zd, y, x, part(k)], send_sem.at[0],
            recv_sem.at[number("recv", ("gz", zd, k))], device_id=core, device_id_type=MESH).wait_recv())

    def gather_z(v, k):
        guarded(v, lambda: relay(v, k, [(2, 1, 2, True), (2, 3, 2, True), (3, 2, 3, True)]))

    def relay_one(v, k):
        def go():
            relay_wait(v, k, 2, 3)
            relay_wait(v, k, 1, 2)
            relay(v, k, [(2, 1, 3, False), (1, 0, 2, False)])

        guarded(v, go)

    def relay_two(v, k):
        def go():
            relay_wait(v, k, 1, 3)
            relay(v, k, [(1, 0, 3, False)])

        guarded(v, go)

    def gather_b(v, k):
        def go():
            g = group_of[v]
            relay_wait(v, k, 0, 2)
            relay_wait(v, k, 0, 3)
            relay_wait(v, k, 3, 2)
            start(gb_moves, v, k)

        guarded(v, go)

    def gather_a(v, k):
        def go():
            wait_recvs(gb_moves, v, k)
            g = group_of[v]
            start(ga_moves, v, k)
            start(gc_first, v, k)

        guarded(v, go)

    def hb_moves(v, k):
        g = group_of[v]
        return [
            (("hb0", g, k, d), lambda peer=peer: same(copy_out.at[s, z, y, x, part_lo(k)], peer))
            for d, peer in enumerate(y_peers)
        ] + [
            (("hb1", g, k, d), lambda peer=peer: same(copy_out.at[s, z, y, x, part_hi(k)], peer))
            for d, peer in enumerate(x_peers)
        ]

    def ha_moves(v, k):
        g = group_of[v]
        return [
            (("ha0", g, k, d), lambda peer=peer: same(copy_out.at[s, z, :, x, part_lo(k)], peer))
            for d, peer in enumerate(x_peers)
        ] + [
            (("ha1", g, k, d), lambda peer=peer: same(copy_out.at[s, z, y, :, part_hi(k)], peer))
            for d, peer in enumerate(y_peers)
        ]

    def owner_place(v):
        return lambda: place_of(v) >= 2

    def h_b(v, k):
        when(place_of(v) >= 2, lambda: start(hb_moves, v, k, more(v, owner_place(v))))

    def h_a(v, k):
        def go():
            wait_recvs(hb_moves, v, k)
            start(ha_moves, v, k, more(v, owner_place(v)))

        when(place_of(v) >= 2, go)

    def plane_ends(v, k, owner, end):
        return lambda: same(copy_out.at[s, z_at(v, owner), :, :, part(k)], chip(z_at(v, end), y, x))

    def plane_send(v, k, at, end, owner):
        when(place_of(v) == at, lambda: remote(
            ("hz", z_at(v, owner), k, at, end), plane_ends(v, k, owner, end), guard=more(v, lambda: place_of(v) == at),
            recv=lambda: number("recv", ("hz", z_at(v, owner), k))))

    def plane_wait(v, k, at, owner):
        when(place_of(v) == at, lambda: copy_of(
            ("hz", z_at(v, owner), k, 2, 1), plane_ends(v, k, owner, 2),
            lambda: number("recv", ("hz", z_at(v, owner), k))).wait_recv())

    def h_z(v, k):
        when(place_of(v) >= 2, lambda: wait_recvs(ha_moves, v, k))
        plane_send(v, k, 2, 1, 2)
        plane_send(v, k, 2, 3, 2)
        plane_send(v, k, 3, 2, 3)

    def h_r1(v, k):
        plane_wait(v, k, 2, 3)
        plane_wait(v, k, 1, 2)
        plane_send(v, k, 2, 1, 3)
        plane_send(v, k, 1, 0, 2)

    def h_r2(v, k):
        plane_wait(v, k, 1, 3)
        plane_send(v, k, 1, 0, 3)

    def gather_core(v, k):
        def go():
            if (v, k) in Z_LAST:
                plane_wait(v, k, 0, 2)
                plane_wait(v, k, 0, 3)
                plane_wait(v, k, 3, 2)
                start(gc_moves, v, k)
            else:
                wait_recvs(ga_moves, v, k)
                start(gc_second, v, k)

        guarded(v, go)

    def gather_end(v, k):
        if (v, k) in Z_LAST:
            wait_recvs(gc_moves, v, k)
        else:
            wait_recvs(gc_first, v, k)
            wait_recvs(gc_second, v, k)

    wide_piece = piece
    tile = hidden // 3
    tile_pieces = tile // wide_piece
    steps = tile_pieces // 2

    tiles = []

    def kv_copy(hp):
        cols = pl.ds(pl.multiple_of(hp * 128, 128), 128)
        return pltpu.make_async_remote_copy(
            kv_box.at[:, cols], kv_box.at[:, cols], kv_send_sem.at[hp], kv_recv_sem.at[hp],
            device_id=core, device_id_type=MESH)

    def tile_loads(c):
        slot = c % 2
        copies = []
        for p in range(tile_pieces):
            at = p * 3 * wide_piece + c * wide_piece
            to = pl.ds(p * wide_piece, wide_piece)
            for k, (src, dst) in enumerate((
                (ffn_in.at[:, pl.ds(at, wide_piece)], tiles[0].at[slot, :, to]),
                (ffn_in.at[:, pl.ds(hidden + at, wide_piece)], tiles[1].at[slot, :, to]),
                (ffn_out.at[pl.ds(at, wide_piece)], tiles[2].at[slot, to]),
            )):
                copies.append(pltpu.make_async_copy(src, dst, local_sem.at[slot, k, p]))
        return copies

    def forward_scope(raw, w_in):
        w_out = kv_box
        loads = [load(src, dst, load_sem.at[1 + k]) for k, (src, dst) in enumerate((
            (streams, raw), (attn_in, w_in), (cos_table.at[pl.ds(0, EIGHTH)], starts.at[0]),
            (sin_table.at[pl.ds(0, EIGHTH)], starts.at[1]), (attn_out, w_out)))]
        plain_rows = [pl.ds(EIGHTH, 3 * EIGHTH), pl.ds(0, 3 * EIGHTH)]
        plain_loads = [
            [pltpu.make_async_copy(table.at[pl.ds(side * 3 * EIGHTH, 3 * EIGHTH)], own.at[plain_rows[side]],
                                   load_sem.at[11 + k])
             for k, (table, own) in enumerate(((cos_table, cosine), (sin_table, sine)))]
            for side in range(2)
        ]
        for side in range(2):
            @pl.when(s == side)
            def _(side=side):
                for copy in plain_loads[side]:
                    copy.start()

        carry_first = sum(depth_one[j] * read_two[j] for j in range(NS))
        carry_stream = [sum(mix[i][j] * read_two[j] for j in range(NS)) for i in range(NS)]
        loads[0].wait()

        def norm_block(i, carry):
            r = pl.ds(i * 64, 64)
            parts = unpacked(raw[r])
            branch = sum(parts[k] * read_one[k] for k in range(NS))
            read[r] = sum(parts[k] * carry_stream[k] for k in range(NS))
            normal, _ = normal_of(branch)
            normed[r] = (normal * gains[0:1].astype(f32)).astype(bf16)
            return carry

        lax.fori_loop(0, rows // 64, norm_block, 0)
        for copy in loads[1:]:
            copy.wait()
        load(cotangent, raw, load_sem.at[6])
        for c in range(2):
            for copy in tile_loads(c):
                copy.start()

        def tables(side):
            first_special = 7 * EIGHTH * side
            special = pl.ds(3 * EIGHTH * side, EIGHTH)
            place = lax.broadcasted_iota(jnp.int32, (EIGHTH, EIGHTH), 0) + first_special
            start = doc_starts(docs, place)
            lane = lax.broadcasted_iota(jnp.int32, (EIGHTH, EIGHTH), 1)
            pick = (place - start == lane).astype(f32)
            for k, own in enumerate((cosine, sine)):
                own[special] = jnp.dot(
                    pick, starts[k], precision=lax.Precision.HIGHEST, preferred_element_type=f32)
            for copy in plain_loads[side]:
                copy.wait()

        for side in range(2):
            pl.when(s == side)(lambda side=side: tables(side))

        own_rows = pl.ds(s * rows, rows)

        def rotated(dest, dest_rows, offset):
            def body(j, carry):
                cols = pl.ds(pl.multiple_of(j * 256, 256), 256)
                source = pl.ds(pl.multiple_of(offset + j * 256, 256), 256)
                part = nn(normed[...], w_in[:, source])
                halves = []
                for k in range(2):
                    turn = part[:, k * 128 : (k + 1) * 128]
                    halves.append(turn * cosine[...] + swapped(turn) * sine[...])
                dest[dest_rows, cols] = jnp.concatenate(halves, axis=1).astype(bf16)
                return carry

            lax.fori_loop(0, width // 256, body, 0)

        def plain(j, carry):
            cols = pl.ds(pl.multiple_of(j * 256, 256), 256)
            source = pl.ds(pl.multiple_of(2 * width + j * 256, 256), 256)
            values[own_rows, cols] = nn(normed[...], w_in[:, source]).astype(bf16)
            return carry

        lax.fori_loop(0, width // 256, plain, 0)
        rotated(keys, own_rows, width)
        pl.semaphore_wait(barrier, len(peers))
        shared = pl.ds(EIGHTH, 3 * EIGHTH)
        copies = [
            pltpu.make_async_remote_copy(
                ref.at[shared], ref.at[shared], kv_send_sem.at[6 + i], kv_recv_sem.at[6 + i],
                device_id=core, device_id_type=MESH)
            for i, ref in enumerate((keys, values))
        ]

        @pl.when(zero)
        def _():
            for copy in copies:
                copy.start()

        rotated(queries, pl.ds(0, rows), 0)

        def attend(side):
            blocks = q_blocks(side)
            masks = [block_mask(docs, side, block) for block in blocks]

            def pair(hp, carry):
                jobs = [
                    (2 * hp + q, pl.ds(pl.multiple_of((2 * hp + q) * 128, 128), 128), bi,
                     pl.ds(row * EIGHTH, EIGHTH), pl.ds(key * EIGHTH, count * EIGHTH))
                    for q in range(2) for bi, (row, key, count, _) in enumerate(blocks)
                ]
                scores = [
                    masked_scores(keys[kr, cols], two_heads(queries[r, cols]) * HD ** (-0.5), masks[bi])
                    for _, cols, bi, r, kr in jobs
                ]
                tops = [jnp.max(score, axis=0, keepdims=True) for score in scores]
                lifted = [jnp.exp(score - top) for score, top in zip(scores, tops)]
                totals = [jnp.sum(lift, axis=0, keepdims=True) for lift in lifted]
                probs = [(lift * (1.0 / total)).astype(bf16) for lift, total in zip(lifted, totals)]
                outs = [tn(values[job[4], job[1]], prob) for job, prob in zip(jobs, probs)]
                for (pair_at, cols, bi, r, kr), out, top, total in zip(jobs, outs, tops, totals):
                    context[r, cols] = one_pair(out).astype(bf16)
                    lse[pl.ds(bi * 8 + pair_at, 1), :] = top + jnp.log(total)
                return carry

            lax.fori_loop(0, width // 256, pair, 0)

        @pl.when(zero)
        def _():
            attend(0)
            for copy in copies:
                copy.wait_send()

        @pl.when(one)
        def _():
            for copy in copies:
                copy.wait_recv()
            attend(1)

        def out_block(j, carry):
            cols = pl.ds(pl.multiple_of(j * 256, 256), 256)
            part = nn(context[...], w_out[:, cols])
            first[:, cols] = part
            read[:, cols] += part * carry_first
            return carry

        lax.fori_loop(0, width // 256, out_block, 0)

    def ffn_scope(raw, normed_two, normed_two_t, dsecond, gate_s, up_s, dhid_s, hid, dgate, dup):
        pltpu.make_async_copy(cotangent, raw, load_sem.at[6]).wait()

        def first_block(i, carry):
            r = pl.ds(i * 64, 64)
            parts = unpacked(raw[r])
            dsecond[r] = sum(parts[j] * depth_two[j] for j in range(NS)).astype(bf16)
            gfirst[r] = sum(parts[j] * depth_one[j] for j in range(NS))
            normal, _ = normal_of(read[r])
            normed_two[r] = (normal * gains[1:2].astype(f32)).astype(bf16)
            second[r] = jnp.zeros((64, width), f32)
            dread[r] = jnp.zeros((64, width), f32)
            return carry

        lax.fori_loop(0, rows // 64, first_block, 0)
        normed_two_t[...] = normed_two[...].T

        if True:
            def sub(step, carry):
                c, u = step // steps, step % steps
                slot = c % 2
                for k in range(3):
                    def arrive(k=k):
                        for copy in tile_loads(k):
                            copy.wait()

                    pl.when(step == k * steps)(arrive)
                cols = pl.ds(pl.multiple_of(u * 2 * wide_piece, 2 * wide_piece), 2 * wide_piece)
                wg, wu, wo = tiles[0][slot, :, cols], tiles[1][slot, :, cols], tiles[2][slot, cols]
                gate_s[...] = nn(normed_two[...], wg)
                up_s[...] = nn(normed_two[...], wu)
                dhid_s[...] = nt(dsecond[...], wo)
                for i in range(rows // 64):
                    r = pl.ds(i * 64, 64)
                    gate, up, dhid = gate_s[r], up_s[r], dhid_s[r]
                    sig = 1.0 / (1.0 + jnp.exp(-gate))
                    silu = gate * sig
                    hid[r] = (silu * up).astype(bf16)
                    dgate[r] = (dhid * up * sig * (1.0 + gate - silu)).astype(bf16)
                    dup[r] = (dhid * silu).astype(bf16)
                second[...] += nn(hid[...], wo)
                dread[...] += nt(dgate[...], wg) + nt(dup[...], wu)
                dwo = tn(hid[...], dsecond[...]).astype(bf16)
                for q in range(2):
                    p = 2 * u + q
                    zi, yi, xi = planes + p // (ny * nx), (p // nx) % ny, p % nx
                    for lane in range(6):
                        grads[1, zi, yi, xi, c, pl.ds(lane * piece, piece)] = dwo[
                            q * piece : (q + 1) * piece, lane * 128 : (lane + 1) * 128]
                blocks = 2 * (hidden // width)
                part = shard // blocks
                for k, dact in enumerate((dgate, dup)):
                    dwi = nn(normed_two_t[...], dact[...]).astype(bf16)
                    j = u + k * (blocks // 2)
                    for b in range(width // part):
                        at_half, at = b // (width // part // 2), b % (width // part // 2)
                        at = at + (nz * ny * nx // 2 if at_half == 0 else 0)
                        zi, yi, xi = at // (ny * nx), (at // nx) % ny, at % nx
                        for q in range(2):
                            grads[at_half, zi, yi, xi, c, pl.ds(pl.multiple_of(q * half + j * part, 16), part)] = dwi[
                                b * part : (b + 1) * part, q * 128 : (q + 1) * 128]
                def more_weights():
                    for copy in tile_loads(2):
                        copy.start()

                pl.when(step == steps - 1)(more_weights)
                poll_loop(1, 3 * steps, step)
                return carry

            lax.fori_loop(0, 3 * steps, sub, 0)

    stages = {
        CORE_SEND: core_send,
        ADD_CORE: add_core,
        ADD_A: add_a,
        ADD_B: add_b,
        Z_MID: z_mid,
        Z_LAST: z_last,
        GATHER_Z: gather_z,
        RELAY_ONE: relay_one,
        RELAY_TWO: relay_two,
        GATHER_B: gather_b,
        GATHER_A: gather_a,
        GATHER_CORE: gather_core,
        GATHER_END: gather_end,
        H_B: h_b,
        H_A: h_a,
        H_Z: h_z,
        H_R1: h_r1,
        H_R2: h_r2,
    }

    def run(actions):
        for name, v, c in actions:
            unit_now.append(v)
            stages[name](v, c)
            unit_now.pop()

    def poll(at):
        for side in range(2):
            actions = PLAN.get(at, ((), ()))[side]
            if actions:
                pl.when(s == side)(lambda actions=actions: run(actions))

    def poll_loop(first, count, step):
        for i in range(count):
            for side in range(2):
                actions = PLAN.get(first + i, ((), ()))[side]
                if actions:
                    pl.when((step == i) & (s == side))(lambda actions=actions: run(actions))

    def both_scopes(raw, gate_w, up_w, out_w):
        tiles.extend((gate_w, up_w, out_w))
        pl.run_scoped(
            functools.partial(forward_scope, raw),
            pltpu.VMEM(attn_in.shape, bf16))
        pl.run_scoped(
            functools.partial(ffn_scope, raw),
            pltpu.VMEM((rows, width), bf16), pltpu.VMEM((width, rows), bf16), pltpu.VMEM((rows, width), bf16),
            pltpu.VMEM((rows, 2 * piece), f32), pltpu.VMEM((rows, 2 * piece), f32), pltpu.VMEM((rows, 2 * piece), f32),
            pltpu.VMEM((rows, 2 * piece), bf16), pltpu.VMEM((rows, 2 * piece), bf16), pltpu.VMEM((rows, 2 * piece), bf16))

    pl.run_scoped(
        both_scopes,
        pltpu.VMEM((rows, NS, width), bf16), pltpu.VMEM((2, width, tile), bf16),
        pltpu.VMEM((2, width, tile), bf16), pltpu.VMEM((2, tile, width), bf16))

    gain_sums = {}

    def attention_scope(w_in, w_out, dfirst, dcontext, dkeys, dvalues, own_keys, own_values, dproject, turned):
        loads = [load(attn_out, w_out, load_sem.at[7]), load(attn_in, w_in, load_sem.at[8])]
        carry_first = sum(depth_one[j] * read_two[j] for j in range(NS))

        def norm_block(i, total):
            r = pl.ds(i * 64, 64)
            normal, scaling = normal_of(read[r])
            grad = dread[r]
            total = total + jnp.sum((grad * normal).reshape(8, 8, width), axis=0)
            scaled = grad * gains[1:2].astype(f32)
            centre = jnp.mean(scaled, axis=-1, keepdims=True)
            along = jnp.mean(scaled * normal, axis=-1, keepdims=True)
            value = scaling * (scaled - centre - normal * along)
            dread[r] = value
            dfirst[r] = (gfirst[r] + carry_first * value).astype(bf16)
            return total

        gain_two = lax.fori_loop(0, rows // 64, norm_block, jnp.zeros((8, width), f32))
        row = jnp.sum(gain_two, axis=0, keepdims=True)
        for k in range(width // 128):
            small_box[0, s, width // 128 + k : width // 128 + k + 1, :] = row[:, k * 128 : (k + 1) * 128]

        loads[0].wait()
        poll(13)

        def context_block(j, carry):
            cols = pl.ds(pl.multiple_of(j * 256, 256), 256)
            dcontext[:, cols] = nt(dfirst[...], w_out[cols]).astype(bf16)
            return carry

        lax.fori_loop(0, width // 256, context_block, 0)
        turned[...] = context[...].T
        shards_in = w_in.shape[1] // width * (width // piece) // 3

        def out_block(j, carry):
            cols = pl.ds(pl.multiple_of(j * 256, 256), 256)
            part = nn(turned[...], dfirst[:, cols]).astype(bf16)
            for b in range(width // piece):
                at, c = shards_in + b // 3, b % 3
                zi, yi, xi = at // (ny * nx), (at // nx) % ny, at % nx
                for q in range(2):
                    grads[0, zi, yi, xi, c, pl.ds(pl.multiple_of((2 * j + q) * piece, piece), piece)] = part[
                        b * piece : (b + 1) * piece, q * 128 : (q + 1) * 128]
            return carry

        lax.fori_loop(0, width // 256, out_block, 0)
        poll(14)

        def blocks_back(side, hp):
            blocks = q_blocks(side)
            cols = pl.ds(pl.multiple_of(hp * 128, 128), 128)
            spans = [
                (pl.ds(row * EIGHTH, EIGHTH), pl.ds(key * EIGHTH, count * EIGHTH)) for row, key, count, _ in blocks
            ]
            qs = [two_heads(queries[r, cols]) * HD ** (-0.5) for r, kr in spans]
            dstack = [two_heads(dcontext[r, cols]) for r, kr in spans]
            scores = [
                masked_scores(keys[kr, cols], qs[bi], block_mask(docs, side, blocks[bi]))
                for bi, (r, kr) in enumerate(spans)
            ]
            dprobs = [nt(values[kr, cols], dstack[bi]) for bi, (r, kr) in enumerate(spans)]
            probs = [jnp.exp(score - lse[pl.ds(bi * 8 + hp, 1), :]) for bi, score in enumerate(scores)]
            inner = [jnp.sum(p * dp, axis=0, keepdims=True) for p, dp in zip(probs, dprobs)]
            dscores = [(p * (dp - i)).astype(bf16) for p, dp, i in zip(probs, dprobs, inner)]
            for bi, (r, kr) in enumerate(spans):
                dkeys[kr] += nn(dscores[bi], qs[bi])
                dvalues[kr] += nn(probs[bi].astype(bf16), dstack[bi])
            dqs = [tn(keys[kr, cols], dscores[bi]) for bi, (r, kr) in enumerate(spans)]
            for bi, (r, kr) in enumerate(spans):
                dq = one_pair(dqs[bi]) * HD ** (-0.5)
                dproject[r, cols] = (dq * cosine[r] - swapped(dq) * sine[r]).astype(bf16)

        shared = pl.ds(EIGHTH, 3 * EIGHTH)

        key_rows, value_rows = pl.ds(0, 3 * EIGHTH), pl.ds(3 * EIGHTH, 3 * EIGHTH)

        def turned_back(dk):
            return (dk * cosine[...] - swapped(dk) * sine[...]).astype(bf16)

        def pair_back(hp, carry):
            cols = pl.ds(pl.multiple_of(hp * 128, 128), 128)
            key_cols = pl.ds(pl.multiple_of(width + hp * 128, 128), 128)
            value_cols = pl.ds(pl.multiple_of(2 * width + hp * 128, 128), 128)
            dkeys[...] = jnp.zeros_like(dkeys)
            dvalues[...] = jnp.zeros_like(dvalues)

            @pl.when(zero)
            def _():
                blocks_back(0, hp)
                own_keys[:, cols] = dkeys[pl.ds(0, rows)]
                own_values[:, cols] = dvalues[pl.ds(0, rows)]

            @pl.when(one)
            def _():
                blocks_back(1, hp)
                kv_box[key_rows, cols] = dkeys[shared].astype(bf16)
                kv_box[value_rows, cols] = dvalues[shared].astype(bf16)
                kv_copy(hp).start()
                dproject[:, key_cols] = turned_back(dkeys[pl.ds(rows, rows)])
                dproject[:, value_cols] = dvalues[pl.ds(rows, rows)].astype(bf16)

            poll_loop(15, width // 128, hp)
            return carry

        lax.fori_loop(0, width // 128, pair_back, 0)

        @pl.when(zero)
        def _():
            def finish(hp, carry):
                cols = pl.ds(pl.multiple_of(hp * 128, 128), 128)
                key_cols = pl.ds(pl.multiple_of(width + hp * 128, 128), 128)
                value_cols = pl.ds(pl.multiple_of(2 * width + hp * 128, 128), 128)
                kv_copy(hp).wait_recv()
                own_keys[shared, cols] += kv_box[key_rows, cols].astype(f32)
                own_values[shared, cols] += kv_box[value_rows, cols].astype(f32)
                dproject[:, key_cols] = turned_back(own_keys[:, cols])
                dproject[:, value_cols] = own_values[:, cols].astype(bf16)
                return carry

            lax.fori_loop(0, width // 128, finish, 0)

        @pl.when(one)
        def _():
            def finish(hp, carry):
                kv_copy(hp).wait_send()
                return carry

            lax.fori_loop(0, width // 128, finish, 0)

        poll(21)
        loads[1].wait()
        turned[...] = normed[...].T

        for j in range(w_in.shape[1] // width):
            def in_block(cb, carry, j=j):
                cols = pl.ds(pl.multiple_of(j * width + cb * 256, 256), 256)
                part = nn(turned[...], dproject[:, cols]).astype(bf16)
                for b in range(width // piece):
                    zi, yi, xi = b // (ny * nx), (b // nx) % ny, b % nx
                    for q in range(2):
                        grads[0, zi, yi, xi, j, pl.ds(pl.multiple_of((2 * cb + q) * piece, piece), piece)] = part[
                            b * piece : (b + 1) * piece, q * 128 : (q + 1) * 128]
                return carry

            lax.fori_loop(0, width // 256, in_block, 0)
            poll(22 + j)

        def dnormed_block(j, carry):
            cols = pl.ds(pl.multiple_of(j * 256, 256), 256)
            gfirst[:, cols] = nt(dproject[...], w_in[cols])
            return carry

        lax.fori_loop(0, width // 256, dnormed_block, 0)
        poll(25)

    pl.run_scoped(
        attention_scope,
        pltpu.VMEM(attn_in.shape, bf16), pltpu.VMEM(attn_out.shape, bf16),
        pltpu.VMEM((rows, width), bf16), pltpu.VMEM((rows, width), bf16),
        pltpu.VMEM((2 * rows, 128), f32), pltpu.VMEM((2 * rows, 128), f32),
        pltpu.VMEM((rows, width), f32), pltpu.VMEM((rows, width), f32),
        pltpu.VMEM((rows, 3 * width), bf16), pltpu.VMEM((width, rows), bf16),
    )

    def tail_scope(raw_h, raw_g, new_box, back_box, state, flat, sums_box):
        axes = [(s, [core], 2), (x, x_peers, nx), (y, y_peers, ny), (z, z_peers, nz)]

        def small_copies(k):
            first = sum(len(axis[1]) for axis in axes[:k])
            place, others, count = axes[k]
            return [
                pltpu.make_async_remote_copy(
                    small_box.at[k, place], small_box.at[k, place], small_send.at[first + i], small_recv.at[first + i],
                    device_id=peer, device_id_type=MESH)
                for i, peer in enumerate(others)
            ]

        def rows_of(j):
            line = small_rows[j : j + 1]
            count = line.shape[1]
            pieces = [line[:, k * 128 : (k + 1) * 128] for k in range(count // 128)]
            rest = count % 128
            if rest:
                pieces.append(jnp.concatenate([line[:, count - rest :], jnp.zeros((1, 128 - rest), f32)], axis=1))
            pieces.append(jnp.zeros((small_box.shape[2] - len(pieces), 128), f32))
            return jnp.concatenate(pieces, axis=0)

        def small_stage(v, k):
            if k > 0:
                for copy in small_copies(k - 1):
                    copy.wait()
                total = small_box[k - 1, 0]
                for j in range(1, axes[k - 1][2]):
                    total = total + small_box[k - 1, j]
            if k == len(axes):
                grad = total * (1.0 / token_count)
                new = adam_step(tuple(rows_of(j) for j in range(3)), grad)
                for k2, value in enumerate(new + (grad,)):
                    small_out[k2] = value
                return
            if k > 0:
                small_box[k, axes[k][0]] = total
            for copy in small_copies(k):
                copy.start()

        stages[SMALL] = small_stage
        stages[OWNER] = lambda v, c: owner_update((v,), state, flat, sums_box)
        loads = [load(streams, raw_h, load_sem.at[9]), load(cotangent, raw_g, load_sem.at[10]),
                 load(state_in, state, load_sem.at[0])]
        for copy in loads[:2]:
            copy.wait()
        poll(26)
        mixed_read = [sum(mix[i][j] * read_two[j] for j in range(NS)) for i in range(NS)]
        pairs = 33
        block = 32

        def out_copies(i, slot):
            r = pl.ds(i * block, block)
            return [pltpu.make_async_copy(new_box.at[slot], new_out.at[r], out_sem.at[0, slot]),
                    pltpu.make_async_copy(back_box.at[slot], stream_grad_out.at[r], out_sem.at[1, slot])]

        def body(i, carry):
            gain_one, sums = carry
            r = pl.ds(i * block, block)
            slot = i % 2

            @pl.when(i >= 2)
            def _():
                for copy in out_copies(i, slot):
                    copy.wait()

            hs, gs = unpacked(raw_h[r]), unpacked(raw_g[r])
            first_r, second_r, dread_r = first[r], second[r], dread[r]
            branch = sum(hs[k] * read_one[k] for k in range(NS))
            normal, scaling = normal_of(branch)
            grad = gfirst[r]
            gain_one = gain_one + jnp.sum((grad * normal).reshape(block // 8, 8, width), axis=0)
            scaled = grad * gains[0:1].astype(f32)
            centre = jnp.mean(scaled, axis=-1, keepdims=True)
            along = jnp.mean(scaled * normal, axis=-1, keepdims=True)
            dbranch = scaling * (scaled - centre - normal * along)
            back = [
                (sum(gs[j] * mix[k][j] for j in range(NS)) + dread_r * mixed_read[k] + dbranch * read_one[k]).astype(bf16)
                for k in range(NS)
            ]
            back_box[slot] = packed_streams(back)
            new = [
                (sum(hs[k] * mix[k][j] for k in range(NS)) + first_r * depth_one[j] + second_r * depth_two[j]).astype(bf16)
                for j in range(NS)
            ]
            new_box[slot] = packed_streams(new)
            for copy in out_copies(i, slot):
                copy.start()
            products = [(hs[a], gs[b]) for a in range(NS) for b in range(NS)]
            products += [(hs[a], dread_r) for a in range(NS)]
            products += [(hs[a], dbranch) for a in range(NS)]
            products += [(first_r, gs[b]) for b in range(NS)] + [(first_r, dread_r)]
            products += [(second_r, gs[b]) for b in range(NS)]
            new_sums = []
            for total, (a, b) in zip(sums, products):
                p = jnp.sum((a * b).reshape(block // 8, 8, width), axis=0)
                new_sums.append(total + sum(p[:, q * 128 : (q + 1) * 128] for q in range(width // 128)))
            poll_loop(27, rows // block - 1, i)
            return gain_one, tuple(new_sums)

        zero_tile = jnp.zeros((8, 128), f32)
        gain_one, sums = lax.fori_loop(
            0, rows // block, body, (jnp.zeros((8, width), f32), tuple(zero_tile for _ in range(pairs))))
        for i in (rows // block - 2, rows // block - 1):
            for copy in out_copies(i, i % 2):
                copy.wait()
        row = jnp.sum(gain_one, axis=0, keepdims=True)
        for k in range(width // 128):
            small_box[0, s, k : k + 1, :] = row[:, k * 128 : (k + 1) * 128]
        sums = [jnp.sum(jnp.sum(t, axis=0, keepdims=True), axis=1, keepdims=True) for t in sums]
        hg = [[sums[a * NS + b] for b in range(NS)] for a in range(NS)]
        h_read = sums[16:20]
        h_branch = sums[20:24]
        first_g, first_read, second_g = sums[24:28], sums[28], sums[29:33]
        lane = lax.broadcasted_iota(jnp.int32, (1, 128), 1)
        line = jnp.zeros((1, 128), f32)
        for i in range(NS):
            entries = [hg[i][j] + read_two[j] * h_read[i] for j in range(NS)]
            entries.append(h_branch[i])
            entries.append(first_g[i] + read_two[i] * first_read)
            entries.append(sum(mix[k][i] * h_read[k] for k in range(NS)) + depth_one[i] * first_read)
            entries.append(second_g[i])
            for j, value in enumerate(entries):
                line = jnp.where(lane == i * 2 * NS + j, value, line)
        last = 2 * width // 128
        small_box[0, s, last : last + 1, :] = line
        small_box[0, s, last + 1 :, :] = jnp.zeros((small_box.shape[2] - last - 1, 128), f32)

        poll(42)
        wait_sends()
        pltpu.make_async_copy(read.at[pl.ds(0, shard)], grad_out, store_sem.at[0]).wait()

    pl.run_scoped(
        tail_scope,
        pltpu.VMEM((rows, NS, width), bf16), pltpu.VMEM((rows, NS, width), bf16),
        pltpu.VMEM((2, 32, NS, width), bf16), pltpu.VMEM((2, 32, NS, width), bf16),
        pltpu.VMEM((3, shard, width), f32), pltpu.VMEM((6, shard, 128), f32),
        pltpu.VMEM((3, unit, 128), f32),
    )
    assert ids["send"] <= send_sem.shape[0] and ids["recv"] <= recv_sem.shape[0], ids


def finish_kernel(
    new_in, back_in, copy_in, grad_in, state_in,
    new_out, back_out, copy_out, weight_out, first_out, second_out, grad_out,
    new_box, back_box, copy_box, grad, state, weight, first, second, in_sem, out_sem, copy_sem,
):
    parts = 4
    rows = grad.shape[0] // parts
    tokens = new_box.shape[0] // parts

    def of_rows(k):
        return pl.ds(k * rows, rows)

    def of_tokens(k):
        return pl.ds(k * tokens, tokens)

    def loads(k):
        return [
            pltpu.make_async_copy(grad_in.at[of_rows(k)], grad.at[of_rows(k)], in_sem.at[0, k]),
            pltpu.make_async_copy(state_in.at[:, of_rows(k)], state.at[:, of_rows(k)], in_sem.at[1, k]),
            pltpu.make_async_copy(new_in.at[of_tokens(k)], new_box.at[of_tokens(k)], in_sem.at[2, k]),
            pltpu.make_async_copy(back_in.at[of_tokens(k)], back_box.at[of_tokens(k)], in_sem.at[3, k]),
        ]

    def stores(k):
        pairs = [(box.at[of_rows(k)], out.at[of_rows(k)]) for box, out in (
            (grad, grad_out), (weight, weight_out), (first, first_out), (second, second_out))]
        pairs += [(new_box.at[of_tokens(k)], new_out.at[of_tokens(k)]), (back_box.at[of_tokens(k)], back_out.at[of_tokens(k)])]
        return [pltpu.make_async_copy(a, b, out_sem.at[i, k]) for i, (a, b) in enumerate(pairs)]

    pieces = copy_sem.shape[1]
    copy_rows = copy_box.shape[0] // pieces

    def move(k, out):
        r = pl.ds(k * copy_rows, copy_rows)
        if out:
            return pltpu.make_async_copy(copy_box.at[r], copy_out.at[r], copy_sem.at[1, k])
        return pltpu.make_async_copy(copy_in.at[r], copy_box.at[r], copy_sem.at[0, k])

    for k in range(parts):
        for copy in loads(k):
            copy.start()
    for k in range(pieces):
        move(k, False).start()
    for k in range(parts):
        for copy in loads(k):
            copy.wait()

        def body(i, carry, k=k):
            r = pl.ds(k * rows + i * 16, 16)
            weight[r], first[r], second[r] = adam_step((state[0, r], state[1, r], state[2, r]), grad[r])
            return carry

        lax.fori_loop(0, rows // 16, body, 0)
        for copy in stores(k):
            copy.start()
    for k in range(pieces):
        move(k, False).wait()
        move(k, True).start()
    for k in range(parts):
        for copy in stores(k):
            copy.wait()
    for k in range(pieces):
        move(k, True).wait()


def finish(new, back, copy, grad, big_state):
    shape = jax.ShapeDtypeStruct
    hbm = pl.BlockSpec(memory_space=pl.ANY)
    like = shape(grad.shape, grad.dtype)
    box = pltpu.VMEM(grad.shape, grad.dtype)
    return pl.pallas_call(
        finish_kernel,
        out_shape=[shape(new.shape, new.dtype), shape(back.shape, back.dtype), shape(copy.shape, copy.dtype),
                   like, like, like, like],
        in_specs=[hbm] * 5,
        out_specs=[hbm] * 7,
        scratch_shapes=[
            pltpu.VMEM(new.shape, new.dtype), pltpu.VMEM(back.shape, back.dtype),
            pltpu.VMEM(copy.shape, copy.dtype), box, pltpu.VMEM(big_state.shape, big_state.dtype), box, box, box,
            pltpu.SemaphoreType.DMA((4, 4)), pltpu.SemaphoreType.DMA((6, 4)), pltpu.SemaphoreType.DMA((2, 12)),
        ],
        compiler_params=pltpu.CompilerParams(vmem_limit_bytes=60 * 2**20),
        name="finish",
    )(new, back, copy, grad, big_state)


def layer_part(dims, token_count, docs, small_state, gains, streams, cotangent, weights, big_state):
    attn_in, attn_out, ffn_in, ffn_out = weights
    nz, ny, nx = dims
    rows, width = streams.shape[0], attn_out.shape[0]
    shard = big_state.shape[1]
    unit, half, hidden = 2 * shard, shard, ffn_out.shape[0]
    bf16, f32 = jnp.bfloat16, jnp.float32
    shape = jax.ShapeDtypeStruct
    cos_table, sin_table = rope_constants(6 * EIGHTH, HD)
    small_count = small_state.shape[1]
    small_shape = (-(-small_count // 1024) * 8, 128)
    smem = pl.BlockSpec(memory_space=pltpu.SMEM)
    vmem = pl.BlockSpec(memory_space=pltpu.VMEM)
    hbm = pl.BlockSpec(memory_space=pl.ANY)
    state_shape = shape((shard, width), f32)
    stream_shape = shape((rows, NS, width), bf16)
    outs = pl.pallas_call(
        functools.partial(layer_kernel, dims, token_count),
        out_shape=[
            stream_shape, stream_shape, shape((2, nz, ny, nx, shard, width), bf16),
            state_shape, shape((4,) + small_shape, f32),
            shape((nz, ny, nx, 3, unit, 128), bf16),
        ],
        in_specs=[smem, smem, vmem, vmem] + [hbm] * 9,
        out_specs=[hbm] * 4 + [vmem, hbm],
        scratch_shapes=[
            pltpu.VMEM((2, nz, ny, nx, 3, unit, 128), bf16),
            pltpu.VMEM((max(nx - 1, 1), nz, ny, 3, half, 128), bf16),
            pltpu.VMEM((max(ny - 1, 1), nz, nx, 3, half, 128), bf16),
            pltpu.VMEM((max(ny - 1, 1), nz, 3, half, 128), bf16),
            pltpu.VMEM((max(nx - 1, 1), nz, 3, half, 128), bf16),
            pltpu.VMEM((2, 3, 3, unit, 128), bf16),
            pltpu.VMEM((nz // 2, ny, nx, unit, 128), bf16),
            pltpu.VMEM((6 * EIGHTH, width), bf16),
            pltpu.VMEM((rows, width), f32), pltpu.VMEM((rows, width), f32), pltpu.VMEM((rows, width), f32),
            pltpu.VMEM((rows, width), f32), pltpu.VMEM((rows, width), f32),
            pltpu.VMEM((rows, width), bf16), pltpu.VMEM((rows, width), bf16),
            pltpu.VMEM((2 * rows, width), bf16), pltpu.VMEM((2 * rows, width), bf16),
            pltpu.VMEM((rows, width), bf16), pltpu.VMEM((32, 2 * EIGHTH), f32),
            pltpu.VMEM((rows, 128), f32), pltpu.VMEM((rows, 128), f32), pltpu.VMEM((2, EIGHTH, EIGHTH), f32),
            pltpu.VMEM((shard, width), bf16),
            pltpu.VMEM((4, max(2, nx, ny, nz)) + small_shape, f32),
            pltpu.SemaphoreType.DMA((8,)), pltpu.SemaphoreType.DMA((8,)),
            pltpu.SemaphoreType.DMA((260,)), pltpu.SemaphoreType.DMA((220,)),
            pltpu.SemaphoreType.DMA((16,)), pltpu.SemaphoreType.DMA((2, 3, 8)),
            pltpu.SemaphoreType.DMA((2,)), pltpu.SemaphoreType.DMA((5,)), pltpu.SemaphoreType.DMA((2, 2)),
            pltpu.SemaphoreType.DMA((8,)), pltpu.SemaphoreType.DMA((8,)),
        ],
        compiler_params=pltpu.CompilerParams(
            collective_id=1, has_side_effects=True, vmem_limit_bytes=255 * 2**18
        ),
        name="layer_step",
    )(docs, small_state, gains, small_state, streams, cotangent, attn_in, attn_out, ffn_in, ffn_out, big_state,
      jnp.asarray(cos_table), jnp.asarray(sin_table))
    small_out = outs[4].reshape(4, -1)[:, :small_count]
    copy = outs[2].reshape(-1, width)
    new, back, copy, weight_new, first_new, second_new, grad = finish(outs[0], outs[1], copy, outs[3], big_state)
    return new, back, copy, weight_new, first_new, second_new, grad, small_out


def torus(mesh):
    wide = mesh.shape["wide"]
    where = [getattr(d, "coords", None) for d in mesh.devices.flat]
    if all(c is not None for c in where):
        x, y, z = (len({c[i] for c in where}) for i in range(3))
        if x * y * z == wide:
            return z, y, x
    known = {16: (4, 2, 2), 64: (4, 4, 4)}
    return known.get(wide, (wide, 1, 1))


def sync_kernel(
    dims, rows, half, lr_consts,
    grads, small_in, state_in,
    copy_out, weight_out, first_out, second_out, grad_out, small_out,
    acc, from_core, from_a0, from_a1, from_b0, from_b1, from_c,
    state, new_w, new_m, new_v, new_g, low, small_box,
    load_sem, store_sem, send_sem, recv_sem, small_send, small_recv,
):
    nz, ny, nx = dims
    chunk = 2 * half
    chunks = rows // chunk
    s = lax.axis_index("seq")
    w = lax.axis_index("wide")
    z, y, x = w // (ny * nx), (w // nx) % ny, w % nx

    def chip(cz, cy, cx):
        return (s, (cz * ny + cy) * nx + cx)

    core = (1 - s, w)
    z_peers = [chip((z + d) % nz, y, x) for d in range(1, nz)]
    y_peers = [chip(z, (y + d) % ny, x) for d in range(1, ny)]
    x_peers = [chip(z, y, (x + d) % nx) for d in range(1, nx)]
    peers = [core] + z_peers + y_peers + x_peers

    barrier = pltpu.get_barrier_semaphore()
    for peer in peers:
        pl.semaphore_signal(barrier, inc=1, device_id=peer, device_id_type=MESH)

    loads = [
        pltpu.make_async_copy(
            grads.at[s, :, :, :, pl.ds(c * chunk, chunk)],
            acc.at[:, :, :, pl.ds(c * chunk, chunk)],
            load_sem.at[c],
        )
        for c in range(chunks)
    ]
    for copy in loads:
        copy.start()
    state_load = pltpu.make_async_copy(state_in, state, load_sem.at[chunks])
    state_load.start()
    pl.semaphore_wait(barrier, len(peers))

    sends = []
    counter = [0]

    def remote(src, dst, peer):
        i = counter[0]
        counter[0] += 1
        copy = pltpu.make_async_remote_copy(
            src, dst, send_sem.at[i], recv_sem.at[i], device_id=peer, device_id_type=MESH
        )
        copy.start()
        sends.append(copy)
        return copy

    def lo(c):
        return pl.ds(c * chunk, half)

    def hi(c):
        return pl.ds(c * chunk + half, half)

    def both(c):
        return pl.ds(c * chunk, chunk)

    def packed(c):
        return pl.ds(c * half, half)

    f32 = jnp.float32

    def add_into(count, where, terms):
        def body(i, carry):
            ref, index = where(i)
            total = ref[index].astype(f32)
            for term_ref, term_index in terms(i):
                total = total + term_ref[term_index].astype(f32)
            ref[index] = total.astype(ref.dtype)
            return carry

        lax.fori_loop(0, count, body, 0)

    def small_step(k, mine, others, count):
        copies = []
        for j, peer in enumerate(others):
            i = small_index[0]
            small_index[0] += 1
            copy = pltpu.make_async_remote_copy(
                small_box.at[k, mine], small_box.at[k, mine], small_send.at[i], small_recv.at[i],
                device_id=peer, device_id_type=MESH,
            )
            copy.start()
            copies.append(copy)
        return copies

    def small_sum(k, copies, count):
        for copy in copies:
            copy.wait()
        total = small_box[k, 0]
        for j in range(1, count):
            total = total + small_box[k, j]
        return total

    small_index = [0]
    axes = [(s, [core], 2), (x, x_peers, nx), (y, y_peers, ny), (z, z_peers, nz)]
    small_box[0, s] = small_in[...]
    small_copies = [small_step(0, s, [core], 2)]

    def small_stage(k):
        total = small_sum(k, small_copies[k], axes[k][2])
        if k + 1 < len(axes):
            place, others, count = axes[k + 1]
            small_box[k + 1, place] = total
            small_copies.append(small_step(k + 1, place, others, count))
        else:
            small_out[...] = total

    state_done = [False]
    flying = {}

    def stage(k, c):
        if k == 0:
            loads[c].wait()
            for copy in flying[0, c]:
                copy.wait_recv()

            def where(i):
                return acc, (i // (ny * nx), (i // nx) % ny, i % nx, both(c))

            def terms(i):
                return [(from_core, (i // (ny * nx), (i // nx) % ny, i % nx, both(c)))]

            add_into(nz * ny * nx, where, terms)
            out = []
            for d in range(1, nx):
                out.append(remote(
                    acc.at[:, :, (x + d) % nx, lo(c)], from_a0.at[d - 1, :, :, packed(c)], x_peers[d - 1]))
            for d in range(1, ny):
                out.append(remote(
                    acc.at[:, (y + d) % ny, :, hi(c)], from_a1.at[d - 1, :, :, packed(c)], y_peers[d - 1]))
            flying[1, c] = out
        elif k == 1:
            for copy in flying[1, c]:
                copy.wait_recv()
            add_into(
                nz * ny,
                lambda i: (acc, (i // ny, i % ny, x, lo(c))),
                lambda i: [(from_a0, (d, i // ny, i % ny, packed(c))) for d in range(nx - 1)],
            )
            add_into(
                nz * nx,
                lambda i: (acc, (i // nx, y, i % nx, hi(c))),
                lambda i: [(from_a1, (d, i // nx, i % nx, packed(c))) for d in range(ny - 1)],
            )
            out = []
            for d in range(1, ny):
                out.append(remote(
                    acc.at[:, (y + d) % ny, x, lo(c)], from_b0.at[d - 1, :, packed(c)], y_peers[d - 1]))
            for d in range(1, nx):
                out.append(remote(
                    acc.at[:, y, (x + d) % nx, hi(c)], from_b1.at[d - 1, :, packed(c)], x_peers[d - 1]))
            flying[2, c] = out
        elif k == 2:
            for copy in flying[2, c]:
                copy.wait_recv()
            add_into(
                nz,
                lambda i: (acc, (i, y, x, lo(c))),
                lambda i: [(from_b0, (d, i, packed(c))) for d in range(ny - 1)],
            )
            add_into(
                nz,
                lambda i: (acc, (i, y, x, hi(c))),
                lambda i: [(from_b1, (d, i, packed(c))) for d in range(nx - 1)],
            )
            out = []
            for d in range(1, nz):
                out.append(remote(
                    acc.at[(z + d) % nz, y, x, both(c)], from_c.at[d - 1, both(c)], z_peers[d - 1]))
            flying[3, c] = out
        elif k == 3:
            for copy in flying[3, c]:
                copy.wait_recv()
            if not state_done[0]:
                state_load.wait()
                state_done[0] = True
            step = 16

            def body(i, carry):
                r = pl.ds(c * chunk + i * step, step)
                total = acc[z, y, x, r].astype(f32)
                for d in range(nz - 1):
                    total = total + from_c[d, r].astype(f32)
                grad = total * lr_consts
                w_new, m_new, v_new = adam_step((state[0, r], state[1, r], state[2, r]), grad)
                new_g[r] = grad
                new_w[r] = w_new
                new_m[r] = m_new
                new_v[r] = v_new
                low[r] = w_new.astype(low.dtype)
                return carry

            lax.fori_loop(0, chunk // step, body, 0)
            out = []
            for peer in z_peers:
                out.append(remote(low.at[both(c)], copy_out.at[s, z, y, x, both(c)], peer))
            own = pltpu.make_async_copy(low.at[both(c)], copy_out.at[s, z, y, x, both(c)], store_sem.at[0, c])
            own.start()
            for j, (a, b) in enumerate(((new_w, weight_out), (new_m, first_out), (new_v, second_out), (new_g, grad_out))):
                st = pltpu.make_async_copy(a.at[both(c)], b.at[both(c)], store_sem.at[j + 1, c])
                st.start()
                stores.append(st)
            flying[4, c] = (out, own)
        elif k == 4:
            out, own = flying[4, c]
            own.wait()
            for copy in out:
                copy.wait_recv()
            nxt = []
            for peer in y_peers:
                nxt.append(remote(copy_out.at[s, :, y, x, lo(c)], copy_out.at[s, :, y, x, lo(c)], peer))
            for peer in x_peers:
                nxt.append(remote(copy_out.at[s, :, y, x, hi(c)], copy_out.at[s, :, y, x, hi(c)], peer))
            flying[5, c] = nxt
        elif k == 5:
            for copy in flying[5, c]:
                copy.wait_recv()
            nxt = []
            for peer in x_peers:
                nxt.append(remote(copy_out.at[s, :, :, x, lo(c)], copy_out.at[s, :, :, x, lo(c)], peer))
            for peer in y_peers:
                nxt.append(remote(copy_out.at[s, :, y, :, hi(c)], copy_out.at[s, :, y, :, hi(c)], peer))
            flying[6, c] = nxt
        elif k == 6:
            for copy in flying[6, c]:
                copy.wait_recv()
            flying[7, c] = [
                remote(copy_out.at[s, :, :, :, both(c)], copy_out.at[s, :, :, :, both(c)], core)]
        elif k == 7:
            for copy in flying[7, c]:
                copy.wait_recv()

    stores = []
    for c in range(chunks):
        flying[0, c] = [remote(
            grads.at[1 - s, :, :, :, both(c)], from_core.at[:, :, :, both(c)], core)]
    stages = 8
    for t in range(chunks + stages - 1):
        for k in reversed(range(stages)):
            c = t - k
            if 0 <= c < chunks:
                stage(k, c)
        if 1 <= t <= 4:
            small_stage(t - 1)
    for copy in sends:
        copy.wait_send()
    for copy in stores:
        copy.wait()


def sync_grads(dims, flat_low, small_local, big_state, token_count):
    nz, ny, nx = dims
    wide = nz * ny * nx
    model_width = flat_low.shape[1]
    rows = big_state.shape[1]
    half = next(h for h in (48, 32, 16) if rows % (2 * h) == 0)
    chunks = rows // (2 * half)
    bf16, f32 = jnp.bfloat16, jnp.float32
    copies = chunks * (2 + 4 * (nx - 1) + 4 * (ny - 1) + 2 * (nz - 1))
    small_copies = 1 + (nx - 1) + (ny - 1) + (nz - 1)
    hbm = pl.BlockSpec(memory_space=pl.ANY)
    vmem = pl.BlockSpec(memory_space=pltpu.VMEM)
    state_shape = jax.ShapeDtypeStruct((rows, model_width), f32)
    small_shape = small_local.shape
    outs = pl.pallas_call(
        functools.partial(sync_kernel, dims, rows, half, 1.0 / token_count),
        out_shape=[
            jax.ShapeDtypeStruct((2, nz, ny, nx, rows, model_width), bf16),
            state_shape, state_shape, state_shape, state_shape,
            jax.ShapeDtypeStruct(small_shape, f32),
        ],
        in_specs=[hbm, vmem, hbm],
        out_specs=[hbm] * 5 + [vmem],
        scratch_shapes=[
            pltpu.VMEM((nz, ny, nx, rows, model_width), bf16),
            pltpu.VMEM((nz, ny, nx, rows, model_width), bf16),
            pltpu.VMEM((max(nx - 1, 1), nz, ny, rows // 2, model_width), bf16),
            pltpu.VMEM((max(ny - 1, 1), nz, nx, rows // 2, model_width), bf16),
            pltpu.VMEM((max(ny - 1, 1), nz, rows // 2, model_width), bf16),
            pltpu.VMEM((max(nx - 1, 1), nz, rows // 2, model_width), bf16),
            pltpu.VMEM((max(nz - 1, 1), rows, model_width), bf16),
            pltpu.VMEM((3, rows, model_width), f32),
            pltpu.VMEM((rows, model_width), f32),
            pltpu.VMEM((rows, model_width), f32),
            pltpu.VMEM((rows, model_width), f32),
            pltpu.VMEM((rows, model_width), f32),
            pltpu.VMEM((rows, model_width), bf16),
            pltpu.VMEM((4, max(2, nx, ny, nz)) + small_shape, f32),
            pltpu.SemaphoreType.DMA((chunks + 1,)),
            pltpu.SemaphoreType.DMA((5, chunks)),
            pltpu.SemaphoreType.DMA((copies,)),
            pltpu.SemaphoreType.DMA((copies,)),
            pltpu.SemaphoreType.DMA((small_copies,)),
            pltpu.SemaphoreType.DMA((small_copies,)),
        ],
        compiler_params=pltpu.CompilerParams(
            collective_id=1, has_side_effects=True, vmem_limit_bytes=56 * 2**20
        ),
        name="sync_grads",
    )(
        flat_low.reshape(2, nz, ny, nx, rows, model_width), small_local, big_state
    )
    return (outs[0].reshape(2 * wide * rows, model_width),) + tuple(outs[1:])


def on_device(
    dims,
    streams,
    cotangent,
    doc_lengths,
    attn_in,
    attn_out,
    ffn_in,
    ffn_out,
    norm_gains,
    big_state,
    small_state,
):
    row_count = streams.shape[1]
    model_width = attn_out.shape[0]
    fits = (
        big_state.shape[1] == 384 and model_width == 768 and row_count == 512
        and ffn_out.shape[0] == 3072 and dims == (4, 2, 2)
    )
    if fits:
        token_count = 2 * row_count * lax.axis_size("wide")
        result, stream_grad, gathered, weight_new, first_new, second_new, owned_grads, small_out = layer_part(
            dims, token_count, doc_lengths, small_state, norm_gains.T, streams[0], cotangent[0],
            (attn_in, attn_out, ffn_in, ffn_out), big_state,
        )
        gains_copy = small_out[0, : 2 * model_width].reshape(2, model_width).T.astype(jnp.bfloat16)
        return (
            result[None], stream_grad[None], weight_new, first_new, second_new, owned_grads,
            small_out[0], small_out[1], small_out[2], small_out[3], gathered, gains_copy,
        )
    member = lax.axis_index("seq")
    token_total = row_count * lax.axis_size("seq")
    token_count = token_total * lax.axis_size("wide")
    segment, position = doc_layout(doc_lengths[0], token_total)
    own_start = member * row_count
    own_index = own_start + jnp.arange(row_count, dtype=jnp.int32)
    seg_query = lax.dynamic_slice_in_dim(segment, own_start, row_count)
    pos_query = lax.dynamic_slice_in_dim(position, own_start, row_count)
    padded_seg = jnp.concatenate([jnp.full((row_count,), -1, jnp.int32), segment])
    key_seg = lax.dynamic_slice_in_dim(padded_seg, own_start, 2 * row_count)
    key_index = own_start - row_count + jnp.arange(2 * row_count, dtype=jnp.int32)
    allowed = (key_seg[None, :] == seg_query[:, None]) & (key_index[None, :] <= own_index[:, None])
    cosine, sine_table = rope_tables(pos_query, HD)
    weights = (attn_in, attn_out, ffn_in, ffn_out)
    gain_values = norm_gains.astype(jnp.float32)
    mixing = small_state[0, 2 * model_width :].reshape(NS, NS + 4)
    stream_values = streams[0].astype(jnp.float32)
    result, saved = forward_layer(
        stream_values, weights, gain_values, mixing, allowed, cosine, sine_table
    )
    grad_out = cotangent[0].astype(jnp.float32)
    stream_grad, matrix_grads, gains_local, mixing_local = backward_layer(
        stream_values, grad_out, weights, gain_values, mixing, cosine, sine_table, saved
    )
    flat_low = jnp.concatenate(
        [grad.astype(jnp.bfloat16).reshape(-1, model_width) for grad in matrix_grads], axis=0
    )
    small_local = jnp.concatenate([gains_local.T.reshape(-1), mixing_local.reshape(-1)])
    small_count = small_local.shape[0]
    padded = jnp.pad(small_local, (0, -small_count % 1024)).reshape(-1, 128)
    gathered, weight_new, first_new, second_new, owned_grads, small_total = sync_grads(
        dims, flat_low, padded, big_state, token_count
    )
    small_grads = small_total.reshape(-1)[:small_count] / token_count
    small_weight, small_first, small_second = adam_step(small_state, small_grads)
    gains_copy = small_weight[: 2 * model_width].reshape(2, model_width).T.astype(jnp.bfloat16)
    return (
        result.astype(jnp.bfloat16)[None],
        stream_grad.astype(jnp.bfloat16)[None],
        weight_new,
        first_new,
        second_new,
        owned_grads,
        small_weight,
        small_first,
        small_second,
        small_grads,
        gathered,
        gains_copy,
    )


def solution(mesh):
    in_specs = (
        P("wide", "seq", None, None),
        P("wide", "seq", None, None),
        P("wide", None),
        P(),
        P(),
        P(),
        P(),
        P(),
        P(None, ("seq", "wide"), None),
        P(),
    )
    out_specs = (
        P("wide", "seq", None, None),
        P("wide", "seq", None, None),
        P(("seq", "wide"), None),
        P(("seq", "wide"), None),
        P(("seq", "wide"), None),
        P(("seq", "wide"), None),
        P(),
        P(),
        P(),
        P(),
        P(),
        P(),
    )
    return jax.shard_map(
        functools.partial(on_device, torus(mesh)), mesh=mesh, in_specs=in_specs, out_specs=out_specs, check_vma=False
    )
```
